32 devices in a mesh: dp: 4 (over y, x), expert: 8 (over z, core).
Axes of the slice: x: 2, y: 2, z: 4, core: 2. Of those that a mesh axis runs over, the one named last changes fastest.
Arguments:
- hidden_in: bfloat16 [8, 1024, 1024], P('expert', 'dp')
- lengths: int32 [8], P('expert'), may hold values from 128 to 1024, as said below
- value_pick: int32 [8, 1024, 4, 2], P('expert', 'dp'), may hold values from 0 to 4, all different within a row
- output_pick: int32 [8, 1024, 4, 2], P('expert', 'dp'), may hold values from 0 to 4, all different within a row
- expert_pick: int32 [8, 1024, 16], P('expert', 'dp'), may hold values from 0 to 47, all different within a row; in each aligned block of 256 rows (0 to 255, 256 to 511, ..., all dimensions but the last counted through in order) at most 128 rows name the same one
- query_weight: bfloat16 [1024, 512], replicated, may hold values from -0.25 to 0.25
- key_weight: bfloat16 [1024, 512], replicated, may hold values from -0.25 to 0.25
- value_weight: bfloat16 [1024, 2560], replicated, may hold values from -0.1875 to 0.1875
- output_weight: bfloat16 [2560, 1024], replicated, may hold values from -2 to 2
- value_router: bfloat16 [1024, 20], replicated, may hold values from -0.125 to 0.125
- output_router: bfloat16 [1024, 20], replicated, may hold values from -0.125 to 0.125
- expert_router: bfloat16 [1024, 48], replicated
- attention_gain: bfloat16 [1024], replicated, may hold values from 0.5 to 1.5
- feedforward_gain: bfloat16 [1024], replicated, may hold values from 0.5 to 1.5
- expert_up: bfloat16 [48, 1024, 128], P('expert'), may hold values from -0.1875 to 0.1875
- expert_down: bfloat16 [48, 128, 1024], P('expert'), may hold values from -0.5 to 0.5
- cotangent: bfloat16 [8, 1024, 1024], P('expert', 'dp'), may hold values from -6 to 6
Outputs:
- block_out: bfloat16 [8, 1024, 1024], P('expert', 'dp')
- grad_input: float32 [8, 1024, 1024], P('expert', 'dp')
- grad_query_weight: float32 [1024, 512], P(('dp', 'expert'))
- grad_key_weight: float32 [1024, 512], P(('dp', 'expert'))
- grad_value_weight: float32 [1024, 2560], P(('dp', 'expert'))
- grad_output_weight: float32 [2560, 1024], P(None, ('dp', 'expert'))
- grad_value_router: float32 [1024, 20], P(('dp', 'expert'))
- grad_output_router: float32 [1024, 20], P(('dp', 'expert'))
- grad_expert_router: float32 [1024, 48], P(('dp', 'expert'))
- grad_attention_gain: float32 [1024], P(('dp', 'expert'))
- grad_feedforward_gain: float32 [1024], P(('dp', 'expert'))
- grad_expert_up: float32 [48, 1024, 128], P('expert', 'dp')
- grad_expert_down: float32 [48, 128, 1024], P('expert', None, 'dp')
- residual_norms: float32 [4], replicated
The draws below stay inside these ranges and needn't reach their ends.
Inputs may be any that keep to these rules, and one draw needn't show every extreme that they name: `lengths`: in every draw one bucket holds a sequence of 1024 positions and another one of 128. `value_pick`: the experts that a token names for one head are different. `output_pick`: the experts that a token names for one head are different. `expert_pick`: each token names 16 different experts; among the 256 tokens of one device no expert is named more than 128 times, and in every draw some expert exactly 128 times; every expert is named somewhere.
All inputs are finite; a program needn't handle non-finite values.
Results may differ from the reference program's by a relative error of at most 0.018.
Values may be sent and summed in bfloat16 or wider, within the bound.
A program may use at most 192 MiB of HBM per device.

```python
import math
import jax
import jax.numpy as jnp
import numpy as np
from jax import lax

D = 1024
HEADS = 4
HEAD_DIM = 128
VE = 5
FE = 128
PICK = 2
TOPK = 16
TOK_DEV = 256
MINLEN = 128
SEQ = 1024
BUCKETS = 8
EXPERTS = 48
CAP = 128
N_DP = 4


def draw_hidden_in(key, part):
    first, second = jax.random.split(key)
    rising = jnp.sqrt(1.0 + 2.0 * jnp.arange(BUCKETS, dtype=jnp.float32) / max(BUCKETS - 1, 1))
    row_scale = 10.0 ** (jax.random.uniform(second, (BUCKETS, SEQ, 1), jnp.float32) - 0.5)
    base = jnp.clip(jax.random.normal(first, (BUCKETS, SEQ, D), jnp.float32), -6.0, 6.0)
    return (base * row_scale * rising[:, None, None]).astype(jnp.bfloat16)


def draw_lengths(key, part):
    first, second, third = jax.random.split(key, 3)
    drawn = jax.random.randint(first, (BUCKETS,), MINLEN, SEQ + 1)
    longest = jax.random.randint(second, (), 0, BUCKETS)
    shortest = (longest + jax.random.randint(third, (), 1, BUCKETS)) % BUCKETS
    return drawn.at[longest].set(SEQ).at[shortest].set(MINLEN).astype(jnp.int32)


def draw_expert_router(key, part):
    key = jax.random.fold_in(key, 11)
    first, second = jax.random.split(key)
    base = jnp.clip(jax.random.normal(first, (D, EXPERTS), jnp.float32), -6.0, 6.0) * (4.0 * D) ** (-0.5)
    column_part = jnp.clip(jax.random.normal(second, (1, EXPERTS), jnp.float32), -3.0, 3.0) * 0.04
    return (base + column_part).astype(jnp.bfloat16)


def with_spikes(values, key, source, target, parts, factor):
    owner, partner = [(jnp.arange(values.shape[position]) // (values.shape[position] // parts)).reshape([-1 if axis == position else 1 for axis in range(values.ndim)]) for position in (source, target)]
    chosen = jax.random.permutation(key, parts)[partner]
    strong = (owner == chosen) | (owner == (partner + parts // 2) % parts)
    return jnp.where(strong, factor * values, values)


def levels(rng, dims, pieces, smallest, largest):
    gain = 1.0
    for axis_at, blocks in pieces:
        draws = jax.random.uniform(jax.random.fold_in(jax.random.fold_in(rng, 6), axis_at), (blocks,), jnp.float32, smallest / len(pieces), largest / len(pieces))
        gain = gain * jnp.repeat(jnp.exp(draws), dims[axis_at] // blocks).reshape((-1,) + (1,) * (len(dims) - 1 - axis_at))
    return gain


def choose_distinct(stream_key, rows, number_of, top, lift):
    ranking = jax.random.permutation(jax.random.fold_in(stream_key, 1), number_of)
    boost = ranking
    for power in range(3):
        boost = boost * boost // number_of
    boost = boost * lift // number_of
    tickets = jax.random.randint(jax.random.fold_in(stream_key, 2), (rows, number_of), 0, 4096) + boost
    fixed_rows = jax.random.permutation(jax.random.fold_in(stream_key, 3), rows)[jnp.arange(number_of) % rows]
    tickets = jnp.where(jnp.arange(rows)[:, None] == fixed_rows[None, :], 1 << 14, tickets)
    score = tickets * number_of + jnp.arange(number_of)
    return lax.top_k(score.astype(jnp.int32), top)[1].astype(jnp.int32)


def shared_out(own_key, own, number, rows, amount, top, bound, slope):
    sequence = jax.random.permutation(own_key, amount)
    crowded, common = shares(amount, rows * top, bound, slope, True), shares(amount, rows * top, bound, slope, False)
    places = jnp.arange(amount)

    def named(sizes, rotation):
        used = int((sizes > 0).sum())
        fixed = max(1, used // 4)
        shifted = fixed + (places - fixed + rotation * (used - fixed)) % max(1, amount - fixed)
        return jnp.zeros((amount,), jnp.int32).at[sequence[jnp.where(places < fixed, places, shifted)]].set(jnp.asarray(sizes, jnp.int32))

    sizes = jnp.where(number % 4 == 0, named(crowded, number // 4), named(common, number - number // 4 - 1))
    mixed = jax.random.permutation(jax.random.fold_in(own, 3), amount)
    donor, receiver = mixed[0:amount // 2 * 2:2], mixed[1:amount // 2 * 2:2]
    margin = jnp.minimum(sizes[donor] - 1, bound - sizes[receiver]) // 2
    margin = jnp.where((donor == sequence[0]) | (receiver == sequence[0]) | (sizes[receiver] == 0), 0, jnp.maximum(margin, 0))
    shifted = jax.random.randint(jax.random.fold_in(own, 4), (amount // 2,), 0, 1 << 20) % (margin + 1)
    sizes = sizes.at[donor].add(-shifted).at[receiver].add(shifted)
    members = jnp.searchsorted(jnp.cumsum(sizes), jnp.arange(rows * top), side="right").astype(jnp.int32)
    table = members.reshape(top, rows).T
    table = table[jax.random.permutation(jax.random.fold_in(own, 1), rows)]
    rotation = jax.random.randint(jax.random.fold_in(own, 2), (rows, 1), 0, top)
    return jnp.take_along_axis(table, (jnp.arange(top)[None, :] + rotation) % top, axis=1)


def shares(number_of, total, reach, slope, full):
    weights = [(1 << 20) // math.isqrt(standing ** slope) + 1 for standing in range(1, number_of + 1)]
    largest = reach if full else min(reach, max(-(-total // number_of), total * weights[0] // sum(weights)))
    least = 1 if total - largest >= number_of - 1 else 0
    counts, spare = [largest] + [least] * (number_of - 1), total - largest - least * (number_of - 1)
    while spare > 0:
        free = [i for i in range(1, number_of) if counts[i] < largest] or [i for i in range(1, number_of) if counts[i] < reach]
        pool, budget = sum([weights[i] for i in free]), spare
        for i in free:
            more = min(reach - counts[i], max(1, budget * weights[i] // pool), spare)
            counts[i] = counts[i] + more
            spare = spare - more
    return np.array(counts)


def centred(own_key, extent, scale, most, shards=(), held_as=jnp.bfloat16):
    level = levels(own_key, extent, shards, -0.22, 0.18) if shards else 1.0
    values = jax.random.normal(own_key, extent, jnp.float32) * scale * level
    return jnp.minimum(jnp.maximum(values, -most), most).astype(held_as)


def heavy_noise(stream_key, shape, deviation, limit, cuts, heavy, kind=jnp.bfloat16):
    entries = deviation * jax.random.normal(stream_key, shape, jnp.float32)
    if cuts:
        entries = entries * levels(stream_key, shape, cuts, -0.22, 0.18)
    return jnp.clip(with_spikes(entries, jax.random.fold_in(stream_key, 3), *heavy), -limit, limit).astype(kind)


def setup_inputs(seed: int = 0) -> dict:
    key_list = jax.random.split(jax.random.key(seed), 18)
    hidden_in = draw_hidden_in(jax.random.fold_in(key_list[17], 71), 0)
    lengths = draw_lengths(jax.random.fold_in(key_list[17], 71), 0)
    value_pick = choose_distinct(key_list[2], BUCKETS * SEQ * HEADS, VE, PICK, 0).reshape((BUCKETS, SEQ, HEADS, PICK))
    output_pick = choose_distinct(key_list[3], BUCKETS * SEQ * HEADS, VE, PICK, 0).reshape((BUCKETS, SEQ, HEADS, PICK))
    expert_pick_keys = jax.random.split(jax.random.fold_in(key_list[4], 1), BUCKETS * SEQ // TOK_DEV)
    expert_pick_turns = jax.random.permutation(jax.random.fold_in(key_list[4], 3), BUCKETS * SEQ // TOK_DEV)
    expert_pick = jax.vmap(lambda own, number: shared_out(jax.random.fold_in(key_list[4], 2), own, number, TOK_DEV, EXPERTS, TOPK, CAP, 1))(expert_pick_keys, expert_pick_turns).reshape((BUCKETS, SEQ, TOPK))
    query_weight = centred(key_list[5], (D, HEADS * HEAD_DIM), (D // 2) ** -0.5, 0.25)
    key_weight = centred(key_list[6], (D, HEADS * HEAD_DIM), (D // 2) ** -0.5, 0.25)
    value_weight = centred(key_list[7], (D, HEADS * VE * HEAD_DIM), D ** -0.5, 0.1875)
    output_weight = centred(key_list[8], (HEADS * VE * HEAD_DIM, D), 8 ** -0.5, 2.0)
    value_router = centred(key_list[9], (D, HEADS * VE), (2 * D) ** -0.5, 0.125)
    output_router = centred(key_list[10], (D, HEADS * VE), (2 * D) ** -0.5, 0.125)
    expert_router = draw_expert_router(jax.random.fold_in(key_list[17], 71), 0)
    attention_gain = jnp.clip(1.0 + 0.1 * jax.random.normal(key_list[12], (D,), jnp.float32), 0.5, 1.5).astype(jnp.bfloat16)
    feedforward_gain = jnp.clip(1.0 + 0.1 * jax.random.normal(key_list[13], (D,), jnp.float32), 0.5, 1.5).astype(jnp.bfloat16)
    expert_up = centred(key_list[14], (EXPERTS, D, FE), D ** -0.5, 0.1875, ((0, 8),))
    expert_down = centred(key_list[15], (EXPERTS, FE, D), FE ** -0.5, 0.5, ((0, 8),))
    cotangent = heavy_noise(key_list[16], (BUCKETS, SEQ, D), 1.0, 6.0, ((0, 8), (1, 4)), (0, 2, 8, 2.0))
    return {"hidden_in": hidden_in, "lengths": lengths, "value_pick": value_pick, "output_pick": output_pick, "expert_pick": expert_pick, "query_weight": query_weight, "key_weight": key_weight, "value_weight": value_weight, "output_weight": output_weight, "value_router": value_router, "output_router": output_router, "expert_router": expert_router, "attention_gain": attention_gain, "feedforward_gain": feedforward_gain, "expert_up": expert_up, "expert_down": expert_down, "cotangent": cotangent}


@jax.custom_vjp
def low(v):
    return lax.optimization_barrier(v.astype(jnp.bfloat16)).astype(jnp.float32)

@jax.custom_vjp
def low_back(v):
    return v

def low_keep(v):
    return (low(v), None)

def low_pass(kept, grad):
    return (grad,)

def back_keep(v):
    return (v, None)

def back_low(kept, grad):
    return (low(grad),)
low.defvjp(low_keep, low_pass)
low_back.defvjp(back_keep, back_low)
EPSILON = 1e-05
NEGATIVE = -1000000000.0
PRECISE = lax.Precision.HIGHEST

def exact_dot(left_side, right_side):
    return jnp.dot(left_side, right_side, precision=PRECISE)

def layer_norm(field, scale_gain):
    center = field - lax.optimization_barrier(jnp.mean(field, axis=-1, keepdims=True))
    spread = lax.optimization_barrier(jnp.mean(center * center, axis=-1, keepdims=True))
    return center * lax.rsqrt(spread + EPSILON) * scale_gain

def choose(select, count):
    return lax.optimization_barrier(jnp.sum((select[..., None] == jnp.arange(count, dtype=jnp.int32)).astype(jnp.float32), axis=-2))

def bucket(bucket_in, length, value_sel, output_sel, expert_sel, params):
    query_weight, key_weight, value_weight, output_weight, value_router, output_router, expert_router, attention_gain, feedforward_gain, expert_up, expert_down = params
    positions = jnp.arange(SEQ, dtype=jnp.int32)
    live_mask = (positions < length).astype(jnp.float32)[:, None]
    normed_one = low(layer_norm(bucket_in, attention_gain))
    queries = low(low_back(exact_dot(normed_one, query_weight))).reshape(SEQ, HEADS, HEAD_DIM)
    key_rows = low(low_back(exact_dot(normed_one, key_weight))).reshape(SEQ, HEADS, HEAD_DIM)
    value_gate = jax.nn.sigmoid(exact_dot(normed_one, value_router)).reshape(SEQ, HEADS, VE) * choose(value_sel, VE)
    value_all = low_back(exact_dot(bucket_in, value_weight)).reshape(SEQ, HEADS, VE, HEAD_DIM)
    value_rows = low(low_back(lax.optimization_barrier(jnp.sum(value_gate[..., None] * value_all, axis=2))))
    score_scale = HEAD_DIM ** (-0.5)
    block_rows = min(512, SEQ)

    def attend(first_row):
        query_block = lax.dynamic_slice_in_dim(queries, first_row, block_rows, 0)
        raw_scores = low_back(jnp.einsum('qhd,khd->hqk', query_block, key_rows, precision=PRECISE))
        query_pos = first_row + jnp.arange(block_rows, dtype=jnp.int32)
        allowed = (positions[None, :] <= query_pos[:, None]) & (positions[None, :] < length)
        scores = jnp.where(allowed[None], raw_scores * score_scale, NEGATIVE)
        exp_terms = jnp.exp(scores - lax.optimization_barrier(jnp.max(scores, axis=-1, keepdims=True)))
        soft_probs = low(exp_terms / lax.optimization_barrier(jnp.sum(exp_terms, axis=-1, keepdims=True)))
        return low_back(jnp.einsum('hqk,khd->qhd', soft_probs, value_rows, precision=PRECISE))
    block_starts = jnp.arange(SEQ // block_rows, dtype=jnp.int32) * block_rows
    attended = lax.map(jax.checkpoint(attend), block_starts).reshape(SEQ, HEADS, HEAD_DIM)
    output_gate = jax.nn.sigmoid(exact_dot(normed_one, output_router)).reshape(SEQ, HEADS, VE) * choose(output_sel, VE)
    mixed = low(output_gate[..., None] * attended[:, :, None, :]).reshape(SEQ, HEADS * VE * HEAD_DIM)
    attention_out = live_mask * low_back(exact_dot(mixed, output_weight))
    middle = bucket_in + attention_out
    normed_two = low(layer_norm(middle, feedforward_gain))
    router_sig = jax.nn.sigmoid(exact_dot(normed_two, expert_router))
    expert_gate = jnp.take_along_axis(router_sig, expert_sel.astype(jnp.int32), axis=1) * live_mask
    flat_pick = expert_sel.reshape(N_DP, TOK_DEV * TOPK).astype(jnp.int32)
    one_hot = (flat_pick[..., None] == jnp.arange(EXPERTS, dtype=jnp.int32)).astype(jnp.int32)
    running_count = jnp.cumsum(one_hot, axis=1, dtype=jnp.int32).astype(jnp.int32)
    slot_rank = lax.optimization_barrier(jnp.sum((running_count - one_hot) * one_hot, axis=-1, dtype=jnp.int32)).astype(jnp.int32)
    block_base = jnp.arange(N_DP, dtype=jnp.int32)[:, None] * CAP
    slot_index = (flat_pick * (N_DP * CAP) + block_base + slot_rank).reshape(-1).astype(jnp.int32)
    token_of = jnp.arange(SEQ * TOPK, dtype=jnp.int32) // TOPK
    middle_low = low(middle)
    dispatch = jnp.zeros((EXPERTS * N_DP * CAP, D), jnp.float32).at[slot_index].set(middle_low[token_of])
    dispatch = low_back(dispatch).reshape(EXPERTS, N_DP * CAP, D)
    preact = low_back(jnp.einsum('ecd,edf->ecf', dispatch, expert_up, precision=PRECISE))
    hidden = low(jax.nn.silu(preact))
    returned = low(low_back(jnp.einsum('ecf,efd->ecd', hidden, expert_down, precision=PRECISE)))
    picked = returned.reshape(EXPERTS * N_DP * CAP, D)[slot_index].reshape(SEQ, TOPK, D)
    feedforward_out = lax.optimization_barrier(jnp.sum(expert_gate[..., None] * picked, axis=1))
    final_rows = middle + feedforward_out
    bucket_stats = jnp.stack([jnp.sum(live_mask * bucket_in * bucket_in), jnp.sum(attention_out * attention_out), jnp.sum(feedforward_out * feedforward_out), jnp.sum(live_mask * final_rows * final_rows), jnp.sum(live_mask)])
    return (final_rows, bucket_stats)

def reference(hidden_in, lengths, value_pick, output_pick, expert_pick, query_weight, key_weight, value_weight, output_weight, value_router, output_router, expert_router, attention_gain, feedforward_gain, expert_up, expert_down, cotangent):
    params = tuple((weight.astype(jnp.float32) for weight in (query_weight, key_weight, value_weight, output_weight, value_router, output_router, expert_router, attention_gain, feedforward_gain, expert_up, expert_down)))

    def forward(input_rows, *weights_in):

        def bucket_step(running, bucket_item):
            bucket_in, length, value_sel, output_sel, expert_sel = bucket_item
            final_rows, bucket_stats = bucket(bucket_in, length, value_sel, output_sel, expert_sel, weights_in)
            return (running, (final_rows, bucket_stats))
        running, (all_rows, all_stats) = lax.scan(jax.checkpoint(bucket_step), jnp.zeros((), jnp.float32), (input_rows, lengths.astype(jnp.int32), value_pick, output_pick, expert_pick))
        return (all_rows, all_stats)
    block_out, pullback, all_stats = jax.vjp(forward, hidden_in.astype(jnp.float32), *params, has_aux=True)
    gradients = pullback(cotangent.astype(jnp.float32))
    summed = lax.optimization_barrier(jnp.sum(all_stats, axis=0))
    residual_norms = jnp.sqrt(summed[:4] / (summed[4] * D))
    return (block_out.astype(jnp.bfloat16), gradients[0], gradients[1], gradients[2], gradients[3], gradients[4], gradients[5], gradients[6], gradients[7], gradients[8], gradients[9], gradients[10], gradients[11], residual_norms)
```

```python
import jax
import jax.numpy as jnp
from jax import lax
from jax.sharding import PartitionSpec as P

D = 1024
HEADS = 4
HEAD_DIM = 128
VE = 5


EPSILON = 1e-05
NEGATIVE = -1000000000.0


def low_dot(left_side, right_side):
    return jnp.dot(left_side, right_side, preferred_element_type=jnp.float32)


def layer_norm(field, scale_gain):
    center = field - jnp.mean(field, axis=-1, keepdims=True)
    spread = jnp.mean(center * center, axis=-1, keepdims=True)
    return center * lax.rsqrt(spread + EPSILON) * scale_gain


def choose(select, count):
    return jnp.sum(
        (select[..., None] == jnp.arange(count, dtype=jnp.int32)).astype(jnp.float32), axis=-2
    )


def attention_probs(query_heads, key_heads, query_pos, length):
    key_pos = jnp.arange(key_heads.shape[0], dtype=jnp.int32)
    raw_scores = jnp.einsum(
        "qhd,khd->hqk", query_heads, key_heads, preferred_element_type=jnp.float32
    )
    allowed = (key_pos[None, :] <= query_pos[:, None]) & (key_pos[None, :] < length)
    scores = jnp.where(allowed[None], raw_scores * HEAD_DIM ** (-0.5), NEGATIVE)
    exp_terms = jnp.exp(scores - jnp.max(scores, axis=-1, keepdims=True))
    return exp_terms / jnp.sum(exp_terms, axis=-1, keepdims=True)


def expert_visit(sent, cotangent, expert_up, expert_down):
    local_experts = expert_up.shape[0]
    group = lax.axis_index("expert")
    cot_all = lax.all_gather(cotangent, "expert", axis=0, tiled=True)
    sent_all = lax.all_gather(sent, "expert", axis=0, tiled=True)
    rows_all = sent_all[:, :D]
    total_experts = sent.shape[1] - D
    gate_all = lax.dynamic_slice_in_dim(
        sent_all[:, D:], group * local_experts, local_experts, 1
    ).astype(jnp.float32).T[:, :, None]
    preact = jnp.einsum("td,xdf->xtf", rows_all, expert_up, preferred_element_type=jnp.float32)
    pre_sig = jax.nn.sigmoid(preact)
    hidden = preact * pre_sig
    back = jnp.einsum("td,xfd->xtf", cot_all, expert_down, preferred_element_type=jnp.float32)
    gate_grad = jnp.sum(hidden * back, axis=2).T
    gated = (gate_all * hidden).astype(jnp.bfloat16)
    grad_pre = (gate_all * back * (pre_sig * (1.0 + preact * (1.0 - pre_sig)))).astype(jnp.bfloat16)
    partial_out = jnp.einsum("xtf,xfd->td", gated, expert_down, preferred_element_type=jnp.float32)
    partial_grad = jnp.einsum("xtf,xdf->td", grad_pre, expert_up, preferred_element_type=jnp.float32)
    wide_grad = lax.dynamic_update_slice_in_dim(
        jnp.zeros((gate_grad.shape[0], total_experts), jnp.bfloat16),
        gate_grad.astype(jnp.bfloat16),
        group * local_experts,
        1,
    )
    returned = lax.psum_scatter(
        jnp.concatenate(
            [partial_out.astype(jnp.bfloat16), partial_grad.astype(jnp.bfloat16), wide_grad], axis=1
        ),
        "expert",
        scatter_dimension=0,
        tiled=True,
    )
    grad_down = jnp.einsum("xtf,td->xfd", gated, cot_all, preferred_element_type=jnp.float32)
    grad_up = jnp.einsum("td,xtf->xdf", rows_all, grad_pre, preferred_element_type=jnp.float32)
    return returned, grad_up, grad_down


def shards(
    hidden_in,
    lengths,
    value_pick,
    output_pick,
    expert_pick,
    query_weight,
    key_weight,
    value_weight,
    output_weight,
    value_router,
    output_router,
    expert_router,
    attention_gain,
    feedforward_gain,
    expert_up,
    expert_down,
    cotangent,
):
    row_count = hidden_in.shape[1]
    total_experts = expert_router.shape[1]
    input_low = hidden_in[0]
    input_full = input_low.astype(jnp.float32)
    length = lengths[0]
    query_pos = lax.axis_index("dp") * row_count + jnp.arange(row_count, dtype=jnp.int32)
    live_mask = (query_pos < length).astype(jnp.float32)[:, None]
    gain_one = attention_gain.astype(jnp.float32)
    gain_two = feedforward_gain.astype(jnp.float32)
    normed_one = layer_norm(input_full, gain_one)
    normed_low = normed_one.astype(jnp.bfloat16)
    queries = low_dot(normed_low, query_weight).astype(jnp.bfloat16)
    key_local = low_dot(normed_low, key_weight).astype(jnp.bfloat16)
    value_sig = jax.nn.sigmoid(low_dot(normed_low, value_router)).reshape(row_count, HEADS, VE)
    value_hot = choose(value_pick[0], VE)
    value_gate = value_sig * value_hot
    value_all = low_dot(input_low, value_weight).reshape(row_count, HEADS, VE, HEAD_DIM)
    value_local = (
        jnp.sum(value_gate[..., None] * value_all, axis=2)
        .astype(jnp.bfloat16)
        .reshape(row_count, HEADS * HEAD_DIM)
    )
    key_all, value_rows = (
        lax.all_gather(key_local, "dp", axis=0, tiled=True),
        lax.all_gather(value_local, "dp", axis=0, tiled=True),
    )
    query_heads = queries.reshape(row_count, HEADS, HEAD_DIM)
    key_heads = key_all.reshape(-1, HEADS, HEAD_DIM)
    value_heads = value_rows.reshape(-1, HEADS, HEAD_DIM)
    soft_probs = attention_probs(query_heads, key_heads, query_pos, length)
    attended = jnp.einsum(
        "hqk,khd->qhd",
        soft_probs.astype(jnp.bfloat16),
        value_heads,
        preferred_element_type=jnp.float32,
    )
    output_sig = jax.nn.sigmoid(low_dot(normed_low, output_router)).reshape(row_count, HEADS, VE)
    output_hot = choose(output_pick[0], VE)
    output_gate = output_sig * output_hot
    mixed = (
        (output_gate[..., None] * attended[:, :, None, :])
        .astype(jnp.bfloat16)
        .reshape(row_count, HEADS * VE * HEAD_DIM)
    )
    attention_out = live_mask * low_dot(mixed, output_weight)
    middle = input_full + attention_out
    normed_two = layer_norm(middle, gain_two)
    normed_two_low = normed_two.astype(jnp.bfloat16)
    router_sig = jax.nn.sigmoid(low_dot(normed_two_low, expert_router))
    hot = jnp.any(
        expert_pick[0][:, :, None] == jnp.arange(total_experts, dtype=jnp.int32), axis=1
    ).astype(jnp.float32)
    picked_hot = hot * live_mask
    expert_gate = router_sig * picked_hot
    middle_low = middle.astype(jnp.bfloat16)
    sent = jnp.concatenate([middle_low, expert_gate.astype(jnp.bfloat16)], axis=1)
    groups = lax.axis_size("expert")
    rounds = max(1, groups // 8)

    def visit(grads, item):
        returned, grad_up, grad_down = expert_visit(*item, expert_up, expert_down)
        return (grads[0] + grad_up, grads[1] + grad_down), returned

    if rounds == 1:
        returned, grad_up, grad_down = expert_visit(sent, cotangent[0], expert_up, expert_down)
    else:
        zeros = jnp.zeros(expert_up.shape, jnp.float32), jnp.zeros(expert_down.shape, jnp.float32)
        (grad_up, grad_down), returned = lax.scan(
            visit,
            zeros,
            (
                sent.reshape(rounds, -1, sent.shape[1]),
                cotangent[0].reshape(rounds, -1, D),
            ),
        )
        returned = returned.reshape(row_count, -1)
    returned = returned.astype(jnp.float32)
    feedforward_out = returned[:, :D]
    final_rows = middle + feedforward_out
    total_sums = lax.psum(
        (
            jnp.sum(live_mask * input_full * input_full),
            jnp.sum(attention_out * attention_out),
            jnp.sum(feedforward_out * feedforward_out),
            jnp.sum(live_mask * final_rows * final_rows),
            jnp.sum(live_mask),
        ),
        ("dp", "expert"),
    )
    residual_norms = jnp.sqrt(jnp.stack(total_sums[:4]) / (total_sums[4] * D))
    grad_final = cotangent[0].astype(jnp.float32)
    grad_middle = grad_final + returned[:, D : 2 * D]
    grad_logit = (
        returned[:, 2 * D :] * picked_hot * router_sig * (1.0 - router_sig)
    ).astype(jnp.bfloat16)
    grad_expert_router = low_dot(normed_two_low.T, grad_logit)
    grad_normed_two = low_dot(grad_logit, expert_router.T)
    unused_two, norm_two_back = jax.vjp(layer_norm, middle, gain_two)
    grad_middle_norm, grad_gain_two = norm_two_back(grad_normed_two)
    grad_middle = grad_middle + grad_middle_norm
    grad_branch = (live_mask * grad_middle).astype(jnp.bfloat16)
    grad_mixed = jnp.einsum(
        "td,md->tm", grad_branch, output_weight, preferred_element_type=jnp.float32
    ).reshape(row_count, HEADS, VE, HEAD_DIM)
    grad_output_weight = jnp.einsum(
        "td,tm->dm", grad_branch, mixed, preferred_element_type=jnp.float32
    )
    grad_attended = jnp.sum(output_gate[..., None] * grad_mixed, axis=2)
    grad_output_logit = (
        jnp.sum(attended[:, :, None, :] * grad_mixed, axis=3)
        * output_hot
        * output_sig
        * (1.0 - output_sig)
    ).reshape(row_count, HEADS * VE)
    grad_attended_low = grad_attended.astype(jnp.bfloat16)
    grad_probs = jnp.einsum(
        "qhd,khd->hqk", grad_attended_low, value_heads, preferred_element_type=jnp.float32
    )
    row_dot = jnp.sum(soft_probs * grad_probs, axis=-1, keepdims=True)
    grad_scores = (soft_probs * (grad_probs - row_dot) * HEAD_DIM ** (-0.5)).astype(jnp.bfloat16)
    grad_query = (
        jnp.einsum("hqk,khd->qhd", grad_scores, key_heads, preferred_element_type=jnp.float32)
        .astype(jnp.bfloat16)
        .reshape(row_count, HEADS * HEAD_DIM)
    )
    grad_key_all = jnp.einsum(
        "hqk,qhd->khd", grad_scores, query_heads, preferred_element_type=jnp.float32
    ).reshape(-1, HEADS * HEAD_DIM)
    grad_value_rows = jnp.einsum(
        "hqk,qhd->khd",
        soft_probs.astype(jnp.bfloat16),
        grad_attended_low,
        preferred_element_type=jnp.float32,
    ).reshape(-1, HEADS * HEAD_DIM)
    grad_key_sum, grad_value_sum = (
        lax.psum_scatter(
            grad_key_all.astype(jnp.bfloat16), "dp", scatter_dimension=0, tiled=True
        ).astype(jnp.float32),
        lax.psum_scatter(
            grad_value_rows.astype(jnp.bfloat16), "dp", scatter_dimension=0, tiled=True
        ).astype(jnp.float32),
    )
    grad_key = grad_key_sum.astype(jnp.bfloat16)
    grad_value_low = (
        grad_value_sum.astype(jnp.bfloat16)
        .astype(jnp.float32)
        .reshape(row_count, HEADS, 1, HEAD_DIM)
    )
    grad_value_each = (
        (value_gate[..., None] * grad_value_low)
        .astype(jnp.bfloat16)
        .reshape(row_count, HEADS * VE * HEAD_DIM)
    )
    grad_value_logit = (
        jnp.sum(value_all * grad_value_low, axis=3) * value_hot * value_sig * (1.0 - value_sig)
    ).reshape(row_count, HEADS * VE)
    grad_value_weight = jnp.einsum(
        "td,tm->dm", input_low, grad_value_each, preferred_element_type=jnp.float32
    )
    grad_query_weight = jnp.einsum(
        "td,tm->dm", normed_low, grad_query, preferred_element_type=jnp.float32
    )
    grad_key_weight = jnp.einsum(
        "td,tm->dm", normed_low, grad_key, preferred_element_type=jnp.float32
    )
    grad_value_logit = grad_value_logit.astype(jnp.bfloat16)
    grad_output_logit = grad_output_logit.astype(jnp.bfloat16)
    grad_value_router = low_dot(normed_low.T, grad_value_logit)
    grad_output_router = low_dot(normed_low.T, grad_output_logit)
    grad_normed_one = (
        jnp.einsum("tm,dm->td", grad_query, query_weight, preferred_element_type=jnp.float32)
        + jnp.einsum("tm,dm->td", grad_key, key_weight, preferred_element_type=jnp.float32)
        + low_dot(grad_value_logit, value_router.T)
        + low_dot(grad_output_logit, output_router.T)
    )
    unused_one, norm_one_back = jax.vjp(layer_norm, input_full, gain_one)
    grad_input_norm, grad_gain_one = norm_one_back(grad_normed_one)
    grad_input = (
        grad_middle
        + jnp.einsum("tm,dm->td", grad_value_each, value_weight, preferred_element_type=jnp.float32)
        + grad_input_norm
    )
    parts = (
        grad_query_weight,
        grad_key_weight,
        grad_value_weight,
        grad_output_weight,
        grad_value_router,
        grad_output_router,
        grad_expert_router,
        grad_gain_one[:, None],
        grad_gain_two[:, None],
    )
    summed = lax.psum_scatter(
        jnp.concatenate([part.astype(jnp.bfloat16) for part in parts], axis=1),
        ("dp", "expert"),
        scatter_dimension=0,
        tiled=True,
    ).astype(jnp.float32)
    dense_grads = []
    start = 0
    for part in parts:
        dense_grads.append(summed[:, start : start + part.shape[1]])
        start += part.shape[1]
    dense_grads[3] = dense_grads[3].T
    dense_grads[7] = dense_grads[7][:, 0]
    dense_grads[8] = dense_grads[8][:, 0]
    expert_grads = (
        lax.psum_scatter(
            grad_up.astype(jnp.bfloat16), "dp", scatter_dimension=1, tiled=True
        ).astype(jnp.float32),
        lax.psum_scatter(
            grad_down.astype(jnp.bfloat16), "dp", scatter_dimension=2, tiled=True
        ).astype(jnp.float32),
    )
    return (
        final_rows.astype(jnp.bfloat16)[None],
        grad_input[None],
        dense_grads[0],
        dense_grads[1],
        dense_grads[2],
        dense_grads[3],
        dense_grads[4],
        dense_grads[5],
        dense_grads[6],
        dense_grads[7],
        dense_grads[8],
        expert_grads[0],
        expert_grads[1],
        residual_norms,
    )


def solution(mesh):
    placed = (
        P("expert", "dp", None),
        P("expert"),
        P("expert", "dp", None, None),
        P("expert", "dp", None, None),
        P("expert", "dp", None),
        P(),
        P(),
        P(),
        P(),
        P(),
        P(),
        P(),
        P(),
        P(),
        P("expert", None, None),
        P("expert", None, None),
        P("expert", "dp", None),
    )
    return jax.shard_map(
        shards,
        mesh=mesh,
        in_specs=placed,
        out_specs=(
            P("expert", "dp", None),
            P("expert", "dp", None),
            P(("dp", "expert"), None),
            P(("dp", "expert"), None),
            P(("dp", "expert"), None),
            P(None, ("dp", "expert")),
            P(("dp", "expert"), None),
            P(("dp", "expert"), None),
            P(("dp", "expert"), None),
            P(("dp", "expert")),
            P(("dp", "expert")),
            P("expert", "dp", None),
            P("expert", None, "dp"),
            P(),
        ),
        check_vma=False,
    )
```

```python
import functools

import jax
import jax.numpy as jnp
from jax import lax
from jax.experimental import pallas as pl
from jax.experimental.pallas import tpu as pltpu
from jax.sharding import PartitionSpec as P

D = 1024
HEADS = 4
HEAD_DIM = 128
VE = 5


MESH = pl.DeviceIdType.MESH
ROWS = 32
CHUNK = 512
EPSILON = 1e-05
NEGATIVE = -1000000000.0


def low_dot(left_side, right_side):
    return jnp.dot(left_side, right_side, preferred_element_type=jnp.float32)


def layer_norm(field, scale_gain):
    center = field - jnp.mean(field, axis=-1, keepdims=True)
    spread = jnp.mean(center * center, axis=-1, keepdims=True)
    return center * lax.rsqrt(spread + EPSILON) * scale_gain


def choose(select, count):
    return jnp.sum(
        (select[..., None] == jnp.arange(count, dtype=jnp.int32)).astype(jnp.float32), axis=-2
    )


def attention_probs(query_heads, key_heads, query_pos, length):
    key_pos = jnp.arange(key_heads.shape[0], dtype=jnp.int32)
    raw_scores = jnp.einsum(
        "qhd,khd->hqk", query_heads, key_heads, preferred_element_type=jnp.float32
    )
    allowed = (key_pos[None, :] <= query_pos[:, None]) & (key_pos[None, :] < length)
    scores = jnp.where(allowed[None], raw_scores * HEAD_DIM ** (-0.5), NEGATIVE)
    exp_terms = jnp.exp(scores - jnp.max(scores, axis=-1, keepdims=True))
    return exp_terms / jnp.sum(exp_terms, axis=-1, keepdims=True)


def expert_visit(sent, cotangent, expert_up, expert_down):
    local_experts = expert_up.shape[0]
    group = lax.axis_index("expert")
    cot_all = lax.all_gather(cotangent, "expert", axis=0, tiled=True)
    sent_all = lax.all_gather(sent, "expert", axis=0, tiled=True)
    rows_all = sent_all[:, :D]
    total_experts = sent.shape[1] - D
    gate_all = lax.dynamic_slice_in_dim(
        sent_all[:, D:], group * local_experts, local_experts, 1
    ).astype(jnp.float32).T[:, :, None]
    preact = jnp.einsum("td,xdf->xtf", rows_all, expert_up, preferred_element_type=jnp.float32)
    pre_sig = jax.nn.sigmoid(preact)
    hidden = preact * pre_sig
    back = jnp.einsum("td,xfd->xtf", cot_all, expert_down, preferred_element_type=jnp.float32)
    gate_grad = jnp.sum(hidden * back, axis=2).T
    gated = (gate_all * hidden).astype(jnp.bfloat16)
    grad_pre = (gate_all * back * (pre_sig * (1.0 + preact * (1.0 - pre_sig)))).astype(jnp.bfloat16)
    partial_out = jnp.einsum("xtf,xfd->td", gated, expert_down, preferred_element_type=jnp.float32)
    partial_grad = jnp.einsum("xtf,xdf->td", grad_pre, expert_up, preferred_element_type=jnp.float32)
    wide_grad = lax.dynamic_update_slice_in_dim(
        jnp.zeros((gate_grad.shape[0], total_experts), jnp.bfloat16),
        gate_grad.astype(jnp.bfloat16),
        group * local_experts,
        1,
    )
    returned = lax.psum_scatter(
        jnp.concatenate(
            [partial_out.astype(jnp.bfloat16), partial_grad.astype(jnp.bfloat16), wide_grad], axis=1
        ),
        "expert",
        scatter_dimension=0,
        tiled=True,
    )
    grad_down = jnp.einsum("xtf,td->xfd", gated, cot_all, preferred_element_type=jnp.float32)
    grad_up = jnp.einsum("td,xtf->xdf", rows_all, grad_pre, preferred_element_type=jnp.float32)
    return returned, grad_up, grad_down


def dense_sum_kernel(widths, *refs):
    n = len(widths)
    grads, stats = refs[:n], refs[n]
    outs, stats_out = refs[n + 1 : 2 * n + 1], refs[2 * n + 1]
    core_in, near_in, far_in, line_in, total_in, send, recv = refs[2 * n + 2 :]
    dp, ex = lax.axis_index("dp"), lax.axis_index("expert")
    y, x, z, core = dp // 2, dp % 2, ex // 2, ex % 2
    sibling = (dp, z * 2 + 1 - core)
    beside = (y * 2 + 1 - x, ex)
    behind = ((1 - y) * 2 + x, ex)
    line = [(dp, ((z + k) % 4) * 2 + core) for k in (1, 2, 3)]
    barrier = pltpu.get_barrier_semaphore()
    for place in (sibling, beside, behind, *line):
        pl.semaphore_signal(barrier, inc=1, device_id=place, device_id_type=MESH)
    pl.semaphore_wait(barrier, 6)

    pieces = []
    for which, width in enumerate(widths):
        for start in range(0, width, CHUNK):
            pieces.append((which, start, min(CHUNK, width - start)))

    def copy(source, target, slot, place):
        made = pltpu.make_async_remote_copy(
            src_ref=source, dst_ref=target, send_sem=send.at[slot], recv_sem=recv.at[slot],
            device_id=place, device_id_type=MESH)
        made.start()
        return made

    def add(target, source):
        target[...] = (target[...].astype(jnp.float32) + source[...].astype(jnp.float32)).astype(target.dtype)

    count = len(pieces)
    first, second, third, fourth = {}, {}, {}, {}

    def halve_core(i):
        which, start, width = pieces[i]
        columns = pl.ds(start, width)
        first[i] = copy(grads[which].at[:, :, 1 - core, :, columns], core_in.at[i, :, :, :, pl.ds(0, width)], (i, 0), sibling)

    def halve_near(i):
        which, start, width = pieces[i]
        first[i].wait()
        held = core_in.at[i, :, :, :, pl.ds(0, width)]
        add(held, grads[which].at[:, :, core, :, pl.ds(start, width)])
        for half in range(2):
            if i % 2 == 0:
                source = core_in.at[i, half * 2 + 1 - x, :, :, pl.ds(0, width)]
            else:
                source = core_in.at[i, (1 - y) * 2 + half, :, :, pl.ds(0, width)]
            second[i, half] = copy(source, near_in.at[i, half, :, :, pl.ds(0, width)], (i, 1 + half), beside if i % 2 == 0 else behind)

    def halve_far(i):
        which, start, width = pieces[i]
        for half in range(2):
            second[i, half].wait()
            kept = half * 2 + x if i % 2 == 0 else y * 2 + half
            add(near_in.at[i, half, :, :, pl.ds(0, width)], core_in.at[i, kept, :, :, pl.ds(0, width)])
        other = 1 - y if i % 2 == 0 else 1 - x
        third[i] = copy(near_in.at[i, other, :, :, pl.ds(0, width)], far_in.at[i, :, :, pl.ds(0, width)], (i, 3), behind if i % 2 == 0 else beside)

    def spread_line(i):
        which, start, width = pieces[i]
        third[i].wait()
        add(far_in.at[i, :, :, pl.ds(0, width)], near_in.at[i, y if i % 2 == 0 else x, :, :, pl.ds(0, width)])
        for k in (1, 2, 3):
            fourth[i, k] = copy(far_in.at[i, (z + k) % 4, :, pl.ds(0, width)], line_in.at[i, k - 1, :, pl.ds(0, width)], (i, 3 + k), line[k - 1])

    def finish(i):
        which, start, width = pieces[i]
        columns = pl.ds(0, width)
        total = far_in[i, z, :, columns].astype(jnp.float32)
        for k in (1, 2, 3):
            fourth[i, k].wait()
            total = total + line_in[i, k - 1, :, columns].astype(jnp.float32)
        outs[which][:, pl.ds(start, width)] = total

    for i in range(count):
        halve_core(i)
    total_in[0] = stats[...]
    rounds = [[sibling], [beside], [behind], line]
    place = 1
    for r, partners in enumerate(rounds):
        copies = [copy(total_in.at[0], total_in.at[place + j], (count + j, r), p) for j, p in enumerate(partners)]
        for made in copies:
            made.wait()
        summed = total_in[0]
        for j in range(len(partners)):
            summed = summed + total_in[place + j]
        total_in[0] = summed
        place += len(partners)
    stats_out[...] = total_in[0]

    lead, lag, tail = 4, 3, 2
    for step in range(count + lead + lag + tail):
        if step < count:
            halve_near(step)
        if 0 <= step - lead < count:
            halve_far(step - lead)
        if 0 <= step - lead - lag < count:
            spread_line(step - lead - lag)
        if 0 <= step - lead - lag - tail < count:
            finish(step - lead - lag - tail)

def dense_sum(grads, stats):
    widths = [g.shape[1] for g in grads]
    count = sum(-(-w // CHUNK) for w in widths)
    vmem = pl.BlockSpec(memory_space=pltpu.VMEM)
    low = jnp.bfloat16
    outs = pl.pallas_call(
        functools.partial(dense_sum_kernel, widths),
        out_shape=[jax.ShapeDtypeStruct((ROWS, w), jnp.float32) for w in widths] + [jax.ShapeDtypeStruct((8, 128), jnp.float32)],
        in_specs=[vmem] * (len(widths) + 1),
        out_specs=[vmem] * (len(widths) + 1),
        scratch_shapes=[
            pltpu.VMEM((count, 4, 4, ROWS, CHUNK), low),
            pltpu.VMEM((count, 2, 4, ROWS, CHUNK), low),
            pltpu.VMEM((count, 4, ROWS, CHUNK), low),
            pltpu.VMEM((count, 3, ROWS, CHUNK), low),
            pltpu.VMEM((7, 8, 128), jnp.float32),
            pltpu.SemaphoreType.DMA((count + 3, 7)),
            pltpu.SemaphoreType.DMA((count + 3, 7)),
        ],
        compiler_params=pltpu.CompilerParams(collective_id=4, has_side_effects=True, vmem_limit_bytes=56 * 2**20),
        name="dense_sum",
    )(*[g.reshape(4, 4, 2, ROWS, g.shape[1]) for g in grads], stats)
    return outs[:-1], outs[-1]


def shards(
    hidden_in,
    lengths,
    value_pick,
    output_pick,
    expert_pick,
    query_weight,
    key_weight,
    value_weight,
    output_weight,
    value_router,
    output_router,
    expert_router,
    attention_gain,
    feedforward_gain,
    expert_up,
    expert_down,
    cotangent,
):
    row_count = hidden_in.shape[1]
    total_experts = expert_router.shape[1]
    input_low = hidden_in[0]
    input_full = input_low.astype(jnp.float32)
    length = lengths[0]
    query_pos = lax.axis_index("dp") * row_count + jnp.arange(row_count, dtype=jnp.int32)
    live_mask = (query_pos < length).astype(jnp.float32)[:, None]
    gain_one = attention_gain.astype(jnp.float32)
    gain_two = feedforward_gain.astype(jnp.float32)
    normed_one = layer_norm(input_full, gain_one)
    normed_low = normed_one.astype(jnp.bfloat16)
    queries = low_dot(normed_low, query_weight).astype(jnp.bfloat16)
    key_local = low_dot(normed_low, key_weight).astype(jnp.bfloat16)
    value_sig = jax.nn.sigmoid(low_dot(normed_low, value_router)).reshape(row_count, HEADS, VE)
    value_hot = choose(value_pick[0], VE)
    value_gate = value_sig * value_hot
    value_all = low_dot(input_low, value_weight).reshape(row_count, HEADS, VE, HEAD_DIM)
    value_local = (
        jnp.sum(value_gate[..., None] * value_all, axis=2)
        .astype(jnp.bfloat16)
        .reshape(row_count, HEADS * HEAD_DIM)
    )
    key_all, value_rows = (
        lax.all_gather(key_local, "dp", axis=0, tiled=True),
        lax.all_gather(value_local, "dp", axis=0, tiled=True),
    )
    query_heads = queries.reshape(row_count, HEADS, HEAD_DIM)
    key_heads = key_all.reshape(-1, HEADS, HEAD_DIM)
    value_heads = value_rows.reshape(-1, HEADS, HEAD_DIM)
    soft_probs = attention_probs(query_heads, key_heads, query_pos, length)
    attended = jnp.einsum(
        "hqk,khd->qhd",
        soft_probs.astype(jnp.bfloat16),
        value_heads,
        preferred_element_type=jnp.float32,
    )
    output_sig = jax.nn.sigmoid(low_dot(normed_low, output_router)).reshape(row_count, HEADS, VE)
    output_hot = choose(output_pick[0], VE)
    output_gate = output_sig * output_hot
    mixed = (
        (output_gate[..., None] * attended[:, :, None, :])
        .astype(jnp.bfloat16)
        .reshape(row_count, HEADS * VE * HEAD_DIM)
    )
    attention_out = live_mask * low_dot(mixed, output_weight)
    middle = input_full + attention_out
    normed_two = layer_norm(middle, gain_two)
    normed_two_low = normed_two.astype(jnp.bfloat16)
    router_sig = jax.nn.sigmoid(low_dot(normed_two_low, expert_router))
    hot = jnp.any(
        expert_pick[0][:, :, None] == jnp.arange(total_experts, dtype=jnp.int32), axis=1
    ).astype(jnp.float32)
    picked_hot = hot * live_mask
    expert_gate = router_sig * picked_hot
    middle_low = middle.astype(jnp.bfloat16)
    sent = jnp.concatenate([middle_low, expert_gate.astype(jnp.bfloat16)], axis=1)
    groups = lax.axis_size("expert")
    rounds = max(1, groups // 8)

    def visit(grads, item):
        returned, grad_up, grad_down = expert_visit(*item, expert_up, expert_down)
        return (grads[0] + grad_up, grads[1] + grad_down), returned

    if rounds == 1:
        returned, grad_up, grad_down = expert_visit(sent, cotangent[0], expert_up, expert_down)
    else:
        zeros = jnp.zeros(expert_up.shape, jnp.float32), jnp.zeros(expert_down.shape, jnp.float32)
        (grad_up, grad_down), returned = lax.scan(
            visit,
            zeros,
            (
                sent.reshape(rounds, -1, sent.shape[1]),
                cotangent[0].reshape(rounds, -1, D),
            ),
        )
        returned = returned.reshape(row_count, -1)
    returned = returned.astype(jnp.float32)
    feedforward_out = returned[:, :D]
    final_rows = middle + feedforward_out
    sums = jnp.stack(
        [
            jnp.sum(live_mask * input_full * input_full),
            jnp.sum(attention_out * attention_out),
            jnp.sum(feedforward_out * feedforward_out),
            jnp.sum(live_mask * final_rows * final_rows),
            jnp.sum(live_mask),
        ]
    )
    grad_final = cotangent[0].astype(jnp.float32)
    grad_middle = grad_final + returned[:, D : 2 * D]
    grad_logit = (
        returned[:, 2 * D :] * picked_hot * router_sig * (1.0 - router_sig)
    ).astype(jnp.bfloat16)
    grad_expert_router = low_dot(normed_two_low.T, grad_logit)
    grad_normed_two = low_dot(grad_logit, expert_router.T)
    unused_two, norm_two_back = jax.vjp(layer_norm, middle, gain_two)
    grad_middle_norm, grad_gain_two = norm_two_back(grad_normed_two)
    grad_middle = grad_middle + grad_middle_norm
    grad_branch = (live_mask * grad_middle).astype(jnp.bfloat16)
    grad_mixed = jnp.einsum(
        "td,md->tm", grad_branch, output_weight, preferred_element_type=jnp.float32
    ).reshape(row_count, HEADS, VE, HEAD_DIM)
    grad_output_weight = jnp.einsum(
        "td,tm->dm", grad_branch, mixed, preferred_element_type=jnp.float32
    )
    grad_attended = jnp.sum(output_gate[..., None] * grad_mixed, axis=2)
    grad_output_logit = (
        jnp.sum(attended[:, :, None, :] * grad_mixed, axis=3)
        * output_hot
        * output_sig
        * (1.0 - output_sig)
    ).reshape(row_count, HEADS * VE)
    grad_attended_low = grad_attended.astype(jnp.bfloat16)
    grad_probs = jnp.einsum(
        "qhd,khd->hqk", grad_attended_low, value_heads, preferred_element_type=jnp.float32
    )
    row_dot = jnp.sum(soft_probs * grad_probs, axis=-1, keepdims=True)
    grad_scores = (soft_probs * (grad_probs - row_dot) * HEAD_DIM ** (-0.5)).astype(jnp.bfloat16)
    grad_query = (
        jnp.einsum("hqk,khd->qhd", grad_scores, key_heads, preferred_element_type=jnp.float32)
        .astype(jnp.bfloat16)
        .reshape(row_count, HEADS * HEAD_DIM)
    )
    grad_key_all = jnp.einsum(
        "hqk,qhd->khd", grad_scores, query_heads, preferred_element_type=jnp.float32
    ).reshape(-1, HEADS * HEAD_DIM)
    grad_value_rows = jnp.einsum(
        "hqk,qhd->khd",
        soft_probs.astype(jnp.bfloat16),
        grad_attended_low,
        preferred_element_type=jnp.float32,
    ).reshape(-1, HEADS * HEAD_DIM)
    grad_key_sum, grad_value_sum = (
        lax.psum_scatter(
            grad_key_all.astype(jnp.bfloat16), "dp", scatter_dimension=0, tiled=True
        ).astype(jnp.float32),
        lax.psum_scatter(
            grad_value_rows.astype(jnp.bfloat16), "dp", scatter_dimension=0, tiled=True
        ).astype(jnp.float32),
    )
    grad_key = grad_key_sum.astype(jnp.bfloat16)
    grad_value_low = (
        grad_value_sum.astype(jnp.bfloat16)
        .astype(jnp.float32)
        .reshape(row_count, HEADS, 1, HEAD_DIM)
    )
    grad_value_each = (
        (value_gate[..., None] * grad_value_low)
        .astype(jnp.bfloat16)
        .reshape(row_count, HEADS * VE * HEAD_DIM)
    )
    grad_value_logit = (
        jnp.sum(value_all * grad_value_low, axis=3) * value_hot * value_sig * (1.0 - value_sig)
    ).reshape(row_count, HEADS * VE)
    grad_value_weight = jnp.einsum(
        "td,tm->dm", input_low, grad_value_each, preferred_element_type=jnp.float32
    )
    grad_query_weight = jnp.einsum(
        "td,tm->dm", normed_low, grad_query, preferred_element_type=jnp.float32
    )
    grad_key_weight = jnp.einsum(
        "td,tm->dm", normed_low, grad_key, preferred_element_type=jnp.float32
    )
    grad_value_logit = grad_value_logit.astype(jnp.bfloat16)
    grad_output_logit = grad_output_logit.astype(jnp.bfloat16)
    grad_value_router = low_dot(normed_low.T, grad_value_logit)
    grad_output_router = low_dot(normed_low.T, grad_output_logit)
    grad_normed_one = (
        jnp.einsum("tm,dm->td", grad_query, query_weight, preferred_element_type=jnp.float32)
        + jnp.einsum("tm,dm->td", grad_key, key_weight, preferred_element_type=jnp.float32)
        + low_dot(grad_value_logit, value_router.T)
        + low_dot(grad_output_logit, output_router.T)
    )
    unused_one, norm_one_back = jax.vjp(layer_norm, input_full, gain_one)
    grad_input_norm, grad_gain_one = norm_one_back(grad_normed_one)
    grad_input = (
        grad_middle
        + jnp.einsum("tm,dm->td", grad_value_each, value_weight, preferred_element_type=jnp.float32)
        + grad_input_norm
    )
    small_grads = jnp.concatenate(
        [
            grad_value_router,
            grad_output_router,
            grad_expert_router,
            grad_gain_one[:, None],
            grad_gain_two[:, None],
        ],
        axis=1,
    )
    small_count = small_grads.shape[1]
    small_grads = jnp.pad(small_grads, ((0, 0), (0, -small_count % 128)))
    low_grads = [
        part.astype(jnp.bfloat16)
        for part in (
            grad_query_weight,
            grad_key_weight,
            grad_value_weight,
            grad_output_weight,
            small_grads,
        )
    ]
    if lax.axis_size("dp") == 4 and lax.axis_size("expert") == 8:
        dense_grads, sums_tile = dense_sum(low_grads, jnp.pad(sums[None], ((0, 7), (0, 123))))
        total_sums = sums_tile[0, :5]
    else:
        summed = lax.psum_scatter(
            jnp.concatenate(low_grads, axis=1), ("dp", "expert"), scatter_dimension=0, tiled=True
        ).astype(jnp.float32)
        dense_grads = jnp.split(summed, [512, 1024, 3584, 6144], axis=1)
        total_sums = lax.psum(sums, ("dp", "expert"))
    residual_norms = jnp.sqrt(total_sums[:4] / (total_sums[4] * D))
    small = dense_grads[4]
    router_end = 2 * HEADS * VE + expert_router.shape[1]
    dense_grads = [
        dense_grads[0],
        dense_grads[1],
        dense_grads[2],
        dense_grads[3].T,
        small[:, : HEADS * VE],
        small[:, HEADS * VE : 2 * HEADS * VE],
        small[:, 2 * HEADS * VE : router_end],
        small[:, router_end],
        small[:, router_end + 1],
    ]
    expert_grads = (
        lax.psum_scatter(
            grad_up.astype(jnp.bfloat16), "dp", scatter_dimension=1, tiled=True
        ).astype(jnp.float32),
        lax.psum_scatter(
            grad_down.astype(jnp.bfloat16), "dp", scatter_dimension=2, tiled=True
        ).astype(jnp.float32),
    )
    return (
        final_rows.astype(jnp.bfloat16)[None],
        grad_input[None],
        dense_grads[0],
        dense_grads[1],
        dense_grads[2],
        dense_grads[3],
        dense_grads[4],
        dense_grads[5],
        dense_grads[6],
        dense_grads[7],
        dense_grads[8],
        expert_grads[0],
        expert_grads[1],
        residual_norms,
    )


def solution(mesh):
    placed = (
        P("expert", "dp", None),
        P("expert"),
        P("expert", "dp", None, None),
        P("expert", "dp", None, None),
        P("expert", "dp", None),
        P(),
        P(),
        P(),
        P(),
        P(),
        P(),
        P(),
        P(),
        P(),
        P("expert", None, None),
        P("expert", None, None),
        P("expert", "dp", None),
    )
    return jax.shard_map(
        shards,
        mesh=mesh,
        in_specs=placed,
        out_specs=(
            P("expert", "dp", None),
            P("expert", "dp", None),
            P(("dp", "expert"), None),
            P(("dp", "expert"), None),
            P(("dp", "expert"), None),
            P(None, ("dp", "expert")),
            P(("dp", "expert"), None),
            P(("dp", "expert"), None),
            P(("dp", "expert"), None),
            P(("dp", "expert")),
            P(("dp", "expert")),
            P("expert", "dp", None),
            P("expert", None, "dp"),
            P(),
        ),
        check_vma=False,
    )
```

```python
import functools

import jax
import jax.numpy as jnp
from jax import lax
from jax.experimental import pallas as pl
from jax.experimental.pallas import tpu as pltpu
from jax.sharding import PartitionSpec as P

D = 1024
HEADS = 4
HEAD_DIM = 128
VE = 5


MESH = pl.DeviceIdType.MESH
ROWS = 32
CHUNK = 512
EPSILON = 1e-05
NEGATIVE = -1000000000.0


def low_dot(left_side, right_side):
    return jnp.dot(left_side, right_side, preferred_element_type=jnp.float32)


def layer_norm(field, scale_gain):
    center = field - jnp.mean(field, axis=-1, keepdims=True)
    spread = jnp.mean(center * center, axis=-1, keepdims=True)
    return center * lax.rsqrt(spread + EPSILON) * scale_gain


def choose(select, count):
    return jnp.sum(
        (select[..., None] == jnp.arange(count, dtype=jnp.int32)).astype(jnp.float32), axis=-2
    )


def attention_probs(query_heads, key_heads, query_pos, length):
    key_pos = jnp.arange(key_heads.shape[0], dtype=jnp.int32)
    raw_scores = jnp.einsum(
        "qhd,khd->hqk", query_heads, key_heads, preferred_element_type=jnp.float32
    )
    allowed = (key_pos[None, :] <= query_pos[:, None]) & (key_pos[None, :] < length)
    scores = jnp.where(allowed[None], raw_scores * HEAD_DIM ** (-0.5), NEGATIVE)
    exp_terms = jnp.exp(scores - jnp.max(scores, axis=-1, keepdims=True))
    return exp_terms / jnp.sum(exp_terms, axis=-1, keepdims=True)


def dot_last(left_side, right_side):
    return lax.dot_general(
        left_side, right_side, (((1,), (1,)), ((), ())), preferred_element_type=jnp.float32
    )

def dot_first(left_side, right_side):
    return lax.dot_general(
        left_side, right_side, (((0,), (0,)), ((), ())), preferred_element_type=jnp.float32
    )


def visit_kernel(
    sent, cot, up, down, back_out, up_out, down_out,
    rows, cot_other, up_wide, chosen, cots, gated, grad_pre, gated_turned, pre_turned, partial, paired_in, chain_in, up_low, down_low, up_in, down_in,
    row_send, row_recv, cot_send, cot_recv, pair_send, pair_recv, chain_send, chain_recv, grad_send, grad_recv,
):
    experts = up.shape[0]
    wide = down.shape[0]
    hidden = wide // experts
    dp, ex = lax.axis_index("dp"), lax.axis_index("expert")
    y, x, z, core = dp // 2, dp % 2, ex // 2, ex % 2
    half = z // 2
    inner = z + half * (3 - 2 * z)
    onward = 1 - 2 * half
    sibling = (dp, z * 2 + 1 - core)
    beside, behind = (y * 2 + 1 - x, ex), ((1 - y) * 2 + x, ex)

    def at_z(place):
        return (dp, place * 2 + core)

    barrier = pltpu.get_barrier_semaphore()
    for place in (sibling, beside, behind):
        pl.semaphore_signal(barrier, inc=1, device_id=place, device_id_type=MESH)

    @pl.when(z < 3)
    def _():
        pl.semaphore_signal(barrier, inc=1, device_id=at_z(z + 1), device_id_type=MESH)

    @pl.when(z > 0)
    def _():
        pl.semaphore_signal(barrier, inc=1, device_id=at_z(z - 1), device_id_type=MESH)

    pl.semaphore_wait(barrier, 4 + inner)

    def remote(source, target, send, recv, place):
        return pltpu.make_async_remote_copy(
            src_ref=source, dst_ref=target, send_sem=send, recv_sem=recv, device_id=place, device_id_type=MESH
        )

    def row_copy(way, at, source=None):
        place = (sibling, at_z(z + 1), at_z(z - 1))[way]
        block = rows.at[at]
        target = block if way else rows.at[4 + at]
        return remote(block if source is None else source, target, row_send.at[way, at], row_recv.at[0 if way else 1, at], place)

    def cot_copy(at):
        return remote(cot.at[at], cot_other.at[at], cot_send.at[at], cot_recv.at[at], sibling)

    own = row_copy(0, z, sent), row_copy(1, z, sent), row_copy(2, z, sent)

    @pl.when(z < 3)
    def _():
        own[1].start()

    @pl.when(z > 0)
    def _():
        own[2].start()

    own[0].start()
    cot_copy(z).start()
    for k in (1, 2, 3):
        cot_copy((z + k) % 4).start()
    rows[z] = sent[...]
    for e in range(experts):
        up_wide[:, e * hidden : (e + 1) * hidden] = up[e]
    chosen[...] = (
        lax.broadcasted_iota(jnp.int32, (128, wide), 0)
        == 2 * HEADS * VE + ex * experts + lax.broadcasted_iota(jnp.int32, (128, wide), 1) // hidden
    ).astype(jnp.float32).astype(jnp.bfloat16)

    def order(p):
        later = (p + 2) // 3
        step = p - inner // (p + 1 - later)
        return later * (step + half * (3 - 2 * step)) + (1 - later) * z

    def pair_copy(at):
        return remote(partial.at[1, at], paired_in.at[at], pair_send.at[at], pair_recv.at[at], sibling)

    spans = (pl.ds(0, D), pl.ds(D, D + 128))

    def chain_copy(dest, slot, to, stage, part):
        span = spans[part]
        return remote(
            partial.at[0, dest, :, span], chain_in.at[slot, :, span],
            chain_send.at[stage, part], chain_recv.at[slot, part], at_z(to),
        )

    def add(target, source):
        def some(i, carry):
            part = pl.ds(pl.multiple_of(i * 32, 32), 32)
            target[part, :] = (
                target[part, :].astype(jnp.float32) + source[part, :].astype(jnp.float32)
            ).astype(target.dtype)
            return carry

        lax.fori_loop(0, target.shape[0] // 32, some, 0)

    def visit(q, carry):
        p, other = q // 2, q % 2
        at = order(p)
        block = other * 4 + at

        @pl.when((other == 0) & (p > 0))
        def _():
            row_copy(1, at).wait_recv()
            row_copy(0, at).start()

            @pl.when((at < z) & (z < 3))
            def _():
                row_copy(1, at).start()

            @pl.when((at > z) & (z > 0))
            def _():
                row_copy(2, at).start()

        @pl.when(other == 1)
        def _():
            row_copy(0, at).wait_recv()
            cot_copy(at).wait_recv()
            cots[...] = cot_other[at]

        @pl.when(other == 0)
        def _():
            cots[...] = cot[at]

        count = rows.shape[1]
        places = pl.ds(pl.multiple_of(block * count, count), count)

        def columns(n, gate_grad):
            span = pl.ds(pl.multiple_of(n * 256, 256), 256)
            pre = jnp.dot(rows[block, :, :D], up_wide[:, span], preferred_element_type=jnp.float32)
            back = dot_last(cots[...], down[span, :])
            mark = chosen[:, span]
            gate = jnp.dot(rows[block, :, D:], mark, preferred_element_type=jnp.float32)
            sig = jax.nn.sigmoid(pre)
            act = pre * sig
            act_low = (gate * act).astype(jnp.bfloat16)
            pre_low = (gate * back * (sig * (1.0 + pre * (1.0 - sig)))).astype(jnp.bfloat16)
            gated[:, span] = act_low
            grad_pre[:, span] = pre_low
            gated_turned[span, places] = act_low.T
            pre_turned[span, places] = pre_low.T
            return gate_grad + dot_last((act * back).astype(jnp.bfloat16), mark)

        partial[other, at, :, 2 * D :] = lax.fori_loop(
            0, wide // 256, columns, jnp.zeros((count, 128), jnp.float32)
        ).astype(jnp.bfloat16)

        def outward(n, carry):
            span = pl.ds(pl.multiple_of(n * 256, 256), 256)
            partial[other, at, :, span] = jnp.dot(
                gated[...], down[:, span], preferred_element_type=jnp.float32
            ).astype(jnp.bfloat16)
            partial[other, at, :, pl.ds(pl.multiple_of(D + n * 256, 256), 256)] = dot_last(
                grad_pre[...], up_wide[span, :]
            ).astype(jnp.bfloat16)
            return carry

        lax.fori_loop(0, D // 256, outward, 0)

        @pl.when(other == 1)
        def _():
            pair_copy(at).start()
            pair_copy(at).wait_recv()
            add(partial.at[0, at], paired_in.at[at])

        @pl.when((inner == 0) & (q == 3))
        def _():
            chain_copy(*nearest, 0).start()

        @pl.when((inner == 0) & (q == 5))
        def _():
            chain_copy(*next_one, 0).start()

        return carry

    nearest = (z + onward, z + onward, z + onward, 0)
    farthest = (3 * (1 - half), 3 * (1 - half), z + onward, 1)
    backward = (3 * half, 3 * half, z - onward, 2)
    next_one = (2 - half, 2 - half + inner * (2 + half), z + onward, 3)
    lax.fori_loop(0, 8, visit, 0)

    def relay(dest, slot, to, stage, part):
        chain_copy(dest, dest, to, stage, part).wait_recv()
        add(partial.at[0, dest, :, spans[part]], chain_in.at[dest, :, spans[part]])
        chain_copy(dest, slot, to, stage, part).start()

    @pl.when(inner == 0)
    def _():
        chain_copy(*farthest, 0).start()
        chain_copy(*farthest, 1).start()
        chain_copy(*next_one, 1).start()
        chain_copy(*nearest, 1).start()

    @pl.when(inner == 1)
    def _():
        relay(*next_one, 0)

    tokens_all = rows.reshape(rows.shape[0] * rows.shape[1], rows.shape[2])
    cots_own = cot.reshape(cot.shape[0] * cot.shape[1], D)
    cots_other = cot_other.reshape(cot.shape[0] * cot.shape[1], D)
    place = cots_own.shape[0]
    quarter = D // 4


    def up_copy(j):
        return remote(up_low.at[j], up_in.at[j], grad_send.at[0, j], grad_recv.at[0, j], behind if j == 2 else beside)

    def down_copy(j):
        return remote(down_low.at[j], down_in.at[j], grad_send.at[1, j], grad_recv.at[1, j], beside if j == 1 else behind)

    def weight_grads(j, carry):
        across, aside = 1 - j % 2, 1 - j // 2
        at = (y + across * (1 - 2 * y)) * 2 + x + aside * (1 - 2 * x)
        span = pl.ds(pl.multiple_of(at * quarter, quarter), quarter)
        up_low[j] = jnp.dot(
            pre_turned[...], tokens_all[:, span], preferred_element_type=jnp.float32
        ).astype(jnp.bfloat16)
        down_low[j] = (
            jnp.dot(gated_turned[:, :place], cots_own[:, span], preferred_element_type=jnp.float32)
            + jnp.dot(gated_turned[:, place:], cots_other[:, span], preferred_element_type=jnp.float32)
        ).astype(jnp.bfloat16)

        @pl.when(j == 0)
        def _():
            up_copy(0).start()
            down_copy(0).start()

        @pl.when(j == 1)
        def _():
            up_copy(1).start()

        @pl.when(j == 2)
        def _():
            down_copy(2).start()

        return carry

    lax.fori_loop(0, 4, weight_grads, 0)
    up_copy(0).wait()
    add(up_low.at[2], up_in.at[0])
    up_copy(2).start()
    down_copy(0).wait()
    add(down_low.at[1], down_in.at[0])
    down_copy(1).start()

    @pl.when(inner == 1)
    def _():
        for way, part in ((farthest, 0), (backward, 0), (farthest, 1), (backward, 1), (next_one, 1)):
            relay(*way, part)

    up_sum = up_low[3].astype(jnp.float32)
    down_sum = down_low[3].astype(jnp.float32)
    for j in (1, 2):
        up_copy(j).wait()
        up_sum += up_in[j].astype(jnp.float32)
        down_copy(j).wait()
        down_sum += down_in[j].astype(jnp.float32)
    for e in range(experts):
        up_out[e] = up_sum[e * hidden : (e + 1) * hidden, :].T
        down_out[e] = down_sum[e * hidden : (e + 1) * hidden, :]

    for part in range(2):
        span = spans[part]
        chain_copy(z, z, z, 0, part).wait_recv()
        back_out[:, span] = partial[0, z, :, span].astype(jnp.float32) + chain_in[z, :, span].astype(jnp.float32)

        @pl.when(inner == 1)
        def _():
            chain_copy(z, 4, z, 0, part).wait_recv()
            back_out[:, span] = back_out[:, span] + chain_in[4, :, span].astype(jnp.float32)

    for at in range(4):
        row_copy(0, at).wait_send()
        cot_copy(at).wait_send()
        pair_copy(at).wait_send()

        @pl.when((at <= z) & (z < 3))
        def _():
            row_copy(1, at).wait_send()

        @pl.when((at >= z) & (z > 0))
        def _():
            row_copy(2, at).wait_send()

    for part in range(2):

        @pl.when(inner == 0)
        def _():
            chain_copy(z, 0, z, 0, part).wait_send()

        @pl.when(inner == 1)
        def _():
            chain_copy(z, 0, z, 2, part).wait_send()

        chain_copy(z, 0, z, 1, part).wait_send()
        chain_copy(z, 0, z, 3, part).wait_send()

def expert_kernel_visit(sent, cot_line, up, down):
    tokens = sent.shape[0]
    experts, _, hidden = up.shape
    wide = experts * hidden
    low = jnp.bfloat16
    vmem = pl.BlockSpec(memory_space=pltpu.VMEM)
    dma = pltpu.SemaphoreType.DMA
    f32 = jnp.float32
    return pl.pallas_call(
        visit_kernel,
        out_shape=[
            jax.ShapeDtypeStruct((tokens, 2 * D + 128), f32),
            jax.ShapeDtypeStruct((experts, D // 4, hidden), f32),
            jax.ShapeDtypeStruct((experts, hidden, D // 4), f32),
        ],
        in_specs=[vmem] * 4,
        out_specs=[vmem] * 3,
        scratch_shapes=[
            pltpu.VMEM((8, tokens, D + 128), low),
            pltpu.VMEM((4, tokens, D), low),
            pltpu.VMEM((D, wide), low),
            pltpu.VMEM((128, wide), low),
            pltpu.VMEM((tokens, D), low),
            pltpu.VMEM((tokens, wide), low),
            pltpu.VMEM((tokens, wide), low),
            pltpu.VMEM((wide, 8 * tokens), low),
            pltpu.VMEM((wide, 8 * tokens), low),
            pltpu.VMEM((2, 4, tokens, 2 * D + 128), low),
            pltpu.VMEM((4, tokens, 2 * D + 128), low),
            pltpu.VMEM((5, tokens, 2 * D + 128), low),
            pltpu.VMEM((4, wide, D // 4), low),
            pltpu.VMEM((4, wide, D // 4), low),
            pltpu.VMEM((3, wide, D // 4), low),
            pltpu.VMEM((3, wide, D // 4), low),
            dma((3, 4)), dma((2, 4)), dma((4,)), dma((4,)), dma((4,)), dma((4,)), dma((4, 2)), dma((5, 2)), dma((2, 3)), dma((2, 3)),
        ],
        compiler_params=pltpu.CompilerParams(collective_id=2, has_side_effects=True, vmem_limit_bytes=58 * 2**20),
        name="expert_visit",
    )(sent, cot_line, up, down.reshape(wide, D))


def attend_kernel(
    expert_total, lengths, hidden, cot, value_pick, output_pick, expert_pick, routers, gains,
    key_weight_at, value_weight_at, query_weight_at, output_weight_at,
    middle, sent, normed_one, normed_two, queries, key_value, probs, value_all, attended,
    gates, slopes, cot_line,
    key_weight, value_weight, query_weight, output_weight, mixed, hot_turned, hot,
    fetch, pair_send, pair_recv, cot_send, cot_recv, own_sem,
):
    dp, ex = lax.axis_index("dp"), lax.axis_index("expert")
    z, core = ex // 2, ex % 2
    half = z // 2
    inner = z + half * (3 - 2 * z)
    count = hidden.shape[0]
    width = HEADS * HEAD_DIM
    low = jnp.bfloat16
    length = lengths[0]
    spread = HEADS * VE
    total = expert_total
    weights = [
        pltpu.make_async_copy(source, target, fetch.at[i])
        for i, (source, target) in enumerate(
            (
                (key_weight_at, key_weight),
                (value_weight_at, value_weight),
                (query_weight_at, query_weight),
                (output_weight_at, output_weight),
            )
        )
    ]
    for made in weights:
        made.start()

    def at_z(place):
        return (dp, place * 2 + core)

    barrier = pltpu.get_barrier_semaphore()
    for k in (1, 2, 3):
        pl.semaphore_signal(barrier, inc=1, device_id=((dp + k) % 4, ex), device_id_type=MESH)

    @pl.when(z < 3)
    def _():
        pl.semaphore_signal(barrier, inc=1, device_id=at_z(z + 1), device_id_type=MESH)

    @pl.when(z > 0)
    def _():
        pl.semaphore_signal(barrier, inc=1, device_id=at_z(z - 1), device_id_type=MESH)

    pl.semaphore_wait(barrier, 4 + inner)

    def cot_copy(way, at, source=None):
        block = cot_line.at[at]
        return pltpu.make_async_remote_copy(
            src_ref=block if source is None else source, dst_ref=block,
            send_sem=cot_send.at[way, at], recv_sem=cot_recv.at[at],
            device_id=at_z(z + 1 - 2 * way), device_id_type=MESH,
        )

    def pass_on(distance):
        @pl.when(z >= distance)
        def _():
            cot_copy(0, z - distance).wait_recv()

        @pl.when((z >= distance) & (z < 3))
        def _():
            cot_copy(0, z - distance).start()

        @pl.when(z + distance <= 3)
        def _():
            cot_copy(1, z + distance).wait_recv()

        @pl.when((z + distance <= 3) & (z > 0))
        def _():
            cot_copy(1, z + distance).start()

    @pl.when(z < 3)
    def _():
        cot_copy(0, z, cot).start()

    @pl.when(z > 0)
    def _():
        cot_copy(1, z, cot).start()

    keep = pltpu.make_async_copy(cot, cot_line.at[z], own_sem)
    keep.start()

    def norm(field, gain):
        center = field - jnp.mean(field, axis=-1, keepdims=True)
        spread = jnp.mean(center * center, axis=-1, keepdims=True)
        return (center * lax.rsqrt(spread + EPSILON) * gain).astype(low)

    parts = (pl.ds(0, width), pl.ds(width, width))

    def pair_copy(step, part, block):
        return pltpu.make_async_remote_copy(
            src_ref=key_value.at[block, :, parts[part]], dst_ref=key_value.at[block, :, parts[part]],
            send_sem=pair_send.at[step, part], recv_sem=pair_recv.at[block, part],
            device_id=((dp + step) % 4, ex), device_id_type=MESH,
        )

    def send_part(part):
        for step in (1, 2, 3):

            @pl.when(dp + step < 4)
            def _():
                pair_copy(step, part, dp).start()

    normed_one[...] = norm(hidden[...].astype(jnp.float32), gains[0:1, :])
    weights[0].wait()
    key_value[dp, :, parts[0]] = jnp.dot(
        normed_one[...], key_weight[...], preferred_element_type=jnp.float32
    ).astype(low)
    send_part(0)

    hot_turned[...] = jnp.zeros(hot_turned.shape, jnp.float32)

    def mark(picks, base, size):
        place = lax.broadcasted_iota(jnp.int32, (size, count), 0)
        found = jnp.zeros((size, count), jnp.float32)
        for pick in picks:
            found = jnp.where(place == pick, 1.0, found)
        hot_turned[base : base + size, :] = found

    mark([value_pick[h, i : i + 1, :] + h * VE for h in range(HEADS) for i in range(value_pick.shape[1])], 0, spread)
    mark(
        [output_pick[h, i : i + 1, :] + h * VE for h in range(HEADS) for i in range(output_pick.shape[1])],
        spread,
        spread,
    )
    mark([expert_pick[i : i + 1, :] for i in range(expert_pick.shape[0])], 2 * spread, total)
    hot[...] = hot_turned[...].T
    sig = jax.nn.sigmoid(dot_last(normed_one[...], routers[...]))
    gates[...] = sig * hot[...]
    slopes[...] = gates[...] * (1.0 - sig)
    weights[1].wait()

    def values(n, carry):
        span = pl.ds(pl.multiple_of(n * 256, 256), 256)
        value_all[:, span] = jnp.dot(
            hidden[...], value_weight[:, span], preferred_element_type=jnp.float32
        ).astype(low)
        return carry

    lax.fori_loop(0, HEADS * VE * HEAD_DIM // 256, values, 0)
    for h in range(HEADS):
        row = jnp.zeros((count, HEAD_DIM), jnp.float32)
        for e in range(h * VE, (h + 1) * VE):
            row += gates[:, e : e + 1] * value_all[:, e * HEAD_DIM : (e + 1) * HEAD_DIM].astype(jnp.float32)
        key_value[dp, :, width + h * HEAD_DIM : width + (h + 1) * HEAD_DIM] = row.astype(low)
    send_part(1)

    weights[2].wait()
    queries[...] = jnp.dot(normed_one[...], query_weight[...], preferred_element_type=jnp.float32).astype(low)
    for block in range(4):

        @pl.when(block > dp)
        def _():
            key_value[block] = jnp.zeros((count, 2 * width), low)

    pass_on(1)

    def wait_part(part):
        for block in range(3):

            @pl.when(block < dp)
            def _():
                pair_copy(1, part, block).wait_recv()

    wait_part(0)
    pair_all = key_value.reshape(4 * count, 2 * width)
    query_pos = dp * count + lax.broadcasted_iota(jnp.int32, (count, 4 * count), 0)
    key_pos = lax.broadcasted_iota(jnp.int32, (count, 4 * count), 1)
    allowed = (key_pos <= query_pos) & (key_pos < length)

    def score(h, carry):
        span = pl.ds(pl.multiple_of(h * HEAD_DIM, HEAD_DIM), HEAD_DIM)
        raw = dot_last(queries[:, span], pair_all[:, span])
        scores = jnp.where(allowed, raw * HEAD_DIM ** (-0.5), NEGATIVE)
        terms = jnp.exp(scores - jnp.max(scores, axis=-1, keepdims=True))
        probs[h] = (terms * (1.0 / jnp.sum(terms, axis=-1, keepdims=True))).astype(low)
        return carry

    lax.fori_loop(0, HEADS, score, 0)
    wait_part(1)
    pass_on(2)

    def collect(h, carry):
        span = pl.ds(pl.multiple_of(h * HEAD_DIM, HEAD_DIM), HEAD_DIM)
        value_span = pl.ds(pl.multiple_of(width + h * HEAD_DIM, HEAD_DIM), HEAD_DIM)
        attended[:, span] = jnp.dot(probs[h], pair_all[:, value_span], preferred_element_type=jnp.float32)
        return carry

    lax.fori_loop(0, HEADS, collect, 0)
    for h in range(HEADS):
        row = attended[:, h * HEAD_DIM : (h + 1) * HEAD_DIM]
        for e in range(h * VE, (h + 1) * VE):
            mixed[:, e * HEAD_DIM : (e + 1) * HEAD_DIM] = (gates[:, spread + e : spread + e + 1] * row).astype(low)

    place = dp * count + lax.broadcasted_iota(jnp.int32, (count, 1), 0)
    live = jnp.where(place < length, 1.0, 0.0)
    weights[3].wait()

    def outward(n, carry):
        span = pl.ds(pl.multiple_of(n * 256, 256), 256)
        branch = jnp.dot(mixed[...], output_weight[:, span], preferred_element_type=jnp.float32)
        middle[:, span] = hidden[:, span].astype(jnp.float32) + live * branch
        return carry

    lax.fori_loop(0, D // 256, outward, 0)
    sent[:, :D] = middle[...].astype(low)
    normed_two[...] = norm(middle[...], gains[1:2, :])
    sig = jax.nn.sigmoid(dot_last(normed_two[...], routers[...]))
    gate = sig * hot[...] * live
    sent[:, D:] = gate.astype(low)
    lane = lax.broadcasted_iota(jnp.int32, (count, 128), 1)
    slopes[...] = jnp.where(lane < 2 * spread, slopes[...], gate * (1.0 - sig))

    pass_on(3)
    keep.wait()
    for part in range(2):
        for step in (1, 2, 3):

            @pl.when(dp + step < 4)
            def _():
                pair_copy(step, part, dp).wait_send()

    for at in range(4):

        @pl.when((at <= z) & (z < 3))
        def _():
            cot_copy(0, at).wait_send()

        @pl.when((at >= z) & (z > 0))
        def _():
            cot_copy(1, at).wait_send()


def attend(total, lengths, *operands):
    count = operands[0].shape[0]
    low, full = jnp.bfloat16, jnp.float32
    vmem = pl.BlockSpec(memory_space=pltpu.VMEM)
    anywhere = pl.BlockSpec(memory_space=pl.ANY)
    dma = pltpu.SemaphoreType.DMA
    width, wide = HEADS * HEAD_DIM, HEADS * VE * HEAD_DIM
    shapes = [
        ((count, D), full),
        ((count, D + 128), low),
        ((count, D), low),
        ((count, D), low),
        ((count, width), low),
        ((4, count, 2 * width), low),
        ((HEADS, count, 4 * count), low),
        ((count, wide), low),
        ((count, width), full),
        ((count, 128), full),
        ((count, 128), full),
        ((4, count, D), low),
    ]
    return pl.pallas_call(
        functools.partial(attend_kernel, total),
        out_shape=[jax.ShapeDtypeStruct(*shape) for shape in shapes],
        in_specs=[pl.BlockSpec(memory_space=pltpu.SMEM)] + [vmem] * (len(operands) - 4) + [anywhere] * 4,
        out_specs=[vmem] * len(shapes),
        scratch_shapes=[pltpu.VMEM(a.shape, a.dtype) for a in operands[-4:]]
        + [
            pltpu.VMEM((count, wide), low),
            pltpu.VMEM((128, count), full),
            pltpu.VMEM((count, 128), full),
            dma((4,)),
            dma((4, 2)),
            dma((4, 2)),
            dma((2, 4)),
            dma((4,)),
            dma,
        ],
        compiler_params=pltpu.CompilerParams(
            collective_id=1, has_side_effects=True, vmem_limit_bytes=58 * 2**20
        ),
        name="attend",
    )(lengths, *operands)


def backward_kernel(
    total_experts, lengths, gates, slopes, routers, gains,
    returned_at, middle_at, cot_at, hidden_at, normed_one_at, queries_at, key_value_at, probs_at, value_all_at,
    attended_at, normed_two_at, query_weight_at, key_weight_at, value_weight_at, output_weight_at,
    block_out, grad_in, out_query, out_key, out_value, out_output, out_small, sums_out,
    returned, middle, cot, hidden, normed_one, queries, key_value, probs, value_all,
    attended, normed_two, query_weight, key_weight, value_part, output_part,
    branch, branch_turned, one_turned, hidden_turned, grad_att, grad_query, leave, arrive, grad_key, grad_value,
    grad_each, grad_middle, grad_one, logit_one, logit_two, small_turned, mixed,
    grads, grads_small, core_in, plane_in, last_in, sums_in,
    fetch, part_fetch, leave_send, leave_recv, send, recv,
):
    dp, ex = lax.axis_index("dp"), lax.axis_index("expert")
    y, x, z, core = dp // 2, dp % 2, ex // 2, ex % 2
    count = hidden.shape[0]
    width = HEADS * HEAD_DIM
    low, full = jnp.bfloat16, jnp.float32
    length = lengths[0]
    sibling = (dp, z * 2 + 1 - core)
    beside = (y * 2 + 1 - x, ex)
    behind = ((1 - y) * 2 + x, ex)
    across = ((1 - y) * 2 + 1 - x, ex)
    line = [(dp, ((z + k) % 4) * 2 + core) for k in (1, 2, 3)]
    barrier = pltpu.get_barrier_semaphore()
    for place in (sibling, beside, behind, across, *line):
        pl.semaphore_signal(barrier, inc=1, device_id=place, device_id_type=MESH)

    held = dict(
        returned=(returned_at, returned),
        middle=(middle_at, middle),
        cot=(cot_at, cot),
        hidden=(hidden_at, hidden),
        attended=(attended_at, attended),
        key_value=(key_value_at, key_value),
        probs=(probs_at, probs),
        queries=(queries_at, queries),
        normed_one=(normed_one_at, normed_one),
        query_weight=(query_weight_at, query_weight),
        value_all=(value_all_at, value_all),
        key_weight=(key_weight_at, key_weight),
        normed_two=(normed_two_at, normed_two),
    )
    got = {
        name: pltpu.make_async_copy(source, target, fetch.at[i])
        for i, (name, (source, target)) in enumerate(held.items())
    }

    def output_copy(n):
        return pltpu.make_async_copy(
            output_weight_at.at[pl.ds(n * 512, 512)], output_part.at[n % 2], part_fetch.at[0, n % 2]
        )

    def value_copy(n):
        return pltpu.make_async_copy(
            value_weight_at.at[:, pl.ds(n * 512, 512)], value_part.at[n % 2], part_fetch.at[1, n % 2]
        )

    first_held = ("returned", "middle", "cot", "hidden")
    for name in first_held:
        got[name].start()
    for n in range(2):
        output_copy(n).start()
    for name in held:
        if name not in first_held:
            got[name].start()
    for n in range(2):
        value_copy(n).start()

    pieces = (
        [(out_output, 512 * n, 512, n) for n in range(5)]
        + [(out_query, 0, 512, 5), (out_key, 0, 512, 6)]
        + [(out_value, 512 * n, 512, n) for n in range(5)]
        + [(out_small, 0, 128, None)]
    )
    along_line = (0, 1, 2, 3)
    in_plane = [i for i in range(len(pieces)) if i not in along_line]
    x_first = {i: n % 2 == 0 for n, i in enumerate(in_plane)}

    def remote(source, target, slot, place):
        return pltpu.make_async_remote_copy(
            src_ref=source, dst_ref=target, send_sem=send.at[slot], recv_sem=recv.at[slot],
            device_id=place, device_id_type=MESH,
        )

    def add(target, source):
        target[...] = (target[...].astype(full) + source[...].astype(full)).astype(target.dtype)

    def own(i):
        slot = pieces[i][3]
        return grads_small if slot is None else grads.at[slot]

    def columns(i):
        return pl.ds(0, pieces[i][2])

    started = {}

    def begin(key, source, target, slot, place):
        started[key] = remote(source, target, slot, place)
        started[key].start()

    def halve_core(i):
        begin((i, 0), own(i).at[:, :, 1 - core], core_in.at[i, :, :, :, columns(i)], (i, 0), sibling)

    def halve_near(i):
        span = columns(i)
        started[i, 0].wait()
        add(core_in.at[i, :, :, :, span], own(i).at[:, :, core])
        if i in along_line:
            for k in (1, 2, 3):
                begin(
                    (i, k), core_in.at[i, :, (z + k) % 4, :, span],
                    plane_in.at[i, pl.ds(4 * k - 4, 4), :, span], (i, k), line[k - 1],
                )
            return
        for part in range(2):
            if x_first[i]:
                source = core_in.at[i, part * 2 + 1 - x, :, :, span]
            else:
                source = core_in.at[i, (1 - y) * 2 + part, :, :, span]
            target = plane_in.at[i, pl.ds(part * 4, 4), :, span]
            begin((i, 1 + part), source, target, (i, 1 + part), beside if x_first[i] else behind)

    def halve_far(i):
        span = columns(i)
        if i in along_line:
            held = core_in.at[i, :, z, :, span]
            for k in (1, 2, 3):
                started[i, k].wait()
                add(held, plane_in.at[i, pl.ds(4 * k - 4, 4), :, span])
            for part in range(2):
                begin(
                    (i, 4 + part), core_in.at[i, part * 2 + 1 - x, z, :, span],
                    last_in.at[i, part, :, span], (i, 4 + part), beside,
                )
            return
        for part in range(2):
            started[i, 1 + part].wait()
            kept = part * 2 + x if x_first[i] else y * 2 + part
            add(plane_in.at[i, pl.ds(part * 4, 4), :, span], core_in.at[i, kept, :, :, span])
        other = 1 - y if x_first[i] else 1 - x
        begin(
            (i, 3), plane_in.at[i, pl.ds(other * 4, 4), :, span], plane_in.at[i, pl.ds(8, 4), :, span],
            (i, 3), behind if x_first[i] else beside,
        )

    def spread(i):
        span = columns(i)
        if i in along_line:
            for part in range(2):
                started[i, 4 + part].wait()
                add(last_in.at[i, part, :, span], core_in.at[i, part * 2 + x, z, :, span])
            begin((i, 6), last_in.at[i, 1 - y, :, span], last_in.at[i, 2, :, span], (i, 6), behind)
            return
        started[i, 3].wait()
        add(plane_in.at[i, pl.ds(8, 4), :, span], plane_in.at[i, pl.ds((y if x_first[i] else x) * 4, 4), :, span])
        for k in (1, 2, 3):
            begin(
                (i, 3 + k), plane_in.at[i, 8 + (z + k) % 4, :, span],
                last_in.at[i, k - 1, :, span], (i, 3 + k), line[k - 1],
            )

    def finish(i):
        out, start, size, _ = pieces[i]
        span = columns(i)
        if i in along_line:
            started[i, 6].wait()
            total = last_in[i, y, :, span].astype(full) + last_in[i, 2, :, span].astype(full)
        else:
            total = plane_in[i, 8 + z, :, span].astype(full)
            for k in (1, 2, 3):
                started[i, 3 + k].wait()
                total = total + last_in[i, k - 1, :, span].astype(full)
        out[:, pl.ds(start, size)] = total

    rows_each = 64
    lane = lax.broadcasted_iota(jnp.int32, (1, 128), 1)
    for name in first_held:
        got[name].wait()
    logit_two[...] = (returned[:, 2 * D :] * slopes[...]).astype(low)

    def live_rows(start):
        place = dp * count + start + lax.broadcasted_iota(jnp.int32, (rows_each, 1), 0)
        return jnp.where(place < length, 1.0, 0.0)

    def norm_back(field, grad, gain):
        center = field - jnp.mean(field, axis=-1, keepdims=True)
        scale = lax.rsqrt(jnp.mean(center * center, axis=-1, keepdims=True) + EPSILON)
        unit = center * scale
        part = grad * gain
        back = scale * (
            part
            - jnp.mean(part, axis=-1, keepdims=True)
            - unit * jnp.mean(part * unit, axis=-1, keepdims=True)
        )
        return back, jnp.sum(grad * unit, axis=0, keepdims=True)

    def square(field, live, at):
        total = jnp.sum(jnp.sum(field * field, axis=1, keepdims=True) * live, axis=0, keepdims=True)
        return jnp.where(lane == at, total, 0.0)

    def first_rows(n, carry):
        gain_sum, sums = carry
        start = pl.multiple_of(n * rows_each, rows_each)
        rows = pl.ds(start, rows_each)
        live = live_rows(start)
        field = middle[rows, :]
        forward = returned[rows, :D]
        final = field + forward
        block_out[rows, :] = final.astype(low)
        source = hidden[rows, :].astype(full)
        one = jnp.ones((rows_each, 1), full)
        sums += square(source, live, 0) + square(field - source, one, 1)
        sums += square(forward, one, 2) + square(final, live, 3)
        sums += jnp.where(lane == 4, jnp.sum(live, axis=0, keepdims=True), 0.0)
        grad = jnp.dot(logit_two[rows, :], routers[...], preferred_element_type=full)
        back, gain_part = norm_back(field, grad, gains[1:2, :])
        total = cot[rows, :].astype(full) + returned[rows, D : 2 * D] + back
        grad_middle[rows, :] = total
        branch[rows, :] = (live * total).astype(low)
        return gain_sum + gain_part, sums

    gain_two_sum, sums = lax.fori_loop(
        0, count // rows_each, first_rows, (jnp.zeros((1, D), full), jnp.zeros((1, 128), full))
    )
    sums_in[0] = jnp.broadcast_to(sums, (8, 128))
    pl.semaphore_wait(barrier, 7)

    def weight_grad(i, turned, right, size):
        flat = own(i)
        flat = flat.reshape(D, size)

        def some(n, carry):
            rows = pl.ds(pl.multiple_of(n * 256, 256), 256)
            flat[rows, :] = jnp.dot(turned[rows, :], right, preferred_element_type=full).astype(low)
            return carry

        lax.fori_loop(0, D // 256, some, 0)
        halve_core(i)

    branch_turned[...] = branch[...].T
    got["attended"].wait()

    def head_of(c):
        return slice((c // VE) * HEAD_DIM, (c // VE + 1) * HEAD_DIM)

    spread_count = HEADS * VE
    for n in range(5):
        for j in range(4):
            c = 4 * n + j
            gate = gates[:, spread_count + c : spread_count + c + 1]
            mixed[:, j * HEAD_DIM : (j + 1) * HEAD_DIM] = (gate * attended[:, head_of(c)]).astype(low)
        weight_grad(n, branch_turned, mixed[...], 512)
    logit_one[...] = jnp.zeros(logit_one.shape, full)
    grad_att[...] = jnp.zeros(grad_att.shape, full)
    for n in range(5):
        output_copy(n).wait()
        for j in range(4):
            c = 4 * n + j
            grad_mixed = dot_last(branch[...], output_part[n % 2, j * HEAD_DIM : (j + 1) * HEAD_DIM, :])
            col = spread_count + c
            grad_att[:, head_of(c)] += gates[:, col : col + 1] * grad_mixed
            dots = jnp.sum(attended[:, head_of(c)] * grad_mixed, axis=1, keepdims=True)
            logit_one[:, col : col + 1] = dots * slopes[:, col : col + 1]
        if n + 2 < 5:
            output_copy(n + 2).start()
        halve_near(n)

    pair_all = key_value.reshape(4 * count, 2 * width)
    for name in ("key_value", "probs", "queries"):
        got[name].wait()

    def leave_copy(k, h):
        rows = pl.ds(h * 2 * HEAD_DIM, 2 * HEAD_DIM)
        return pltpu.make_async_remote_copy(
            src_ref=leave.at[(dp + 4 - k) % 4, rows], dst_ref=arrive.at[k - 1, rows],
            send_sem=leave_send.at[k - 1, h], recv_sem=leave_recv.at[k - 1, h],
            device_id=((dp + 4 - k) % 4, ex), device_id_type=MESH,
        )

    def head(h, carry):
        start = pl.multiple_of(h * HEAD_DIM, HEAD_DIM)
        span = pl.ds(start, HEAD_DIM)
        grad = grad_att[:, span].astype(low)
        prob = probs[h].astype(full)
        grad_prob = dot_last(grad, pair_all[:, pl.ds(width + start, HEAD_DIM)])
        dots = jnp.sum(prob * grad_prob, axis=-1, keepdims=True)
        grad_score = (prob * (grad_prob - dots) * HEAD_DIM ** (-0.5)).astype(low)
        grad_query[:, span] = jnp.dot(grad_score, pair_all[:, span], preferred_element_type=full).astype(low)
        key_part = dot_first(queries[:, span], grad_score).astype(low)
        value_part_all = dot_first(grad, probs[h]).astype(low)
        key_rows = pl.ds(pl.multiple_of(2 * h * HEAD_DIM, 2 * HEAD_DIM), HEAD_DIM)
        value_rows = pl.ds(pl.multiple_of((2 * h + 1) * HEAD_DIM, HEAD_DIM), HEAD_DIM)
        for j in range(4):
            leave[j, key_rows, :] = key_part[:, j * count : (j + 1) * count]
            leave[j, value_rows, :] = value_part_all[:, j * count : (j + 1) * count]
        for k in (1, 2, 3):

            @pl.when(dp >= k)
            def _():
                leave_copy(k, h).start()

        return carry

    lax.fori_loop(0, HEADS, head, 0)

    for name in ("normed_one", "query_weight"):
        got[name].wait()
    one_turned[...] = normed_one[...].T
    weight_grad(5, one_turned, grad_query[...], 512)
    hidden_turned[...] = hidden[...].T
    grad_one[...] = dot_last(grad_query[...], query_weight[...])
    halve_near(5)

    for h in range(HEADS):
        rows = pl.ds(h * 2 * HEAD_DIM, 2 * HEAD_DIM)
        total = leave[dp, rows, :].astype(full)
        for k in (1, 2, 3):

            @pl.when(dp + k < 4)
            def _():
                leave_copy(k, h).wait_recv()

            @pl.when(dp + k >= 4)
            def _():
                arrive[k - 1, rows, :] = jnp.zeros((2 * HEAD_DIM, count), low)

            total += arrive[k - 1, rows, :].astype(full)
        turned = total.T
        grad_key[:, h * HEAD_DIM : (h + 1) * HEAD_DIM] = turned[:, :HEAD_DIM].astype(low)
        grad_value[:, h * HEAD_DIM : (h + 1) * HEAD_DIM] = turned[:, HEAD_DIM:].astype(low)

    got["value_all"].wait()
    for n in range(5):
        for j in range(4):
            c = 4 * n + j
            grad = grad_value[:, head_of(c)].astype(full)
            here = slice(c * HEAD_DIM, (c + 1) * HEAD_DIM)
            grad_each[:, here] = (gates[:, c : c + 1] * grad).astype(low)
            dots = jnp.sum(value_all[:, here].astype(full) * grad, axis=1, keepdims=True)
            logit_one[:, c : c + 1] = dots * slopes[:, c : c + 1]
        weight_grad(7 + n, hidden_turned, grad_each[:, n * 512 : (n + 1) * 512], 512)
        if n:
            halve_near(6 + n)
    weight_grad(6, one_turned, grad_key[...], 512)
    halve_near(11)
    got["key_weight"].wait()
    grad_one[...] += dot_last(grad_key[...], key_weight[...])
    halve_near(6)
    grad_one[...] += jnp.dot(logit_one[...].astype(low), routers[...], preferred_element_type=full)
    halve_far(5)

    def first_norm(n, gain_sum):
        rows = pl.ds(pl.multiple_of(n * rows_each, rows_each), rows_each)
        back, gain_part = norm_back(hidden[rows, :].astype(full), grad_one[rows, :], gains[0:1, :])
        grad_in[rows, :] = grad_middle[rows, :] + back
        return gain_sum + gain_part

    gain_one_sum = lax.fori_loop(0, count // rows_each, first_norm, jnp.zeros((1, D), full))
    halve_far(7)
    spread(5)
    got["normed_two"].wait()
    small_turned[...] = dot_first(logit_one[...].astype(low), normed_one[...]) + dot_first(
        logit_two[...], normed_two[...]
    )
    small_rows = 2 * spread_count + total_experts
    small_turned[small_rows : small_rows + 1, :] = gain_one_sum
    small_turned[small_rows + 1 : small_rows + 2, :] = gain_two_sum
    grads_small.reshape(D, 128)[...] = small_turned[...].T.astype(low)
    halve_core(12)

    rounds = [[sibling], [beside], [behind], line]
    offset = [1, 2, 3, 4]

    def sum_start(r):
        for j, place in enumerate(rounds[r]):
            begin(("sum", r, j), sums_in.at[0], sums_in.at[offset[r] + j], (len(pieces) + j, r), place)

    def sum_end(r):
        for j in range(len(rounds[r])):
            started["sum", r, j].wait()
        total = sums_in[0]
        for j in range(len(rounds[r])):
            total = total + sums_in[offset[r] + j]
        sums_in[0] = total

    sum_start(0)
    for n in range(5):
        value_copy(n).wait()
        part = dot_last(grad_each[:, n * 512 : (n + 1) * 512], value_part[n % 2])
        grad_in[...] += part
        if n + 2 < 5:
            value_copy(n + 2).start()
        if n == 0:
            halve_near(12)
            sum_end(0)
            sum_start(1)
        if n == 1:
            halve_far(8)
            spread(7)
        if n == 2:
            finish(5)
            halve_far(9)
            spread(8)
            sum_end(1)
            sum_start(2)
        if n == 3:
            halve_far(0)
            finish(7)
        if n == 4:
            sum_end(2)
            sum_start(3)
            halve_far(10)
            spread(9)

    for action, i in (
        (halve_far, 1), (spread, 0), (finish, 8), (halve_far, 4), (halve_far, 11), (spread, 10), (finish, 0), (finish, 9),
        (sum_end, 3),
        (halve_far, 2), (spread, 1), (spread, 4), (halve_far, 6), (spread, 11), (finish, 10), (finish, 1),
        (halve_far, 12), (spread, 2), (spread, 6), (finish, 4), (finish, 11), (halve_far, 3), (spread, 12), (finish, 2),
        (finish, 6), (spread, 3), (finish, 12), (finish, 3),
    ):
        action(i)
    sums_out[...] = sums_in[0]
    for h in range(HEADS):
        for k in (1, 2, 3):

            @pl.when(dp >= k)
            def _():
                leave_copy(k, h).wait_send()


def backward(total_experts, lengths, gates, slopes, routers, gains, *arrays):
    low, full = jnp.bfloat16, jnp.float32
    count = gates.shape[0]
    width, wide = HEADS * HEAD_DIM, HEADS * VE * HEAD_DIM
    vmem = pl.BlockSpec(memory_space=pltpu.VMEM)
    anywhere = pl.BlockSpec(memory_space=pl.ANY)
    dma = pltpu.SemaphoreType.DMA
    whole = [pltpu.VMEM(a.shape, a.dtype) for a in arrays[:13]]
    n = 13
    return pl.pallas_call(
        functools.partial(backward_kernel, total_experts),
        out_shape=[
            jax.ShapeDtypeStruct((count, D), low),
            jax.ShapeDtypeStruct((count, D), full),
            jax.ShapeDtypeStruct((ROWS, width), full),
            jax.ShapeDtypeStruct((ROWS, width), full),
            jax.ShapeDtypeStruct((ROWS, wide), full),
            jax.ShapeDtypeStruct((ROWS, wide), full),
            jax.ShapeDtypeStruct((ROWS, 128), full),
            jax.ShapeDtypeStruct((8, 128), full),
        ],
        in_specs=[pl.BlockSpec(memory_space=pltpu.SMEM)] + [vmem] * 4 + [anywhere] * len(arrays),
        out_specs=[vmem] * 8,
        scratch_shapes=whole
        + [
            pltpu.VMEM((2, D, 512), low),
            pltpu.VMEM((2, 512, D), low),
            pltpu.VMEM((count, D), low),
            pltpu.VMEM((D, count), low),
            pltpu.VMEM((D, count), low),
            pltpu.VMEM((D, count), low),
            pltpu.VMEM((count, width), full),
            pltpu.VMEM((count, width), low),
            pltpu.VMEM((4, 2 * width, count), low),
            pltpu.VMEM((3, 2 * width, count), low),
            pltpu.VMEM((count, width), low),
            pltpu.VMEM((count, width), low),
            pltpu.VMEM((count, wide), low),
            pltpu.VMEM((count, D), full),
            pltpu.VMEM((count, D), full),
            pltpu.VMEM((count, 128), full),
            pltpu.VMEM((count, 128), low),
            pltpu.VMEM((128, D), full),
            pltpu.VMEM((count, 512), low),
            pltpu.VMEM((7, 4, 4, 2, ROWS, 512), low),
            pltpu.VMEM((4, 4, 2, ROWS, 128), low),
            pltpu.VMEM((n, 4, 4, ROWS, 512), low),
            pltpu.VMEM((n, 12, ROWS, 512), low),
            pltpu.VMEM((n, 3, ROWS, 512), low),
            pltpu.VMEM((7, 8, 128), full),
            dma((13,)),
            dma((2, 2)),
            dma((3, HEADS)),
            dma((3, HEADS)),
            dma((n + 3, 7)),
            dma((n + 3, 7)),
        ],
        compiler_params=pltpu.CompilerParams(
            collective_id=3, has_side_effects=True, vmem_limit_bytes=62 * 2**20
        ),
        name="backward",
    )(lengths, gates, slopes, routers, gains, *arrays)


def expert_visit(sent, cotangent, expert_up, expert_down):
    local_experts = expert_up.shape[0]
    group = lax.axis_index("expert")
    cot_all = lax.all_gather(cotangent, "expert", axis=0, tiled=True)
    sent_all = lax.all_gather(sent, "expert", axis=0, tiled=True)
    rows_all = sent_all[:, :D]
    total_experts = sent.shape[1] - D
    gate_all = lax.dynamic_slice_in_dim(
        sent_all[:, D:], group * local_experts, local_experts, 1
    ).astype(jnp.float32).T[:, :, None]
    preact = jnp.einsum("td,xdf->xtf", rows_all, expert_up, preferred_element_type=jnp.float32)
    pre_sig = jax.nn.sigmoid(preact)
    hidden = preact * pre_sig
    back = jnp.einsum("td,xfd->xtf", cot_all, expert_down, preferred_element_type=jnp.float32)
    gate_grad = jnp.sum(hidden * back, axis=2).T
    gated = (gate_all * hidden).astype(jnp.bfloat16)
    grad_pre = (gate_all * back * (pre_sig * (1.0 + preact * (1.0 - pre_sig)))).astype(jnp.bfloat16)
    partial_out = jnp.einsum("xtf,xfd->td", gated, expert_down, preferred_element_type=jnp.float32)
    partial_grad = jnp.einsum("xtf,xdf->td", grad_pre, expert_up, preferred_element_type=jnp.float32)
    wide_grad = lax.dynamic_update_slice_in_dim(
        jnp.zeros((gate_grad.shape[0], total_experts), jnp.bfloat16),
        gate_grad.astype(jnp.bfloat16),
        group * local_experts,
        1,
    )
    returned = lax.psum_scatter(
        jnp.concatenate(
            [partial_out.astype(jnp.bfloat16), partial_grad.astype(jnp.bfloat16), wide_grad], axis=1
        ),
        "expert",
        scatter_dimension=0,
        tiled=True,
    )
    grad_down = jnp.einsum("xtf,td->xfd", gated, cot_all, preferred_element_type=jnp.float32)
    grad_up = jnp.einsum("td,xtf->xdf", rows_all, grad_pre, preferred_element_type=jnp.float32)
    return returned, grad_up, grad_down


def dot_last(left_side, right_side):
    return lax.dot_general(
        left_side, right_side, (((1,), (1,)), ((), ())), preferred_element_type=jnp.float32
    )

def visit_kernel(
    sent, cot, up, down, back_out, up_out, down_out,
    rows, cot_other, up_wide, chosen, cots, gated, grad_pre, gated_turned, pre_turned, partial, paired_in, chain_in, up_low, down_low, up_in, down_in,
    row_send, row_recv, cot_send, cot_recv, pair_send, pair_recv, chain_send, chain_recv, grad_send, grad_recv,
):
    experts = up.shape[0]
    wide = down.shape[0]
    hidden = wide // experts
    dp, ex = lax.axis_index("dp"), lax.axis_index("expert")
    y, x, z, core = dp // 2, dp % 2, ex // 2, ex % 2
    half = z // 2
    inner = z + half * (3 - 2 * z)
    onward = 1 - 2 * half
    sibling = (dp, z * 2 + 1 - core)
    beside, behind = (y * 2 + 1 - x, ex), ((1 - y) * 2 + x, ex)

    def at_z(place):
        return (dp, place * 2 + core)

    barrier = pltpu.get_barrier_semaphore()
    for place in (sibling, beside, behind):
        pl.semaphore_signal(barrier, inc=1, device_id=place, device_id_type=MESH)

    @pl.when(z < 3)
    def _():
        pl.semaphore_signal(barrier, inc=1, device_id=at_z(z + 1), device_id_type=MESH)

    @pl.when(z > 0)
    def _():
        pl.semaphore_signal(barrier, inc=1, device_id=at_z(z - 1), device_id_type=MESH)

    pl.semaphore_wait(barrier, 4 + inner)

    def remote(source, target, send, recv, place):
        return pltpu.make_async_remote_copy(
            src_ref=source, dst_ref=target, send_sem=send, recv_sem=recv, device_id=place, device_id_type=MESH
        )

    def row_copy(way, at, source=None):
        place = (sibling, at_z(z + 1), at_z(z - 1))[way]
        block = rows.at[at]
        target = block if way else rows.at[4 + at]
        return remote(block if source is None else source, target, row_send.at[way, at], row_recv.at[0 if way else 1, at], place)

    def cot_copy(at):
        return remote(cot.at[at], cot_other.at[at], cot_send.at[at], cot_recv.at[at], sibling)

    own = row_copy(0, z, sent), row_copy(1, z, sent), row_copy(2, z, sent)

    @pl.when(z < 3)
    def _():
        own[1].start()

    @pl.when(z > 0)
    def _():
        own[2].start()

    own[0].start()
    cot_copy(z).start()
    for k in (1, 2, 3):
        cot_copy((z + k) % 4).start()
    rows[z] = sent[...]
    for e in range(experts):
        up_wide[:, e * hidden : (e + 1) * hidden] = up[e]
    chosen[...] = (
        lax.broadcasted_iota(jnp.int32, (128, wide), 0)
        == 2 * HEADS * VE + ex * experts + lax.broadcasted_iota(jnp.int32, (128, wide), 1) // hidden
    ).astype(jnp.float32).astype(jnp.bfloat16)

    def order(p):
        later = (p + 2) // 3
        step = p - inner // (p + 1 - later)
        return later * (step + half * (3 - 2 * step)) + (1 - later) * z

    def pair_copy(at):
        return remote(partial.at[1, at], paired_in.at[at], pair_send.at[at], pair_recv.at[at], sibling)

    spans = (pl.ds(0, D), pl.ds(D, D + 128))

    def chain_copy(dest, slot, to, stage, part):
        span = spans[part]
        return remote(
            partial.at[0, dest, :, span], chain_in.at[slot, :, span],
            chain_send.at[stage, part], chain_recv.at[slot, part], at_z(to),
        )

    def add(target, source):
        def some(i, carry):
            part = pl.ds(pl.multiple_of(i * 32, 32), 32)
            target[part, :] = (
                target[part, :].astype(jnp.float32) + source[part, :].astype(jnp.float32)
            ).astype(target.dtype)
            return carry

        lax.fori_loop(0, target.shape[0] // 32, some, 0)

    def visit(q, carry):
        p, other = q // 2, q % 2
        at = order(p)
        block = other * 4 + at

        @pl.when((other == 0) & (p > 0))
        def _():
            row_copy(1, at).wait_recv()
            row_copy(0, at).start()

            @pl.when((at < z) & (z < 3))
            def _():
                row_copy(1, at).start()

            @pl.when((at > z) & (z > 0))
            def _():
                row_copy(2, at).start()

        @pl.when(other == 1)
        def _():
            row_copy(0, at).wait_recv()
            cot_copy(at).wait_recv()
            cots[...] = cot_other[at]

        @pl.when(other == 0)
        def _():
            cots[...] = cot[at]

        count = rows.shape[1]
        places = pl.ds(pl.multiple_of(block * count, count), count)

        def columns(n, gate_grad):
            span = pl.ds(pl.multiple_of(n * 256, 256), 256)
            pre = jnp.dot(rows[block, :, :D], up_wide[:, span], preferred_element_type=jnp.float32)
            back = dot_last(cots[...], down[span, :])
            mark = chosen[:, span]
            gate = jnp.dot(rows[block, :, D:], mark, preferred_element_type=jnp.float32)
            sig = jax.nn.sigmoid(pre)
            act = pre * sig
            act_low = (gate * act).astype(jnp.bfloat16)
            pre_low = (gate * back * (sig * (1.0 + pre * (1.0 - sig)))).astype(jnp.bfloat16)
            gated[:, span] = act_low
            grad_pre[:, span] = pre_low
            gated_turned[span, places] = act_low.T
            pre_turned[span, places] = pre_low.T
            return gate_grad + dot_last((act * back).astype(jnp.bfloat16), mark)

        partial[other, at, :, 2 * D :] = lax.fori_loop(
            0, wide // 256, columns, jnp.zeros((count, 128), jnp.float32)
        ).astype(jnp.bfloat16)

        def outward(n, carry):
            span = pl.ds(pl.multiple_of(n * 256, 256), 256)
            partial[other, at, :, span] = jnp.dot(
                gated[...], down[:, span], preferred_element_type=jnp.float32
            ).astype(jnp.bfloat16)
            partial[other, at, :, pl.ds(pl.multiple_of(D + n * 256, 256), 256)] = dot_last(
                grad_pre[...], up_wide[span, :]
            ).astype(jnp.bfloat16)
            return carry

        lax.fori_loop(0, D // 256, outward, 0)

        @pl.when(other == 1)
        def _():
            pair_copy(at).start()
            pair_copy(at).wait_recv()
            add(partial.at[0, at], paired_in.at[at])

        @pl.when((inner == 0) & (q == 3))
        def _():
            chain_copy(*nearest, 0).start()

        @pl.when((inner == 0) & (q == 5))
        def _():
            chain_copy(*next_one, 0).start()

        return carry

    nearest = (z + onward, z + onward, z + onward, 0)
    farthest = (3 * (1 - half), 3 * (1 - half), z + onward, 1)
    backward = (3 * half, 3 * half, z - onward, 2)
    next_one = (2 - half, 2 - half + inner * (2 + half), z + onward, 3)
    lax.fori_loop(0, 8, visit, 0)

    def relay(dest, slot, to, stage, part):
        chain_copy(dest, dest, to, stage, part).wait_recv()
        add(partial.at[0, dest, :, spans[part]], chain_in.at[dest, :, spans[part]])
        chain_copy(dest, slot, to, stage, part).start()

    @pl.when(inner == 0)
    def _():
        chain_copy(*farthest, 0).start()
        chain_copy(*farthest, 1).start()
        chain_copy(*next_one, 1).start()
        chain_copy(*nearest, 1).start()

    @pl.when(inner == 1)
    def _():
        relay(*next_one, 0)

    tokens_all = rows.reshape(rows.shape[0] * rows.shape[1], rows.shape[2])
    cots_own = cot.reshape(cot.shape[0] * cot.shape[1], D)
    cots_other = cot_other.reshape(cot.shape[0] * cot.shape[1], D)
    place = cots_own.shape[0]
    quarter = D // 4


    def up_copy(j):
        return remote(up_low.at[j], up_in.at[j], grad_send.at[0, j], grad_recv.at[0, j], behind if j == 2 else beside)

    def down_copy(j):
        return remote(down_low.at[j], down_in.at[j], grad_send.at[1, j], grad_recv.at[1, j], beside if j == 1 else behind)

    def weight_grads(j, carry):
        across, aside = 1 - j % 2, 1 - j // 2
        at = (y + across * (1 - 2 * y)) * 2 + x + aside * (1 - 2 * x)
        span = pl.ds(pl.multiple_of(at * quarter, quarter), quarter)
        up_low[j] = jnp.dot(
            pre_turned[...], tokens_all[:, span], preferred_element_type=jnp.float32
        ).astype(jnp.bfloat16)
        down_low[j] = (
            jnp.dot(gated_turned[:, :place], cots_own[:, span], preferred_element_type=jnp.float32)
            + jnp.dot(gated_turned[:, place:], cots_other[:, span], preferred_element_type=jnp.float32)
        ).astype(jnp.bfloat16)

        @pl.when(j == 0)
        def _():
            up_copy(0).start()
            down_copy(0).start()

        @pl.when(j == 1)
        def _():
            up_copy(1).start()

        @pl.when(j == 2)
        def _():
            down_copy(2).start()

        return carry

    lax.fori_loop(0, 4, weight_grads, 0)
    up_copy(0).wait()
    add(up_low.at[2], up_in.at[0])
    up_copy(2).start()
    down_copy(0).wait()
    add(down_low.at[1], down_in.at[0])
    down_copy(1).start()

    @pl.when(inner == 1)
    def _():
        for way, part in ((farthest, 0), (backward, 0), (farthest, 1), (backward, 1), (next_one, 1)):
            relay(*way, part)

    up_sum = up_low[3].astype(jnp.float32)
    down_sum = down_low[3].astype(jnp.float32)
    for j in (1, 2):
        up_copy(j).wait()
        up_sum += up_in[j].astype(jnp.float32)
        down_copy(j).wait()
        down_sum += down_in[j].astype(jnp.float32)
    for e in range(experts):
        up_out[e] = up_sum[e * hidden : (e + 1) * hidden, :].T
        down_out[e] = down_sum[e * hidden : (e + 1) * hidden, :]

    for part in range(2):
        span = spans[part]
        chain_copy(z, z, z, 0, part).wait_recv()
        back_out[:, span] = partial[0, z, :, span].astype(jnp.float32) + chain_in[z, :, span].astype(jnp.float32)

        @pl.when(inner == 1)
        def _():
            chain_copy(z, 4, z, 0, part).wait_recv()
            back_out[:, span] = back_out[:, span] + chain_in[4, :, span].astype(jnp.float32)

    for at in range(4):
        row_copy(0, at).wait_send()
        cot_copy(at).wait_send()
        pair_copy(at).wait_send()

        @pl.when((at <= z) & (z < 3))
        def _():
            row_copy(1, at).wait_send()

        @pl.when((at >= z) & (z > 0))
        def _():
            row_copy(2, at).wait_send()

    for part in range(2):

        @pl.when(inner == 0)
        def _():
            chain_copy(z, 0, z, 0, part).wait_send()

        @pl.when(inner == 1)
        def _():
            chain_copy(z, 0, z, 2, part).wait_send()

        chain_copy(z, 0, z, 1, part).wait_send()
        chain_copy(z, 0, z, 3, part).wait_send()

def expert_kernel_visit(sent, cot_line, up, down):
    tokens = sent.shape[0]
    experts, _, hidden = up.shape
    wide = experts * hidden
    low = jnp.bfloat16
    vmem = pl.BlockSpec(memory_space=pltpu.VMEM)
    dma = pltpu.SemaphoreType.DMA
    f32 = jnp.float32
    return pl.pallas_call(
        visit_kernel,
        out_shape=[
            jax.ShapeDtypeStruct((tokens, 2 * D + 128), f32),
            jax.ShapeDtypeStruct((experts, D // 4, hidden), f32),
            jax.ShapeDtypeStruct((experts, hidden, D // 4), f32),
        ],
        in_specs=[vmem] * 4,
        out_specs=[vmem] * 3,
        scratch_shapes=[
            pltpu.VMEM((8, tokens, D + 128), low),
            pltpu.VMEM((4, tokens, D), low),
            pltpu.VMEM((D, wide), low),
            pltpu.VMEM((128, wide), low),
            pltpu.VMEM((tokens, D), low),
            pltpu.VMEM((tokens, wide), low),
            pltpu.VMEM((tokens, wide), low),
            pltpu.VMEM((wide, 8 * tokens), low),
            pltpu.VMEM((wide, 8 * tokens), low),
            pltpu.VMEM((2, 4, tokens, 2 * D + 128), low),
            pltpu.VMEM((4, tokens, 2 * D + 128), low),
            pltpu.VMEM((5, tokens, 2 * D + 128), low),
            pltpu.VMEM((4, wide, D // 4), low),
            pltpu.VMEM((4, wide, D // 4), low),
            pltpu.VMEM((3, wide, D // 4), low),
            pltpu.VMEM((3, wide, D // 4), low),
            dma((3, 4)), dma((2, 4)), dma((4,)), dma((4,)), dma((4,)), dma((4,)), dma((4, 2)), dma((5, 2)), dma((2, 3)), dma((2, 3)),
        ],
        compiler_params=pltpu.CompilerParams(collective_id=2, has_side_effects=True, vmem_limit_bytes=58 * 2**20),
        name="expert_visit",
    )(sent, cot_line, up, down.reshape(wide, D))


def attend_kernel(
    expert_total, lengths, hidden, cot, value_pick, output_pick, expert_pick, routers, gains,
    key_weight_at, value_weight_at, query_weight_at, output_weight_at,
    middle, sent, normed_one, normed_two, queries, key_value, probs, value_all, attended,
    gates, slopes, cot_line,
    key_weight, value_weight, query_weight, output_weight, mixed, hot_turned, hot,
    fetch, pair_send, pair_recv, cot_send, cot_recv, own_sem,
):
    dp, ex = lax.axis_index("dp"), lax.axis_index("expert")
    z, core = ex // 2, ex % 2
    half = z // 2
    inner = z + half * (3 - 2 * z)
    count = hidden.shape[0]
    width = HEADS * HEAD_DIM
    low = jnp.bfloat16
    length = lengths[0]
    spread = HEADS * VE
    total = expert_total
    weights = [
        pltpu.make_async_copy(source, target, fetch.at[i])
        for i, (source, target) in enumerate(
            (
                (key_weight_at, key_weight),
                (value_weight_at, value_weight),
                (query_weight_at, query_weight),
                (output_weight_at, output_weight),
            )
        )
    ]
    for made in weights:
        made.start()

    def at_z(place):
        return (dp, place * 2 + core)

    barrier = pltpu.get_barrier_semaphore()
    for k in (1, 2, 3):
        pl.semaphore_signal(barrier, inc=1, device_id=((dp + k) % 4, ex), device_id_type=MESH)

    @pl.when(z < 3)
    def _():
        pl.semaphore_signal(barrier, inc=1, device_id=at_z(z + 1), device_id_type=MESH)

    @pl.when(z > 0)
    def _():
        pl.semaphore_signal(barrier, inc=1, device_id=at_z(z - 1), device_id_type=MESH)

    pl.semaphore_wait(barrier, 4 + inner)

    def cot_copy(way, at, source=None):
        block = cot_line.at[at]
        return pltpu.make_async_remote_copy(
            src_ref=block if source is None else source, dst_ref=block,
            send_sem=cot_send.at[way, at], recv_sem=cot_recv.at[at],
            device_id=at_z(z + 1 - 2 * way), device_id_type=MESH,
        )

    def pass_on(distance):
        @pl.when(z >= distance)
        def _():
            cot_copy(0, z - distance).wait_recv()

        @pl.when((z >= distance) & (z < 3))
        def _():
            cot_copy(0, z - distance).start()

        @pl.when(z + distance <= 3)
        def _():
            cot_copy(1, z + distance).wait_recv()

        @pl.when((z + distance <= 3) & (z > 0))
        def _():
            cot_copy(1, z + distance).start()

    @pl.when(z < 3)
    def _():
        cot_copy(0, z, cot).start()

    @pl.when(z > 0)
    def _():
        cot_copy(1, z, cot).start()

    keep = pltpu.make_async_copy(cot, cot_line.at[z], own_sem)
    keep.start()

    def norm(field, gain):
        center = field - jnp.mean(field, axis=-1, keepdims=True)
        spread = jnp.mean(center * center, axis=-1, keepdims=True)
        return (center * lax.rsqrt(spread + EPSILON) * gain).astype(low)

    parts = (pl.ds(0, width), pl.ds(width, width))

    def pair_copy(step, part, block):
        return pltpu.make_async_remote_copy(
            src_ref=key_value.at[block, :, parts[part]], dst_ref=key_value.at[block, :, parts[part]],
            send_sem=pair_send.at[step, part], recv_sem=pair_recv.at[block, part],
            device_id=((dp + step) % 4, ex), device_id_type=MESH,
        )

    def send_part(part):
        for step in (1, 2, 3):

            @pl.when(dp + step < 4)
            def _():
                pair_copy(step, part, dp).start()

    normed_one[...] = norm(hidden[...].astype(jnp.float32), gains[0:1, :])
    weights[0].wait()
    key_value[dp, :, parts[0]] = jnp.dot(
        normed_one[...], key_weight[...], preferred_element_type=jnp.float32
    ).astype(low)
    send_part(0)

    hot_turned[...] = jnp.zeros(hot_turned.shape, jnp.float32)

    def mark(picks, base, size):
        place = lax.broadcasted_iota(jnp.int32, (size, count), 0)
        found = jnp.zeros((size, count), jnp.float32)
        for pick in picks:
            found = jnp.where(place == pick, 1.0, found)
        hot_turned[base : base + size, :] = found

    mark([value_pick[h, i : i + 1, :] + h * VE for h in range(HEADS) for i in range(value_pick.shape[1])], 0, spread)
    mark(
        [output_pick[h, i : i + 1, :] + h * VE for h in range(HEADS) for i in range(output_pick.shape[1])],
        spread,
        spread,
    )
    mark([expert_pick[i : i + 1, :] for i in range(expert_pick.shape[0])], 2 * spread, total)
    hot[...] = hot_turned[...].T
    sig = jax.nn.sigmoid(dot_last(normed_one[...], routers[...]))
    gates[...] = sig * hot[...]
    slopes[...] = gates[...] * (1.0 - sig)
    weights[1].wait()

    def values(n, carry):
        span = pl.ds(pl.multiple_of(n * 256, 256), 256)
        value_all[:, span] = jnp.dot(
            hidden[...], value_weight[:, span], preferred_element_type=jnp.float32
        ).astype(low)
        return carry

    lax.fori_loop(0, HEADS * VE * HEAD_DIM // 256, values, 0)
    for h in range(HEADS):
        row = jnp.zeros((count, HEAD_DIM), jnp.float32)
        for e in range(h * VE, (h + 1) * VE):
            row += gates[:, e : e + 1] * value_all[:, e * HEAD_DIM : (e + 1) * HEAD_DIM].astype(jnp.float32)
        key_value[dp, :, width + h * HEAD_DIM : width + (h + 1) * HEAD_DIM] = row.astype(low)
    send_part(1)

    weights[2].wait()
    queries[...] = jnp.dot(normed_one[...], query_weight[...], preferred_element_type=jnp.float32).astype(low)
    for block in range(4):

        @pl.when(block > dp)
        def _():
            key_value[block] = jnp.zeros((count, 2 * width), low)

    pass_on(1)

    def wait_part(part):
        for block in range(3):

            @pl.when(block < dp)
            def _():
                pair_copy(1, part, block).wait_recv()

    wait_part(0)
    pair_all = key_value.reshape(4 * count, 2 * width)
    query_pos = dp * count + lax.broadcasted_iota(jnp.int32, (count, 4 * count), 0)
    key_pos = lax.broadcasted_iota(jnp.int32, (count, 4 * count), 1)
    allowed = (key_pos <= query_pos) & (key_pos < length)

    def score(h, carry):
        span = pl.ds(pl.multiple_of(h * HEAD_DIM, HEAD_DIM), HEAD_DIM)
        raw = dot_last(queries[:, span], pair_all[:, span])
        scores = jnp.where(allowed, raw * HEAD_DIM ** (-0.5), NEGATIVE)
        terms = jnp.exp(scores - jnp.max(scores, axis=-1, keepdims=True))
        probs[h] = (terms * (1.0 / jnp.sum(terms, axis=-1, keepdims=True))).astype(low)
        return carry

    lax.fori_loop(0, HEADS, score, 0)
    wait_part(1)
    pass_on(2)

    def collect(h, carry):
        span = pl.ds(pl.multiple_of(h * HEAD_DIM, HEAD_DIM), HEAD_DIM)
        value_span = pl.ds(pl.multiple_of(width + h * HEAD_DIM, HEAD_DIM), HEAD_DIM)
        attended[:, span] = jnp.dot(probs[h], pair_all[:, value_span], preferred_element_type=jnp.float32)
        return carry

    lax.fori_loop(0, HEADS, collect, 0)
    for h in range(HEADS):
        row = attended[:, h * HEAD_DIM : (h + 1) * HEAD_DIM]
        for e in range(h * VE, (h + 1) * VE):
            mixed[:, e * HEAD_DIM : (e + 1) * HEAD_DIM] = (gates[:, spread + e : spread + e + 1] * row).astype(low)

    place = dp * count + lax.broadcasted_iota(jnp.int32, (count, 1), 0)
    live = jnp.where(place < length, 1.0, 0.0)
    weights[3].wait()

    def outward(n, carry):
        span = pl.ds(pl.multiple_of(n * 256, 256), 256)
        branch = jnp.dot(mixed[...], output_weight[:, span], preferred_element_type=jnp.float32)
        middle[:, span] = hidden[:, span].astype(jnp.float32) + live * branch
        return carry

    lax.fori_loop(0, D // 256, outward, 0)
    sent[:, :D] = middle[...].astype(low)
    normed_two[...] = norm(middle[...], gains[1:2, :])
    sig = jax.nn.sigmoid(dot_last(normed_two[...], routers[...]))
    gate = sig * hot[...] * live
    sent[:, D:] = gate.astype(low)
    lane = lax.broadcasted_iota(jnp.int32, (count, 128), 1)
    slopes[...] = jnp.where(lane < 2 * spread, slopes[...], gate * (1.0 - sig))

    pass_on(3)
    keep.wait()
    for part in range(2):
        for step in (1, 2, 3):

            @pl.when(dp + step < 4)
            def _():
                pair_copy(step, part, dp).wait_send()

    for at in range(4):

        @pl.when((at <= z) & (z < 3))
        def _():
            cot_copy(0, at).wait_send()

        @pl.when((at >= z) & (z > 0))
        def _():
            cot_copy(1, at).wait_send()


def attend(total, lengths, *operands):
    count = operands[0].shape[0]
    low, full = jnp.bfloat16, jnp.float32
    vmem = pl.BlockSpec(memory_space=pltpu.VMEM)
    anywhere = pl.BlockSpec(memory_space=pl.ANY)
    dma = pltpu.SemaphoreType.DMA
    width, wide = HEADS * HEAD_DIM, HEADS * VE * HEAD_DIM
    shapes = [
        ((count, D), full),
        ((count, D + 128), low),
        ((count, D), low),
        ((count, D), low),
        ((count, width), low),
        ((4, count, 2 * width), low),
        ((HEADS, count, 4 * count), low),
        ((count, wide), low),
        ((count, width), full),
        ((count, 128), full),
        ((count, 128), full),
        ((4, count, D), low),
    ]
    return pl.pallas_call(
        functools.partial(attend_kernel, total),
        out_shape=[jax.ShapeDtypeStruct(*shape) for shape in shapes],
        in_specs=[pl.BlockSpec(memory_space=pltpu.SMEM)] + [vmem] * (len(operands) - 4) + [anywhere] * 4,
        out_specs=[vmem] * len(shapes),
        scratch_shapes=[pltpu.VMEM(a.shape, a.dtype) for a in operands[-4:]]
        + [
            pltpu.VMEM((count, wide), low),
            pltpu.VMEM((128, count), full),
            pltpu.VMEM((count, 128), full),
            dma((4,)),
            dma((4, 2)),
            dma((4, 2)),
            dma((2, 4)),
            dma((4,)),
            dma,
        ],
        compiler_params=pltpu.CompilerParams(
            collective_id=1, has_side_effects=True, vmem_limit_bytes=58 * 2**20
        ),
        name="attend",
    )(lengths, *operands)


def backward_kernel(
    total_experts, lengths, gates, slopes, routers, gains,
    returned_at, middle_at, cot_at, hidden_at, normed_one_at, queries_at, key_value_at, probs_at, value_all_at,
    attended_at, normed_two_at, query_weight_at, key_weight_at, value_weight_at, output_weight_at,
    block_out, grad_in, out_query, out_key, out_value, out_output, out_small, sums_out,
    returned, middle, cot, hidden, normed_one, queries, key_value, probs, value_all,
    attended, normed_two, query_weight, key_weight, value_part, output_part,
    branch, branch_turned, one_turned, hidden_turned, grad_att, grad_query, leave, arrive, grad_key, grad_value,
    grad_each, grad_middle, grad_one, logit_one, logit_two, small_turned, mixed,
    grads, grads_small, core_in, plane_in, last_in, sums_in,
    fetch, part_fetch, leave_send, leave_recv, send, recv,
):
    dp, ex = lax.axis_index("dp"), lax.axis_index("expert")
    y, x, z, core = dp // 2, dp % 2, ex // 2, ex % 2
    count = hidden.shape[0]
    width = HEADS * HEAD_DIM
    low, full = jnp.bfloat16, jnp.float32
    length = lengths[0]
    sibling = (dp, z * 2 + 1 - core)
    beside = (y * 2 + 1 - x, ex)
    behind = ((1 - y) * 2 + x, ex)
    across = ((1 - y) * 2 + 1 - x, ex)
    line = [(dp, ((z + k) % 4) * 2 + core) for k in (1, 2, 3)]
    barrier = pltpu.get_barrier_semaphore()
    for place in (sibling, beside, behind, across, *line):
        pl.semaphore_signal(barrier, inc=1, device_id=place, device_id_type=MESH)

    held = dict(
        returned=(returned_at, returned),
        middle=(middle_at, middle),
        cot=(cot_at, cot),
        hidden=(hidden_at, hidden),
        attended=(attended_at, attended),
        key_value=(key_value_at, key_value),
        probs=(probs_at, probs),
        queries=(queries_at, queries),
        normed_one=(normed_one_at, normed_one),
        query_weight=(query_weight_at, query_weight),
        value_all=(value_all_at, value_all),
        key_weight=(key_weight_at, key_weight),
        normed_two=(normed_two_at, normed_two),
    )
    got = {
        name: pltpu.make_async_copy(source, target, fetch.at[i])
        for i, (name, (source, target)) in enumerate(held.items())
    }

    def output_copy(n):
        return pltpu.make_async_copy(
            output_weight_at.at[pl.ds(n * 512, 512)], output_part.at[n % 2], part_fetch.at[0, n % 2]
        )

    def value_copy(n):
        return pltpu.make_async_copy(
            value_weight_at.at[:, pl.ds(n * 512, 512)], value_part.at[n % 2], part_fetch.at[1, n % 2]
        )

    first_held = ("returned", "middle", "cot", "hidden")
    for name in first_held:
        got[name].start()
    for n in range(2):
        output_copy(n).start()
    for name in held:
        if name not in first_held:
            got[name].start()
    for n in range(2):
        value_copy(n).start()

    pieces = (
        [(out_output, 512 * n, 512, n) for n in range(5)]
        + [(out_query, 0, 512, 5), (out_key, 0, 512, 6)]
        + [(out_value, 512 * n, 512, n) for n in range(5)]
        + [(out_small, 0, 128, None)]
    )
    along_line = (0, 1, 2, 3)
    in_plane = [i for i in range(len(pieces)) if i not in along_line]
    x_first = {i: n % 2 == 0 for n, i in enumerate(in_plane)}

    def remote(source, target, slot, place):
        return pltpu.make_async_remote_copy(
            src_ref=source, dst_ref=target, send_sem=send.at[slot], recv_sem=recv.at[slot],
            device_id=place, device_id_type=MESH,
        )

    def add(target, source):
        target[...] = (target[...].astype(full) + source[...].astype(full)).astype(target.dtype)

    def own(i):
        slot = pieces[i][3]
        return grads_small if slot is None else grads.at[slot]

    def columns(i):
        return pl.ds(0, pieces[i][2])

    started = {}

    def begin(key, source, target, slot, place):
        started[key] = remote(source, target, slot, place)
        started[key].start()

    def halve_core(i):
        begin((i, 0), own(i).at[:, :, 1 - core], core_in.at[i, :, :, :, columns(i)], (i, 0), sibling)

    def halve_near(i):
        span = columns(i)
        started[i, 0].wait()
        add(core_in.at[i, :, :, :, span], own(i).at[:, :, core])
        if i in along_line:
            for k in (1, 2, 3):
                begin(
                    (i, k), core_in.at[i, :, (z + k) % 4, :, span],
                    plane_in.at[i, pl.ds(4 * k - 4, 4), :, span], (i, k), line[k - 1],
                )
            return
        for part in range(2):
            if x_first[i]:
                source = core_in.at[i, part * 2 + 1 - x, :, :, span]
            else:
                source = core_in.at[i, (1 - y) * 2 + part, :, :, span]
            target = plane_in.at[i, pl.ds(part * 4, 4), :, span]
            begin((i, 1 + part), source, target, (i, 1 + part), beside if x_first[i] else behind)

    def halve_far(i):
        span = columns(i)
        if i in along_line:
            held = core_in.at[i, :, z, :, span]
            for k in (1, 2, 3):
                started[i, k].wait()
                add(held, plane_in.at[i, pl.ds(4 * k - 4, 4), :, span])
            for part in range(2):
                begin(
                    (i, 4 + part), core_in.at[i, part * 2 + 1 - x, z, :, span],
                    last_in.at[i, part, :, span], (i, 4 + part), beside,
                )
            return
        for part in range(2):
            started[i, 1 + part].wait()
            kept = part * 2 + x if x_first[i] else y * 2 + part
            add(plane_in.at[i, pl.ds(part * 4, 4), :, span], core_in.at[i, kept, :, :, span])
        other = 1 - y if x_first[i] else 1 - x
        begin(
            (i, 3), plane_in.at[i, pl.ds(other * 4, 4), :, span], plane_in.at[i, pl.ds(8, 4), :, span],
            (i, 3), behind if x_first[i] else beside,
        )

    def spread(i):
        span = columns(i)
        if i in along_line:
            for part in range(2):
                started[i, 4 + part].wait()
                add(last_in.at[i, part, :, span], core_in.at[i, part * 2 + x, z, :, span])
            begin((i, 6), last_in.at[i, 1 - y, :, span], last_in.at[i, 2, :, span], (i, 6), behind)
            return
        started[i, 3].wait()
        add(plane_in.at[i, pl.ds(8, 4), :, span], plane_in.at[i, pl.ds((y if x_first[i] else x) * 4, 4), :, span])
        for k in (1, 2, 3):
            begin(
                (i, 3 + k), plane_in.at[i, 8 + (z + k) % 4, :, span],
                last_in.at[i, k - 1, :, span], (i, 3 + k), line[k - 1],
            )

    def finish(i):
        out, start, size, _ = pieces[i]
        span = columns(i)
        if i in along_line:
            started[i, 6].wait()
            total = last_in[i, y, :, span].astype(full) + last_in[i, 2, :, span].astype(full)
        else:
            total = plane_in[i, 8 + z, :, span].astype(full)
            for k in (1, 2, 3):
                started[i, 3 + k].wait()
                total = total + last_in[i, k - 1, :, span].astype(full)
        out[:, pl.ds(start, size)] = total

    rows_each = 64
    lane = lax.broadcasted_iota(jnp.int32, (1, 128), 1)
    for name in first_held:
        got[name].wait()
    logit_two[...] = (returned[:, 2 * D :] * slopes[...]).astype(low)

    def live_rows(start):
        place = dp * count + start + lax.broadcasted_iota(jnp.int32, (rows_each, 1), 0)
        return jnp.where(place < length, 1.0, 0.0)

    def norm_back(field, grad, gain):
        center = field - jnp.mean(field, axis=-1, keepdims=True)
        scale = lax.rsqrt(jnp.mean(center * center, axis=-1, keepdims=True) + EPSILON)
        unit = center * scale
        part = grad * gain
        back = scale * (
            part
            - jnp.mean(part, axis=-1, keepdims=True)
            - unit * jnp.mean(part * unit, axis=-1, keepdims=True)
        )
        return back, jnp.sum(grad * unit, axis=0, keepdims=True)

    def square(field, live, at):
        total = jnp.sum(jnp.sum(field * field, axis=1, keepdims=True) * live, axis=0, keepdims=True)
        return jnp.where(lane == at, total, 0.0)

    def first_rows(n, carry):
        gain_sum, sums = carry
        start = pl.multiple_of(n * rows_each, rows_each)
        rows = pl.ds(start, rows_each)
        live = live_rows(start)
        field = middle[rows, :]
        forward = returned[rows, :D]
        final = field + forward
        block_out[rows, :] = final.astype(low)
        source = hidden[rows, :].astype(full)
        one = jnp.ones((rows_each, 1), full)
        sums += square(source, live, 0) + square(field - source, one, 1)
        sums += square(forward, one, 2) + square(final, live, 3)
        sums += jnp.where(lane == 4, jnp.sum(live, axis=0, keepdims=True), 0.0)
        grad = jnp.dot(logit_two[rows, :], routers[...], preferred_element_type=full)
        back, gain_part = norm_back(field, grad, gains[1:2, :])
        total = cot[rows, :].astype(full) + returned[rows, D : 2 * D] + back
        grad_middle[rows, :] = total
        branch[rows, :] = (live * total).astype(low)
        return gain_sum + gain_part, sums

    gain_two_sum, sums = lax.fori_loop(
        0, count // rows_each, first_rows, (jnp.zeros((1, D), full), jnp.zeros((1, 128), full))
    )
    sums_in[0] = jnp.broadcast_to(sums, (8, 128))
    pl.semaphore_wait(barrier, 7)

    def weight_grad(i, turned, right, size):
        flat = own(i)
        flat = flat.reshape(D, size)

        def some(n, carry):
            rows = pl.ds(pl.multiple_of(n * 256, 256), 256)
            flat[rows, :] = jnp.dot(turned[rows, :], right, preferred_element_type=full).astype(low)
            return carry

        lax.fori_loop(0, D // 256, some, 0)
        halve_core(i)

    branch_turned[...] = branch[...].T
    got["attended"].wait()

    def head_of(c):
        return slice((c // VE) * HEAD_DIM, (c // VE + 1) * HEAD_DIM)

    spread_count = HEADS * VE
    for n in range(5):
        for j in range(4):
            c = 4 * n + j
            gate = gates[:, spread_count + c : spread_count + c + 1]
            mixed[:, j * HEAD_DIM : (j + 1) * HEAD_DIM] = (gate * attended[:, head_of(c)]).astype(low)
        weight_grad(n, branch_turned, mixed[...], 512)
    logit_one[...] = jnp.zeros(logit_one.shape, full)
    grad_att[...] = jnp.zeros(grad_att.shape, full)
    for n in range(5):
        output_copy(n).wait()
        for j in range(4):
            c = 4 * n + j
            grad_mixed = dot_last(branch[...], output_part[n % 2, j * HEAD_DIM : (j + 1) * HEAD_DIM, :])
            col = spread_count + c
            grad_att[:, head_of(c)] += gates[:, col : col + 1] * grad_mixed
            dots = jnp.sum(attended[:, head_of(c)] * grad_mixed, axis=1, keepdims=True)
            logit_one[:, col : col + 1] = dots * slopes[:, col : col + 1]
        if n + 2 < 5:
            output_copy(n + 2).start()
        halve_near(n)

    pair_all = key_value.reshape(4 * count, 2 * width)
    for name in ("key_value", "probs", "queries"):
        got[name].wait()

    def leave_copy(k, h):
        rows = pl.ds(h * 2 * HEAD_DIM, 2 * HEAD_DIM)
        return pltpu.make_async_remote_copy(
            src_ref=leave.at[(dp + 4 - k) % 4, rows], dst_ref=arrive.at[k - 1, rows],
            send_sem=leave_send.at[k - 1, h], recv_sem=leave_recv.at[k - 1, h],
            device_id=((dp + 4 - k) % 4, ex), device_id_type=MESH,
        )

    def head(h, carry):
        start = pl.multiple_of(h * HEAD_DIM, HEAD_DIM)
        span = pl.ds(start, HEAD_DIM)
        grad = grad_att[:, span].astype(low)
        prob = probs[h].astype(full)
        grad_prob = dot_last(grad, pair_all[:, pl.ds(width + start, HEAD_DIM)])
        dots = jnp.sum(prob * grad_prob, axis=-1, keepdims=True)
        grad_score = (prob * (grad_prob - dots) * HEAD_DIM ** (-0.5)).astype(low)
        grad_query[:, span] = jnp.dot(grad_score, pair_all[:, span], preferred_element_type=full).astype(low)
        key_part = dot_first(queries[:, span], grad_score).astype(low)
        value_part_all = dot_first(grad, probs[h]).astype(low)
        key_rows = pl.ds(pl.multiple_of(2 * h * HEAD_DIM, 2 * HEAD_DIM), HEAD_DIM)
        value_rows = pl.ds(pl.multiple_of((2 * h + 1) * HEAD_DIM, HEAD_DIM), HEAD_DIM)
        for j in range(4):
            leave[j, key_rows, :] = key_part[:, j * count : (j + 1) * count]
            leave[j, value_rows, :] = value_part_all[:, j * count : (j + 1) * count]
        for k in (1, 2, 3):

            @pl.when(dp >= k)
            def _():
                leave_copy(k, h).start()

        return carry

    lax.fori_loop(0, HEADS, head, 0)

    for name in ("normed_one", "query_weight"):
        got[name].wait()
    one_turned[...] = normed_one[...].T
    weight_grad(5, one_turned, grad_query[...], 512)
    hidden_turned[...] = hidden[...].T
    grad_one[...] = dot_last(grad_query[...], query_weight[...])
    halve_near(5)

    for h in range(HEADS):
        rows = pl.ds(h * 2 * HEAD_DIM, 2 * HEAD_DIM)
        total = leave[dp, rows, :].astype(full)
        for k in (1, 2, 3):

            @pl.when(dp + k < 4)
            def _():
                leave_copy(k, h).wait_recv()

            @pl.when(dp + k >= 4)
            def _():
                arrive[k - 1, rows, :] = jnp.zeros((2 * HEAD_DIM, count), low)

            total += arrive[k - 1, rows, :].astype(full)
        turned = total.T
        grad_key[:, h * HEAD_DIM : (h + 1) * HEAD_DIM] = turned[:, :HEAD_DIM].astype(low)
        grad_value[:, h * HEAD_DIM : (h + 1) * HEAD_DIM] = turned[:, HEAD_DIM:].astype(low)

    got["value_all"].wait()
    for n in range(5):
        for j in range(4):
            c = 4 * n + j
            grad = grad_value[:, head_of(c)].astype(full)
            here = slice(c * HEAD_DIM, (c + 1) * HEAD_DIM)
            grad_each[:, here] = (gates[:, c : c + 1] * grad).astype(low)
            dots = jnp.sum(value_all[:, here].astype(full) * grad, axis=1, keepdims=True)
            logit_one[:, c : c + 1] = dots * slopes[:, c : c + 1]
        weight_grad(7 + n, hidden_turned, grad_each[:, n * 512 : (n + 1) * 512], 512)
        if n:
            halve_near(6 + n)
    weight_grad(6, one_turned, grad_key[...], 512)
    halve_near(11)
    got["key_weight"].wait()
    grad_one[...] += dot_last(grad_key[...], key_weight[...])
    halve_near(6)
    grad_one[...] += jnp.dot(logit_one[...].astype(low), routers[...], preferred_element_type=full)
    halve_far(5)

    def first_norm(n, gain_sum):
        rows = pl.ds(pl.multiple_of(n * rows_each, rows_each), rows_each)
        back, gain_part = norm_back(hidden[rows, :].astype(full), grad_one[rows, :], gains[0:1, :])
        grad_in[rows, :] = grad_middle[rows, :] + back
        return gain_sum + gain_part

    gain_one_sum = lax.fori_loop(0, count // rows_each, first_norm, jnp.zeros((1, D), full))
    halve_far(7)
    spread(5)
    got["normed_two"].wait()
    small_turned[...] = dot_first(logit_one[...].astype(low), normed_one[...]) + dot_first(
        logit_two[...], normed_two[...]
    )
    small_rows = 2 * spread_count + total_experts
    small_turned[small_rows : small_rows + 1, :] = gain_one_sum
    small_turned[small_rows + 1 : small_rows + 2, :] = gain_two_sum
    grads_small.reshape(D, 128)[...] = small_turned[...].T.astype(low)
    halve_core(12)

    rounds = [[sibling], [beside], [behind], line]
    offset = [1, 2, 3, 4]

    def sum_start(r):
        for j, place in enumerate(rounds[r]):
            begin(("sum", r, j), sums_in.at[0], sums_in.at[offset[r] + j], (len(pieces) + j, r), place)

    def sum_end(r):
        for j in range(len(rounds[r])):
            started["sum", r, j].wait()
        total = sums_in[0]
        for j in range(len(rounds[r])):
            total = total + sums_in[offset[r] + j]
        sums_in[0] = total

    sum_start(0)
    for n in range(5):
        value_copy(n).wait()
        part = dot_last(grad_each[:, n * 512 : (n + 1) * 512], value_part[n % 2])
        grad_in[...] += part
        if n + 2 < 5:
            value_copy(n + 2).start()
        if n == 0:
            halve_near(12)
            sum_end(0)
            sum_start(1)
        if n == 1:
            halve_far(8)
            spread(7)
        if n == 2:
            finish(5)
            halve_far(9)
            spread(8)
            sum_end(1)
            sum_start(2)
        if n == 3:
            halve_far(0)
            finish(7)
        if n == 4:
            sum_end(2)
            sum_start(3)
            halve_far(10)
            spread(9)

    for action, i in (
        (halve_far, 1), (spread, 0), (finish, 8), (halve_far, 4), (halve_far, 11), (spread, 10), (finish, 0), (finish, 9),
        (sum_end, 3),
        (halve_far, 2), (spread, 1), (spread, 4), (halve_far, 6), (spread, 11), (finish, 10), (finish, 1),
        (halve_far, 12), (spread, 2), (spread, 6), (finish, 4), (finish, 11), (halve_far, 3), (spread, 12), (finish, 2),
        (finish, 6), (spread, 3), (finish, 12), (finish, 3),
    ):
        action(i)
    sums_out[...] = sums_in[0]
    for h in range(HEADS):
        for k in (1, 2, 3):

            @pl.when(dp >= k)
            def _():
                leave_copy(k, h).wait_send()


def backward(total_experts, lengths, gates, slopes, routers, gains, *arrays):
    low, full = jnp.bfloat16, jnp.float32
    count = gates.shape[0]
    width, wide = HEADS * HEAD_DIM, HEADS * VE * HEAD_DIM
    vmem = pl.BlockSpec(memory_space=pltpu.VMEM)
    anywhere = pl.BlockSpec(memory_space=pl.ANY)
    dma = pltpu.SemaphoreType.DMA
    whole = [pltpu.VMEM(a.shape, a.dtype) for a in arrays[:13]]
    n = 13
    return pl.pallas_call(
        functools.partial(backward_kernel, total_experts),
        out_shape=[
            jax.ShapeDtypeStruct((count, D), low),
            jax.ShapeDtypeStruct((count, D), full),
            jax.ShapeDtypeStruct((ROWS, width), full),
            jax.ShapeDtypeStruct((ROWS, width), full),
            jax.ShapeDtypeStruct((ROWS, wide), full),
            jax.ShapeDtypeStruct((ROWS, wide), full),
            jax.ShapeDtypeStruct((ROWS, 128), full),
            jax.ShapeDtypeStruct((8, 128), full),
        ],
        in_specs=[pl.BlockSpec(memory_space=pltpu.SMEM)] + [vmem] * 4 + [anywhere] * len(arrays),
        out_specs=[vmem] * 8,
        scratch_shapes=whole
        + [
            pltpu.VMEM((2, D, 512), low),
            pltpu.VMEM((2, 512, D), low),
            pltpu.VMEM((count, D), low),
            pltpu.VMEM((D, count), low),
            pltpu.VMEM((D, count), low),
            pltpu.VMEM((D, count), low),
            pltpu.VMEM((count, width), full),
            pltpu.VMEM((count, width), low),
            pltpu.VMEM((4, 2 * width, count), low),
            pltpu.VMEM((3, 2 * width, count), low),
            pltpu.VMEM((count, width), low),
            pltpu.VMEM((count, width), low),
            pltpu.VMEM((count, wide), low),
            pltpu.VMEM((count, D), full),
            pltpu.VMEM((count, D), full),
            pltpu.VMEM((count, 128), full),
            pltpu.VMEM((count, 128), low),
            pltpu.VMEM((128, D), full),
            pltpu.VMEM((count, 512), low),
            pltpu.VMEM((7, 4, 4, 2, ROWS, 512), low),
            pltpu.VMEM((4, 4, 2, ROWS, 128), low),
            pltpu.VMEM((n, 4, 4, ROWS, 512), low),
            pltpu.VMEM((n, 12, ROWS, 512), low),
            pltpu.VMEM((n, 3, ROWS, 512), low),
            pltpu.VMEM((7, 8, 128), full),
            dma((13,)),
            dma((2, 2)),
            dma((3, HEADS)),
            dma((3, HEADS)),
            dma((n + 3, 7)),
            dma((n + 3, 7)),
        ],
        compiler_params=pltpu.CompilerParams(
            collective_id=3, has_side_effects=True, vmem_limit_bytes=62 * 2**20
        ),
        name="backward",
    )(lengths, gates, slopes, routers, gains, *arrays)


def expert_visit(sent, cotangent, expert_up, expert_down):
    local_experts = expert_up.shape[0]
    group = lax.axis_index("expert")
    cot_all = lax.all_gather(cotangent, "expert", axis=0, tiled=True)
    sent_all = lax.all_gather(sent, "expert", axis=0, tiled=True)
    rows_all = sent_all[:, :D]
    total_experts = sent.shape[1] - D
    gate_all = lax.dynamic_slice_in_dim(
        sent_all[:, D:], group * local_experts, local_experts, 1
    ).astype(jnp.float32).T[:, :, None]
    preact = jnp.einsum("td,xdf->xtf", rows_all, expert_up, preferred_element_type=jnp.float32)
    pre_sig = jax.nn.sigmoid(preact)
    hidden = preact * pre_sig
    back = jnp.einsum("td,xfd->xtf", cot_all, expert_down, preferred_element_type=jnp.float32)
    gate_grad = jnp.sum(hidden * back, axis=2).T
    gated = (gate_all * hidden).astype(jnp.bfloat16)
    grad_pre = (gate_all * back * (pre_sig * (1.0 + preact * (1.0 - pre_sig)))).astype(jnp.bfloat16)
    partial_out = jnp.einsum("xtf,xfd->td", gated, expert_down, preferred_element_type=jnp.float32)
    partial_grad = jnp.einsum("xtf,xdf->td", grad_pre, expert_up, preferred_element_type=jnp.float32)
    wide_grad = lax.dynamic_update_slice_in_dim(
        jnp.zeros((gate_grad.shape[0], total_experts), jnp.bfloat16),
        gate_grad.astype(jnp.bfloat16),
        group * local_experts,
        1,
    )
    returned = lax.psum_scatter(
        jnp.concatenate(
            [partial_out.astype(jnp.bfloat16), partial_grad.astype(jnp.bfloat16), wide_grad], axis=1
        ),
        "expert",
        scatter_dimension=0,
        tiled=True,
    )
    grad_down = jnp.einsum("xtf,td->xfd", gated, cot_all, preferred_element_type=jnp.float32)
    grad_up = jnp.einsum("td,xtf->xdf", rows_all, grad_pre, preferred_element_type=jnp.float32)
    return returned, grad_up, grad_down


def dense_sum_kernel(widths, *refs):
    n = len(widths)
    grads, stats = refs[:n], refs[n]
    outs, stats_out = refs[n + 1 : 2 * n + 1], refs[2 * n + 1]
    core_in, near_in, far_in, line_in, total_in, send, recv = refs[2 * n + 2 :]
    dp, ex = lax.axis_index("dp"), lax.axis_index("expert")
    y, x, z, core = dp // 2, dp % 2, ex // 2, ex % 2
    sibling = (dp, z * 2 + 1 - core)
    beside = (y * 2 + 1 - x, ex)
    behind = ((1 - y) * 2 + x, ex)
    line = [(dp, ((z + k) % 4) * 2 + core) for k in (1, 2, 3)]
    barrier = pltpu.get_barrier_semaphore()
    for place in (sibling, beside, behind, *line):
        pl.semaphore_signal(barrier, inc=1, device_id=place, device_id_type=MESH)
    pl.semaphore_wait(barrier, 6)

    pieces = []
    for which, width in enumerate(widths):
        for start in range(0, width, CHUNK):
            pieces.append((which, start, min(CHUNK, width - start)))

    def copy(source, target, slot, place):
        made = pltpu.make_async_remote_copy(
            src_ref=source, dst_ref=target, send_sem=send.at[slot], recv_sem=recv.at[slot],
            device_id=place, device_id_type=MESH)
        made.start()
        return made

    def add(target, source):
        target[...] = (target[...].astype(jnp.float32) + source[...].astype(jnp.float32)).astype(target.dtype)

    count = len(pieces)
    first, second, third, fourth = {}, {}, {}, {}

    def halve_core(i):
        which, start, width = pieces[i]
        columns = pl.ds(start, width)
        first[i] = copy(grads[which].at[:, :, 1 - core, :, columns], core_in.at[i, :, :, :, pl.ds(0, width)], (i, 0), sibling)

    def halve_near(i):
        which, start, width = pieces[i]
        first[i].wait()
        held = core_in.at[i, :, :, :, pl.ds(0, width)]
        add(held, grads[which].at[:, :, core, :, pl.ds(start, width)])
        for half in range(2):
            if i % 2 == 0:
                source = core_in.at[i, half * 2 + 1 - x, :, :, pl.ds(0, width)]
            else:
                source = core_in.at[i, (1 - y) * 2 + half, :, :, pl.ds(0, width)]
            second[i, half] = copy(source, near_in.at[i, half, :, :, pl.ds(0, width)], (i, 1 + half), beside if i % 2 == 0 else behind)

    def halve_far(i):
        which, start, width = pieces[i]
        for half in range(2):
            second[i, half].wait()
            kept = half * 2 + x if i % 2 == 0 else y * 2 + half
            add(near_in.at[i, half, :, :, pl.ds(0, width)], core_in.at[i, kept, :, :, pl.ds(0, width)])
        other = 1 - y if i % 2 == 0 else 1 - x
        third[i] = copy(near_in.at[i, other, :, :, pl.ds(0, width)], far_in.at[i, :, :, pl.ds(0, width)], (i, 3), behind if i % 2 == 0 else beside)

    def spread_line(i):
        which, start, width = pieces[i]
        third[i].wait()
        add(far_in.at[i, :, :, pl.ds(0, width)], near_in.at[i, y if i % 2 == 0 else x, :, :, pl.ds(0, width)])
        for k in (1, 2, 3):
            fourth[i, k] = copy(far_in.at[i, (z + k) % 4, :, pl.ds(0, width)], line_in.at[i, k - 1, :, pl.ds(0, width)], (i, 3 + k), line[k - 1])

    def finish(i):
        which, start, width = pieces[i]
        columns = pl.ds(0, width)
        total = far_in[i, z, :, columns].astype(jnp.float32)
        for k in (1, 2, 3):
            fourth[i, k].wait()
            total = total + line_in[i, k - 1, :, columns].astype(jnp.float32)
        outs[which][:, pl.ds(start, width)] = total

    for i in range(count):
        halve_core(i)
    total_in[0] = stats[...]
    rounds = [[sibling], [beside], [behind], line]
    place = 1
    for r, partners in enumerate(rounds):
        copies = [copy(total_in.at[0], total_in.at[place + j], (count + j, r), p) for j, p in enumerate(partners)]
        for made in copies:
            made.wait()
        summed = total_in[0]
        for j in range(len(partners)):
            summed = summed + total_in[place + j]
        total_in[0] = summed
        place += len(partners)
    stats_out[...] = total_in[0]

    lead, lag, tail = 4, 3, 2
    for step in range(count + lead + lag + tail):
        if step < count:
            halve_near(step)
        if 0 <= step - lead < count:
            halve_far(step - lead)
        if 0 <= step - lead - lag < count:
            spread_line(step - lead - lag)
        if 0 <= step - lead - lag - tail < count:
            finish(step - lead - lag - tail)

def dense_sum(grads, stats):
    widths = [g.shape[1] for g in grads]
    count = sum(-(-w // CHUNK) for w in widths)
    vmem = pl.BlockSpec(memory_space=pltpu.VMEM)
    low = jnp.bfloat16
    outs = pl.pallas_call(
        functools.partial(dense_sum_kernel, widths),
        out_shape=[jax.ShapeDtypeStruct((ROWS, w), jnp.float32) for w in widths] + [jax.ShapeDtypeStruct((8, 128), jnp.float32)],
        in_specs=[vmem] * (len(widths) + 1),
        out_specs=[vmem] * (len(widths) + 1),
        scratch_shapes=[
            pltpu.VMEM((count, 4, 4, ROWS, CHUNK), low),
            pltpu.VMEM((count, 2, 4, ROWS, CHUNK), low),
            pltpu.VMEM((count, 4, ROWS, CHUNK), low),
            pltpu.VMEM((count, 3, ROWS, CHUNK), low),
            pltpu.VMEM((7, 8, 128), jnp.float32),
            pltpu.SemaphoreType.DMA((count + 3, 7)),
            pltpu.SemaphoreType.DMA((count + 3, 7)),
        ],
        compiler_params=pltpu.CompilerParams(collective_id=4, has_side_effects=True, vmem_limit_bytes=56 * 2**20),
        name="dense_sum",
    )(*[g.reshape(4, 4, 2, ROWS, g.shape[1]) for g in grads], stats)
    return outs[:-1], outs[-1]


def shards(
    hidden_in,
    lengths,
    value_pick,
    output_pick,
    expert_pick,
    query_weight,
    key_weight,
    value_weight,
    output_weight,
    value_router,
    output_router,
    expert_router,
    attention_gain,
    feedforward_gain,
    expert_up,
    expert_down,
    cotangent,
):
    row_count = hidden_in.shape[1]
    total_experts = expert_router.shape[1]
    input_low = hidden_in[0]
    input_full = input_low.astype(jnp.float32)
    length = lengths[0]
    query_pos = lax.axis_index("dp") * row_count + jnp.arange(row_count, dtype=jnp.int32)
    live_mask = (query_pos < length).astype(jnp.float32)[:, None]
    gain_one = attention_gain.astype(jnp.float32)
    gain_two = feedforward_gain.astype(jnp.float32)
    normed_one = layer_norm(input_full, gain_one)
    normed_low = normed_one.astype(jnp.bfloat16)
    queries = low_dot(normed_low, query_weight).astype(jnp.bfloat16)
    key_local = low_dot(normed_low, key_weight).astype(jnp.bfloat16)
    value_sig = jax.nn.sigmoid(low_dot(normed_low, value_router)).reshape(row_count, HEADS, VE)
    value_hot = choose(value_pick[0], VE)
    value_gate = value_sig * value_hot
    value_all = low_dot(input_low, value_weight).reshape(row_count, HEADS, VE, HEAD_DIM)
    value_local = (
        jnp.sum(value_gate[..., None] * value_all, axis=2)
        .astype(jnp.bfloat16)
        .reshape(row_count, HEADS * HEAD_DIM)
    )
    key_all, value_rows = (
        lax.all_gather(key_local, "dp", axis=0, tiled=True),
        lax.all_gather(value_local, "dp", axis=0, tiled=True),
    )
    query_heads = queries.reshape(row_count, HEADS, HEAD_DIM)
    key_heads = key_all.reshape(-1, HEADS, HEAD_DIM)
    value_heads = value_rows.reshape(-1, HEADS, HEAD_DIM)
    soft_probs = attention_probs(query_heads, key_heads, query_pos, length)
    attended = jnp.einsum(
        "hqk,khd->qhd",
        soft_probs.astype(jnp.bfloat16),
        value_heads,
        preferred_element_type=jnp.float32,
    )
    output_sig = jax.nn.sigmoid(low_dot(normed_low, output_router)).reshape(row_count, HEADS, VE)
    output_hot = choose(output_pick[0], VE)
    output_gate = output_sig * output_hot
    mixed = (
        (output_gate[..., None] * attended[:, :, None, :])
        .astype(jnp.bfloat16)
        .reshape(row_count, HEADS * VE * HEAD_DIM)
    )
    attention_out = live_mask * low_dot(mixed, output_weight)
    middle = input_full + attention_out
    normed_two = layer_norm(middle, gain_two)
    normed_two_low = normed_two.astype(jnp.bfloat16)
    router_sig = jax.nn.sigmoid(low_dot(normed_two_low, expert_router))
    hot = jnp.any(
        expert_pick[0][:, :, None] == jnp.arange(total_experts, dtype=jnp.int32), axis=1
    ).astype(jnp.float32)
    picked_hot = hot * live_mask
    expert_gate = router_sig * picked_hot
    middle_low = middle.astype(jnp.bfloat16)
    sent = jnp.concatenate([middle_low, expert_gate.astype(jnp.bfloat16)], axis=1)
    groups = lax.axis_size("expert")
    rounds = max(1, groups // 8)

    def visit(grads, item):
        returned, grad_up, grad_down = expert_visit(*item, expert_up, expert_down)
        return (grads[0] + grad_up, grads[1] + grad_down), returned

    zeros = jnp.zeros(expert_up.shape, jnp.float32), jnp.zeros(expert_down.shape, jnp.float32)
    (up_grad, down_grad), returned = lax.scan(
        visit,
        zeros,
        (
            sent.reshape(rounds, -1, sent.shape[1]),
            cotangent[0].reshape(rounds, -1, D),
        ),
    )
    returned = returned.reshape(row_count, -1).astype(jnp.float32)
    up_grad = lax.psum_scatter(
        up_grad.astype(jnp.bfloat16), "dp", scatter_dimension=1, tiled=True
    ).astype(jnp.float32)
    down_grad = lax.psum_scatter(
        down_grad.astype(jnp.bfloat16), "dp", scatter_dimension=2, tiled=True
    ).astype(jnp.float32)
    feedforward_out = returned[:, :D]
    final_rows = middle + feedforward_out
    sums = jnp.stack(
        [
            jnp.sum(live_mask * input_full * input_full),
            jnp.sum(attention_out * attention_out),
            jnp.sum(feedforward_out * feedforward_out),
            jnp.sum(live_mask * final_rows * final_rows),
            jnp.sum(live_mask),
        ]
    )
    grad_final = cotangent[0].astype(jnp.float32)
    grad_middle = grad_final + returned[:, D : 2 * D]
    grad_logit = (
        returned[:, 2 * D :] * picked_hot * router_sig * (1.0 - router_sig)
    ).astype(jnp.bfloat16)
    grad_expert_router = low_dot(normed_two_low.T, grad_logit)
    grad_normed_two = low_dot(grad_logit, expert_router.T)
    unused_two, norm_two_back = jax.vjp(layer_norm, middle, gain_two)
    grad_middle_norm, grad_gain_two = norm_two_back(grad_normed_two)
    grad_middle = grad_middle + grad_middle_norm
    grad_branch = (live_mask * grad_middle).astype(jnp.bfloat16)
    grad_mixed = jnp.einsum(
        "td,md->tm", grad_branch, output_weight, preferred_element_type=jnp.float32
    ).reshape(row_count, HEADS, VE, HEAD_DIM)
    grad_output_weight = jnp.einsum(
        "td,tm->dm", grad_branch, mixed, preferred_element_type=jnp.float32
    )
    grad_attended = jnp.sum(output_gate[..., None] * grad_mixed, axis=2)
    grad_output_logit = (
        jnp.sum(attended[:, :, None, :] * grad_mixed, axis=3)
        * output_hot
        * output_sig
        * (1.0 - output_sig)
    ).reshape(row_count, HEADS * VE)
    grad_attended_low = grad_attended.astype(jnp.bfloat16)
    grad_probs = jnp.einsum(
        "qhd,khd->hqk", grad_attended_low, value_heads, preferred_element_type=jnp.float32
    )
    row_dot = jnp.sum(soft_probs * grad_probs, axis=-1, keepdims=True)
    grad_scores = (soft_probs * (grad_probs - row_dot) * HEAD_DIM ** (-0.5)).astype(jnp.bfloat16)
    grad_query = (
        jnp.einsum("hqk,khd->qhd", grad_scores, key_heads, preferred_element_type=jnp.float32)
        .astype(jnp.bfloat16)
        .reshape(row_count, HEADS * HEAD_DIM)
    )
    grad_key_all = jnp.einsum(
        "hqk,qhd->khd", grad_scores, query_heads, preferred_element_type=jnp.float32
    ).reshape(-1, HEADS * HEAD_DIM)
    grad_value_rows = jnp.einsum(
        "hqk,qhd->khd",
        soft_probs.astype(jnp.bfloat16),
        grad_attended_low,
        preferred_element_type=jnp.float32,
    ).reshape(-1, HEADS * HEAD_DIM)
    grad_key_sum, grad_value_sum = (
        lax.psum_scatter(
            grad_key_all.astype(jnp.bfloat16), "dp", scatter_dimension=0, tiled=True
        ).astype(jnp.float32),
        lax.psum_scatter(
            grad_value_rows.astype(jnp.bfloat16), "dp", scatter_dimension=0, tiled=True
        ).astype(jnp.float32),
    )
    grad_key = grad_key_sum.astype(jnp.bfloat16)
    grad_value_low = (
        grad_value_sum.astype(jnp.bfloat16)
        .astype(jnp.float32)
        .reshape(row_count, HEADS, 1, HEAD_DIM)
    )
    grad_value_each = (
        (value_gate[..., None] * grad_value_low)
        .astype(jnp.bfloat16)
        .reshape(row_count, HEADS * VE * HEAD_DIM)
    )
    grad_value_logit = (
        jnp.sum(value_all * grad_value_low, axis=3) * value_hot * value_sig * (1.0 - value_sig)
    ).reshape(row_count, HEADS * VE)
    grad_value_weight = jnp.einsum(
        "td,tm->dm", input_low, grad_value_each, preferred_element_type=jnp.float32
    )
    grad_query_weight = jnp.einsum(
        "td,tm->dm", normed_low, grad_query, preferred_element_type=jnp.float32
    )
    grad_key_weight = jnp.einsum(
        "td,tm->dm", normed_low, grad_key, preferred_element_type=jnp.float32
    )
    grad_value_logit = grad_value_logit.astype(jnp.bfloat16)
    grad_output_logit = grad_output_logit.astype(jnp.bfloat16)
    grad_value_router = low_dot(normed_low.T, grad_value_logit)
    grad_output_router = low_dot(normed_low.T, grad_output_logit)
    grad_normed_one = (
        jnp.einsum("tm,dm->td", grad_query, query_weight, preferred_element_type=jnp.float32)
        + jnp.einsum("tm,dm->td", grad_key, key_weight, preferred_element_type=jnp.float32)
        + low_dot(grad_value_logit, value_router.T)
        + low_dot(grad_output_logit, output_router.T)
    )
    unused_one, norm_one_back = jax.vjp(layer_norm, input_full, gain_one)
    grad_input_norm, grad_gain_one = norm_one_back(grad_normed_one)
    grad_input = (
        grad_middle
        + jnp.einsum("tm,dm->td", grad_value_each, value_weight, preferred_element_type=jnp.float32)
        + grad_input_norm
    )
    small_grads = jnp.concatenate(
        [
            grad_value_router,
            grad_output_router,
            grad_expert_router,
            grad_gain_one[:, None],
            grad_gain_two[:, None],
        ],
        axis=1,
    )
    small_count = small_grads.shape[1]
    small_grads = jnp.pad(small_grads, ((0, 0), (0, -small_count % 128)))
    low_grads = [
        part.astype(jnp.bfloat16)
        for part in (
            grad_query_weight,
            grad_key_weight,
            grad_value_weight,
            grad_output_weight,
            small_grads,
        )
    ]
    summed = lax.psum_scatter(
        jnp.concatenate(low_grads, axis=1), ("dp", "expert"), scatter_dimension=0, tiled=True
    ).astype(jnp.float32)
    dense_grads = jnp.split(summed, [512, 1024, 3584, 6144], axis=1)
    total_sums = lax.psum(sums, ("dp", "expert"))
    residual_norms = jnp.sqrt(total_sums[:4] / (total_sums[4] * D))
    small = dense_grads[4]
    router_end = 2 * HEADS * VE + expert_router.shape[1]
    dense_grads = [
        dense_grads[0],
        dense_grads[1],
        dense_grads[2],
        dense_grads[3].T,
        small[:, : HEADS * VE],
        small[:, HEADS * VE : 2 * HEADS * VE],
        small[:, 2 * HEADS * VE : router_end],
        small[:, router_end],
        small[:, router_end + 1],
    ]
    return (
        final_rows.astype(jnp.bfloat16)[None],
        grad_input[None],
        dense_grads[0],
        dense_grads[1],
        dense_grads[2],
        dense_grads[3],
        dense_grads[4],
        dense_grads[5],
        dense_grads[6],
        dense_grads[7],
        dense_grads[8],
        up_grad,
        down_grad,
        residual_norms,
    )


def shards_fast(
    hidden_in,
    lengths,
    value_pick,
    output_pick,
    expert_pick,
    query_weight,
    key_weight,
    value_weight,
    output_weight,
    value_router,
    output_router,
    expert_router,
    attention_gain,
    feedforward_gain,
    expert_up,
    expert_down,
    cotangent,
):
    total = expert_router.shape[1]
    spread = HEADS * VE
    routers = jnp.concatenate(
        [value_router.T, output_router.T, expert_router.T, jnp.zeros((128 - 2 * spread - total, D), jnp.bfloat16)]
    )
    gains = jnp.stack([attention_gain, feedforward_gain]).astype(jnp.float32)
    (
        middle,
        sent,
        normed_one,
        normed_two,
        queries,
        key_value,
        probs,
        value_all,
        attended,
        gates,
        slopes,
        cot_line,
    ) = attend(
        total,
        lengths,
        hidden_in[0],
        cotangent[0],
        value_pick[0].transpose(1, 2, 0),
        output_pick[0].transpose(1, 2, 0),
        expert_pick[0].T,
        routers,
        gains,
        key_weight,
        value_weight,
        query_weight,
        output_weight,
    )
    returned, up_grad, down_grad = expert_kernel_visit(sent, cot_line, expert_up, expert_down)
    block_out, grad_input, grad_query, grad_key, grad_value, grad_output, small, sums = backward(
        total,
        lengths,
        gates,
        slopes,
        routers,
        gains,
        returned,
        middle,
        cotangent[0],
        hidden_in[0],
        normed_one,
        queries,
        key_value,
        probs,
        value_all,
        attended,
        normed_two,
        query_weight,
        key_weight,
        value_weight,
        output_weight,
    )
    residual_norms = jnp.sqrt(sums[0, :4] / (sums[0, 4] * D))
    router_end = 2 * spread + total
    return (
        block_out[None],
        grad_input[None],
        grad_query,
        grad_key,
        grad_value,
        grad_output.T,
        small[:, :spread],
        small[:, spread : 2 * spread],
        small[:, 2 * spread : router_end],
        small[:, router_end],
        small[:, router_end + 1],
        up_grad,
        down_grad,
        residual_norms,
    )


def solution(mesh):
    placed = (
        P("expert", "dp", None),
        P("expert"),
        P("expert", "dp", None, None),
        P("expert", "dp", None, None),
        P("expert", "dp", None),
        P(),
        P(),
        P(),
        P(),
        P(),
        P(),
        P(),
        P(),
        P(),
        P("expert", None, None),
        P("expert", None, None),
        P("expert", "dp", None),
    )
    small_mesh = mesh.shape["dp"] == 4 and mesh.shape["expert"] == 8
    return jax.shard_map(
        shards_fast if small_mesh else shards,
        mesh=mesh,
        in_specs=placed,
        out_specs=(
            P("expert", "dp", None),
            P("expert", "dp", None),
            P(("dp", "expert"), None),
            P(("dp", "expert"), None),
            P(("dp", "expert"), None),
            P(None, ("dp", "expert")),
            P(("dp", "expert"), None),
            P(("dp", "expert"), None),
            P(("dp", "expert"), None),
            P(("dp", "expert")),
            P(("dp", "expert")),
            P("expert", "dp", None),
            P("expert", None, "dp"),
            P(),
        ),
        check_vma=False,
    )
```

```python
import functools

import jax
import jax.numpy as jnp
from jax import lax
from jax.experimental import pallas as pl
from jax.experimental.pallas import tpu as pltpu
from jax.sharding import PartitionSpec as P

D = 1024
HEADS = 4
HEAD_DIM = 128
VE = 5


MESH = pl.DeviceIdType.MESH
ROWS = 32
PIECE = VE * HEAD_DIM
EPSILON = 1e-05
NEGATIVE = -1000000000.0


def low_dot(left_side, right_side):
    return jnp.dot(left_side, right_side, preferred_element_type=jnp.float32)


def layer_norm(field, scale_gain):
    center = field - jnp.mean(field, axis=-1, keepdims=True)
    spread = jnp.mean(center * center, axis=-1, keepdims=True)
    return center * lax.rsqrt(spread + EPSILON) * scale_gain


def choose(select, count):
    return jnp.sum(
        (select[..., None] == jnp.arange(count, dtype=jnp.int32)).astype(jnp.float32), axis=-2
    )


def attention_probs(query_heads, key_heads, query_pos, length):
    key_pos = jnp.arange(key_heads.shape[0], dtype=jnp.int32)
    raw_scores = jnp.einsum(
        "qhd,khd->hqk", query_heads, key_heads, preferred_element_type=jnp.float32
    )
    allowed = (key_pos[None, :] <= query_pos[:, None]) & (key_pos[None, :] < length)
    scores = jnp.where(allowed[None], raw_scores * HEAD_DIM ** (-0.5), NEGATIVE)
    exp_terms = jnp.exp(scores - jnp.max(scores, axis=-1, keepdims=True))
    return exp_terms / jnp.sum(exp_terms, axis=-1, keepdims=True)


def dot_last(left_side, right_side):
    return lax.dot_general(
        left_side, right_side, (((1,), (1,)), ((), ())), preferred_element_type=jnp.float32
    )

def dot_first(left_side, right_side):
    return lax.dot_general(
        left_side, right_side, (((0,), (0,)), ((), ())), preferred_element_type=jnp.float32
    )


def visit_kernel(
    sent, cot, up, down, back_out, up_out, down_out, forward_out,
    rows, cot_other, up_wide, chosen, cots, gated, grad_pre, forward, forward_in, gated_turned, pre_turned, partial, paired_in, chain_in, up_low, down_low, up_in, down_in,
    row_send, row_recv, cot_send, cot_recv, pair_send, pair_recv, forward_send, forward_recv, chain_send, chain_recv, grad_send, grad_recv,
):
    experts = up.shape[0]
    wide = down.shape[0]
    hidden = wide // experts
    dp, ex = lax.axis_index("dp"), lax.axis_index("expert")
    y, x, z, core = dp // 2, dp % 2, ex // 2, ex % 2
    half = z // 2
    inner = z + half * (3 - 2 * z)
    onward = 1 - 2 * half
    sibling = (dp, z * 2 + 1 - core)
    beside, behind = (y * 2 + 1 - x, ex), ((1 - y) * 2 + x, ex)

    def at_z(place):
        return (dp, place * 2 + core)

    barrier = pltpu.get_barrier_semaphore()
    for place in (sibling, beside, behind):
        pl.semaphore_signal(barrier, inc=1, device_id=place, device_id_type=MESH)

    @pl.when(z < 3)
    def _():
        pl.semaphore_signal(barrier, inc=1, device_id=at_z(z + 1), device_id_type=MESH)

    @pl.when(z > 0)
    def _():
        pl.semaphore_signal(barrier, inc=1, device_id=at_z(z - 1), device_id_type=MESH)

    pl.semaphore_wait(barrier, 4 + inner)

    def remote(source, target, send, recv, place):
        return pltpu.make_async_remote_copy(
            src_ref=source, dst_ref=target, send_sem=send, recv_sem=recv, device_id=place, device_id_type=MESH
        )

    def row_copy(way, at, source=None):
        place = (sibling, at_z(z + 1), at_z(z - 1))[way]
        block = rows.at[at]
        target = block if way else rows.at[4 + at]
        return remote(block if source is None else source, target, row_send.at[way, at], row_recv.at[0 if way else 1, at], place)

    def cot_copy(at):
        return remote(cot.at[at], cot_other.at[at], cot_send.at[at], cot_recv.at[at], sibling)

    own = row_copy(0, z, sent), row_copy(1, z, sent), row_copy(2, z, sent)

    @pl.when(z < 3)
    def _():
        own[1].start()

    @pl.when(z > 0)
    def _():
        own[2].start()

    own[0].start()
    cot_copy(z).start()
    for k in (1, 2, 3):
        cot_copy((z + k) % 4).start()
    rows[z] = sent[...]
    for e in range(experts):
        up_wide[:, e * hidden : (e + 1) * hidden] = up[e]
    chosen[...] = (
        lax.broadcasted_iota(jnp.int32, (128, wide), 0)
        == 2 * HEADS * VE + ex * experts + lax.broadcasted_iota(jnp.int32, (128, wide), 1) // hidden
    ).astype(jnp.float32).astype(jnp.bfloat16)

    def order(p):
        later = (p + 2) // 3
        step = p - inner // (p + 1 - later)
        return later * (step + half * (3 - 2 * step)) + (1 - later) * z

    def pair_copy(at):
        return remote(partial.at[1, at], paired_in.at[at], pair_send.at[at], pair_recv.at[at], sibling)

    spans = (pl.ds(0, D // 2), pl.ds(D // 2, D // 2 + 128))

    def chain_copy(dest, slot, to, stage, part):
        span = spans[part]
        return remote(
            partial.at[0, dest, :, span], chain_in.at[slot, :, span],
            chain_send.at[stage, part], chain_recv.at[slot, part], at_z(to),
        )

    def add(target, source):
        def some(i, carry):
            part = pl.ds(pl.multiple_of(i * 32, 32), 32)
            target[part, :] = (
                target[part, :].astype(jnp.float32) + source[part, :].astype(jnp.float32)
            ).astype(target.dtype)
            return carry

        lax.fori_loop(0, target.shape[0] // 32, some, 0)

    def visit(q, carry):
        p, other = q // 2, q % 2
        at = order(p)
        block = other * 4 + at

        @pl.when((other == 0) & (p > 0))
        def _():
            row_copy(1, at).wait_recv()
            row_copy(0, at).start()

            @pl.when((at < z) & (z < 3))
            def _():
                row_copy(1, at).start()

            @pl.when((at > z) & (z > 0))
            def _():
                row_copy(2, at).start()

        @pl.when(other == 1)
        def _():
            row_copy(0, at).wait_recv()
            cot_copy(at).wait_recv()
            cots[...] = cot_other[at]

        @pl.when(other == 0)
        def _():
            cots[...] = cot[at]

        count = rows.shape[1]
        places = pl.ds(pl.multiple_of(block * count, count), count)

        def columns(n, gate_grad):
            span = pl.ds(pl.multiple_of(n * 256, 256), 256)
            pre = jnp.dot(rows[block, :, :D], up_wide[:, span], preferred_element_type=jnp.float32)
            back = dot_last(cots[...], down[span, :])
            mark = chosen[:, span]
            gate = jnp.dot(rows[block, :, D:], mark, preferred_element_type=jnp.float32)
            sig = jax.nn.sigmoid(pre)
            act = pre * sig
            act_low = (gate * act).astype(jnp.bfloat16)
            pre_low = (gate * back * (sig * (1.0 + pre * (1.0 - sig)))).astype(jnp.bfloat16)
            gated[block, :, span] = act_low
            grad_pre[:, span] = pre_low
            gated_turned[span, places] = act_low.T
            pre_turned[span, places] = pre_low.T
            return gate_grad + dot_last((act * back).astype(jnp.bfloat16), mark)

        partial[other, at, :, D:] = lax.fori_loop(
            0, wide // 256, columns, jnp.zeros((count, 128), jnp.float32)
        ).astype(jnp.bfloat16)

        def outward(n, carry):
            span = pl.ds(pl.multiple_of(n * 256, 256), 256)
            partial[other, at, :, span] = dot_last(grad_pre[...], up_wide[span, :]).astype(jnp.bfloat16)
            return carry

        lax.fori_loop(0, D // 256, outward, 0)

        @pl.when(other == 1)
        def _():
            pair_copy(at).start()
            pair_copy(at).wait_recv()
            add(partial.at[0, at], paired_in.at[at])

        @pl.when((inner == 0) & (q == 3))
        def _():
            chain_copy(*nearest, 0).start()

        @pl.when((inner == 0) & (q == 5))
        def _():
            chain_copy(*next_one, 0).start()

        return carry

    nearest = (z + onward, z + onward, z + onward, 0)
    farthest = (3 * (1 - half), 3 * (1 - half), z + onward, 1)
    backward = (3 * half, 3 * half, z - onward, 2)
    next_one = (2 - half, 2 - half + inner * (2 + half), z + onward, 3)
    lax.fori_loop(0, 8, visit, 0)

    def relay(dest, slot, to, stage, part):
        chain_copy(dest, dest, to, stage, part).wait_recv()
        add(partial.at[0, dest, :, spans[part]], chain_in.at[dest, :, spans[part]])
        chain_copy(dest, slot, to, stage, part).start()

    @pl.when(inner == 0)
    def _():
        chain_copy(*farthest, 0).start()
        chain_copy(*farthest, 1).start()
        chain_copy(*next_one, 1).start()
        chain_copy(*nearest, 1).start()

    tokens_all = rows.reshape(rows.shape[0] * rows.shape[1], rows.shape[2])
    cots_own = cot.reshape(cot.shape[0] * cot.shape[1], D)
    cots_other = cot_other.reshape(cot.shape[0] * cot.shape[1], D)
    place = cots_own.shape[0]
    quarter = D // 4


    def up_copy(j):
        return remote(up_low.at[j], up_in.at[j], grad_send.at[0, j], grad_recv.at[0, j], behind if j == 2 else beside)

    def down_copy(j):
        return remote(down_low.at[j], down_in.at[j], grad_send.at[1, j], grad_recv.at[1, j], beside if j == 1 else behind)

    def weight_grads(j, carry):
        across, aside = 1 - j % 2, 1 - j // 2
        at = (y + across * (1 - 2 * y)) * 2 + x + aside * (1 - 2 * x)
        span = pl.ds(pl.multiple_of(at * quarter, quarter), quarter)
        up_low[j] = jnp.dot(
            pre_turned[...], tokens_all[:, span], preferred_element_type=jnp.float32
        ).astype(jnp.bfloat16)
        down_low[j] = (
            jnp.dot(gated_turned[:, :place], cots_own[:, span], preferred_element_type=jnp.float32)
            + jnp.dot(gated_turned[:, place:], cots_other[:, span], preferred_element_type=jnp.float32)
        ).astype(jnp.bfloat16)

        @pl.when(j == 0)
        def _():
            up_copy(0).start()
            down_copy(0).start()

        @pl.when(j == 1)
        def _():
            up_copy(1).start()

        @pl.when(j == 2)
        def _():
            down_copy(2).start()

        return carry

    def relays(*ways):
        @pl.when(inner == 1)
        def _():
            for way, part in ways:
                relay(*way, part)

    def forward_copy(at):
        return remote(forward.at[at], forward_in.at[at], forward_send.at[at], forward_recv.at[at], sibling)

    def forward_block(block, carry):
        def some(n, inside):
            span = pl.ds(pl.multiple_of(n * 256, 256), 256)
            value = jnp.dot(gated[block], down[:, span], preferred_element_type=jnp.float32).astype(jnp.bfloat16)

            @pl.when(block >= 4)
            def _():
                forward[block % 4, :, span] = value

            @pl.when(block < 4)
            def _():
                forward_out[block % 4, :, span] = value

            return inside

        lax.fori_loop(0, D // 256, some, 0)

        @pl.when(block >= 4)
        def _():
            forward_copy(block % 4).start()

        return carry

    relays((next_one, 0))
    lax.fori_loop(0, 1, weight_grads, 0)
    relays((farthest, 0))
    lax.fori_loop(1, 3, weight_grads, 0)
    relays((farthest, 1), (backward, 0))
    lax.fori_loop(3, 4, weight_grads, 0)
    up_copy(0).wait()
    add(up_low.at[2], up_in.at[0])
    up_copy(2).start()
    down_copy(0).wait()
    add(down_low.at[1], down_in.at[0])
    down_copy(1).start()
    lax.fori_loop(4, 8, forward_block, 0)
    relays((backward, 1), (next_one, 1))
    lax.fori_loop(0, 4, forward_block, 0)
    for at in range(4):
        forward_copy(at).wait()
        add(forward_out.at[at], forward_in.at[at])
    up_sum = up_low[3].astype(jnp.float32)
    down_sum = down_low[3].astype(jnp.float32)
    for j in (1, 2):
        up_copy(j).wait()
        up_sum += up_in[j].astype(jnp.float32)
        down_copy(j).wait()
        down_sum += down_in[j].astype(jnp.float32)
    for e in range(experts):
        up_out[e] = up_sum[e * hidden : (e + 1) * hidden, :].T
        down_out[e] = down_sum[e * hidden : (e + 1) * hidden, :]

    for part in range(2):
        span = spans[part]
        chain_copy(z, z, z, 0, part).wait_recv()
        back_out[:, span] = partial[0, z, :, span].astype(jnp.float32) + chain_in[z, :, span].astype(jnp.float32)

        @pl.when(inner == 1)
        def _():
            chain_copy(z, 4, z, 0, part).wait_recv()
            back_out[:, span] = back_out[:, span] + chain_in[4, :, span].astype(jnp.float32)

    for at in range(4):
        row_copy(0, at).wait_send()
        cot_copy(at).wait_send()
        pair_copy(at).wait_send()

        @pl.when((at <= z) & (z < 3))
        def _():
            row_copy(1, at).wait_send()

        @pl.when((at >= z) & (z > 0))
        def _():
            row_copy(2, at).wait_send()

    for part in range(2):

        @pl.when(inner == 0)
        def _():
            chain_copy(z, 0, z, 0, part).wait_send()

        @pl.when(inner == 1)
        def _():
            chain_copy(z, 0, z, 2, part).wait_send()

        chain_copy(z, 0, z, 1, part).wait_send()
        chain_copy(z, 0, z, 3, part).wait_send()

def expert_kernel_visit(sent, cot_line, up, down):
    tokens = sent.shape[0]
    experts, _, hidden = up.shape
    wide = experts * hidden
    low = jnp.bfloat16
    vmem = pl.BlockSpec(memory_space=pltpu.VMEM)
    dma = pltpu.SemaphoreType.DMA
    f32 = jnp.float32
    return pl.pallas_call(
        visit_kernel,
        out_shape=[
            jax.ShapeDtypeStruct((tokens, D + 128), f32),
            jax.ShapeDtypeStruct((experts, D // 4, hidden), f32),
            jax.ShapeDtypeStruct((experts, hidden, D // 4), f32),
            jax.ShapeDtypeStruct((4, tokens, D), low),
        ],
        in_specs=[vmem] * 4,
        out_specs=[vmem] * 4,
        scratch_shapes=[
            pltpu.VMEM((8, tokens, D + 128), low),
            pltpu.VMEM((4, tokens, D), low),
            pltpu.VMEM((D, wide), low),
            pltpu.VMEM((128, wide), low),
            pltpu.VMEM((tokens, D), low),
            pltpu.VMEM((8, tokens, wide), low),
            pltpu.VMEM((tokens, wide), low),
            pltpu.VMEM((4, tokens, D), low),
            pltpu.VMEM((4, tokens, D), low),
            pltpu.VMEM((wide, 8 * tokens), low),
            pltpu.VMEM((wide, 8 * tokens), low),
            pltpu.VMEM((2, 4, tokens, D + 128), low),
            pltpu.VMEM((4, tokens, D + 128), low),
            pltpu.VMEM((5, tokens, D + 128), low),
            pltpu.VMEM((4, wide, D // 4), low),
            pltpu.VMEM((4, wide, D // 4), low),
            pltpu.VMEM((3, wide, D // 4), low),
            pltpu.VMEM((3, wide, D // 4), low),
            dma((3, 4)), dma((2, 4)), dma((4,)), dma((4,)), dma((4,)), dma((4,)), dma((4,)), dma((4,)), dma((4, 2)), dma((5, 2)), dma((2, 3)), dma((2, 3)),
        ],
        compiler_params=pltpu.CompilerParams(collective_id=2, has_side_effects=True, vmem_limit_bytes=58 * 2**20),
        name="expert_visit",
    )(sent, cot_line, up, down.reshape(wide, D))


def attend_kernel(
    expert_total, lengths, hidden, cot, value_pick, output_pick, expert_pick, routers, gains,
    key_weight_at, value_weight_at, query_weight_at, output_weight_at,
    middle, sent, normed_one, normed_two, queries, key_value, probs, value_all, attended,
    gates, slopes, cot_line,
    key_weight, value_weight, query_weight, output_weight, mixed, hot_turned, hot,
    fetch, pair_send, pair_recv, cot_send, cot_recv, own_sem,
):
    dp, ex = lax.axis_index("dp"), lax.axis_index("expert")
    z, core = ex // 2, ex % 2
    half = z // 2
    inner = z + half * (3 - 2 * z)
    count = hidden.shape[0]
    width = HEADS * HEAD_DIM
    low = jnp.bfloat16
    length = lengths[0]
    spread = HEADS * VE
    total = expert_total
    weights = [
        pltpu.make_async_copy(source, target, fetch.at[i])
        for i, (source, target) in enumerate(
            (
                (key_weight_at, key_weight),
                (value_weight_at, value_weight),
                (query_weight_at, query_weight),
                (output_weight_at, output_weight),
            )
        )
    ]
    for made in weights:
        made.start()

    def at_z(place):
        return (dp, place * 2 + core)

    barrier = pltpu.get_barrier_semaphore()
    for k in (1, 2, 3):
        pl.semaphore_signal(barrier, inc=1, device_id=((dp + k) % 4, ex), device_id_type=MESH)

    @pl.when(z < 3)
    def _():
        pl.semaphore_signal(barrier, inc=1, device_id=at_z(z + 1), device_id_type=MESH)

    @pl.when(z > 0)
    def _():
        pl.semaphore_signal(barrier, inc=1, device_id=at_z(z - 1), device_id_type=MESH)

    pl.semaphore_wait(barrier, 4 + inner)

    def cot_copy(way, at, source=None):
        block = cot_line.at[at]
        return pltpu.make_async_remote_copy(
            src_ref=block if source is None else source, dst_ref=block,
            send_sem=cot_send.at[way, at], recv_sem=cot_recv.at[at],
            device_id=at_z(z + 1 - 2 * way), device_id_type=MESH,
        )

    def pass_on(distance):
        @pl.when(z >= distance)
        def _():
            cot_copy(0, z - distance).wait_recv()

        @pl.when((z >= distance) & (z < 3))
        def _():
            cot_copy(0, z - distance).start()

        @pl.when(z + distance <= 3)
        def _():
            cot_copy(1, z + distance).wait_recv()

        @pl.when((z + distance <= 3) & (z > 0))
        def _():
            cot_copy(1, z + distance).start()

    @pl.when(z < 3)
    def _():
        cot_copy(0, z, cot).start()

    @pl.when(z > 0)
    def _():
        cot_copy(1, z, cot).start()

    keep = pltpu.make_async_copy(cot, cot_line.at[z], own_sem)
    keep.start()

    def norm(field, gain):
        center = field - jnp.mean(field, axis=-1, keepdims=True)
        spread = jnp.mean(center * center, axis=-1, keepdims=True)
        return (center * lax.rsqrt(spread + EPSILON) * gain).astype(low)

    parts = (pl.ds(0, width), pl.ds(width, width))

    def pair_copy(step, part, block):
        return pltpu.make_async_remote_copy(
            src_ref=key_value.at[block, :, parts[part]], dst_ref=key_value.at[block, :, parts[part]],
            send_sem=pair_send.at[step, part], recv_sem=pair_recv.at[block, part],
            device_id=((dp + step) % 4, ex), device_id_type=MESH,
        )

    def send_part(part):
        for step in (1, 2, 3):

            @pl.when(dp + step < 4)
            def _():
                pair_copy(step, part, dp).start()

    normed_one[...] = norm(hidden[...].astype(jnp.float32), gains[0:1, :])
    weights[0].wait()
    key_value[dp, :, parts[0]] = jnp.dot(
        normed_one[...], key_weight[...], preferred_element_type=jnp.float32
    ).astype(low)
    send_part(0)

    hot_turned[...] = jnp.zeros(hot_turned.shape, jnp.float32)

    def mark(picks, base, size):
        place = lax.broadcasted_iota(jnp.int32, (size, count), 0)
        found = jnp.zeros((size, count), jnp.float32)
        for pick in picks:
            found = jnp.where(place == pick, 1.0, found)
        hot_turned[base : base + size, :] = found

    mark([value_pick[h, i : i + 1, :] + h * VE for h in range(HEADS) for i in range(value_pick.shape[1])], 0, spread)
    mark(
        [output_pick[h, i : i + 1, :] + h * VE for h in range(HEADS) for i in range(output_pick.shape[1])],
        spread,
        spread,
    )
    mark([expert_pick[i : i + 1, :] for i in range(expert_pick.shape[0])], 2 * spread, total)
    hot[...] = hot_turned[...].T
    sig = jax.nn.sigmoid(dot_last(normed_one[...], routers[...]))
    gates[...] = sig * hot[...]
    slopes[...] = gates[...] * (1.0 - sig)
    weights[1].wait()

    def values(n, carry):
        span = pl.ds(pl.multiple_of(n * 256, 256), 256)
        value_all[:, span] = jnp.dot(
            hidden[...], value_weight[:, span], preferred_element_type=jnp.float32
        ).astype(low)
        return carry

    lax.fori_loop(0, HEADS * VE * HEAD_DIM // 256, values, 0)
    for h in range(HEADS):
        row = jnp.zeros((count, HEAD_DIM), jnp.float32)
        for e in range(h * VE, (h + 1) * VE):
            row += gates[:, e : e + 1] * value_all[:, e * HEAD_DIM : (e + 1) * HEAD_DIM].astype(jnp.float32)
        key_value[dp, :, width + h * HEAD_DIM : width + (h + 1) * HEAD_DIM] = row.astype(low)
    send_part(1)

    weights[2].wait()
    queries[...] = jnp.dot(normed_one[...], query_weight[...], preferred_element_type=jnp.float32).astype(low)
    for block in range(4):

        @pl.when(block > dp)
        def _():
            key_value[block] = jnp.zeros((count, 2 * width), low)

    pass_on(1)

    def wait_part(part):
        for block in range(3):

            @pl.when(block < dp)
            def _():
                pair_copy(1, part, block).wait_recv()

    wait_part(0)
    pair_all = key_value.reshape(4 * count, 2 * width)
    query_pos = dp * count + lax.broadcasted_iota(jnp.int32, (count, 4 * count), 0)
    key_pos = lax.broadcasted_iota(jnp.int32, (count, 4 * count), 1)
    allowed = (key_pos <= query_pos) & (key_pos < length)

    def score(h, carry):
        span = pl.ds(pl.multiple_of(h * HEAD_DIM, HEAD_DIM), HEAD_DIM)
        raw = dot_last(queries[:, span], pair_all[:, span])
        scores = jnp.where(allowed, raw * HEAD_DIM ** (-0.5), NEGATIVE)
        terms = jnp.exp(scores - jnp.max(scores, axis=-1, keepdims=True))
        probs[h] = (terms * (1.0 / jnp.sum(terms, axis=-1, keepdims=True))).astype(low)
        return carry

    lax.fori_loop(0, HEADS, score, 0)
    wait_part(1)
    pass_on(2)

    def collect(h, carry):
        span = pl.ds(pl.multiple_of(h * HEAD_DIM, HEAD_DIM), HEAD_DIM)
        value_span = pl.ds(pl.multiple_of(width + h * HEAD_DIM, HEAD_DIM), HEAD_DIM)
        attended[:, span] = jnp.dot(probs[h], pair_all[:, value_span], preferred_element_type=jnp.float32)
        return carry

    lax.fori_loop(0, HEADS, collect, 0)
    for h in range(HEADS):
        row = attended[:, h * HEAD_DIM : (h + 1) * HEAD_DIM]
        for e in range(h * VE, (h + 1) * VE):
            mixed[:, e * HEAD_DIM : (e + 1) * HEAD_DIM] = (gates[:, spread + e : spread + e + 1] * row).astype(low)

    place = dp * count + lax.broadcasted_iota(jnp.int32, (count, 1), 0)
    live = jnp.where(place < length, 1.0, 0.0)
    weights[3].wait()

    def outward(n, carry):
        span = pl.ds(pl.multiple_of(n * 256, 256), 256)
        branch = jnp.dot(mixed[...], output_weight[:, span], preferred_element_type=jnp.float32)
        middle[:, span] = hidden[:, span].astype(jnp.float32) + live * branch
        return carry

    lax.fori_loop(0, D // 256, outward, 0)
    sent[:, :D] = middle[...].astype(low)
    normed_two[...] = norm(middle[...], gains[1:2, :])
    sig = jax.nn.sigmoid(dot_last(normed_two[...], routers[...]))
    gate = sig * hot[...] * live
    sent[:, D:] = gate.astype(low)
    lane = lax.broadcasted_iota(jnp.int32, (count, 128), 1)
    slopes[...] = jnp.where(lane < 2 * spread, slopes[...], gate * (1.0 - sig))

    pass_on(3)
    keep.wait()
    for part in range(2):
        for step in (1, 2, 3):

            @pl.when(dp + step < 4)
            def _():
                pair_copy(step, part, dp).wait_send()

    for at in range(4):

        @pl.when((at <= z) & (z < 3))
        def _():
            cot_copy(0, at).wait_send()

        @pl.when((at >= z) & (z > 0))
        def _():
            cot_copy(1, at).wait_send()


def attend(total, lengths, *operands):
    count = operands[0].shape[0]
    low, full = jnp.bfloat16, jnp.float32
    vmem = pl.BlockSpec(memory_space=pltpu.VMEM)
    anywhere = pl.BlockSpec(memory_space=pl.ANY)
    dma = pltpu.SemaphoreType.DMA
    width, wide = HEADS * HEAD_DIM, HEADS * VE * HEAD_DIM
    shapes = [
        ((count, D), full),
        ((count, D + 128), low),
        ((count, D), low),
        ((count, D), low),
        ((count, width), low),
        ((4, count, 2 * width), low),
        ((HEADS, count, 4 * count), low),
        ((count, wide), low),
        ((count, width), full),
        ((count, 128), full),
        ((count, 128), full),
        ((4, count, D), low),
    ]
    return pl.pallas_call(
        functools.partial(attend_kernel, total),
        out_shape=[jax.ShapeDtypeStruct(*shape) for shape in shapes],
        in_specs=[pl.BlockSpec(memory_space=pltpu.SMEM)] + [vmem] * (len(operands) - 4) + [anywhere] * 4,
        out_specs=[vmem] * len(shapes),
        scratch_shapes=[pltpu.VMEM(a.shape, a.dtype) for a in operands[-4:]]
        + [
            pltpu.VMEM((count, wide), low),
            pltpu.VMEM((128, count), full),
            pltpu.VMEM((count, 128), full),
            dma((4,)),
            dma((4, 2)),
            dma((4, 2)),
            dma((2, 4)),
            dma((4,)),
            dma,
        ],
        compiler_params=pltpu.CompilerParams(
            collective_id=1, has_side_effects=True, vmem_limit_bytes=58 * 2**20
        ),
        name="attend",
    )(lengths, *operands)


def backward_kernel(
    total_experts, lengths, gates, slopes, routers, gains,
    forward_at, returned_at, middle_at, cot_at, hidden_at, normed_one_at, queries_at, key_value_at, probs_at, value_all_at,
    attended_at, normed_two_at, query_weight_at, key_weight_at, value_weight_at, output_weight_at,
    block_out, grad_in, out_query, out_key, out_value, out_output, out_small, sums_out,
    forward, returned, middle, cot, hidden, normed_one, queries, key_value, probs, value_all,
    attended, normed_two, query_weight, key_weight, value_part, output_part,
    branch, branch_turned, one_turned, hidden_turned, grad_att, grad_query, leave, arrive, grad_key,
    grad_each, grad_middle, grad_one, logit_one, logit_two, small_turned, mixed,
    grads, grads_small, core_in, plane_in, last_in, sums_in, forward_in,
    fetch, part_fetch, leave_send, leave_recv, send, recv, forward_send, forward_recv,
):
    dp, ex = lax.axis_index("dp"), lax.axis_index("expert")
    y, x, z, core = dp // 2, dp % 2, ex // 2, ex % 2
    count = hidden.shape[0]
    width = HEADS * HEAD_DIM
    low, full = jnp.bfloat16, jnp.float32
    length = lengths[0]
    sibling = (dp, z * 2 + 1 - core)
    beside = (y * 2 + 1 - x, ex)
    behind = ((1 - y) * 2 + x, ex)
    across = ((1 - y) * 2 + 1 - x, ex)
    line = [(dp, ((z + k) % 4) * 2 + core) for k in (1, 2, 3)]
    barrier = pltpu.get_barrier_semaphore()
    for place in (sibling, beside, behind, across, *line):
        pl.semaphore_signal(barrier, inc=1, device_id=place, device_id_type=MESH)

    held = dict(
        forward=(forward_at, forward),
        returned=(returned_at, returned),
        middle=(middle_at, middle),
        cot=(cot_at, cot),
        hidden=(hidden_at, hidden),
        attended=(attended_at, attended),
        key_value=(key_value_at, key_value),
        probs=(probs_at, probs),
        queries=(queries_at, queries),
        normed_one=(normed_one_at, normed_one),
        query_weight=(query_weight_at, query_weight),
        value_all=(value_all_at, value_all),
        key_weight=(key_weight_at, key_weight),
        normed_two=(normed_two_at, normed_two),
    )
    got = {
        name: pltpu.make_async_copy(source, target, fetch.at[i])
        for i, (name, (source, target)) in enumerate(held.items())
    }

    def output_copy(n):
        return pltpu.make_async_copy(
            output_weight_at.at[pl.ds(n * PIECE, PIECE)], output_part.at[n % 2], part_fetch.at[0, n % 2]
        )

    def value_copy(n):
        return pltpu.make_async_copy(
            value_weight_at.at[:, pl.ds(n * PIECE, PIECE)], value_part.at[n % 2], part_fetch.at[1, n % 2]
        )

    first_held = ("forward", "returned", "middle", "cot", "hidden")
    for name in first_held:
        got[name].start()
    for n in range(2):
        output_copy(n).start()
    for name in held:
        if name not in first_held:
            got[name].start()
    for n in range(2):
        value_copy(n).start()

    pieces = (
        [(out_output, PIECE * n, PIECE, n) for n in range(HEADS)]
        + [(out_query, 0, width, 4)]
        + [(out_value, PIECE * n, PIECE, n) for n in range(HEADS)]
        + [(out_key, 0, width, 5), (out_small, 0, 128, None)]
    )
    along_line = (0, 1)
    in_plane = [i for i in range(len(pieces)) if i not in along_line]
    x_first = {i: n % 2 == 0 for n, i in enumerate(in_plane)}

    def remote(source, target, slot, place):
        return pltpu.make_async_remote_copy(
            src_ref=source, dst_ref=target, send_sem=send.at[slot], recv_sem=recv.at[slot],
            device_id=place, device_id_type=MESH,
        )

    def add(target, source):
        target[...] = (target[...].astype(full) + source[...].astype(full)).astype(target.dtype)

    def own(i):
        slot = pieces[i][3]
        return grads_small if slot is None else grads.at[slot, :, :, :, :, columns(i)]

    def columns(i):
        return pl.ds(0, pieces[i][2])

    started = {}

    def begin(key, source, target, slot, place):
        started[key] = remote(source, target, slot, place)
        started[key].start()

    def halve_core(i):
        begin((i, 0), own(i).at[:, :, 1 - core], core_in.at[i, :, :, :, columns(i)], (i, 0), sibling)

    def halve_near(i):
        span = columns(i)
        started[i, 0].wait()
        add(core_in.at[i, :, :, :, span], own(i).at[:, :, core])
        if i in along_line:
            for k in (1, 2, 3):
                begin(
                    (i, k), core_in.at[i, :, (z + k) % 4, :, span],
                    plane_in.at[i, pl.ds(4 * k - 4, 4), :, span], (i, k), line[k - 1],
                )
            return
        for part in range(2):
            if x_first[i]:
                source = core_in.at[i, part * 2 + 1 - x, :, :, span]
            else:
                source = core_in.at[i, (1 - y) * 2 + part, :, :, span]
            target = plane_in.at[i, pl.ds(part * 4, 4), :, span]
            begin((i, 1 + part), source, target, (i, 1 + part), beside if x_first[i] else behind)

    def halve_far(i):
        span = columns(i)
        if i in along_line:
            held = core_in.at[i, :, z, :, span]
            for k in (1, 2, 3):
                started[i, k].wait()
                add(held, plane_in.at[i, pl.ds(4 * k - 4, 4), :, span])
            for part in range(2):
                begin(
                    (i, 4 + part), core_in.at[i, part * 2 + 1 - x, z, :, span],
                    last_in.at[i, part, :, span], (i, 4 + part), beside,
                )
            return
        for part in range(2):
            started[i, 1 + part].wait()
            kept = part * 2 + x if x_first[i] else y * 2 + part
            add(plane_in.at[i, pl.ds(part * 4, 4), :, span], core_in.at[i, kept, :, :, span])
        other = 1 - y if x_first[i] else 1 - x
        begin(
            (i, 3), plane_in.at[i, pl.ds(other * 4, 4), :, span], plane_in.at[i, pl.ds(8, 4), :, span],
            (i, 3), behind if x_first[i] else beside,
        )

    def spread(i):
        span = columns(i)
        if i in along_line:
            for part in range(2):
                started[i, 4 + part].wait()
                add(last_in.at[i, part, :, span], core_in.at[i, part * 2 + x, z, :, span])
            begin((i, 6), last_in.at[i, 1 - y, :, span], last_in.at[i, 2, :, span], (i, 6), behind)
            return
        started[i, 3].wait()
        add(plane_in.at[i, pl.ds(8, 4), :, span], plane_in.at[i, pl.ds((y if x_first[i] else x) * 4, 4), :, span])
        for k in (1, 2, 3):
            begin(
                (i, 3 + k), plane_in.at[i, 8 + (z + k) % 4, :, span],
                last_in.at[i, k - 1, :, span], (i, 3 + k), line[k - 1],
            )

    def finish(i):
        out, start, size, _ = pieces[i]
        span = columns(i)
        if i in along_line:
            started[i, 6].wait()
            total = last_in[i, y, :, span].astype(full) + last_in[i, 2, :, span].astype(full)
        else:
            total = plane_in[i, 8 + z, :, span].astype(full)
            for k in (1, 2, 3):
                started[i, 3 + k].wait()
                total = total + last_in[i, k - 1, :, span].astype(full)
        out[:, pl.ds(start, size)] = total

    rows_each = 64
    lane = lax.broadcasted_iota(jnp.int32, (1, 128), 1)
    for name in first_held:
        got[name].wait()
    logit_two[...] = (returned[:, D:] * slopes[...]).astype(low)

    half = z // 2
    inner = z + half * (3 - 2 * z)
    onward = 1 - 2 * half
    nearest = (z + onward, z + onward, z + onward, 0)
    farthest = (3 * (1 - half), 3 * (1 - half), z + onward, 1)
    backward = (3 * half, 3 * half, z - onward, 2)
    next_one = (2 - half, 2 - half + inner * (2 + half), z + onward, 3)

    def forward_copy(dest, slot, to, stage, part):
        span = pl.ds(part * (D // 2), D // 2)
        return pltpu.make_async_remote_copy(
            src_ref=forward.at[dest, :, span], dst_ref=forward_in.at[slot, :, span],
            send_sem=forward_send.at[stage, part], recv_sem=forward_recv.at[slot, part],
            device_id=(dp, to * 2 + core), device_id_type=MESH,
        )

    def relays(*ways):
        @pl.when(inner == 1)
        def _():
            for (dest, slot, to, stage), part in ways:
                span = pl.ds(part * (D // 2), D // 2)
                forward_copy(dest, dest, to, stage, part).wait_recv()
                add(forward.at[dest, :, span], forward_in.at[dest, :, span])
                forward_copy(dest, slot, to, stage, part).start()

    pl.semaphore_wait(barrier, 7)

    @pl.when(inner == 0)
    def _():
        for way in (farthest, next_one, nearest):
            for part in range(2):
                forward_copy(*way, part).start()

    def live_rows(start):
        place = dp * count + start + lax.broadcasted_iota(jnp.int32, (rows_each, 1), 0)
        return jnp.where(place < length, 1.0, 0.0)

    def norm_back(field, grad, gain):
        center = field - jnp.mean(field, axis=-1, keepdims=True)
        scale = lax.rsqrt(jnp.mean(center * center, axis=-1, keepdims=True) + EPSILON)
        unit = center * scale
        part = grad * gain
        back = scale * (
            part
            - jnp.mean(part, axis=-1, keepdims=True)
            - unit * jnp.mean(part * unit, axis=-1, keepdims=True)
        )
        return back, jnp.sum(grad * unit, axis=0, keepdims=True)

    def first_rows(n, gain_sum):
        start = pl.multiple_of(n * rows_each, rows_each)
        rows = pl.ds(start, rows_each)
        grad = jnp.dot(logit_two[rows, :], routers[...], preferred_element_type=full)
        back, gain_part = norm_back(middle[rows, :], grad, gains[1:2, :])
        total = cot[rows, :].astype(full) + returned[rows, :D] + back
        grad_middle[rows, :] = total
        branch[rows, :] = (live_rows(start) * total).astype(low)
        return gain_sum + gain_part

    gain_two_sum = lax.fori_loop(0, count // rows_each, first_rows, jnp.zeros((1, D), full))
    relays((farthest, 0))

    def square(field, live, at):
        total = jnp.sum(jnp.sum(field * field, axis=1, keepdims=True) * live, axis=0, keepdims=True)
        return jnp.where(lane == at, total, 0.0)

    def last_rows(n, sums):
        start = pl.multiple_of(n * rows_each, rows_each)
        rows = pl.ds(start, rows_each)
        live = live_rows(start)
        field = middle[rows, :]
        step = forward[z, rows, :].astype(full)
        final = field + step
        block_out[rows, :] = final.astype(low)
        source = hidden[rows, :].astype(full)
        one = jnp.ones((rows_each, 1), full)
        sums += square(source, live, 0) + square(field - source, one, 1)
        sums += square(step, one, 2) + square(final, live, 3)
        return sums + jnp.where(lane == 4, jnp.sum(live, axis=0, keepdims=True), 0.0)

    def output_rows():
        for part in range(2):
            span = pl.ds(part * (D // 2), D // 2)
            forward_copy(z, z, z, 0, part).wait_recv()
            add(forward.at[z, :, span], forward_in.at[z, :, span])

            @pl.when(inner == 1)
            def _():
                forward_copy(z, 4, z, 0, part).wait_recv()
                add(forward.at[z, :, span], forward_in.at[4, :, span])

        sums = lax.fori_loop(0, count // rows_each, last_rows, jnp.zeros((1, 128), full))
        sums_in[0] = jnp.broadcast_to(sums, (8, 128))

    def weight_grad(i, turned, right):
        def some(n, carry):
            rows = pl.ds(pl.multiple_of(n * 256, 256), 256)
            value = jnp.dot(turned[rows, :], right, preferred_element_type=full).astype(low)
            own(i)[n] = value.reshape(4, 2, ROWS, pieces[i][2])
            return carry

        lax.fori_loop(0, D // 256, some, 0)
        halve_core(i)

    got["attended"].wait()
    spread_count = HEADS * VE

    def head_of(c):
        return slice((c // VE) * HEAD_DIM, (c // VE + 1) * HEAD_DIM)

    logit_one[...] = jnp.zeros(logit_one.shape, full)
    grad_att[...] = jnp.zeros(grad_att.shape, full)
    for n in range(HEADS):
        output_copy(n).wait()
        for j in range(VE):
            c = VE * n + j
            grad_mixed = dot_last(branch[...], output_part[n % 2, j * HEAD_DIM : (j + 1) * HEAD_DIM, :])
            col = spread_count + c
            grad_att[:, head_of(c)] += gates[:, col : col + 1] * grad_mixed
            dots = jnp.sum(attended[:, head_of(c)] * grad_mixed, axis=1, keepdims=True)
            logit_one[:, col : col + 1] = dots * slopes[:, col : col + 1]
        if n + 2 < HEADS:
            output_copy(n + 2).start()
    relays((farthest, 1), (backward, 0))

    pair_all = key_value.reshape(4 * count, 2 * width)
    for name in ("key_value", "probs", "queries"):
        got[name].wait()

    def leave_copy(k, h):
        rows = pl.ds(h * 2 * HEAD_DIM, 2 * HEAD_DIM)
        return pltpu.make_async_remote_copy(
            src_ref=leave.at[(dp + 4 - k) % 4, rows], dst_ref=arrive.at[k - 1, rows],
            send_sem=leave_send.at[k - 1, h], recv_sem=leave_recv.at[k - 1, h],
            device_id=((dp + 4 - k) % 4, ex), device_id_type=MESH,
        )

    def head(h, carry):
        start = pl.multiple_of(h * HEAD_DIM, HEAD_DIM)
        span = pl.ds(start, HEAD_DIM)
        grad = grad_att[:, span].astype(low)
        prob = probs[h].astype(full)
        grad_prob = dot_last(grad, pair_all[:, pl.ds(width + start, HEAD_DIM)])
        dots = jnp.sum(prob * grad_prob, axis=-1, keepdims=True)
        grad_score = (prob * (grad_prob - dots) * HEAD_DIM ** (-0.5)).astype(low)
        grad_query[:, span] = jnp.dot(grad_score, pair_all[:, span], preferred_element_type=full).astype(low)
        key_part = dot_first(queries[:, span], grad_score).astype(low)
        value_part_all = dot_first(grad, probs[h]).astype(low)
        key_rows = pl.ds(pl.multiple_of(2 * h * HEAD_DIM, 2 * HEAD_DIM), HEAD_DIM)
        value_rows = pl.ds(pl.multiple_of((2 * h + 1) * HEAD_DIM, HEAD_DIM), HEAD_DIM)
        for j in range(4):
            leave[j, key_rows, :] = key_part[:, j * count : (j + 1) * count]
            leave[j, value_rows, :] = value_part_all[:, j * count : (j + 1) * count]
        for k in (1, 2, 3):

            @pl.when(dp >= k)
            def _():
                leave_copy(k, h).start()

        return carry

    lax.fori_loop(0, HEADS, head, 0)

    relays((backward, 1), (next_one, 0), (next_one, 1))
    branch_turned[...] = branch[...].T
    for n in range(HEADS):
        for j in range(VE):
            c = VE * n + j
            gate = gates[:, spread_count + c : spread_count + c + 1]
            mixed[:, j * HEAD_DIM : (j + 1) * HEAD_DIM] = (gate * attended[:, head_of(c)]).astype(low)
        weight_grad(n, branch_turned, mixed[...])
        if n:
            halve_near(n - 1)
    for name in ("normed_one", "query_weight"):
        got[name].wait()
    one_turned[...] = normed_one[...].T
    weight_grad(4, one_turned, grad_query[...])
    halve_near(3)
    hidden_turned[...] = hidden[...].T
    grad_one[...] = dot_last(grad_query[...], query_weight[...])
    halve_near(4)
    got["value_all"].wait()

    for h in range(HEADS):
        rows = pl.ds(h * 2 * HEAD_DIM, 2 * HEAD_DIM)
        total = leave[dp, rows, :].astype(full)
        for k in (1, 2, 3):

            @pl.when(dp + k < 4)
            def _():
                leave_copy(k, h).wait_recv()

            @pl.when(dp + k >= 4)
            def _():
                arrive[k - 1, rows, :] = jnp.zeros((2 * HEAD_DIM, count), low)

            total += arrive[k - 1, rows, :].astype(full)
        turned = total.T
        grad_key[:, h * HEAD_DIM : (h + 1) * HEAD_DIM] = turned[:, :HEAD_DIM].astype(low)
        grad = turned[:, HEAD_DIM:].astype(low).astype(full)
        for c in range(h * VE, (h + 1) * VE):
            here = slice(c * HEAD_DIM, (c + 1) * HEAD_DIM)
            grad_each[:, here] = (gates[:, c : c + 1] * grad).astype(low)
            dots = jnp.sum(value_all[:, here].astype(full) * grad, axis=1, keepdims=True)
            logit_one[:, c : c + 1] = dots * slopes[:, c : c + 1]
        weight_grad(5 + h, hidden_turned, grad_each[:, h * PIECE : (h + 1) * PIECE])
        if h:
            halve_near(4 + h)
    weight_grad(9, one_turned, grad_key[...])
    halve_near(8)
    got["key_weight"].wait()
    grad_one[...] += dot_last(grad_key[...], key_weight[...])
    halve_near(9)
    halve_far(2)
    grad_one[...] += jnp.dot(logit_one[...].astype(low), routers[...], preferred_element_type=full)

    def first_norm(n, gain_sum):
        rows = pl.ds(pl.multiple_of(n * rows_each, rows_each), rows_each)
        back, gain_part = norm_back(hidden[rows, :].astype(full), grad_one[rows, :], gains[0:1, :])
        grad_in[rows, :] = grad_middle[rows, :] + back
        return gain_sum + gain_part

    gain_one_sum = lax.fori_loop(0, count // rows_each, first_norm, jnp.zeros((1, D), full))
    halve_far(3)
    got["normed_two"].wait()
    small_turned[...] = dot_first(logit_one[...].astype(low), normed_one[...]) + dot_first(
        logit_two[...], normed_two[...]
    )
    small_rows = 2 * spread_count + total_experts
    small_turned[small_rows : small_rows + 1, :] = gain_one_sum
    small_turned[small_rows + 1 : small_rows + 2, :] = gain_two_sum
    grads_small[...] = small_turned[...].T.astype(low).reshape(grads_small.shape)
    halve_core(10)
    spread(2)
    halve_far(4)
    output_rows()

    rounds = [[sibling], [beside], [behind], line]
    offset = [1, 2, 3, 4]

    def sum_start(r):
        for j, place in enumerate(rounds[r]):
            begin(("sum", r, j), sums_in.at[0], sums_in.at[offset[r] + j], (len(pieces) + j, r), place)

    def sum_end(r):
        for j in range(len(rounds[r])):
            started["sum", r, j].wait()
        total = sums_in[0]
        for j in range(len(rounds[r])):
            total = total + sums_in[offset[r] + j]
        sums_in[0] = total

    def value_side(n):
        value_copy(n).wait()
        grad_in[...] += dot_last(grad_each[:, n * PIECE : (n + 1) * PIECE], value_part[n % 2])
        if n + 2 < HEADS:
            value_copy(n + 2).start()

    for action, i in (
        (sum_start, 0), (halve_near, 10), (spread, 3),
        (value_side, 0), (sum_end, 0), (sum_start, 1), (halve_far, 5), (halve_far, 0), (spread, 4), (finish, 2),
        (value_side, 1), (sum_end, 1), (sum_start, 2), (halve_far, 6), (spread, 0), (finish, 3), (spread, 5),
        (value_side, 2), (sum_end, 2), (sum_start, 3), (halve_far, 7), (finish, 4), (spread, 6),
        (value_side, 3), (finish, 0), (halve_far, 1), (halve_far, 8), (finish, 5), (spread, 7), (sum_end, 3),
        (spread, 1), (halve_far, 9), (finish, 6), (spread, 8), (halve_far, 10), (finish, 7), (finish, 1), (spread, 9),
        (spread, 10), (finish, 8), (finish, 9), (finish, 10),
    ):
        action(i)
    sums_out[...] = sums_in[0]
    for h in range(HEADS):
        for k in (1, 2, 3):

            @pl.when(dp >= k)
            def _():
                leave_copy(k, h).wait_send()

    for part in range(2):
        forward_copy(z, 0, z, 1, part).wait_send()
        forward_copy(z, 0, z, 3, part).wait_send()

        @pl.when(inner == 0)
        def _():
            forward_copy(z, 0, z, 0, part).wait_send()

        @pl.when(inner == 1)
        def _():
            forward_copy(z, 0, z, 2, part).wait_send()


def backward(total_experts, lengths, gates, slopes, routers, gains, *arrays):
    low, full = jnp.bfloat16, jnp.float32
    count = gates.shape[0]
    width, wide = HEADS * HEAD_DIM, HEADS * VE * HEAD_DIM
    vmem = pl.BlockSpec(memory_space=pltpu.VMEM)
    anywhere = pl.BlockSpec(memory_space=pl.ANY)
    dma = pltpu.SemaphoreType.DMA
    whole = [pltpu.VMEM(a.shape, a.dtype) for a in arrays[:14]]
    n = 11
    return pl.pallas_call(
        functools.partial(backward_kernel, total_experts),
        out_shape=[
            jax.ShapeDtypeStruct((count, D), low),
            jax.ShapeDtypeStruct((count, D), full),
            jax.ShapeDtypeStruct((ROWS, width), full),
            jax.ShapeDtypeStruct((ROWS, width), full),
            jax.ShapeDtypeStruct((ROWS, wide), full),
            jax.ShapeDtypeStruct((ROWS, wide), full),
            jax.ShapeDtypeStruct((ROWS, 128), full),
            jax.ShapeDtypeStruct((8, 128), full),
        ],
        in_specs=[pl.BlockSpec(memory_space=pltpu.SMEM)] + [vmem] * 4 + [anywhere] * len(arrays),
        out_specs=[vmem] * 8,
        scratch_shapes=whole
        + [
            pltpu.VMEM((2, D, PIECE), low),
            pltpu.VMEM((2, PIECE, D), low),
            pltpu.VMEM((count, D), low),
            pltpu.VMEM((D, count), low),
            pltpu.VMEM((D, count), low),
            pltpu.VMEM((D, count), low),
            pltpu.VMEM((count, width), full),
            pltpu.VMEM((count, width), low),
            pltpu.VMEM((4, 2 * width, count), low),
            pltpu.VMEM((3, 2 * width, count), low),
            pltpu.VMEM((count, width), low),
            pltpu.VMEM((count, wide), low),
            pltpu.VMEM((count, D), full),
            pltpu.VMEM((count, D), full),
            pltpu.VMEM((count, 128), full),
            pltpu.VMEM((count, 128), low),
            pltpu.VMEM((128, D), full),
            pltpu.VMEM((count, PIECE), low),
            pltpu.VMEM((6, 4, 4, 2, ROWS, PIECE), low),
            pltpu.VMEM((4, 4, 2, ROWS, 128), low),
            pltpu.VMEM((n, 4, 4, ROWS, PIECE), low),
            pltpu.VMEM((n, 12, ROWS, PIECE), low),
            pltpu.VMEM((n, 3, ROWS, PIECE), low),
            pltpu.VMEM((7, 8, 128), full),
            pltpu.VMEM((5, count, D), low),
            dma((14,)),
            dma((2, 2)),
            dma((3, HEADS)),
            dma((3, HEADS)),
            dma((n + 3, 7)),
            dma((n + 3, 7)),
            dma((4, 2)),
            dma((5, 2)),
        ],
        compiler_params=pltpu.CompilerParams(
            collective_id=3, has_side_effects=True, vmem_limit_bytes=62 * 2**20
        ),
        name="backward",
    )(lengths, gates, slopes, routers, gains, *arrays)


def expert_visit(sent, cotangent, expert_up, expert_down):
    local_experts = expert_up.shape[0]
    group = lax.axis_index("expert")
    cot_all = lax.all_gather(cotangent, "expert", axis=0, tiled=True)
    sent_all = lax.all_gather(sent, "expert", axis=0, tiled=True)
    rows_all = sent_all[:, :D]
    total_experts = sent.shape[1] - D
    gate_all = lax.dynamic_slice_in_dim(
        sent_all[:, D:], group * local_experts, local_experts, 1
    ).astype(jnp.float32).T[:, :, None]
    preact = jnp.einsum("td,xdf->xtf", rows_all, expert_up, preferred_element_type=jnp.float32)
    pre_sig = jax.nn.sigmoid(preact)
    hidden = preact * pre_sig
    back = jnp.einsum("td,xfd->xtf", cot_all, expert_down, preferred_element_type=jnp.float32)
    gate_grad = jnp.sum(hidden * back, axis=2).T
    gated = (gate_all * hidden).astype(jnp.bfloat16)
    grad_pre = (gate_all * back * (pre_sig * (1.0 + preact * (1.0 - pre_sig)))).astype(jnp.bfloat16)
    partial_out = jnp.einsum("xtf,xfd->td", gated, expert_down, preferred_element_type=jnp.float32)
    partial_grad = jnp.einsum("xtf,xdf->td", grad_pre, expert_up, preferred_element_type=jnp.float32)
    wide_grad = lax.dynamic_update_slice_in_dim(
        jnp.zeros((gate_grad.shape[0], total_experts), jnp.bfloat16),
        gate_grad.astype(jnp.bfloat16),
        group * local_experts,
        1,
    )
    returned = lax.psum_scatter(
        jnp.concatenate(
            [partial_out.astype(jnp.bfloat16), partial_grad.astype(jnp.bfloat16), wide_grad], axis=1
        ),
        "expert",
        scatter_dimension=0,
        tiled=True,
    )
    grad_down = jnp.einsum("xtf,td->xfd", gated, cot_all, preferred_element_type=jnp.float32)
    grad_up = jnp.einsum("td,xtf->xdf", rows_all, grad_pre, preferred_element_type=jnp.float32)
    return returned, grad_up, grad_down


def shards(
    hidden_in,
    lengths,
    value_pick,
    output_pick,
    expert_pick,
    query_weight,
    key_weight,
    value_weight,
    output_weight,
    value_router,
    output_router,
    expert_router,
    attention_gain,
    feedforward_gain,
    expert_up,
    expert_down,
    cotangent,
):
    row_count = hidden_in.shape[1]
    total_experts = expert_router.shape[1]
    input_low = hidden_in[0]
    input_full = input_low.astype(jnp.float32)
    length = lengths[0]
    query_pos = lax.axis_index("dp") * row_count + jnp.arange(row_count, dtype=jnp.int32)
    live_mask = (query_pos < length).astype(jnp.float32)[:, None]
    gain_one = attention_gain.astype(jnp.float32)
    gain_two = feedforward_gain.astype(jnp.float32)
    normed_one = layer_norm(input_full, gain_one)
    normed_low = normed_one.astype(jnp.bfloat16)
    queries = low_dot(normed_low, query_weight).astype(jnp.bfloat16)
    key_local = low_dot(normed_low, key_weight).astype(jnp.bfloat16)
    value_sig = jax.nn.sigmoid(low_dot(normed_low, value_router)).reshape(row_count, HEADS, VE)
    value_hot = choose(value_pick[0], VE)
    value_gate = value_sig * value_hot
    value_all = low_dot(input_low, value_weight).reshape(row_count, HEADS, VE, HEAD_DIM)
    value_local = (
        jnp.sum(value_gate[..., None] * value_all, axis=2)
        .astype(jnp.bfloat16)
        .reshape(row_count, HEADS * HEAD_DIM)
    )
    key_all, value_rows = (
        lax.all_gather(key_local, "dp", axis=0, tiled=True),
        lax.all_gather(value_local, "dp", axis=0, tiled=True),
    )
    query_heads = queries.reshape(row_count, HEADS, HEAD_DIM)
    key_heads = key_all.reshape(-1, HEADS, HEAD_DIM)
    value_heads = value_rows.reshape(-1, HEADS, HEAD_DIM)
    soft_probs = attention_probs(query_heads, key_heads, query_pos, length)
    attended = jnp.einsum(
        "hqk,khd->qhd",
        soft_probs.astype(jnp.bfloat16),
        value_heads,
        preferred_element_type=jnp.float32,
    )
    output_sig = jax.nn.sigmoid(low_dot(normed_low, output_router)).reshape(row_count, HEADS, VE)
    output_hot = choose(output_pick[0], VE)
    output_gate = output_sig * output_hot
    mixed = (
        (output_gate[..., None] * attended[:, :, None, :])
        .astype(jnp.bfloat16)
        .reshape(row_count, HEADS * VE * HEAD_DIM)
    )
    attention_out = live_mask * low_dot(mixed, output_weight)
    middle = input_full + attention_out
    normed_two = layer_norm(middle, gain_two)
    normed_two_low = normed_two.astype(jnp.bfloat16)
    router_sig = jax.nn.sigmoid(low_dot(normed_two_low, expert_router))
    hot = jnp.any(
        expert_pick[0][:, :, None] == jnp.arange(total_experts, dtype=jnp.int32), axis=1
    ).astype(jnp.float32)
    picked_hot = hot * live_mask
    expert_gate = router_sig * picked_hot
    middle_low = middle.astype(jnp.bfloat16)
    sent = jnp.concatenate([middle_low, expert_gate.astype(jnp.bfloat16)], axis=1)
    groups = lax.axis_size("expert")
    rounds = max(1, groups // 8)

    def visit(grads, item):
        returned, grad_up, grad_down = expert_visit(*item, expert_up, expert_down)
        return (grads[0] + grad_up, grads[1] + grad_down), returned

    zeros = jnp.zeros(expert_up.shape, jnp.float32), jnp.zeros(expert_down.shape, jnp.float32)
    (up_grad, down_grad), returned = lax.scan(
        visit,
        zeros,
        (
            sent.reshape(rounds, -1, sent.shape[1]),
            cotangent[0].reshape(rounds, -1, D),
        ),
    )
    returned = returned.reshape(row_count, -1).astype(jnp.float32)
    up_grad = lax.psum_scatter(
        up_grad.astype(jnp.bfloat16), "dp", scatter_dimension=1, tiled=True
    ).astype(jnp.float32)
    down_grad = lax.psum_scatter(
        down_grad.astype(jnp.bfloat16), "dp", scatter_dimension=2, tiled=True
    ).astype(jnp.float32)
    feedforward_out = returned[:, :D]
    final_rows = middle + feedforward_out
    sums = jnp.stack(
        [
            jnp.sum(live_mask * input_full * input_full),
            jnp.sum(attention_out * attention_out),
            jnp.sum(feedforward_out * feedforward_out),
            jnp.sum(live_mask * final_rows * final_rows),
            jnp.sum(live_mask),
        ]
    )
    grad_final = cotangent[0].astype(jnp.float32)
    grad_middle = grad_final + returned[:, D : 2 * D]
    grad_logit = (
        returned[:, 2 * D :] * picked_hot * router_sig * (1.0 - router_sig)
    ).astype(jnp.bfloat16)
    grad_expert_router = low_dot(normed_two_low.T, grad_logit)
    grad_normed_two = low_dot(grad_logit, expert_router.T)
    unused_two, norm_two_back = jax.vjp(layer_norm, middle, gain_two)
    grad_middle_norm, grad_gain_two = norm_two_back(grad_normed_two)
    grad_middle = grad_middle + grad_middle_norm
    grad_branch = (live_mask * grad_middle).astype(jnp.bfloat16)
    grad_mixed = jnp.einsum(
        "td,md->tm", grad_branch, output_weight, preferred_element_type=jnp.float32
    ).reshape(row_count, HEADS, VE, HEAD_DIM)
    grad_output_weight = jnp.einsum(
        "td,tm->dm", grad_branch, mixed, preferred_element_type=jnp.float32
    )
    grad_attended = jnp.sum(output_gate[..., None] * grad_mixed, axis=2)
    grad_output_logit = (
        jnp.sum(attended[:, :, None, :] * grad_mixed, axis=3)
        * output_hot
        * output_sig
        * (1.0 - output_sig)
    ).reshape(row_count, HEADS * VE)
    grad_attended_low = grad_attended.astype(jnp.bfloat16)
    grad_probs = jnp.einsum(
        "qhd,khd->hqk", grad_attended_low, value_heads, preferred_element_type=jnp.float32
    )
    row_dot = jnp.sum(soft_probs * grad_probs, axis=-1, keepdims=True)
    grad_scores = (soft_probs * (grad_probs - row_dot) * HEAD_DIM ** (-0.5)).astype(jnp.bfloat16)
    grad_query = (
        jnp.einsum("hqk,khd->qhd", grad_scores, key_heads, preferred_element_type=jnp.float32)
        .astype(jnp.bfloat16)
        .reshape(row_count, HEADS * HEAD_DIM)
    )
    grad_key_all = jnp.einsum(
        "hqk,qhd->khd", grad_scores, query_heads, preferred_element_type=jnp.float32
    ).reshape(-1, HEADS * HEAD_DIM)
    grad_value_rows = jnp.einsum(
        "hqk,qhd->khd",
        soft_probs.astype(jnp.bfloat16),
        grad_attended_low,
        preferred_element_type=jnp.float32,
    ).reshape(-1, HEADS * HEAD_DIM)
    grad_key_sum, grad_value_sum = (
        lax.psum_scatter(
            grad_key_all.astype(jnp.bfloat16), "dp", scatter_dimension=0, tiled=True
        ).astype(jnp.float32),
        lax.psum_scatter(
            grad_value_rows.astype(jnp.bfloat16), "dp", scatter_dimension=0, tiled=True
        ).astype(jnp.float32),
    )
    grad_key = grad_key_sum.astype(jnp.bfloat16)
    grad_value_low = (
        grad_value_sum.astype(jnp.bfloat16)
        .astype(jnp.float32)
        .reshape(row_count, HEADS, 1, HEAD_DIM)
    )
    grad_value_each = (
        (value_gate[..., None] * grad_value_low)
        .astype(jnp.bfloat16)
        .reshape(row_count, HEADS * VE * HEAD_DIM)
    )
    grad_value_logit = (
        jnp.sum(value_all * grad_value_low, axis=3) * value_hot * value_sig * (1.0 - value_sig)
    ).reshape(row_count, HEADS * VE)
    grad_value_weight = jnp.einsum(
        "td,tm->dm", input_low, grad_value_each, preferred_element_type=jnp.float32
    )
    grad_query_weight = jnp.einsum(
        "td,tm->dm", normed_low, grad_query, preferred_element_type=jnp.float32
    )
    grad_key_weight = jnp.einsum(
        "td,tm->dm", normed_low, grad_key, preferred_element_type=jnp.float32
    )
    grad_value_logit = grad_value_logit.astype(jnp.bfloat16)
    grad_output_logit = grad_output_logit.astype(jnp.bfloat16)
    grad_value_router = low_dot(normed_low.T, grad_value_logit)
    grad_output_router = low_dot(normed_low.T, grad_output_logit)
    grad_normed_one = (
        jnp.einsum("tm,dm->td", grad_query, query_weight, preferred_element_type=jnp.float32)
        + jnp.einsum("tm,dm->td", grad_key, key_weight, preferred_element_type=jnp.float32)
        + low_dot(grad_value_logit, value_router.T)
        + low_dot(grad_output_logit, output_router.T)
    )
    unused_one, norm_one_back = jax.vjp(layer_norm, input_full, gain_one)
    grad_input_norm, grad_gain_one = norm_one_back(grad_normed_one)
    grad_input = (
        grad_middle
        + jnp.einsum("tm,dm->td", grad_value_each, value_weight, preferred_element_type=jnp.float32)
        + grad_input_norm
    )
    small_grads = jnp.concatenate(
        [
            grad_value_router,
            grad_output_router,
            grad_expert_router,
            grad_gain_one[:, None],
            grad_gain_two[:, None],
        ],
        axis=1,
    )
    small_count = small_grads.shape[1]
    small_grads = jnp.pad(small_grads, ((0, 0), (0, -small_count % 128)))
    low_grads = [
        part.astype(jnp.bfloat16)
        for part in (
            grad_query_weight,
            grad_key_weight,
            grad_value_weight,
            grad_output_weight,
            small_grads,
        )
    ]
    summed = lax.psum_scatter(
        jnp.concatenate(low_grads, axis=1), ("dp", "expert"), scatter_dimension=0, tiled=True
    ).astype(jnp.float32)
    dense_grads = jnp.split(summed, [512, 1024, 3584, 6144], axis=1)
    total_sums = lax.psum(sums, ("dp", "expert"))
    residual_norms = jnp.sqrt(total_sums[:4] / (total_sums[4] * D))
    small = dense_grads[4]
    router_end = 2 * HEADS * VE + expert_router.shape[1]
    dense_grads = [
        dense_grads[0],
        dense_grads[1],
        dense_grads[2],
        dense_grads[3].T,
        small[:, : HEADS * VE],
        small[:, HEADS * VE : 2 * HEADS * VE],
        small[:, 2 * HEADS * VE : router_end],
        small[:, router_end],
        small[:, router_end + 1],
    ]
    return (
        final_rows.astype(jnp.bfloat16)[None],
        grad_input[None],
        dense_grads[0],
        dense_grads[1],
        dense_grads[2],
        dense_grads[3],
        dense_grads[4],
        dense_grads[5],
        dense_grads[6],
        dense_grads[7],
        dense_grads[8],
        up_grad,
        down_grad,
        residual_norms,
    )


def deliver_kernel(total, sums, small, *refs):
    count = (len(refs) - 7) // 3
    sources, targets = refs[:count], refs[count : 2 * count]
    value_out, output_out, expert_out, gains_out, norms_out = refs[2 * count : 2 * count + 5]
    held = refs[2 * count + 5 : -2]
    inward, outward = refs[-2:]
    arrived = [pltpu.make_async_copy(a, b, inward.at[i]) for i, (a, b) in enumerate(zip(sources, held))]
    left = [pltpu.make_async_copy(a, b, outward.at[i]) for i, (a, b) in enumerate(zip(held, targets))]
    for made in arrived:
        made.start()
    spread = HEADS * VE
    turned = jnp.concatenate([small[...], jnp.zeros((128 - ROWS, 128), jnp.float32)]).T
    value_out[...] = turned[:spread, :ROWS]
    output_out[...] = turned[spread : 2 * spread, :ROWS]
    expert_out[...] = small[:, 2 * spread : 2 * spread + total]
    gains_out[...] = turned[2 * spread + total : 2 * spread + total + 2, :ROWS]
    row = sums[0:1, :]
    norms_out[...] = jnp.sqrt(row[:, :4] / (row[:, 4:5] * D))
    for one, other in zip(arrived, left):
        one.wait()
        other.start()
    for made in left:
        made.wait()


def deliver(total, sums, small, *arrays):
    full = jnp.float32
    vmem = pl.BlockSpec(memory_space=pltpu.VMEM)
    anywhere = pl.BlockSpec(memory_space=pl.ANY)
    spread = HEADS * VE
    return pl.pallas_call(
        functools.partial(deliver_kernel, total),
        out_shape=[jax.ShapeDtypeStruct(a.shape, a.dtype) for a in arrays]
        + [
            jax.ShapeDtypeStruct((spread, ROWS), full),
            jax.ShapeDtypeStruct((spread, ROWS), full),
            jax.ShapeDtypeStruct((ROWS, total), full),
            jax.ShapeDtypeStruct((2, ROWS), full),
            jax.ShapeDtypeStruct((1, 4), full),
        ],
        in_specs=[vmem] * 2 + [anywhere] * len(arrays),
        out_specs=[anywhere] * len(arrays) + [vmem] * 5,
        scratch_shapes=[pltpu.VMEM(a.shape, a.dtype) for a in arrays]
        + [pltpu.SemaphoreType.DMA((len(arrays),))] * 2,
        compiler_params=pltpu.CompilerParams(vmem_limit_bytes=63 * 2**20),
        name="deliver",
    )(sums, small, *arrays)


def shards_fast(
    hidden_in,
    lengths,
    value_pick,
    output_pick,
    expert_pick,
    query_weight,
    key_weight,
    value_weight,
    output_weight,
    value_router,
    output_router,
    expert_router,
    attention_gain,
    feedforward_gain,
    expert_up,
    expert_down,
    cotangent,
):
    total = expert_router.shape[1]
    spread = HEADS * VE
    routers = jnp.concatenate(
        [value_router.T, output_router.T, expert_router.T, jnp.zeros((128 - 2 * spread - total, D), jnp.bfloat16)]
    )
    gains = jnp.stack([attention_gain, feedforward_gain]).astype(jnp.float32)
    (
        middle,
        sent,
        normed_one,
        normed_two,
        queries,
        key_value,
        probs,
        value_all,
        attended,
        gates,
        slopes,
        cot_line,
    ) = attend(
        total,
        lengths,
        hidden_in[0],
        cotangent[0],
        value_pick[0].transpose(1, 2, 0),
        output_pick[0].transpose(1, 2, 0),
        expert_pick[0].T,
        routers,
        gains,
        key_weight,
        value_weight,
        query_weight,
        output_weight,
    )
    returned, up_grad, down_grad, forward = expert_kernel_visit(sent, cot_line, expert_up, expert_down)
    block_out, grad_input, grad_query, grad_key, grad_value, grad_output, small, sums = backward(
        total,
        lengths,
        gates,
        slopes,
        routers,
        gains,
        forward,
        returned,
        middle,
        cotangent[0],
        hidden_in[0],
        normed_one,
        queries,
        key_value,
        probs,
        value_all,
        attended,
        normed_two,
        query_weight,
        key_weight,
        value_weight,
        output_weight,
    )
    kept = (block_out, grad_input, grad_query, grad_key, grad_value, grad_output, up_grad, down_grad)
    delivered = deliver(total, sums, small, *kept)
    block_out, grad_input, grad_query, grad_key, grad_value, grad_output, up_grad, down_grad = delivered[:8]
    value_small, output_small, expert_small, gain_grads, norms = delivered[8:]
    return (
        block_out[None],
        grad_input[None],
        grad_query,
        grad_key,
        grad_value,
        grad_output.T,
        value_small.T,
        output_small.T,
        expert_small,
        gain_grads[0],
        gain_grads[1],
        up_grad,
        down_grad,
        norms[0],
    )


def solution(mesh):
    placed = (
        P("expert", "dp", None),
        P("expert"),
        P("expert", "dp", None, None),
        P("expert", "dp", None, None),
        P("expert", "dp", None),
        P(),
        P(),
        P(),
        P(),
        P(),
        P(),
        P(),
        P(),
        P(),
        P("expert", None, None),
        P("expert", None, None),
        P("expert", "dp", None),
    )
    small_mesh = mesh.shape["dp"] == 4 and mesh.shape["expert"] == 8
    return jax.shard_map(
        shards_fast if small_mesh else shards,
        mesh=mesh,
        in_specs=placed,
        out_specs=(
            P("expert", "dp", None),
            P("expert", "dp", None),
            P(("dp", "expert"), None),
            P(("dp", "expert"), None),
            P(("dp", "expert"), None),
            P(None, ("dp", "expert")),
            P(("dp", "expert"), None),
            P(("dp", "expert"), None),
            P(("dp", "expert"), None),
            P(("dp", "expert")),
            P(("dp", "expert")),
            P("expert", "dp", None),
            P("expert", None, "dp"),
            P(),
        ),
        check_vma=False,
    )
```

```python
import functools

import jax
import jax.numpy as jnp
from jax import lax
from jax.experimental import pallas as pl
from jax.experimental.pallas import tpu as pltpu
from jax.sharding import PartitionSpec as P

D = 1024
HEADS = 4
HEAD_DIM = 128
VE = 5


MESH = pl.DeviceIdType.MESH
ROWS = 32
PIECE = VE * HEAD_DIM
EPSILON = 1e-05
NEGATIVE = -1000000000.0


def low_dot(left_side, right_side):
    return jnp.dot(left_side, right_side, preferred_element_type=jnp.float32)


def layer_norm(field, scale_gain):
    center = field - jnp.mean(field, axis=-1, keepdims=True)
    spread = jnp.mean(center * center, axis=-1, keepdims=True)
    return center * lax.rsqrt(spread + EPSILON) * scale_gain


def choose(select, count):
    return jnp.sum(
        (select[..., None] == jnp.arange(count, dtype=jnp.int32)).astype(jnp.float32), axis=-2
    )


def attention_probs(query_heads, key_heads, query_pos, length):
    key_pos = jnp.arange(key_heads.shape[0], dtype=jnp.int32)
    raw_scores = jnp.einsum(
        "qhd,khd->hqk", query_heads, key_heads, preferred_element_type=jnp.float32
    )
    allowed = (key_pos[None, :] <= query_pos[:, None]) & (key_pos[None, :] < length)
    scores = jnp.where(allowed[None], raw_scores * HEAD_DIM ** (-0.5), NEGATIVE)
    exp_terms = jnp.exp(scores - jnp.max(scores, axis=-1, keepdims=True))
    return exp_terms / jnp.sum(exp_terms, axis=-1, keepdims=True)


def dot_last(left_side, right_side):
    return lax.dot_general(
        left_side, right_side, (((1,), (1,)), ((), ())), preferred_element_type=jnp.float32
    )

def dot_first(left_side, right_side):
    return lax.dot_general(
        left_side, right_side, (((0,), (0,)), ((), ())), preferred_element_type=jnp.float32
    )


def visit_kernel(
    sent, cot_at, up_at, down_at, back_out, weights_out, weights_kept, forward_out,
    cot, up, down, rows, cot_other, up_wide, chosen, cots, gated, grad_pre, forward, forward_in, gated_turned, pre_turned, partial, paired_in, chain_in, up_low, down_low, up_in, down_in,
    fetch, row_send, row_recv, half_send, half_recv, cot_send, cot_recv, pair_send, pair_recv, forward_send, forward_recv, chain_send, chain_recv, grad_send, grad_recv,
):
    experts = up.shape[0]
    wide = down.shape[0]
    hidden = wide // experts
    dp, ex = lax.axis_index("dp"), lax.axis_index("expert")
    y, x, z, core = dp // 2, dp % 2, ex // 2, ex % 2
    half = z // 2
    inner = z + half * (3 - 2 * z)
    onward = 1 - 2 * half
    sibling = (dp, z * 2 + 1 - core)
    beside, behind = (y * 2 + 1 - x, ex), ((1 - y) * 2 + x, ex)

    def at_z(place):
        return (dp, place * 2 + core)

    fetched = [
        pltpu.make_async_copy(source, target, fetch.at[i])
        for i, (source, target) in enumerate(((cot_at, cot), (up_at, up), (down_at, down)))
    ]
    for made in fetched:
        made.start()
    barrier = pltpu.get_barrier_semaphore()
    for place in (sibling, beside, behind):
        pl.semaphore_signal(barrier, inc=1, device_id=place, device_id_type=MESH)

    @pl.when(z < 3)
    def _():
        pl.semaphore_signal(barrier, inc=1, device_id=at_z(z + 1), device_id_type=MESH)

    @pl.when(z > 0)
    def _():
        pl.semaphore_signal(barrier, inc=1, device_id=at_z(z - 1), device_id_type=MESH)

    pl.semaphore_wait(barrier, 4 + inner)

    def remote(source, target, send, recv, place):
        return pltpu.make_async_remote_copy(
            src_ref=source, dst_ref=target, send_sem=send, recv_sem=recv, device_id=place, device_id_type=MESH
        )

    def row_copy(at, source=None):
        block = rows.at[at] if source is None else source
        return remote(block, rows.at[4 + at], row_send.at[at], row_recv.at[at], sibling)

    def half_copy(way, at, part, source=None):
        span = pl.ds(part * (rows.shape[1] // 2), rows.shape[1] // 2)
        block = rows.at[at] if source is None else source
        return remote(
            block.at[span], rows.at[at, span], half_send.at[way, at, part], half_recv.at[at, part], at_z(z + 1 - 2 * way)
        )

    def cot_copy(at):
        return remote(cot.at[at], cot_other.at[at], cot_send.at[at], cot_recv.at[at], sibling)

    @pl.when(z < 3)
    def _():
        for part in range(2):
            half_copy(0, z, part, sent).start()

    @pl.when(z > 0)
    def _():
        for part in range(2):
            half_copy(1, z, part, sent).start()

    row_copy(z, sent).start()
    for made in fetched:
        made.wait()
    cot_copy(z).start()
    for k in (1, 2, 3):
        cot_copy((z + k) % 4).start()
    rows[z] = sent[...]
    for e in range(experts):
        up_wide[:, e * hidden : (e + 1) * hidden] = up[e]
    chosen[...] = (
        lax.broadcasted_iota(jnp.int32, (128, wide), 0)
        == 2 * HEADS * VE + ex * experts + lax.broadcasted_iota(jnp.int32, (128, wide), 1) // hidden
    ).astype(jnp.float32).astype(jnp.bfloat16)

    def order(p):
        later = (p + 2) // 3
        step = p - inner // (p + 1 - later)
        return later * (step + half * (3 - 2 * step)) + (1 - later) * z

    def pair_copy(at):
        return remote(partial.at[1, at], paired_in.at[at], pair_send.at[at], pair_recv.at[at], sibling)

    parts = 4
    size = rows.shape[1] // parts
    spans = [pl.ds(i * size, size) for i in range(parts)]

    def chain_copy(dest, slot, to, stage, part):
        span = spans[part]
        return remote(
            partial.at[0, dest, span], chain_in.at[slot, span],
            chain_send.at[stage, part], chain_recv.at[slot, part], at_z(to),
        )

    def add(target, source):
        def some(i, carry):
            part = pl.ds(pl.multiple_of(i * 32, 32), 32)
            target[part, :] = (
                target[part, :].astype(jnp.float32) + source[part, :].astype(jnp.float32)
            ).astype(target.dtype)
            return carry

        lax.fori_loop(0, target.shape[0] // 32, some, 0)

    def forward_copy(at):
        return remote(forward.at[at], forward_in.at[at], forward_send.at[at], forward_recv.at[at], sibling)

    def forward_block(block):
        at = block % 4
        def some(n, inside):
            span = pl.ds(pl.multiple_of(n * 256, 256), 256)
            value = jnp.dot(gated[block], down[:, span], preferred_element_type=jnp.float32).astype(jnp.bfloat16)

            @pl.when(block >= 4)
            def _():
                forward[at, :, span] = value

            @pl.when(block < 4)
            def _():
                forward_out[at, :, span] = value

            return inside

        lax.fori_loop(0, D // 256, some, 0)

        @pl.when(block >= 4)
        def _():
            forward_copy(at).start()

    def relay(dest, slot, to, stage, part):
        chain_copy(dest, dest, to, stage, part).wait_recv()
        add(partial.at[0, dest, spans[part]], chain_in.at[dest, spans[part]])
        chain_copy(dest, slot, to, stage, part).start()

    def visit(q, carry):
        p, other = q // 2, q % 2
        at = order(p)
        block = other * 4 + at

        @pl.when((other == 0) & (p > 0))
        def _():
            for part in range(2):
                half_copy(0, at, part).wait_recv()

                @pl.when((at < z) & (z < 3))
                def _():
                    half_copy(0, at, part).start()

                @pl.when((at > z) & (z > 0))
                def _():
                    half_copy(1, at, part).start()

            row_copy(at).start()

        @pl.when(other == 1)
        def _():
            row_copy(at).wait_recv()
            cot_copy(at).wait_recv()
            cots[...] = cot_other[at]

        @pl.when(other == 0)
        def _():
            cots[...] = cot[at]

        @pl.when((inner == 1) & (q == 7))
        def _():
            relay(*next_one, 0)
            relay(*next_one, 1)

        count = rows.shape[1]
        places = pl.ds(pl.multiple_of(block * count, count), count)

        def columns(n, gate_grad):
            span = pl.ds(pl.multiple_of(n * 256, 256), 256)
            pre = jnp.dot(rows[block, :, :D], up_wide[:, span], preferred_element_type=jnp.float32)
            back = dot_last(cots[...], down[span, :])
            mark = chosen[:, span]
            gate = jnp.dot(rows[block, :, D:], mark, preferred_element_type=jnp.float32)
            sig = jax.nn.sigmoid(pre)
            act = pre * sig
            act_low = (gate * act).astype(jnp.bfloat16)
            pre_low = (gate * back * (sig * (1.0 + pre * (1.0 - sig)))).astype(jnp.bfloat16)
            gated[block, :, span] = act_low
            grad_pre[:, span] = pre_low
            gated_turned[span, places] = act_low.T
            pre_turned[span, places] = pre_low.T
            return gate_grad + dot_last((act * back).astype(jnp.bfloat16), mark)

        partial[other, at, :, D:] = lax.fori_loop(
            0, wide // 256, columns, jnp.zeros((count, 128), jnp.float32)
        ).astype(jnp.bfloat16)

        def outward(n, carry):
            span = pl.ds(pl.multiple_of(n * 256, 256), 256)
            partial[other, at, :, span] = dot_last(grad_pre[...], up_wide[span, :]).astype(jnp.bfloat16)
            return carry

        lax.fori_loop(0, D // 256, outward, 0)

        @pl.when(other == 1)
        def _():
            pair_copy(at).start()
            pair_copy(at).wait_recv()
            add(partial.at[0, at], paired_in.at[at])

        @pl.when((inner == 0) & (q == 3))
        def _():
            for part in range(parts):
                chain_copy(*nearest, part).start()

        @pl.when((inner == 0) & (q == 5))
        def _():
            for part in range(parts):
                chain_copy(*next_one, part).start()

        @pl.when(q < 6)
        def _():
            forward_block(block)

        return carry

    nearest = (z + onward, z + onward, z + onward, 0)
    farthest = (3 * (1 - half), 3 * (1 - half), z + onward, 1)
    backward = (3 * half, 3 * half, z - onward, 2)
    next_one = (2 - half, 2 - half + inner * (2 + half), z + onward, 3)
    lax.fori_loop(0, 8, visit, 0)

    @pl.when(inner == 0)
    def _():
        for part in range(parts):
            chain_copy(*farthest, part).start()
    tokens_all = rows.reshape(rows.shape[0] * rows.shape[1], rows.shape[2])
    cots_own = cot.reshape(cot.shape[0] * cot.shape[1], D)
    cots_other = cot_other.reshape(cot.shape[0] * cot.shape[1], D)
    place = cots_own.shape[0]
    quarter = D // 4


    def up_copy(j):
        return remote(up_low.at[j], up_in.at[j], grad_send.at[0, j], grad_recv.at[0, j], behind if j == 2 else beside)

    def down_copy(j):
        return remote(down_low.at[j], down_in.at[j], grad_send.at[1, j], grad_recv.at[1, j], beside if j == 1 else behind)

    def span_of(j):
        at = (y + (1 - j % 2) * (1 - 2 * y)) * 2 + x + (1 - j // 2) * (1 - 2 * x)
        return pl.ds(pl.multiple_of(at * quarter, quarter), quarter)

    def up_quarter(j):
        up_low[j] = jnp.dot(
            pre_turned[...], tokens_all[:, span_of(j)], preferred_element_type=jnp.float32
        ).astype(jnp.bfloat16)
        if j < 2:
            up_copy(j).start()

    def down_quarter(j):
        down_low[j] = (
            jnp.dot(gated_turned[:, :place], cots_own[:, span_of(j)], preferred_element_type=jnp.float32)
            + jnp.dot(gated_turned[:, place:], cots_other[:, span_of(j)], preferred_element_type=jnp.float32)
        ).astype(jnp.bfloat16)
        if j in (0, 2):
            down_copy(j).start()

    def relays(*ways):
        @pl.when(inner == 1)
        def _():
            for way, part in ways:
                relay(*way, part)

    def forward_add(p):
        at = order(p)
        forward_copy(at).wait()
        add(forward_out.at[at], forward_in.at[at])

    relays((next_one, 2), (next_one, 3))
    up_quarter(0)
    down_quarter(0)
    relays((farthest, 0))
    up_quarter(1)
    relays((farthest, 1))
    down_quarter(2)
    relays((backward, 0), (farthest, 2))
    forward_block(4 + order(3))
    relays((backward, 1), (farthest, 3))
    up_quarter(2)
    relays((backward, 2))
    forward_add(0)
    forward_add(1)
    down_quarter(1)
    relays((backward, 3))
    forward_block(order(3))
    up_quarter(3)
    down_quarter(3)
    forward_add(2)
    forward_add(3)
    for part in range(parts):
        span = spans[part]
        chain_copy(z, z, z, 0, part).wait_recv()
        back_out[span, :] = partial[0, z, span, :].astype(jnp.float32) + chain_in[z, span, :].astype(jnp.float32)

        @pl.when(inner == 1)
        def _():
            chain_copy(z, 4, z, 0, part).wait_recv()
            back_out[span, :] = back_out[span, :] + chain_in[4, span, :].astype(jnp.float32)

    ends = (
        (up_copy(0), up_low, 2, up_in, 0, weights_out.at[0]),
        (up_copy(1), up_low, 3, up_in, 1, weights_kept.at[0]),
        (down_copy(0), down_low, 1, down_in, 0, weights_out.at[1]),
        (down_copy(2), down_low, 3, down_in, 2, weights_kept.at[1]),
    )
    for made, mine, j, other, slot, target in ends:
        made.wait()
        target[...] = mine[j]
        add(target, other.at[slot])

    for at in range(4):
        row_copy(at).wait_send()
        cot_copy(at).wait_send()
        pair_copy(at).wait_send()
        for part in range(2):

            @pl.when((at <= z) & (z < 3))
            def _():
                half_copy(0, at, part).wait_send()

            @pl.when((at >= z) & (z > 0))
            def _():
                half_copy(1, at, part).wait_send()

    for part in range(parts):

        @pl.when(inner == 0)
        def _():
            chain_copy(z, 0, z, 0, part).wait_send()

        @pl.when(inner == 1)
        def _():
            chain_copy(z, 0, z, 2, part).wait_send()

        chain_copy(z, 0, z, 1, part).wait_send()
        chain_copy(z, 0, z, 3, part).wait_send()

def expert_kernel_visit(sent, cot_line, up, down):
    tokens = sent.shape[0]
    experts, _, hidden = up.shape
    wide = experts * hidden
    low = jnp.bfloat16
    vmem = pl.BlockSpec(memory_space=pltpu.VMEM)
    dma = pltpu.SemaphoreType.DMA
    f32 = jnp.float32
    return pl.pallas_call(
        visit_kernel,
        out_shape=[
            jax.ShapeDtypeStruct((tokens, D + 128), f32),
            jax.ShapeDtypeStruct((2, wide, D // 4), low),
            jax.ShapeDtypeStruct((2, wide, D // 4), low),
            jax.ShapeDtypeStruct((4, tokens, D), low),
        ],
        in_specs=[vmem] + [pl.BlockSpec(memory_space=pl.ANY)] * 3,
        out_specs=[vmem] * 4,
        scratch_shapes=[
            pltpu.VMEM((4, tokens, D), low),
            pltpu.VMEM((experts, D, hidden), low),
            pltpu.VMEM((wide, D), low),
            pltpu.VMEM((8, tokens, D + 128), low),
            pltpu.VMEM((4, tokens, D), low),
            pltpu.VMEM((D, wide), low),
            pltpu.VMEM((128, wide), low),
            pltpu.VMEM((tokens, D), low),
            pltpu.VMEM((8, tokens, wide), low),
            pltpu.VMEM((tokens, wide), low),
            pltpu.VMEM((4, tokens, D), low),
            pltpu.VMEM((4, tokens, D), low),
            pltpu.VMEM((wide, 8 * tokens), low),
            pltpu.VMEM((wide, 8 * tokens), low),
            pltpu.VMEM((2, 4, tokens, D + 128), low),
            pltpu.VMEM((4, tokens, D + 128), low),
            pltpu.VMEM((5, tokens, D + 128), low),
            pltpu.VMEM((4, wide, D // 4), low),
            pltpu.VMEM((4, wide, D // 4), low),
            pltpu.VMEM((3, wide, D // 4), low),
            pltpu.VMEM((3, wide, D // 4), low),
            dma((3,)), dma((4,)), dma((4,)), dma((2, 4, 2)), dma((4, 2)), dma((4,)), dma((4,)), dma((4,)), dma((4,)), dma((4,)), dma((4,)), dma((4, 4)), dma((5, 4)), dma((2, 3)), dma((2, 3)),
        ],
        compiler_params=pltpu.CompilerParams(collective_id=2, has_side_effects=True, vmem_limit_bytes=58 * 2**20),
        name="expert_visit",
    )(sent, cot_line, up, down.reshape(wide, D))


def attend_kernel(
    expert_total, lengths, hidden, cot, value_pick, output_pick, expert_pick, routers, gains,
    key_weight_at, value_weight_at, query_weight_at, output_weight_at,
    middle_at, sent_at, normed_one_at, normed_two_at, queries_at, key_value_at, probs_at, value_all_at, attended_at,
    gates_at, slopes_at, cot_line_at,
    middle, sent, normed_one, normed_two, queries, key_value, probs, value_all, attended,
    gates, slopes, cot_line,
    key_weight, value_weight, query_weight, output_weight, mixed, hot_turned, hot,
    fetch, leave, pair_send, pair_recv, cot_send, cot_recv, own_sem,
):
    dp, ex = lax.axis_index("dp"), lax.axis_index("expert")
    z, core = ex // 2, ex % 2
    half = z // 2
    inner = z + half * (3 - 2 * z)
    count = hidden.shape[0]
    width = HEADS * HEAD_DIM
    low = jnp.bfloat16
    length = lengths[0]
    spread = HEADS * VE
    total = expert_total
    weights = [
        pltpu.make_async_copy(source, target, fetch.at[i])
        for i, (source, target) in enumerate(
            (
                (key_weight_at, key_weight),
                (value_weight_at, value_weight),
                (query_weight_at, query_weight),
                (output_weight_at, output_weight),
            )
        )
    ]
    for made in weights:
        made.start()
    results = (
        (middle, middle_at), (sent, sent_at), (normed_one, normed_one_at), (normed_two, normed_two_at),
        (queries, queries_at), (key_value, key_value_at), (probs, probs_at), (value_all, value_all_at),
        (attended, attended_at), (gates, gates_at), (slopes, slopes_at), (cot_line, cot_line_at),
    )
    leaving = [pltpu.make_async_copy(source, target, leave.at[i]) for i, (source, target) in enumerate(results)]

    def at_z(place):
        return (dp, place * 2 + core)

    barrier = pltpu.get_barrier_semaphore()
    for k in (1, 2, 3):
        pl.semaphore_signal(barrier, inc=1, device_id=((dp + k) % 4, ex), device_id_type=MESH)

    @pl.when(z < 3)
    def _():
        pl.semaphore_signal(barrier, inc=1, device_id=at_z(z + 1), device_id_type=MESH)

    @pl.when(z > 0)
    def _():
        pl.semaphore_signal(barrier, inc=1, device_id=at_z(z - 1), device_id_type=MESH)

    pl.semaphore_wait(barrier, 4 + inner)

    def cot_copy(way, at, source=None):
        block = cot_line.at[at]
        return pltpu.make_async_remote_copy(
            src_ref=block if source is None else source, dst_ref=block,
            send_sem=cot_send.at[way, at], recv_sem=cot_recv.at[at],
            device_id=at_z(z + 1 - 2 * way), device_id_type=MESH,
        )

    def pass_on(distance):
        @pl.when(z >= distance)
        def _():
            cot_copy(0, z - distance).wait_recv()

        @pl.when((z >= distance) & (z < 3))
        def _():
            cot_copy(0, z - distance).start()

        @pl.when(z + distance <= 3)
        def _():
            cot_copy(1, z + distance).wait_recv()

        @pl.when((z + distance <= 3) & (z > 0))
        def _():
            cot_copy(1, z + distance).start()

    @pl.when(z < 3)
    def _():
        cot_copy(0, z, cot).start()

    @pl.when(z > 0)
    def _():
        cot_copy(1, z, cot).start()

    keep = pltpu.make_async_copy(cot, cot_line.at[z], own_sem)
    keep.start()

    def norm(field, gain):
        center = field - jnp.mean(field, axis=-1, keepdims=True)
        spread = jnp.mean(center * center, axis=-1, keepdims=True)
        return (center * lax.rsqrt(spread + EPSILON) * gain).astype(low)

    parts = (pl.ds(0, width), pl.ds(width, width))

    def pair_copy(step, part, block):
        return pltpu.make_async_remote_copy(
            src_ref=key_value.at[block, :, parts[part]], dst_ref=key_value.at[block, :, parts[part]],
            send_sem=pair_send.at[step, part], recv_sem=pair_recv.at[block, part],
            device_id=((dp + step) % 4, ex), device_id_type=MESH,
        )

    def send_part(part):
        for step in (1, 2, 3):

            @pl.when(dp + step < 4)
            def _():
                pair_copy(step, part, dp).start()

    normed_one[...] = norm(hidden[...].astype(jnp.float32), gains[0:1, :])
    leaving[2].start()
    weights[0].wait()
    key_value[dp, :, parts[0]] = jnp.dot(
        normed_one[...], key_weight[...], preferred_element_type=jnp.float32
    ).astype(low)
    send_part(0)

    hot_turned[...] = jnp.zeros(hot_turned.shape, jnp.float32)

    def mark(picks, base, size):
        place = lax.broadcasted_iota(jnp.int32, (size, count), 0)
        found = jnp.zeros((size, count), jnp.float32)
        for pick in picks:
            found = jnp.where(place == pick, 1.0, found)
        hot_turned[base : base + size, :] = found

    mark([value_pick[h, i : i + 1, :] + h * VE for h in range(HEADS) for i in range(value_pick.shape[1])], 0, spread)
    mark(
        [output_pick[h, i : i + 1, :] + h * VE for h in range(HEADS) for i in range(output_pick.shape[1])],
        spread,
        spread,
    )
    mark([expert_pick[i : i + 1, :] for i in range(expert_pick.shape[0])], 2 * spread, total)
    hot[...] = hot_turned[...].T
    sig = jax.nn.sigmoid(dot_last(normed_one[...], routers[...]))
    gates[...] = sig * hot[...]
    slopes[...] = gates[...] * (1.0 - sig)
    weights[1].wait()

    def values(n, carry):
        span = pl.ds(pl.multiple_of(n * 256, 256), 256)
        value_all[:, span] = jnp.dot(
            hidden[...], value_weight[:, span], preferred_element_type=jnp.float32
        ).astype(low)
        return carry

    lax.fori_loop(0, HEADS * VE * HEAD_DIM // 256, values, 0)
    leaving[7].start()
    for h in range(HEADS):
        row = jnp.zeros((count, HEAD_DIM), jnp.float32)
        for e in range(h * VE, (h + 1) * VE):
            row += gates[:, e : e + 1] * value_all[:, e * HEAD_DIM : (e + 1) * HEAD_DIM].astype(jnp.float32)
        key_value[dp, :, width + h * HEAD_DIM : width + (h + 1) * HEAD_DIM] = row.astype(low)
    send_part(1)

    weights[2].wait()
    queries[...] = jnp.dot(normed_one[...], query_weight[...], preferred_element_type=jnp.float32).astype(low)
    leaving[4].start()
    for block in range(4):

        @pl.when(block > dp)
        def _():
            key_value[block] = jnp.zeros((count, 2 * width), low)

    pass_on(1)

    def wait_part(part):
        for block in range(3):

            @pl.when(block < dp)
            def _():
                pair_copy(1, part, block).wait_recv()

    wait_part(0)
    pair_all = key_value.reshape(4 * count, 2 * width)
    query_pos = dp * count + lax.broadcasted_iota(jnp.int32, (count, 4 * count), 0)
    key_pos = lax.broadcasted_iota(jnp.int32, (count, 4 * count), 1)
    allowed = (key_pos <= query_pos) & (key_pos < length)

    def score(h, carry):
        span = pl.ds(pl.multiple_of(h * HEAD_DIM, HEAD_DIM), HEAD_DIM)
        raw = dot_last(queries[:, span], pair_all[:, span])
        scores = jnp.where(allowed, raw * HEAD_DIM ** (-0.5), NEGATIVE)
        terms = jnp.exp(scores - jnp.max(scores, axis=-1, keepdims=True))
        probs[h] = (terms * (1.0 / jnp.sum(terms, axis=-1, keepdims=True))).astype(low)
        return carry

    lax.fori_loop(0, HEADS, score, 0)
    leaving[6].start()
    leaving[9].start()
    wait_part(1)
    leaving[5].start()
    pass_on(2)

    def collect(h, carry):
        span = pl.ds(pl.multiple_of(h * HEAD_DIM, HEAD_DIM), HEAD_DIM)
        value_span = pl.ds(pl.multiple_of(width + h * HEAD_DIM, HEAD_DIM), HEAD_DIM)
        attended[:, span] = jnp.dot(probs[h], pair_all[:, value_span], preferred_element_type=jnp.float32)
        return carry

    lax.fori_loop(0, HEADS, collect, 0)
    leaving[8].start()
    for h in range(HEADS):
        row = attended[:, h * HEAD_DIM : (h + 1) * HEAD_DIM]
        for e in range(h * VE, (h + 1) * VE):
            mixed[:, e * HEAD_DIM : (e + 1) * HEAD_DIM] = (gates[:, spread + e : spread + e + 1] * row).astype(low)

    place = dp * count + lax.broadcasted_iota(jnp.int32, (count, 1), 0)
    live = jnp.where(place < length, 1.0, 0.0)
    weights[3].wait()

    def outward(n, carry):
        span = pl.ds(pl.multiple_of(n * 256, 256), 256)
        branch = jnp.dot(mixed[...], output_weight[:, span], preferred_element_type=jnp.float32)
        middle[:, span] = hidden[:, span].astype(jnp.float32) + live * branch
        return carry

    lax.fori_loop(0, D // 256, outward, 0)
    leaving[0].start()
    sent[:, :D] = middle[...].astype(low)
    normed_two[...] = norm(middle[...], gains[1:2, :])
    sig = jax.nn.sigmoid(dot_last(normed_two[...], routers[...]))
    gate = sig * hot[...] * live
    sent[:, D:] = gate.astype(low)
    lane = lax.broadcasted_iota(jnp.int32, (count, 128), 1)
    slopes[...] = jnp.where(lane < 2 * spread, slopes[...], gate * (1.0 - sig))

    for i in (1, 3, 10):
        leaving[i].start()
    pass_on(3)
    keep.wait()
    leaving[11].start()
    for part in range(2):
        for step in (1, 2, 3):

            @pl.when(dp + step < 4)
            def _():
                pair_copy(step, part, dp).wait_send()

    for at in range(4):

        @pl.when((at <= z) & (z < 3))
        def _():
            cot_copy(0, at).wait_send()

        @pl.when((at >= z) & (z > 0))
        def _():
            cot_copy(1, at).wait_send()

    for made in leaving:
        made.wait()


def attend(total, lengths, *operands):
    count = operands[0].shape[0]
    low, full = jnp.bfloat16, jnp.float32
    vmem = pl.BlockSpec(memory_space=pltpu.VMEM)
    anywhere = pl.BlockSpec(memory_space=pl.ANY)
    dma = pltpu.SemaphoreType.DMA
    width, wide = HEADS * HEAD_DIM, HEADS * VE * HEAD_DIM
    shapes = [
        ((count, D), full),
        ((count, D + 128), low),
        ((count, D), low),
        ((count, D), low),
        ((count, width), low),
        ((4, count, 2 * width), low),
        ((HEADS, count, 4 * count), low),
        ((count, wide), low),
        ((count, width), full),
        ((count, 128), full),
        ((count, 128), full),
        ((4, count, D), low),
    ]
    return pl.pallas_call(
        functools.partial(attend_kernel, total),
        out_shape=[jax.ShapeDtypeStruct(*shape) for shape in shapes],
        in_specs=[pl.BlockSpec(memory_space=pltpu.SMEM)] + [vmem] * (len(operands) - 4) + [anywhere] * 4,
        out_specs=[anywhere] * len(shapes),
        scratch_shapes=[pltpu.VMEM(*shape) for shape in shapes]
        + [pltpu.VMEM(a.shape, a.dtype) for a in operands[-4:]]
        + [
            pltpu.VMEM((count, wide), low),
            pltpu.VMEM((128, count), full),
            pltpu.VMEM((count, 128), full),
            dma((4,)),
            dma((len(shapes),)),
            dma((4, 2)),
            dma((4, 2)),
            dma((2, 4)),
            dma((4,)),
            dma,
        ],
        compiler_params=pltpu.CompilerParams(
            collective_id=1, has_side_effects=True, vmem_limit_bytes=58 * 2**20
        ),
        name="attend",
    )(lengths, *operands)


def backward_kernel(
    total_experts, lengths, gates, slopes, routers, gains,
    weights_at, forward_at, returned_at, middle_at, cot_at, hidden_at, normed_one_at, queries_at, key_value_at, probs_at, value_all_at,
    attended_at, normed_two_at, query_weight_at, key_weight_at, value_weight_at, output_weight_at,
    block_out, grad_in, out_query, out_key, out_value, out_output, out_small, weights_in,
    weights, forward, returned, middle, cot, hidden, normed_one, queries, key_value, probs, value_all,
    attended, normed_two, query_weight, key_weight, value_part, output_part,
    branch, branch_turned, one_turned, hidden_turned, grad_att, grad_query, leave, arrive, grad_key,
    grad_each, grad_middle, logit_one, logit_two, small_turned, mixed,
    grads, grads_small, core_in, plane_in, last_in, forward_in,
    fetch, part_fetch, leave_send, leave_recv, send, recv, forward_send, forward_recv, weights_send, weights_recv,
):
    dp, ex = lax.axis_index("dp"), lax.axis_index("expert")
    y, x, z, core = dp // 2, dp % 2, ex // 2, ex % 2
    count = hidden.shape[0]
    width = HEADS * HEAD_DIM
    low, full = jnp.bfloat16, jnp.float32
    length = lengths[0]
    sibling = (dp, z * 2 + 1 - core)
    beside = (y * 2 + 1 - x, ex)
    behind = ((1 - y) * 2 + x, ex)
    across = ((1 - y) * 2 + 1 - x, ex)
    line = [(dp, ((z + k) % 4) * 2 + core) for k in (1, 2, 3)]
    barrier = pltpu.get_barrier_semaphore()
    for place in (sibling, beside, behind, across, *line):
        pl.semaphore_signal(barrier, inc=1, device_id=place, device_id_type=MESH)

    held = dict(
        weights=(weights_at, weights),
        forward=(forward_at, forward),
        returned=(returned_at, returned),
        middle=(middle_at, middle),
        cot=(cot_at, cot),
        hidden=(hidden_at, hidden),
        attended=(attended_at, attended),
        key_value=(key_value_at, key_value),
        probs=(probs_at, probs),
        queries=(queries_at, queries),
        normed_one=(normed_one_at, normed_one),
        query_weight=(query_weight_at, query_weight),
        value_all=(value_all_at, value_all),
        key_weight=(key_weight_at, key_weight),
        normed_two=(normed_two_at, normed_two),
    )
    got = {
        name: pltpu.make_async_copy(source, target, fetch.at[i])
        for i, (name, (source, target)) in enumerate(held.items())
    }

    def output_copy(n):
        return pltpu.make_async_copy(
            output_weight_at.at[pl.ds(n * PIECE, PIECE)], output_part.at[n % 2], part_fetch.at[0, n % 2]
        )

    def value_copy(n):
        return pltpu.make_async_copy(
            value_weight_at.at[:, pl.ds(n * PIECE, PIECE)], value_part.at[n % 2], part_fetch.at[1, n % 2]
        )

    first_held = ("weights", "forward", "returned", "middle", "cot", "hidden")
    for name in first_held:
        got[name].start()
    for n in range(2):
        output_copy(n).start()
    for name in held:
        if name not in first_held:
            got[name].start()
    for n in range(2):
        value_copy(n).start()

    pieces = (
        [(out_output, PIECE * n, PIECE, n) for n in range(HEADS)]
        + [(out_query, 0, width, 4)]
        + [(out_value, PIECE * n, PIECE, n) for n in range(HEADS)]
        + [(out_key, 0, width, 5), (out_small, 0, 128, None)]
    )
    along_line = (0, 1)
    in_plane = [i for i in range(len(pieces)) if i not in along_line]
    x_first = {i: n % 2 == 0 for n, i in enumerate(in_plane)}

    def remote(source, target, slot, place):
        return pltpu.make_async_remote_copy(
            src_ref=source, dst_ref=target, send_sem=send.at[slot], recv_sem=recv.at[slot],
            device_id=place, device_id_type=MESH,
        )

    def add(target, source):
        target[...] = (target[...].astype(full) + source[...].astype(full)).astype(target.dtype)

    def own(i):
        slot = pieces[i][3]
        return grads_small if slot is None else grads.at[slot, :, :, :, :, columns(i)]

    def columns(i):
        return pl.ds(0, pieces[i][2])

    started = {}

    def begin(key, source, target, slot, place):
        started[key] = remote(source, target, slot, place)
        started[key].start()

    def halve_core(i):
        begin((i, 0), own(i).at[:, :, 1 - core], core_in.at[i, :, :, :, columns(i)], (i, 0), sibling)

    def halve_near(i):
        span = columns(i)
        started[i, 0].wait()
        add(core_in.at[i, :, :, :, span], own(i).at[:, :, core])
        if i in along_line:
            for k in (1, 2, 3):
                begin(
                    (i, k), core_in.at[i, :, (z + k) % 4, :, span],
                    plane_in.at[i, pl.ds(4 * k - 4, 4), :, span], (i, k), line[k - 1],
                )
            return
        for part in range(2):
            if x_first[i]:
                source = core_in.at[i, part * 2 + 1 - x, :, :, span]
            else:
                source = core_in.at[i, (1 - y) * 2 + part, :, :, span]
            target = plane_in.at[i, pl.ds(part * 4, 4), :, span]
            begin((i, 1 + part), source, target, (i, 1 + part), beside if x_first[i] else behind)

    def halve_far(i):
        span = columns(i)
        if i in along_line:
            held = core_in.at[i, :, z, :, span]
            for k in (1, 2, 3):
                started[i, k].wait()
                add(held, plane_in.at[i, pl.ds(4 * k - 4, 4), :, span])
            for part in range(2):
                begin(
                    (i, 4 + part), core_in.at[i, part * 2 + 1 - x, z, :, span],
                    last_in.at[i, part, :, span], (i, 4 + part), beside,
                )
            return
        for part in range(2):
            started[i, 1 + part].wait()
            kept = part * 2 + x if x_first[i] else y * 2 + part
            add(plane_in.at[i, pl.ds(part * 4, 4), :, span], core_in.at[i, kept, :, :, span])
        other = 1 - y if x_first[i] else 1 - x
        begin(
            (i, 3), plane_in.at[i, pl.ds(other * 4, 4), :, span], plane_in.at[i, pl.ds(8, 4), :, span],
            (i, 3), behind if x_first[i] else beside,
        )

    def spread(i):
        span = columns(i)
        if i in along_line:
            for part in range(2):
                started[i, 4 + part].wait()
                add(last_in.at[i, part, :, span], core_in.at[i, part * 2 + x, z, :, span])
            begin((i, 6), last_in.at[i, 1 - y, :, span], last_in.at[i, 2, :, span], (i, 6), behind)
            return
        started[i, 3].wait()
        add(plane_in.at[i, pl.ds(8, 4), :, span], plane_in.at[i, pl.ds((y if x_first[i] else x) * 4, 4), :, span])
        for k in (1, 2, 3):
            begin(
                (i, 3 + k), plane_in.at[i, 8 + (z + k) % 4, :, span],
                last_in.at[i, k - 1, :, span], (i, 3 + k), line[k - 1],
            )

    def finish(i):
        out, start, size, _ = pieces[i]
        span = columns(i)
        if i in along_line:
            started[i, 6].wait()
            total = last_in[i, y, :, span].astype(full) + last_in[i, 2, :, span].astype(full)
        else:
            total = plane_in[i, 8 + z, :, span].astype(full)
            for k in (1, 2, 3):
                started[i, 3 + k].wait()
                total = total + last_in[i, k - 1, :, span].astype(full)
        out[:, pl.ds(start, size)] = total

    rows_each = 64
    lane = lax.broadcasted_iota(jnp.int32, (1, 128), 1)
    for name in first_held:
        got[name].wait()
    logit_two[...] = (returned[:, D:] * slopes[...]).astype(low)

    half = z // 2
    inner = z + half * (3 - 2 * z)
    onward = 1 - 2 * half
    nearest = (z + onward, z + onward, z + onward, 0)
    farthest = (3 * (1 - half), 3 * (1 - half), z + onward, 1)
    backward = (3 * half, 3 * half, z - onward, 2)
    next_one = (2 - half, 2 - half + inner * (2 + half), z + onward, 3)

    def forward_copy(dest, slot, to, stage, part):
        span = pl.ds(part * (count // 2), count // 2)
        return pltpu.make_async_remote_copy(
            src_ref=forward.at[dest, span], dst_ref=forward_in.at[slot, span],
            send_sem=forward_send.at[stage, part], recv_sem=forward_recv.at[slot, part],
            device_id=(dp, to * 2 + core), device_id_type=MESH,
        )

    def relays(*ways):
        @pl.when(inner == 1)
        def _():
            for (dest, slot, to, stage), part in ways:
                span = pl.ds(part * (count // 2), count // 2)
                forward_copy(dest, dest, to, stage, part).wait_recv()
                add(forward.at[dest, span], forward_in.at[dest, span])
                forward_copy(dest, slot, to, stage, part).start()

    pl.semaphore_wait(barrier, 7)
    weight_copies = [
        pltpu.make_async_remote_copy(
            src_ref=weights.at[i], dst_ref=weights_in.at[i], send_sem=weights_send.at[i],
            recv_sem=weights_recv.at[i], device_id=place, device_id_type=MESH,
        )
        for i, place in enumerate((behind, beside))
    ]
    for made in weight_copies:
        made.start()

    @pl.when(inner == 0)
    def _():
        for way in (farthest, next_one, nearest):
            for part in range(2):
                forward_copy(*way, part).start()

    def live_rows(start):
        place = dp * count + start + lax.broadcasted_iota(jnp.int32, (rows_each, 1), 0)
        return jnp.where(place < length, 1.0, 0.0)

    def norm_back(field, grad, gain):
        center = field - jnp.mean(field, axis=-1, keepdims=True)
        scale = lax.rsqrt(jnp.mean(center * center, axis=-1, keepdims=True) + EPSILON)
        unit = center * scale
        part = grad * gain
        back = scale * (
            part
            - jnp.mean(part, axis=-1, keepdims=True)
            - unit * jnp.mean(part * unit, axis=-1, keepdims=True)
        )
        return back, jnp.sum(grad * unit, axis=0, keepdims=True)

    def first_rows(n, gain_sum):
        start = pl.multiple_of(n * rows_each, rows_each)
        rows = pl.ds(start, rows_each)
        grad = jnp.dot(logit_two[rows, :], routers[...], preferred_element_type=full)
        back, gain_part = norm_back(middle[rows, :], grad, gains[1:2, :])
        total = cot[rows, :].astype(full) + returned[rows, :D] + back
        grad_middle[rows, :] = total
        branch[rows, :] = (live_rows(start) * total).astype(low)
        return gain_sum + gain_part

    gain_two_sum = lax.fori_loop(0, count // rows_each, first_rows, jnp.zeros((1, D), full))
    relays((farthest, 0))

    def square(field, live, at):
        total = jnp.sum(jnp.sum(field * field, axis=1, keepdims=True) * live, axis=0, keepdims=True)
        return jnp.where(lane == at, total, 0.0)

    def last_rows(n, sums):
        start = pl.multiple_of(n * rows_each, rows_each)
        rows = pl.ds(start, rows_each)
        live = live_rows(start)
        field = middle[rows, :]
        step = forward[z, rows, :].astype(full)
        final = field + step
        block_out[rows, :] = final.astype(low)
        source = hidden[rows, :].astype(full)
        one = jnp.ones((rows_each, 1), full)
        sums += square(source, live, 0) + square(field - source, one, 1)
        sums += square(step, one, 2) + square(final, live, 3)
        return sums + jnp.where(lane == 4, jnp.sum(live, axis=0, keepdims=True), 0.0)

    def output_rows():
        for part in range(2):
            span = pl.ds(part * (count // 2), count // 2)
            forward_copy(z, z, z, 0, part).wait_recv()
            add(forward.at[z, span], forward_in.at[z, span])

            @pl.when(inner == 1)
            def _():
                forward_copy(z, 4, z, 0, part).wait_recv()
                add(forward.at[z, span], forward_in.at[4, span])

        sums = lax.fori_loop(0, count // rows_each, last_rows, jnp.zeros((1, 128), full))
        return sums

    def weight_grad(i, turned, right):
        def some(n, carry):
            rows = pl.ds(pl.multiple_of(n * 256, 256), 256)
            value = jnp.dot(turned[rows, :], right, preferred_element_type=full).astype(low)
            own(i)[n] = value.reshape(4, 2, ROWS, pieces[i][2])
            return carry

        lax.fori_loop(0, D // 256, some, 0)
        halve_core(i)

    got["attended"].wait()
    spread_count = HEADS * VE

    def head_of(c):
        return slice((c // VE) * HEAD_DIM, (c // VE + 1) * HEAD_DIM)

    logit_one[...] = jnp.zeros(logit_one.shape, full)
    grad_att[...] = jnp.zeros(grad_att.shape, full)
    for n in range(HEADS):
        output_copy(n).wait()
        for j in range(VE):
            c = VE * n + j
            grad_mixed = dot_last(branch[...], output_part[n % 2, j * HEAD_DIM : (j + 1) * HEAD_DIM, :])
            col = spread_count + c
            grad_att[:, head_of(c)] += gates[:, col : col + 1] * grad_mixed
            dots = jnp.sum(attended[:, head_of(c)] * grad_mixed, axis=1, keepdims=True)
            logit_one[:, col : col + 1] = dots * slopes[:, col : col + 1]
        if n + 2 < HEADS:
            output_copy(n + 2).start()
    relays((farthest, 1), (backward, 0))

    pair_all = key_value.reshape(4 * count, 2 * width)
    for name in ("key_value", "probs", "queries"):
        got[name].wait()

    def leave_copy(k, h):
        rows = pl.ds(h * 2 * HEAD_DIM, 2 * HEAD_DIM)
        return pltpu.make_async_remote_copy(
            src_ref=leave.at[(dp + 4 - k) % 4, rows], dst_ref=arrive.at[k - 1, rows],
            send_sem=leave_send.at[k - 1, h], recv_sem=leave_recv.at[k - 1, h],
            device_id=((dp + 4 - k) % 4, ex), device_id_type=MESH,
        )

    def head(h, carry):
        start = pl.multiple_of(h * HEAD_DIM, HEAD_DIM)
        span = pl.ds(start, HEAD_DIM)
        grad = grad_att[:, span].astype(low)
        prob = probs[h].astype(full)
        grad_prob = dot_last(grad, pair_all[:, pl.ds(width + start, HEAD_DIM)])
        dots = jnp.sum(prob * grad_prob, axis=-1, keepdims=True)
        grad_score = (prob * (grad_prob - dots) * HEAD_DIM ** (-0.5)).astype(low)
        grad_query[:, span] = jnp.dot(grad_score, pair_all[:, span], preferred_element_type=full).astype(low)
        key_part = dot_first(queries[:, span], grad_score).astype(low)
        value_part_all = dot_first(grad, probs[h]).astype(low)
        key_rows = pl.ds(pl.multiple_of(2 * h * HEAD_DIM, 2 * HEAD_DIM), HEAD_DIM)
        value_rows = pl.ds(pl.multiple_of((2 * h + 1) * HEAD_DIM, HEAD_DIM), HEAD_DIM)
        for j in range(4):
            leave[j, key_rows, :] = key_part[:, j * count : (j + 1) * count]
            leave[j, value_rows, :] = value_part_all[:, j * count : (j + 1) * count]
        for k in (1, 2, 3):

            @pl.when(dp >= k)
            def _():
                leave_copy(k, h).start()

        return carry

    lax.fori_loop(0, HEADS, head, 0)

    relays((backward, 1), (next_one, 0), (next_one, 1))
    branch_turned[...] = branch[...].T
    for n in range(HEADS):
        for j in range(VE):
            c = VE * n + j
            gate = gates[:, spread_count + c : spread_count + c + 1]
            mixed[:, j * HEAD_DIM : (j + 1) * HEAD_DIM] = (gate * attended[:, head_of(c)]).astype(low)
        weight_grad(n, branch_turned, mixed[...])
        if n:
            halve_near(n - 1)
    for name in ("normed_one", "query_weight"):
        got[name].wait()
    one_turned[...] = normed_one[...].T
    weight_grad(4, one_turned, grad_query[...])
    halve_near(3)
    hidden_turned[...] = hidden[...].T
    returned[:, :D] = dot_last(grad_query[...], query_weight[...])
    halve_near(4)
    got["value_all"].wait()

    for h in range(HEADS):
        rows = pl.ds(h * 2 * HEAD_DIM, 2 * HEAD_DIM)
        total = leave[dp, rows, :].astype(full)
        for k in (1, 2, 3):

            @pl.when(dp + k < 4)
            def _():
                leave_copy(k, h).wait_recv()

            @pl.when(dp + k >= 4)
            def _():
                arrive[k - 1, rows, :] = jnp.zeros((2 * HEAD_DIM, count), low)

            total += arrive[k - 1, rows, :].astype(full)
        turned = total.T
        grad_key[:, h * HEAD_DIM : (h + 1) * HEAD_DIM] = turned[:, :HEAD_DIM].astype(low)
        grad = turned[:, HEAD_DIM:].astype(low).astype(full)
        for c in range(h * VE, (h + 1) * VE):
            here = slice(c * HEAD_DIM, (c + 1) * HEAD_DIM)
            grad_each[:, here] = (gates[:, c : c + 1] * grad).astype(low)
            dots = jnp.sum(value_all[:, here].astype(full) * grad, axis=1, keepdims=True)
            logit_one[:, c : c + 1] = dots * slopes[:, c : c + 1]
        weight_grad(5 + h, hidden_turned, grad_each[:, h * PIECE : (h + 1) * PIECE])
        if h:
            halve_near(4 + h)
    weight_grad(9, one_turned, grad_key[...])
    halve_near(8)
    got["key_weight"].wait()
    returned[:, :D] += dot_last(grad_key[...], key_weight[...])
    halve_near(9)
    halve_far(2)
    returned[:, :D] += jnp.dot(logit_one[...].astype(low), routers[...], preferred_element_type=full)

    def first_norm(n, gain_sum):
        rows = pl.ds(pl.multiple_of(n * rows_each, rows_each), rows_each)
        back, gain_part = norm_back(hidden[rows, :].astype(full), returned[rows, :D], gains[0:1, :])
        grad_in[rows, :] = grad_middle[rows, :] + back
        return gain_sum + gain_part

    gain_one_sum = lax.fori_loop(0, count // rows_each, first_norm, jnp.zeros((1, D), full))
    halve_far(3)
    for made in weight_copies:
        made.wait()
    got["normed_two"].wait()
    small_turned[...] = dot_first(logit_one[...].astype(low), normed_one[...]) + dot_first(
        logit_two[...], normed_two[...]
    )
    small_rows = 2 * spread_count + total_experts
    small_turned[small_rows : small_rows + 1, :] = gain_one_sum
    small_turned[small_rows + 1 : small_rows + 2, :] = gain_two_sum
    sums = output_rows()
    for i in range(5):
        small_turned[small_rows + 2 + i : small_rows + 3 + i, :] = jnp.broadcast_to(sums[:, i : i + 1], (1, D))
    grads_small[...] = small_turned[...].T.astype(low).reshape(grads_small.shape)
    halve_core(10)
    spread(2)
    halve_far(4)
    def value_side(n):
        value_copy(n).wait()
        grad_in[...] += dot_last(grad_each[:, n * PIECE : (n + 1) * PIECE], value_part[n % 2])
        if n + 2 < HEADS:
            value_copy(n + 2).start()

    for action, i in (
        (halve_near, 10), (spread, 3),
        (value_side, 0), (halve_far, 5), (halve_far, 0), (spread, 4), (finish, 2),
        (value_side, 1), (halve_far, 6), (spread, 0), (finish, 3), (spread, 5),
        (value_side, 2), (halve_far, 7), (finish, 4), (spread, 6),
        (value_side, 3), (finish, 0), (halve_far, 1), (halve_far, 8), (finish, 5), (spread, 7),
        (spread, 1), (halve_far, 9), (finish, 6), (spread, 8), (halve_far, 10), (finish, 7), (finish, 1), (spread, 9),
        (spread, 10), (finish, 8), (finish, 9), (finish, 10),
    ):
        action(i)
    for h in range(HEADS):
        for k in (1, 2, 3):

            @pl.when(dp >= k)
            def _():
                leave_copy(k, h).wait_send()

    for part in range(2):
        forward_copy(z, 0, z, 1, part).wait_send()
        forward_copy(z, 0, z, 3, part).wait_send()

        @pl.when(inner == 0)
        def _():
            forward_copy(z, 0, z, 0, part).wait_send()

        @pl.when(inner == 1)
        def _():
            forward_copy(z, 0, z, 2, part).wait_send()


def backward(total_experts, lengths, gates, slopes, routers, gains, *arrays):
    low, full = jnp.bfloat16, jnp.float32
    count = gates.shape[0]
    width, wide = HEADS * HEAD_DIM, HEADS * VE * HEAD_DIM
    vmem = pl.BlockSpec(memory_space=pltpu.VMEM)
    anywhere = pl.BlockSpec(memory_space=pl.ANY)
    dma = pltpu.SemaphoreType.DMA
    whole = [pltpu.VMEM(a.shape, a.dtype) for a in arrays[:15]]
    n = 11
    return pl.pallas_call(
        functools.partial(backward_kernel, total_experts),
        out_shape=[
            jax.ShapeDtypeStruct((count, D), low),
            jax.ShapeDtypeStruct((count, D), full),
            jax.ShapeDtypeStruct((ROWS, width), full),
            jax.ShapeDtypeStruct((ROWS, width), full),
            jax.ShapeDtypeStruct((ROWS, wide), full),
            jax.ShapeDtypeStruct((ROWS, wide), full),
            jax.ShapeDtypeStruct((ROWS, 128), full),
            jax.ShapeDtypeStruct(arrays[0].shape, low),
        ],
        in_specs=[pl.BlockSpec(memory_space=pltpu.SMEM)] + [vmem] * 4 + [anywhere] * len(arrays),
        out_specs=[vmem] * 8,
        scratch_shapes=whole
        + [
            pltpu.VMEM((2, D, PIECE), low),
            pltpu.VMEM((2, PIECE, D), low),
            pltpu.VMEM((count, D), low),
            pltpu.VMEM((D, count), low),
            pltpu.VMEM((D, count), low),
            pltpu.VMEM((D, count), low),
            pltpu.VMEM((count, width), full),
            pltpu.VMEM((count, width), low),
            pltpu.VMEM((4, 2 * width, count), low),
            pltpu.VMEM((3, 2 * width, count), low),
            pltpu.VMEM((count, width), low),
            pltpu.VMEM((count, wide), low),
            pltpu.VMEM((count, D), full),
            pltpu.VMEM((count, 128), full),
            pltpu.VMEM((count, 128), low),
            pltpu.VMEM((128, D), full),
            pltpu.VMEM((count, PIECE), low),
            pltpu.VMEM((6, 4, 4, 2, ROWS, PIECE), low),
            pltpu.VMEM((4, 4, 2, ROWS, 128), low),
            pltpu.VMEM((n, 4, 4, ROWS, PIECE), low),
            pltpu.VMEM((n, 12, ROWS, PIECE), low),
            pltpu.VMEM((n, 3, ROWS, PIECE), low),
            pltpu.VMEM((5, count, D), low),
            dma((15,)),
            dma((2, 2)),
            dma((3, HEADS)),
            dma((3, HEADS)),
            dma((n, 7)),
            dma((n, 7)),
            dma((4, 2)),
            dma((5, 2)),
            dma((2,)),
            dma((2,)),
        ],
        compiler_params=pltpu.CompilerParams(
            collective_id=3, has_side_effects=True, vmem_limit_bytes=62 * 2**20
        ),
        name="backward",
    )(lengths, gates, slopes, routers, gains, *arrays)


def expert_visit(sent, cotangent, expert_up, expert_down):
    local_experts = expert_up.shape[0]
    group = lax.axis_index("expert")
    cot_all = lax.all_gather(cotangent, "expert", axis=0, tiled=True)
    sent_all = lax.all_gather(sent, "expert", axis=0, tiled=True)
    rows_all = sent_all[:, :D]
    total_experts = sent.shape[1] - D
    gate_all = lax.dynamic_slice_in_dim(
        sent_all[:, D:], group * local_experts, local_experts, 1
    ).astype(jnp.float32).T[:, :, None]
    preact = jnp.einsum("td,xdf->xtf", rows_all, expert_up, preferred_element_type=jnp.float32)
    pre_sig = jax.nn.sigmoid(preact)
    hidden = preact * pre_sig
    back = jnp.einsum("td,xfd->xtf", cot_all, expert_down, preferred_element_type=jnp.float32)
    gate_grad = jnp.sum(hidden * back, axis=2).T
    gated = (gate_all * hidden).astype(jnp.bfloat16)
    grad_pre = (gate_all * back * (pre_sig * (1.0 + preact * (1.0 - pre_sig)))).astype(jnp.bfloat16)
    partial_out = jnp.einsum("xtf,xfd->td", gated, expert_down, preferred_element_type=jnp.float32)
    partial_grad = jnp.einsum("xtf,xdf->td", grad_pre, expert_up, preferred_element_type=jnp.float32)
    wide_grad = lax.dynamic_update_slice_in_dim(
        jnp.zeros((gate_grad.shape[0], total_experts), jnp.bfloat16),
        gate_grad.astype(jnp.bfloat16),
        group * local_experts,
        1,
    )
    returned = lax.psum_scatter(
        jnp.concatenate(
            [partial_out.astype(jnp.bfloat16), partial_grad.astype(jnp.bfloat16), wide_grad], axis=1
        ),
        "expert",
        scatter_dimension=0,
        tiled=True,
    )
    grad_down = jnp.einsum("xtf,td->xfd", gated, cot_all, preferred_element_type=jnp.float32)
    grad_up = jnp.einsum("td,xtf->xdf", rows_all, grad_pre, preferred_element_type=jnp.float32)
    return returned, grad_up, grad_down


def shards(
    hidden_in,
    lengths,
    value_pick,
    output_pick,
    expert_pick,
    query_weight,
    key_weight,
    value_weight,
    output_weight,
    value_router,
    output_router,
    expert_router,
    attention_gain,
    feedforward_gain,
    expert_up,
    expert_down,
    cotangent,
):
    row_count = hidden_in.shape[1]
    total_experts = expert_router.shape[1]
    input_low = hidden_in[0]
    input_full = input_low.astype(jnp.float32)
    length = lengths[0]
    query_pos = lax.axis_index("dp") * row_count + jnp.arange(row_count, dtype=jnp.int32)
    live_mask = (query_pos < length).astype(jnp.float32)[:, None]
    gain_one = attention_gain.astype(jnp.float32)
    gain_two = feedforward_gain.astype(jnp.float32)
    normed_one = layer_norm(input_full, gain_one)
    normed_low = normed_one.astype(jnp.bfloat16)
    queries = low_dot(normed_low, query_weight).astype(jnp.bfloat16)
    key_local = low_dot(normed_low, key_weight).astype(jnp.bfloat16)
    value_sig = jax.nn.sigmoid(low_dot(normed_low, value_router)).reshape(row_count, HEADS, VE)
    value_hot = choose(value_pick[0], VE)
    value_gate = value_sig * value_hot
    value_all = low_dot(input_low, value_weight).reshape(row_count, HEADS, VE, HEAD_DIM)
    value_local = (
        jnp.sum(value_gate[..., None] * value_all, axis=2)
        .astype(jnp.bfloat16)
        .reshape(row_count, HEADS * HEAD_DIM)
    )
    key_all, value_rows = (
        lax.all_gather(key_local, "dp", axis=0, tiled=True),
        lax.all_gather(value_local, "dp", axis=0, tiled=True),
    )
    query_heads = queries.reshape(row_count, HEADS, HEAD_DIM)
    key_heads = key_all.reshape(-1, HEADS, HEAD_DIM)
    value_heads = value_rows.reshape(-1, HEADS, HEAD_DIM)
    soft_probs = attention_probs(query_heads, key_heads, query_pos, length)
    attended = jnp.einsum(
        "hqk,khd->qhd",
        soft_probs.astype(jnp.bfloat16),
        value_heads,
        preferred_element_type=jnp.float32,
    )
    output_sig = jax.nn.sigmoid(low_dot(normed_low, output_router)).reshape(row_count, HEADS, VE)
    output_hot = choose(output_pick[0], VE)
    output_gate = output_sig * output_hot
    mixed = (
        (output_gate[..., None] * attended[:, :, None, :])
        .astype(jnp.bfloat16)
        .reshape(row_count, HEADS * VE * HEAD_DIM)
    )
    attention_out = live_mask * low_dot(mixed, output_weight)
    middle = input_full + attention_out
    normed_two = layer_norm(middle, gain_two)
    normed_two_low = normed_two.astype(jnp.bfloat16)
    router_sig = jax.nn.sigmoid(low_dot(normed_two_low, expert_router))
    hot = jnp.any(
        expert_pick[0][:, :, None] == jnp.arange(total_experts, dtype=jnp.int32), axis=1
    ).astype(jnp.float32)
    picked_hot = hot * live_mask
    expert_gate = router_sig * picked_hot
    middle_low = middle.astype(jnp.bfloat16)
    sent = jnp.concatenate([middle_low, expert_gate.astype(jnp.bfloat16)], axis=1)
    groups = lax.axis_size("expert")
    rounds = max(1, groups // 8)

    def visit(grads, item):
        returned, grad_up, grad_down = expert_visit(*item, expert_up, expert_down)
        return (grads[0] + grad_up, grads[1] + grad_down), returned

    zeros = jnp.zeros(expert_up.shape, jnp.float32), jnp.zeros(expert_down.shape, jnp.float32)
    (up_grad, down_grad), returned = lax.scan(
        visit,
        zeros,
        (
            sent.reshape(rounds, -1, sent.shape[1]),
            cotangent[0].reshape(rounds, -1, D),
        ),
    )
    returned = returned.reshape(row_count, -1).astype(jnp.float32)
    up_grad = lax.psum_scatter(
        up_grad.astype(jnp.bfloat16), "dp", scatter_dimension=1, tiled=True
    ).astype(jnp.float32)
    down_grad = lax.psum_scatter(
        down_grad.astype(jnp.bfloat16), "dp", scatter_dimension=2, tiled=True
    ).astype(jnp.float32)
    feedforward_out = returned[:, :D]
    final_rows = middle + feedforward_out
    sums = jnp.stack(
        [
            jnp.sum(live_mask * input_full * input_full),
            jnp.sum(attention_out * attention_out),
            jnp.sum(feedforward_out * feedforward_out),
            jnp.sum(live_mask * final_rows * final_rows),
            jnp.sum(live_mask),
        ]
    )
    grad_final = cotangent[0].astype(jnp.float32)
    grad_middle = grad_final + returned[:, D : 2 * D]
    grad_logit = (
        returned[:, 2 * D :] * picked_hot * router_sig * (1.0 - router_sig)
    ).astype(jnp.bfloat16)
    grad_expert_router = low_dot(normed_two_low.T, grad_logit)
    grad_normed_two = low_dot(grad_logit, expert_router.T)
    unused_two, norm_two_back = jax.vjp(layer_norm, middle, gain_two)
    grad_middle_norm, grad_gain_two = norm_two_back(grad_normed_two)
    grad_middle = grad_middle + grad_middle_norm
    grad_branch = (live_mask * grad_middle).astype(jnp.bfloat16)
    grad_mixed = jnp.einsum(
        "td,md->tm", grad_branch, output_weight, preferred_element_type=jnp.float32
    ).reshape(row_count, HEADS, VE, HEAD_DIM)
    grad_output_weight = jnp.einsum(
        "td,tm->dm", grad_branch, mixed, preferred_element_type=jnp.float32
    )
    grad_attended = jnp.sum(output_gate[..., None] * grad_mixed, axis=2)
    grad_output_logit = (
        jnp.sum(attended[:, :, None, :] * grad_mixed, axis=3)
        * output_hot
        * output_sig
        * (1.0 - output_sig)
    ).reshape(row_count, HEADS * VE)
    grad_attended_low = grad_attended.astype(jnp.bfloat16)
    grad_probs = jnp.einsum(
        "qhd,khd->hqk", grad_attended_low, value_heads, preferred_element_type=jnp.float32
    )
    row_dot = jnp.sum(soft_probs * grad_probs, axis=-1, keepdims=True)
    grad_scores = (soft_probs * (grad_probs - row_dot) * HEAD_DIM ** (-0.5)).astype(jnp.bfloat16)
    grad_query = (
        jnp.einsum("hqk,khd->qhd", grad_scores, key_heads, preferred_element_type=jnp.float32)
        .astype(jnp.bfloat16)
        .reshape(row_count, HEADS * HEAD_DIM)
    )
    grad_key_all = jnp.einsum(
        "hqk,qhd->khd", grad_scores, query_heads, preferred_element_type=jnp.float32
    ).reshape(-1, HEADS * HEAD_DIM)
    grad_value_rows = jnp.einsum(
        "hqk,qhd->khd",
        soft_probs.astype(jnp.bfloat16),
        grad_attended_low,
        preferred_element_type=jnp.float32,
    ).reshape(-1, HEADS * HEAD_DIM)
    grad_key_sum, grad_value_sum = (
        lax.psum_scatter(
            grad_key_all.astype(jnp.bfloat16), "dp", scatter_dimension=0, tiled=True
        ).astype(jnp.float32),
        lax.psum_scatter(
            grad_value_rows.astype(jnp.bfloat16), "dp", scatter_dimension=0, tiled=True
        ).astype(jnp.float32),
    )
    grad_key = grad_key_sum.astype(jnp.bfloat16)
    grad_value_low = (
        grad_value_sum.astype(jnp.bfloat16)
        .astype(jnp.float32)
        .reshape(row_count, HEADS, 1, HEAD_DIM)
    )
    grad_value_each = (
        (value_gate[..., None] * grad_value_low)
        .astype(jnp.bfloat16)
        .reshape(row_count, HEADS * VE * HEAD_DIM)
    )
    grad_value_logit = (
        jnp.sum(value_all * grad_value_low, axis=3) * value_hot * value_sig * (1.0 - value_sig)
    ).reshape(row_count, HEADS * VE)
    grad_value_weight = jnp.einsum(
        "td,tm->dm", input_low, grad_value_each, preferred_element_type=jnp.float32
    )
    grad_query_weight = jnp.einsum(
        "td,tm->dm", normed_low, grad_query, preferred_element_type=jnp.float32
    )
    grad_key_weight = jnp.einsum(
        "td,tm->dm", normed_low, grad_key, preferred_element_type=jnp.float32
    )
    grad_value_logit = grad_value_logit.astype(jnp.bfloat16)
    grad_output_logit = grad_output_logit.astype(jnp.bfloat16)
    grad_value_router = low_dot(normed_low.T, grad_value_logit)
    grad_output_router = low_dot(normed_low.T, grad_output_logit)
    grad_normed_one = (
        jnp.einsum("tm,dm->td", grad_query, query_weight, preferred_element_type=jnp.float32)
        + jnp.einsum("tm,dm->td", grad_key, key_weight, preferred_element_type=jnp.float32)
        + low_dot(grad_value_logit, value_router.T)
        + low_dot(grad_output_logit, output_router.T)
    )
    unused_one, norm_one_back = jax.vjp(layer_norm, input_full, gain_one)
    grad_input_norm, grad_gain_one = norm_one_back(grad_normed_one)
    grad_input = (
        grad_middle
        + jnp.einsum("tm,dm->td", grad_value_each, value_weight, preferred_element_type=jnp.float32)
        + grad_input_norm
    )
    small_grads = jnp.concatenate(
        [
            grad_value_router,
            grad_output_router,
            grad_expert_router,
            grad_gain_one[:, None],
            grad_gain_two[:, None],
        ],
        axis=1,
    )
    small_count = small_grads.shape[1]
    small_grads = jnp.pad(small_grads, ((0, 0), (0, -small_count % 128)))
    low_grads = [
        part.astype(jnp.bfloat16)
        for part in (
            grad_query_weight,
            grad_key_weight,
            grad_value_weight,
            grad_output_weight,
            small_grads,
        )
    ]
    summed = lax.psum_scatter(
        jnp.concatenate(low_grads, axis=1), ("dp", "expert"), scatter_dimension=0, tiled=True
    ).astype(jnp.float32)
    dense_grads = jnp.split(summed, [512, 1024, 3584, 6144], axis=1)
    total_sums = lax.psum(sums, ("dp", "expert"))
    residual_norms = jnp.sqrt(total_sums[:4] / (total_sums[4] * D))
    small = dense_grads[4]
    router_end = 2 * HEADS * VE + expert_router.shape[1]
    dense_grads = [
        dense_grads[0],
        dense_grads[1],
        dense_grads[2],
        dense_grads[3].T,
        small[:, : HEADS * VE],
        small[:, HEADS * VE : 2 * HEADS * VE],
        small[:, 2 * HEADS * VE : router_end],
        small[:, router_end],
        small[:, router_end + 1],
    ]
    return (
        final_rows.astype(jnp.bfloat16)[None],
        grad_input[None],
        dense_grads[0],
        dense_grads[1],
        dense_grads[2],
        dense_grads[3],
        dense_grads[4],
        dense_grads[5],
        dense_grads[6],
        dense_grads[7],
        dense_grads[8],
        up_grad,
        down_grad,
        residual_norms,
    )


def deliver_kernel(total, small, weights_kept, weights_in, *refs):
    count = (len(refs) - 9) // 3
    sources, targets = refs[:count], refs[count : 2 * count]
    value_out, output_out, expert_out, gains_out, norms_out, up_out, down_out = refs[2 * count : 2 * count + 7]
    held = refs[2 * count + 7 : -2]
    inward, outward = refs[-2:]
    arrived = [pltpu.make_async_copy(a, b, inward.at[i]) for i, (a, b) in enumerate(zip(sources, held))]
    left = [pltpu.make_async_copy(a, b, outward.at[i]) for i, (a, b) in enumerate(zip(held, targets))]
    for made in arrived:
        made.start()
    spread = HEADS * VE
    turned = jnp.concatenate([small[...], jnp.zeros((128 - ROWS, 128), jnp.float32)]).T
    value_out[...] = turned[:spread, :ROWS]
    output_out[...] = turned[spread : 2 * spread, :ROWS]
    expert_out[...] = small[:, 2 * spread : 2 * spread + total]
    gains_out[...] = turned[2 * spread + total : 2 * spread + total + 2, :ROWS]
    row = small[0:1, :]
    first = 2 * spread + total + 2
    norms_out[...] = jnp.sqrt(row[:, first : first + 4] / (row[:, first + 4 : first + 5] * D))
    for e in range(up_out.shape[0]):
        rows = slice(e * HEAD_DIM, (e + 1) * HEAD_DIM)
        up_sum, down_sum = [
            weights_kept[i, rows, :].astype(jnp.float32) + weights_in[i, rows, :].astype(jnp.float32)
            for i in range(2)
        ]
        up_out[e] = up_sum.T
        down_out[e] = down_sum
    for one, other in zip(arrived, left):
        one.wait()
        other.start()
    for made in left:
        made.wait()


def deliver(total, small, weights_kept, weights_in, *arrays):
    experts = weights_in.shape[1] // HEAD_DIM
    full = jnp.float32
    vmem = pl.BlockSpec(memory_space=pltpu.VMEM)
    anywhere = pl.BlockSpec(memory_space=pl.ANY)
    spread = HEADS * VE
    return pl.pallas_call(
        functools.partial(deliver_kernel, total),
        out_shape=[jax.ShapeDtypeStruct(a.shape, a.dtype) for a in arrays]
        + [
            jax.ShapeDtypeStruct((spread, ROWS), full),
            jax.ShapeDtypeStruct((spread, ROWS), full),
            jax.ShapeDtypeStruct((ROWS, total), full),
            jax.ShapeDtypeStruct((2, ROWS), full),
            jax.ShapeDtypeStruct((1, 4), full),
            jax.ShapeDtypeStruct((experts, D // 4, HEAD_DIM), full),
            jax.ShapeDtypeStruct((experts, HEAD_DIM, D // 4), full),
        ],
        in_specs=[vmem] * 3 + [anywhere] * len(arrays),
        out_specs=[anywhere] * len(arrays) + [vmem] * 7,
        scratch_shapes=[pltpu.VMEM(a.shape, a.dtype) for a in arrays]
        + [pltpu.SemaphoreType.DMA((len(arrays),))] * 2,
        compiler_params=pltpu.CompilerParams(vmem_limit_bytes=63 * 2**20),
        name="deliver",
    )(small, weights_kept, weights_in, *arrays)


def shards_fast(
    hidden_in,
    lengths,
    value_pick,
    output_pick,
    expert_pick,
    query_weight,
    key_weight,
    value_weight,
    output_weight,
    value_router,
    output_router,
    expert_router,
    attention_gain,
    feedforward_gain,
    expert_up,
    expert_down,
    cotangent,
):
    total = expert_router.shape[1]
    spread = HEADS * VE
    routers = jnp.concatenate(
        [value_router.T, output_router.T, expert_router.T, jnp.zeros((128 - 2 * spread - total, D), jnp.bfloat16)]
    )
    gains = jnp.stack([attention_gain, feedforward_gain]).astype(jnp.float32)
    (
        middle,
        sent,
        normed_one,
        normed_two,
        queries,
        key_value,
        probs,
        value_all,
        attended,
        gates,
        slopes,
        cot_line,
    ) = attend(
        total,
        lengths,
        hidden_in[0],
        cotangent[0],
        value_pick[0].transpose(1, 2, 0),
        output_pick[0].transpose(1, 2, 0),
        expert_pick[0].T,
        routers,
        gains,
        key_weight,
        value_weight,
        query_weight,
        output_weight,
    )
    returned, weights, weights_kept, forward = expert_kernel_visit(sent, cot_line, expert_up, expert_down)
    block_out, grad_input, grad_query, grad_key, grad_value, grad_output, small, weights_in = backward(
        total,
        lengths,
        gates,
        slopes,
        routers,
        gains,
        weights,
        forward,
        returned,
        middle,
        cotangent[0],
        hidden_in[0],
        normed_one,
        queries,
        key_value,
        probs,
        value_all,
        attended,
        normed_two,
        query_weight,
        key_weight,
        value_weight,
        output_weight,
    )
    kept = (block_out, grad_input, grad_query, grad_key, grad_value, grad_output)
    delivered = deliver(total, small, weights_kept, weights_in, *kept)
    block_out, grad_input, grad_query, grad_key, grad_value, grad_output = delivered[:6]
    value_small, output_small, expert_small, gain_grads, norms, up_grad, down_grad = delivered[6:]
    return (
        block_out[None],
        grad_input[None],
        grad_query,
        grad_key,
        grad_value,
        grad_output.T,
        value_small.T,
        output_small.T,
        expert_small,
        gain_grads[0],
        gain_grads[1],
        up_grad,
        down_grad,
        norms[0],
    )


def solution(mesh):
    placed = (
        P("expert", "dp", None),
        P("expert"),
        P("expert", "dp", None, None),
        P("expert", "dp", None, None),
        P("expert", "dp", None),
        P(),
        P(),
        P(),
        P(),
        P(),
        P(),
        P(),
        P(),
        P(),
        P("expert", None, None),
        P("expert", None, None),
        P("expert", "dp", None),
    )
    small_mesh = mesh.shape["dp"] == 4 and mesh.shape["expert"] == 8
    return jax.shard_map(
        shards_fast if small_mesh else shards,
        mesh=mesh,
        in_specs=placed,
        out_specs=(
            P("expert", "dp", None),
            P("expert", "dp", None),
            P(("dp", "expert"), None),
            P(("dp", "expert"), None),
            P(("dp", "expert"), None),
            P(None, ("dp", "expert")),
            P(("dp", "expert"), None),
            P(("dp", "expert"), None),
            P(("dp", "expert"), None),
            P(("dp", "expert")),
            P(("dp", "expert")),
            P("expert", "dp", None),
            P("expert", None, "dp"),
            P(),
        ),
        check_vma=False,
    )
```

```python
import functools

import jax
import jax.numpy as jnp
from jax import lax
from jax.experimental import pallas as pl
from jax.experimental.pallas import tpu as pltpu
from jax.sharding import PartitionSpec as P

D = 1024
HEADS = 4
HEAD_DIM = 128
VE = 5


MESH = pl.DeviceIdType.MESH
ROWS = 32
PIECE = VE * HEAD_DIM
EPSILON = 1e-05
NEGATIVE = -1000000000.0


def low_dot(left_side, right_side):
    return jnp.dot(left_side, right_side, preferred_element_type=jnp.float32)


def layer_norm(field, scale_gain):
    center = field - jnp.mean(field, axis=-1, keepdims=True)
    spread = jnp.mean(center * center, axis=-1, keepdims=True)
    return center * lax.rsqrt(spread + EPSILON) * scale_gain


def choose(select, count):
    return jnp.sum(
        (select[..., None] == jnp.arange(count, dtype=jnp.int32)).astype(jnp.float32), axis=-2
    )


def attention_probs(query_heads, key_heads, query_pos, length):
    key_pos = jnp.arange(key_heads.shape[0], dtype=jnp.int32)
    raw_scores = jnp.einsum(
        "qhd,khd->hqk", query_heads, key_heads, preferred_element_type=jnp.float32
    )
    allowed = (key_pos[None, :] <= query_pos[:, None]) & (key_pos[None, :] < length)
    scores = jnp.where(allowed[None], raw_scores * HEAD_DIM ** (-0.5), NEGATIVE)
    exp_terms = jnp.exp(scores - jnp.max(scores, axis=-1, keepdims=True))
    return exp_terms / jnp.sum(exp_terms, axis=-1, keepdims=True)


def dot_last(left_side, right_side):
    return lax.dot_general(
        left_side, right_side, (((1,), (1,)), ((), ())), preferred_element_type=jnp.float32
    )

def dot_first(left_side, right_side):
    return lax.dot_general(
        left_side, right_side, (((0,), (0,)), ((), ())), preferred_element_type=jnp.float32
    )


def visit_kernel(
    sent, cot_at, up_at, down_at, back_out, weights_out, weights_kept, forward_out,
    cot, up, down, rows, cot_other, up_wide, chosen, cots, gated, grad_pre, forward, forward_in, gated_turned, pre_turned, partial, paired_in, chain_in, up_low, down_low, up_in, down_in,
    fetch, row_send, row_recv, half_send, half_recv, cot_send, cot_recv, pair_send, pair_recv, forward_send, forward_recv, chain_send, chain_recv, grad_send, grad_recv,
):
    experts = up.shape[0]
    wide = down.shape[0]
    hidden = wide // experts
    dp, ex = lax.axis_index("dp"), lax.axis_index("expert")
    y, x, z, core = dp // 2, dp % 2, ex // 2, ex % 2
    half = z // 2
    inner = z + half * (3 - 2 * z)
    onward = 1 - 2 * half
    sibling = (dp, z * 2 + 1 - core)
    beside, behind = (y * 2 + 1 - x, ex), ((1 - y) * 2 + x, ex)

    def at_z(place):
        return (dp, place * 2 + core)

    fetched = [
        pltpu.make_async_copy(source, target, fetch.at[i])
        for i, (source, target) in enumerate(((cot_at, cot), (up_at, up), (down_at, down)))
    ]
    for made in fetched:
        made.start()
    barrier = pltpu.get_barrier_semaphore()
    for place in (sibling, beside, behind):
        pl.semaphore_signal(barrier, inc=1, device_id=place, device_id_type=MESH)

    @pl.when(z < 3)
    def _():
        pl.semaphore_signal(barrier, inc=1, device_id=at_z(z + 1), device_id_type=MESH)

    @pl.when(z > 0)
    def _():
        pl.semaphore_signal(barrier, inc=1, device_id=at_z(z - 1), device_id_type=MESH)

    pl.semaphore_wait(barrier, 4 + inner)

    def remote(source, target, send, recv, place):
        return pltpu.make_async_remote_copy(
            src_ref=source, dst_ref=target, send_sem=send, recv_sem=recv, device_id=place, device_id_type=MESH
        )

    def row_copy(at, source=None):
        block = rows.at[at] if source is None else source
        return remote(block, rows.at[4 + at], row_send.at[at], row_recv.at[at], sibling)

    def half_copy(way, at, part, source=None):
        span = pl.ds(part * (rows.shape[1] // 2), rows.shape[1] // 2)
        block = rows.at[at] if source is None else source
        return remote(
            block.at[span], rows.at[at, span], half_send.at[way, at, part], half_recv.at[at, part], at_z(z + 1 - 2 * way)
        )

    def cot_copy(at):
        return remote(cot.at[at], cot_other.at[at], cot_send.at[at], cot_recv.at[at], sibling)

    @pl.when(z < 3)
    def _():
        for part in range(2):
            half_copy(0, z, part, sent).start()

    @pl.when(z > 0)
    def _():
        for part in range(2):
            half_copy(1, z, part, sent).start()

    row_copy(z, sent).start()
    for made in fetched:
        made.wait()
    cot_copy(z).start()
    for k in (1, 2, 3):
        cot_copy((z + k) % 4).start()
    rows[z] = sent[...]
    for e in range(experts):
        up_wide[:, e * hidden : (e + 1) * hidden] = up[e]
    chosen[...] = (
        lax.broadcasted_iota(jnp.int32, (128, wide), 0)
        == 2 * HEADS * VE + ex * experts + lax.broadcasted_iota(jnp.int32, (128, wide), 1) // hidden
    ).astype(jnp.float32).astype(jnp.bfloat16)

    def order(p):
        later = (p + 2) // 3
        step = p - inner // (p + 1 - later)
        return later * (step + half * (3 - 2 * step)) + (1 - later) * z

    def pair_copy(at):
        return remote(partial.at[1, at], paired_in.at[at], pair_send.at[at], pair_recv.at[at], sibling)

    parts = 4
    size = rows.shape[1] // parts
    spans = [pl.ds(i * size, size) for i in range(parts)]

    def chain_copy(dest, slot, to, stage, part):
        span = spans[part]
        return remote(
            partial.at[0, dest, span], chain_in.at[slot, span],
            chain_send.at[stage, part], chain_recv.at[slot, part], at_z(to),
        )

    def add(target, source):
        def some(i, carry):
            part = pl.ds(pl.multiple_of(i * 32, 32), 32)
            target[part, :] = (
                target[part, :].astype(jnp.float32) + source[part, :].astype(jnp.float32)
            ).astype(target.dtype)
            return carry

        lax.fori_loop(0, target.shape[0] // 32, some, 0)

    def forward_copy(at):
        return remote(forward.at[at], forward_in.at[at], forward_send.at[at], forward_recv.at[at], sibling)

    def forward_block(block):
        at = block % 4
        def some(n, inside):
            span = pl.ds(pl.multiple_of(n * 256, 256), 256)
            value = jnp.dot(gated[block], down[:, span], preferred_element_type=jnp.float32).astype(jnp.bfloat16)

            @pl.when(block >= 4)
            def _():
                forward[at, :, span] = value

            @pl.when(block < 4)
            def _():
                forward_out[at, :, span] = value

            return inside

        lax.fori_loop(0, D // 256, some, 0)

        @pl.when(block >= 4)
        def _():
            forward_copy(at).start()

    def relay(dest, slot, to, stage, part):
        chain_copy(dest, dest, to, stage, part).wait_recv()
        add(partial.at[0, dest, spans[part]], chain_in.at[dest, spans[part]])
        chain_copy(dest, slot, to, stage, part).start()

    def visit(q, carry):
        p, other = q // 2, q % 2
        at = order(p)
        block = other * 4 + at

        @pl.when((other == 0) & (p > 0))
        def _():
            for part in range(2):
                half_copy(0, at, part).wait_recv()

                @pl.when((at < z) & (z < 3))
                def _():
                    half_copy(0, at, part).start()

                @pl.when((at > z) & (z > 0))
                def _():
                    half_copy(1, at, part).start()

            row_copy(at).start()

        @pl.when(other == 1)
        def _():
            row_copy(at).wait_recv()
            cot_copy(at).wait_recv()
            cots[...] = cot_other[at]

        @pl.when(other == 0)
        def _():
            cots[...] = cot[at]

        @pl.when((inner == 1) & (q == 7))
        def _():
            relay(*next_one, 0)
            relay(*next_one, 1)

        count = rows.shape[1]
        places = pl.ds(pl.multiple_of(block * count, count), count)

        def columns(n, gate_grad):
            span = pl.ds(pl.multiple_of(n * 256, 256), 256)
            pre = jnp.dot(rows[block, :, :D], up_wide[:, span], preferred_element_type=jnp.float32)
            back = dot_last(cots[...], down[span, :])
            mark = chosen[:, span]
            gate = jnp.dot(rows[block, :, D:], mark, preferred_element_type=jnp.float32)
            sig = jax.nn.sigmoid(pre)
            act = pre * sig
            act_low = (gate * act).astype(jnp.bfloat16)
            pre_low = (gate * back * (sig * (1.0 + pre * (1.0 - sig)))).astype(jnp.bfloat16)
            gated[block, :, span] = act_low
            grad_pre[:, span] = pre_low
            gated_turned[span, places] = act_low.T
            pre_turned[span, places] = pre_low.T
            return gate_grad + dot_last((act * back).astype(jnp.bfloat16), mark)

        partial[other, at, :, D:] = lax.fori_loop(
            0, wide // 256, columns, jnp.zeros((count, 128), jnp.float32)
        ).astype(jnp.bfloat16)

        def outward(n, carry):
            span = pl.ds(pl.multiple_of(n * 256, 256), 256)
            partial[other, at, :, span] = dot_last(grad_pre[...], up_wide[span, :]).astype(jnp.bfloat16)
            return carry

        lax.fori_loop(0, D // 256, outward, 0)

        @pl.when(other == 1)
        def _():
            pair_copy(at).start()
            pair_copy(at).wait_recv()
            add(partial.at[0, at], paired_in.at[at])

        @pl.when((inner == 0) & (q == 3))
        def _():
            for part in range(parts):
                chain_copy(*nearest, part).start()

        @pl.when((inner == 0) & (q == 5))
        def _():
            for part in range(parts):
                chain_copy(*next_one, part).start()

        @pl.when(q < 6)
        def _():
            forward_block(block)

        return carry

    nearest = (z + onward, z + onward, z + onward, 0)
    farthest = (3 * (1 - half), 3 * (1 - half), z + onward, 1)
    backward = (3 * half, 3 * half, z - onward, 2)
    next_one = (2 - half, 2 - half + inner * (2 + half), z + onward, 3)
    lax.fori_loop(0, 8, visit, 0)

    @pl.when(inner == 0)
    def _():
        for part in range(parts):
            chain_copy(*farthest, part).start()
    tokens_all = rows.reshape(rows.shape[0] * rows.shape[1], rows.shape[2])
    cots_own = cot.reshape(cot.shape[0] * cot.shape[1], D)
    cots_other = cot_other.reshape(cot.shape[0] * cot.shape[1], D)
    place = cots_own.shape[0]
    quarter = D // 4


    def up_copy(j):
        return remote(up_low.at[j], up_in.at[j], grad_send.at[0, j], grad_recv.at[0, j], behind if j == 2 else beside)

    def down_copy(j):
        return remote(down_low.at[j], down_in.at[j], grad_send.at[1, j], grad_recv.at[1, j], beside if j == 1 else behind)

    def span_of(j):
        at = (y + (1 - j % 2) * (1 - 2 * y)) * 2 + x + (1 - j // 2) * (1 - 2 * x)
        return pl.ds(pl.multiple_of(at * quarter, quarter), quarter)

    def up_quarter(j):
        up_low[j] = jnp.dot(
            pre_turned[...], tokens_all[:, span_of(j)], preferred_element_type=jnp.float32
        ).astype(jnp.bfloat16)
        if j < 2:
            up_copy(j).start()

    def down_quarter(j):
        down_low[j] = (
            jnp.dot(gated_turned[:, :place], cots_own[:, span_of(j)], preferred_element_type=jnp.float32)
            + jnp.dot(gated_turned[:, place:], cots_other[:, span_of(j)], preferred_element_type=jnp.float32)
        ).astype(jnp.bfloat16)
        if j in (0, 2):
            down_copy(j).start()

    def relays(*ways):
        @pl.when(inner == 1)
        def _():
            for way, part in ways:
                relay(*way, part)

    def forward_add(p):
        at = order(p)
        forward_copy(at).wait()
        add(forward_out.at[at], forward_in.at[at])

    relays((next_one, 2), (next_one, 3))
    up_quarter(0)
    down_quarter(0)
    relays((farthest, 0))
    up_quarter(1)
    relays((farthest, 1))
    down_quarter(2)
    relays((backward, 0), (farthest, 2))
    forward_block(4 + order(3))
    relays((backward, 1), (farthest, 3))
    up_quarter(2)
    relays((backward, 2))
    forward_add(0)
    forward_add(1)
    down_quarter(1)
    relays((backward, 3))
    forward_block(order(3))
    up_quarter(3)
    down_quarter(3)
    forward_add(2)
    forward_add(3)
    for part in range(parts):
        span = spans[part]
        chain_copy(z, z, z, 0, part).wait_recv()
        back_out[span, :] = partial[0, z, span, :].astype(jnp.float32) + chain_in[z, span, :].astype(jnp.float32)

        @pl.when(inner == 1)
        def _():
            chain_copy(z, 4, z, 0, part).wait_recv()
            back_out[span, :] = back_out[span, :] + chain_in[4, span, :].astype(jnp.float32)

    ends = (
        (up_copy(0), up_low, 2, up_in, 0, weights_out.at[0]),
        (up_copy(1), up_low, 3, up_in, 1, weights_kept.at[0]),
        (down_copy(0), down_low, 1, down_in, 0, weights_out.at[1]),
        (down_copy(2), down_low, 3, down_in, 2, weights_kept.at[1]),
    )
    for made, mine, j, other, slot, target in ends:
        made.wait()
        target[...] = mine[j]
        add(target, other.at[slot])

    for at in range(4):
        row_copy(at).wait_send()
        cot_copy(at).wait_send()
        pair_copy(at).wait_send()
        for part in range(2):

            @pl.when((at <= z) & (z < 3))
            def _():
                half_copy(0, at, part).wait_send()

            @pl.when((at >= z) & (z > 0))
            def _():
                half_copy(1, at, part).wait_send()

    for part in range(parts):

        @pl.when(inner == 0)
        def _():
            chain_copy(z, 0, z, 0, part).wait_send()

        @pl.when(inner == 1)
        def _():
            chain_copy(z, 0, z, 2, part).wait_send()

        chain_copy(z, 0, z, 1, part).wait_send()
        chain_copy(z, 0, z, 3, part).wait_send()

def expert_kernel_visit(sent, cot_line, up, down):
    tokens = sent.shape[0]
    experts, _, hidden = up.shape
    wide = experts * hidden
    low = jnp.bfloat16
    vmem = pl.BlockSpec(memory_space=pltpu.VMEM)
    dma = pltpu.SemaphoreType.DMA
    f32 = jnp.float32
    return pl.pallas_call(
        visit_kernel,
        out_shape=[
            jax.ShapeDtypeStruct((tokens, D + 128), f32),
            jax.ShapeDtypeStruct((2, wide, D // 4), low),
            jax.ShapeDtypeStruct((2, wide, D // 4), low),
            jax.ShapeDtypeStruct((4, tokens, D), low),
        ],
        in_specs=[vmem] + [pl.BlockSpec(memory_space=pl.ANY)] * 3,
        out_specs=[vmem] * 4,
        scratch_shapes=[
            pltpu.VMEM((4, tokens, D), low),
            pltpu.VMEM((experts, D, hidden), low),
            pltpu.VMEM((wide, D), low),
            pltpu.VMEM((8, tokens, D + 128), low),
            pltpu.VMEM((4, tokens, D), low),
            pltpu.VMEM((D, wide), low),
            pltpu.VMEM((128, wide), low),
            pltpu.VMEM((tokens, D), low),
            pltpu.VMEM((8, tokens, wide), low),
            pltpu.VMEM((tokens, wide), low),
            pltpu.VMEM((4, tokens, D), low),
            pltpu.VMEM((4, tokens, D), low),
            pltpu.VMEM((wide, 8 * tokens), low),
            pltpu.VMEM((wide, 8 * tokens), low),
            pltpu.VMEM((2, 4, tokens, D + 128), low),
            pltpu.VMEM((4, tokens, D + 128), low),
            pltpu.VMEM((5, tokens, D + 128), low),
            pltpu.VMEM((4, wide, D // 4), low),
            pltpu.VMEM((4, wide, D // 4), low),
            pltpu.VMEM((3, wide, D // 4), low),
            pltpu.VMEM((3, wide, D // 4), low),
            dma((3,)), dma((4,)), dma((4,)), dma((2, 4, 2)), dma((4, 2)), dma((4,)), dma((4,)), dma((4,)), dma((4,)), dma((4,)), dma((4,)), dma((4, 4)), dma((5, 4)), dma((2, 3)), dma((2, 3)),
        ],
        compiler_params=pltpu.CompilerParams(collective_id=2, has_side_effects=True, vmem_limit_bytes=58 * 2**20),
        name="expert_visit",
    )(sent, cot_line, up, down.reshape(wide, D))


def attend_kernel(
    expert_total, lengths, hidden, cot, value_pick, output_pick, expert_pick, value_router, output_router, expert_router,
    gain_one, gain_two,
    key_weight_at, value_weight_at, query_weight_at, output_weight_at,
    middle_at, sent_at, normed_one_at, normed_two_at, queries_at, key_value_at, probs_at, value_all_at, attended_at,
    gates_at, slopes_at, cot_line_at, routers_at, gains_at,
    middle, sent, normed_one, normed_two, queries, key_value, probs, value_all, attended,
    gates, slopes, cot_line, routers, gains, routers_full,
    key_weight, value_weight, query_weight, output_weight, mixed, hot_turned, hot,
    fetch, leave, pair_send, pair_recv, cot_send, cot_recv, own_sem,
):
    dp, ex = lax.axis_index("dp"), lax.axis_index("expert")
    z, core = ex // 2, ex % 2
    half = z // 2
    inner = z + half * (3 - 2 * z)
    count = hidden.shape[0]
    width = HEADS * HEAD_DIM
    low = jnp.bfloat16
    length = lengths[0]
    spread = HEADS * VE
    total = expert_total
    weights = [
        pltpu.make_async_copy(source, target, fetch.at[i])
        for i, (source, target) in enumerate(
            (
                (key_weight_at, key_weight),
                (value_weight_at, value_weight),
                (query_weight_at, query_weight),
                (output_weight_at, output_weight),
            )
        )
    ]
    for made in weights:
        made.start()
    results = (
        (middle, middle_at), (sent, sent_at), (normed_one, normed_one_at), (normed_two, normed_two_at),
        (queries, queries_at), (key_value, key_value_at), (probs, probs_at), (value_all, value_all_at),
        (attended, attended_at), (gates, gates_at), (slopes, slopes_at), (cot_line, cot_line_at),
        (routers, routers_at), (gains, gains_at),
    )
    leaving = [pltpu.make_async_copy(source, target, leave.at[i]) for i, (source, target) in enumerate(results)]

    def at_z(place):
        return (dp, place * 2 + core)

    barrier = pltpu.get_barrier_semaphore()
    for k in (1, 2, 3):
        pl.semaphore_signal(barrier, inc=1, device_id=((dp + k) % 4, ex), device_id_type=MESH)

    @pl.when(z < 3)
    def _():
        pl.semaphore_signal(barrier, inc=1, device_id=at_z(z + 1), device_id_type=MESH)

    @pl.when(z > 0)
    def _():
        pl.semaphore_signal(barrier, inc=1, device_id=at_z(z - 1), device_id_type=MESH)

    pl.semaphore_wait(barrier, 4 + inner)

    def cot_copy(way, at, source=None):
        block = cot_line.at[at]
        return pltpu.make_async_remote_copy(
            src_ref=block if source is None else source, dst_ref=block,
            send_sem=cot_send.at[way, at], recv_sem=cot_recv.at[at],
            device_id=at_z(z + 1 - 2 * way), device_id_type=MESH,
        )

    def pass_on(distance):
        @pl.when(z >= distance)
        def _():
            cot_copy(0, z - distance).wait_recv()

        @pl.when((z >= distance) & (z < 3))
        def _():
            cot_copy(0, z - distance).start()

        @pl.when(z + distance <= 3)
        def _():
            cot_copy(1, z + distance).wait_recv()

        @pl.when((z + distance <= 3) & (z > 0))
        def _():
            cot_copy(1, z + distance).start()

    @pl.when(z < 3)
    def _():
        cot_copy(0, z, cot).start()

    @pl.when(z > 0)
    def _():
        cot_copy(1, z, cot).start()

    keep = pltpu.make_async_copy(cot, cot_line.at[z], own_sem)
    keep.start()

    def norm(field, gain):
        center = field - jnp.mean(field, axis=-1, keepdims=True)
        spread = jnp.mean(center * center, axis=-1, keepdims=True)
        return (center * lax.rsqrt(spread + EPSILON) * gain).astype(low)

    parts = (pl.ds(0, width), pl.ds(width, width))

    def pair_copy(step, part, block):
        return pltpu.make_async_remote_copy(
            src_ref=key_value.at[block, :, parts[part]], dst_ref=key_value.at[block, :, parts[part]],
            send_sem=pair_send.at[step, part], recv_sem=pair_recv.at[block, part],
            device_id=((dp + step) % 4, ex), device_id_type=MESH,
        )

    def send_part(part):
        for step in (1, 2, 3):

            @pl.when(dp + step < 4)
            def _():
                pair_copy(step, part, dp).start()

    gains[0:1, :] = gain_one[...].astype(jnp.float32).reshape(1, D)
    gains[1:2, :] = gain_two[...].astype(jnp.float32).reshape(1, D)
    normed_one[...] = norm(hidden[...].astype(jnp.float32), gains[0:1, :])
    leaving[2].start()
    weights[0].wait()
    key_value[dp, :, parts[0]] = jnp.dot(
        normed_one[...], key_weight[...], preferred_element_type=jnp.float32
    ).astype(low)
    send_part(0)

    routers_full[...] = jnp.zeros(routers_full.shape, jnp.float32)
    routers_full[0:spread, :] = value_router[...].astype(jnp.float32)
    routers_full[spread : 2 * spread, :] = output_router[...].astype(jnp.float32)
    routers_full[2 * spread : 2 * spread + total, :] = expert_router[...].astype(jnp.float32)
    routers[...] = routers_full[...].astype(low)
    leaving[12].start()
    leaving[13].start()
    hot_turned[...] = jnp.zeros(hot_turned.shape, jnp.float32)

    def mark(picks, base, size):
        place = lax.broadcasted_iota(jnp.int32, (size, count), 0)
        found = jnp.zeros((size, count), jnp.float32)
        for pick in picks:
            found = jnp.where(place == pick, 1.0, found)
        hot_turned[base : base + size, :] = found

    mark([value_pick[h, i : i + 1, :] + h * VE for h in range(HEADS) for i in range(value_pick.shape[1])], 0, spread)
    mark(
        [output_pick[h, i : i + 1, :] + h * VE for h in range(HEADS) for i in range(output_pick.shape[1])],
        spread,
        spread,
    )
    mark([expert_pick[i : i + 1, :] for i in range(expert_pick.shape[0])], 2 * spread, total)
    hot[...] = hot_turned[...].T
    sig = jax.nn.sigmoid(dot_last(normed_one[...], routers[...]))
    gates[...] = sig * hot[...]
    slopes[...] = gates[...] * (1.0 - sig)
    weights[1].wait()

    def values(n, carry):
        span = pl.ds(pl.multiple_of(n * 256, 256), 256)
        value_all[:, span] = jnp.dot(
            hidden[...], value_weight[:, span], preferred_element_type=jnp.float32
        ).astype(low)
        return carry

    lax.fori_loop(0, HEADS * VE * HEAD_DIM // 256, values, 0)
    leaving[7].start()
    for h in range(HEADS):
        row = jnp.zeros((count, HEAD_DIM), jnp.float32)
        for e in range(h * VE, (h + 1) * VE):
            row += gates[:, e : e + 1] * value_all[:, e * HEAD_DIM : (e + 1) * HEAD_DIM].astype(jnp.float32)
        key_value[dp, :, width + h * HEAD_DIM : width + (h + 1) * HEAD_DIM] = row.astype(low)
    send_part(1)

    weights[2].wait()
    queries[...] = jnp.dot(normed_one[...], query_weight[...], preferred_element_type=jnp.float32).astype(low)
    leaving[4].start()
    for block in range(4):

        @pl.when(block > dp)
        def _():
            key_value[block] = jnp.zeros((count, 2 * width), low)

    pass_on(1)

    def wait_part(part):
        for block in range(3):

            @pl.when(block < dp)
            def _():
                pair_copy(1, part, block).wait_recv()

    wait_part(0)
    pair_all = key_value.reshape(4 * count, 2 * width)
    query_pos = dp * count + lax.broadcasted_iota(jnp.int32, (count, 4 * count), 0)
    key_pos = lax.broadcasted_iota(jnp.int32, (count, 4 * count), 1)
    allowed = (key_pos <= query_pos) & (key_pos < length)

    def score(h, carry):
        span = pl.ds(pl.multiple_of(h * HEAD_DIM, HEAD_DIM), HEAD_DIM)
        raw = dot_last(queries[:, span], pair_all[:, span])
        scores = jnp.where(allowed, raw * HEAD_DIM ** (-0.5), NEGATIVE)
        terms = jnp.exp(scores - jnp.max(scores, axis=-1, keepdims=True))
        probs[h] = (terms * (1.0 / jnp.sum(terms, axis=-1, keepdims=True))).astype(low)
        return carry

    lax.fori_loop(0, HEADS, score, 0)
    leaving[6].start()
    leaving[9].start()
    pass_on(2)
    wait_part(1)
    leaving[5].start()

    def collect(h, carry):
        span = pl.ds(pl.multiple_of(h * HEAD_DIM, HEAD_DIM), HEAD_DIM)
        value_span = pl.ds(pl.multiple_of(width + h * HEAD_DIM, HEAD_DIM), HEAD_DIM)
        attended[:, span] = jnp.dot(probs[h], pair_all[:, value_span], preferred_element_type=jnp.float32)
        return carry

    lax.fori_loop(0, HEADS, collect, 0)
    leaving[8].start()
    for h in range(HEADS):
        row = attended[:, h * HEAD_DIM : (h + 1) * HEAD_DIM]
        for e in range(h * VE, (h + 1) * VE):
            mixed[:, e * HEAD_DIM : (e + 1) * HEAD_DIM] = (gates[:, spread + e : spread + e + 1] * row).astype(low)

    place = dp * count + lax.broadcasted_iota(jnp.int32, (count, 1), 0)
    live = jnp.where(place < length, 1.0, 0.0)
    weights[3].wait()

    def outward(n, carry):
        span = pl.ds(pl.multiple_of(n * 256, 256), 256)
        branch = jnp.dot(mixed[...], output_weight[:, span], preferred_element_type=jnp.float32)
        middle[:, span] = hidden[:, span].astype(jnp.float32) + live * branch
        return carry

    lax.fori_loop(0, D // 256, outward, 0)
    leaving[0].start()
    sent[:, :D] = middle[...].astype(low)
    normed_two[...] = norm(middle[...], gains[1:2, :])
    sig = jax.nn.sigmoid(dot_last(normed_two[...], routers[...]))
    gate = sig * hot[...] * live
    sent[:, D:] = gate.astype(low)
    lane = lax.broadcasted_iota(jnp.int32, (count, 128), 1)
    slopes[...] = jnp.where(lane < 2 * spread, slopes[...], gate * (1.0 - sig))

    for i in (1, 3, 10):
        leaving[i].start()
    pass_on(3)
    keep.wait()
    leaving[11].start()
    for part in range(2):
        for step in (1, 2, 3):

            @pl.when(dp + step < 4)
            def _():
                pair_copy(step, part, dp).wait_send()

    for at in range(4):

        @pl.when((at <= z) & (z < 3))
        def _():
            cot_copy(0, at).wait_send()

        @pl.when((at >= z) & (z > 0))
        def _():
            cot_copy(1, at).wait_send()

    for made in leaving:
        made.wait()


def attend(total, lengths, *operands):
    count = operands[0].shape[0]
    low, full = jnp.bfloat16, jnp.float32
    vmem = pl.BlockSpec(memory_space=pltpu.VMEM)
    anywhere = pl.BlockSpec(memory_space=pl.ANY)
    dma = pltpu.SemaphoreType.DMA
    width, wide = HEADS * HEAD_DIM, HEADS * VE * HEAD_DIM
    shapes = [
        ((count, D), full),
        ((count, D + 128), low),
        ((count, D), low),
        ((count, D), low),
        ((count, width), low),
        ((4, count, 2 * width), low),
        ((HEADS, count, 4 * count), low),
        ((count, wide), low),
        ((count, width), full),
        ((count, 128), full),
        ((count, 128), full),
        ((4, count, D), low),
        ((128, D), low),
        ((2, D), full),
    ]
    return pl.pallas_call(
        functools.partial(attend_kernel, total),
        out_shape=[jax.ShapeDtypeStruct(*shape) for shape in shapes],
        in_specs=[pl.BlockSpec(memory_space=pltpu.SMEM)] + [vmem] * (len(operands) - 4) + [anywhere] * 4,
        out_specs=[anywhere] * len(shapes),
        scratch_shapes=[pltpu.VMEM(*shape) for shape in shapes]
        + [pltpu.VMEM((128, D), full)]
        + [pltpu.VMEM(a.shape, a.dtype) for a in operands[-4:]]
        + [
            pltpu.VMEM((count, wide), low),
            pltpu.VMEM((128, count), full),
            pltpu.VMEM((count, 128), full),
            dma((4,)),
            dma((len(shapes),)),
            dma((4, 2)),
            dma((4, 2)),
            dma((2, 4)),
            dma((4,)),
            dma,
        ],
        compiler_params=pltpu.CompilerParams(
            collective_id=1, has_side_effects=True, vmem_limit_bytes=58 * 2**20
        ),
        name="attend",
    )(lengths, *operands)


def backward_kernel(
    total_experts, lengths, gates, slopes, routers, gains,
    weights_at, forward_at, returned_at, middle_at, cot_at, hidden_at, normed_one_at, queries_at, key_value_at, probs_at, value_all_at,
    attended_at, normed_two_at, query_weight_at, key_weight_at, value_weight_at, output_weight_at,
    block_out, grad_in, out_query, out_key, out_value, out_output, out_small, weights_in,
    weights, forward, returned, middle, cot, hidden, normed_one, queries, key_value, probs, value_all,
    attended, normed_two, query_weight, key_weight, value_part, output_part,
    branch, branch_turned, one_turned, hidden_turned, grad_att, grad_query, leave, arrive, grad_key,
    grad_each, grad_middle, logit_one, logit_two, small_turned, mixed,
    grads, grads_small, core_in, plane_in, last_in, forward_in,
    fetch, part_fetch, leave_send, leave_recv, send, recv, forward_send, forward_recv, weights_send, weights_recv,
):
    dp, ex = lax.axis_index("dp"), lax.axis_index("expert")
    y, x, z, core = dp // 2, dp % 2, ex // 2, ex % 2
    count = hidden.shape[0]
    width = HEADS * HEAD_DIM
    low, full = jnp.bfloat16, jnp.float32
    length = lengths[0]
    sibling = (dp, z * 2 + 1 - core)
    beside = (y * 2 + 1 - x, ex)
    behind = ((1 - y) * 2 + x, ex)
    across = ((1 - y) * 2 + 1 - x, ex)
    line = [(dp, ((z + k) % 4) * 2 + core) for k in (1, 2, 3)]
    barrier = pltpu.get_barrier_semaphore()
    for place in (sibling, beside, behind, across, *line):
        pl.semaphore_signal(barrier, inc=1, device_id=place, device_id_type=MESH)

    held = dict(
        weights=(weights_at, weights),
        forward=(forward_at, forward),
        returned=(returned_at, returned),
        middle=(middle_at, middle),
        cot=(cot_at, cot),
        hidden=(hidden_at, hidden),
        attended=(attended_at, attended),
        key_value=(key_value_at, key_value),
        probs=(probs_at, probs),
        queries=(queries_at, queries),
        normed_one=(normed_one_at, normed_one),
        query_weight=(query_weight_at, query_weight),
        value_all=(value_all_at, value_all),
        key_weight=(key_weight_at, key_weight),
        normed_two=(normed_two_at, normed_two),
    )
    got = {
        name: pltpu.make_async_copy(source, target, fetch.at[i])
        for i, (name, (source, target)) in enumerate(held.items())
    }

    def output_copy(n):
        return pltpu.make_async_copy(
            output_weight_at.at[pl.ds(n * PIECE, PIECE)], output_part.at[n % 2], part_fetch.at[0, n % 2]
        )

    def value_copy(n):
        return pltpu.make_async_copy(
            value_weight_at.at[:, pl.ds(n * PIECE, PIECE)], value_part.at[n % 2], part_fetch.at[1, n % 2]
        )

    first_held = ("weights", "forward", "returned", "middle", "cot", "hidden")
    for name in first_held:
        got[name].start()
    for n in range(2):
        output_copy(n).start()
    for name in held:
        if name not in first_held:
            got[name].start()
    for n in range(2):
        value_copy(n).start()

    pieces = (
        [(out_output, PIECE * n, PIECE, n) for n in range(HEADS)]
        + [(out_query, 0, width, 4)]
        + [(out_value, PIECE * n, PIECE, n) for n in range(HEADS)]
        + [(out_key, 0, width, 5), (out_small, 0, 128, None)]
    )
    along_line = (0, 1)
    in_plane = [i for i in range(len(pieces)) if i not in along_line]
    x_first = {i: n % 2 == 0 for n, i in enumerate(in_plane)}

    def remote(source, target, slot, place):
        return pltpu.make_async_remote_copy(
            src_ref=source, dst_ref=target, send_sem=send.at[slot], recv_sem=recv.at[slot],
            device_id=place, device_id_type=MESH,
        )

    def add(target, source):
        target[...] = (target[...].astype(full) + source[...].astype(full)).astype(target.dtype)

    def own(i):
        slot = pieces[i][3]
        return grads_small if slot is None else grads.at[slot, :, :, :, :, columns(i)]

    def columns(i):
        return pl.ds(0, pieces[i][2])

    started = {}

    def begin(key, source, target, slot, place):
        started[key] = remote(source, target, slot, place)
        started[key].start()

    def halve_core(i):
        begin((i, 0), own(i).at[:, :, 1 - core], core_in.at[i, :, :, :, columns(i)], (i, 0), sibling)

    def halve_near(i):
        span = columns(i)
        started[i, 0].wait()
        add(core_in.at[i, :, :, :, span], own(i).at[:, :, core])
        if i in along_line:
            for k in (1, 2, 3):
                begin(
                    (i, k), core_in.at[i, :, (z + k) % 4, :, span],
                    plane_in.at[i, pl.ds(4 * k - 4, 4), :, span], (i, k), line[k - 1],
                )
            return
        for part in range(2):
            if x_first[i]:
                source = core_in.at[i, part * 2 + 1 - x, :, :, span]
            else:
                source = core_in.at[i, (1 - y) * 2 + part, :, :, span]
            target = plane_in.at[i, pl.ds(part * 4, 4), :, span]
            begin((i, 1 + part), source, target, (i, 1 + part), beside if x_first[i] else behind)

    def halve_far(i):
        span = columns(i)
        if i in along_line:
            held = core_in.at[i, :, z, :, span]
            for k in (1, 2, 3):
                started[i, k].wait()
                add(held, plane_in.at[i, pl.ds(4 * k - 4, 4), :, span])
            for part in range(2):
                begin(
                    (i, 4 + part), core_in.at[i, part * 2 + 1 - x, z, :, span],
                    last_in.at[i, part, :, span], (i, 4 + part), beside,
                )
            return
        for part in range(2):
            started[i, 1 + part].wait()
            kept = part * 2 + x if x_first[i] else y * 2 + part
            add(plane_in.at[i, pl.ds(part * 4, 4), :, span], core_in.at[i, kept, :, :, span])
        other = 1 - y if x_first[i] else 1 - x
        begin(
            (i, 3), plane_in.at[i, pl.ds(other * 4, 4), :, span], plane_in.at[i, pl.ds(8, 4), :, span],
            (i, 3), behind if x_first[i] else beside,
        )

    def spread(i):
        span = columns(i)
        if i in along_line:
            for part in range(2):
                started[i, 4 + part].wait()
                add(last_in.at[i, part, :, span], core_in.at[i, part * 2 + x, z, :, span])
            begin((i, 6), last_in.at[i, 1 - y, :, span], last_in.at[i, 2, :, span], (i, 6), behind)
            return
        started[i, 3].wait()
        add(plane_in.at[i, pl.ds(8, 4), :, span], plane_in.at[i, pl.ds((y if x_first[i] else x) * 4, 4), :, span])
        for k in (1, 2, 3):
            begin(
                (i, 3 + k), plane_in.at[i, 8 + (z + k) % 4, :, span],
                last_in.at[i, k - 1, :, span], (i, 3 + k), line[k - 1],
            )

    def finish(i):
        out, start, size, _ = pieces[i]
        span = columns(i)
        if i in along_line:
            started[i, 6].wait()
            total = last_in[i, y, :, span].astype(full) + last_in[i, 2, :, span].astype(full)
        else:
            total = plane_in[i, 8 + z, :, span].astype(full)
            for k in (1, 2, 3):
                started[i, 3 + k].wait()
                total = total + last_in[i, k - 1, :, span].astype(full)
        out[:, pl.ds(start, size)] = total

    rows_each = 64
    lane = lax.broadcasted_iota(jnp.int32, (1, 128), 1)
    for name in first_held:
        got[name].wait()
    logit_two[...] = (returned[:, D:] * slopes[...]).astype(low)

    half = z // 2
    inner = z + half * (3 - 2 * z)
    onward = 1 - 2 * half
    nearest = (z + onward, z + onward, z + onward, 0)
    farthest = (3 * (1 - half), 3 * (1 - half), z + onward, 1)
    backward = (3 * half, 3 * half, z - onward, 2)
    next_one = (2 - half, 2 - half + inner * (2 + half), z + onward, 3)

    def forward_copy(dest, slot, to, stage, part):
        span = pl.ds(part * (count // 2), count // 2)
        return pltpu.make_async_remote_copy(
            src_ref=forward.at[dest, span], dst_ref=forward_in.at[slot, span],
            send_sem=forward_send.at[stage, part], recv_sem=forward_recv.at[slot, part],
            device_id=(dp, to * 2 + core), device_id_type=MESH,
        )

    def relays(*ways):
        @pl.when(inner == 1)
        def _():
            for (dest, slot, to, stage), part in ways:
                span = pl.ds(part * (count // 2), count // 2)
                forward_copy(dest, dest, to, stage, part).wait_recv()
                add(forward.at[dest, span], forward_in.at[dest, span])
                forward_copy(dest, slot, to, stage, part).start()

    pl.semaphore_wait(barrier, 7)
    weight_copies = [
        pltpu.make_async_remote_copy(
            src_ref=weights.at[i], dst_ref=weights_in.at[i], send_sem=weights_send.at[i],
            recv_sem=weights_recv.at[i], device_id=place, device_id_type=MESH,
        )
        for i, place in enumerate((behind, beside))
    ]
    for made in weight_copies:
        made.start()

    @pl.when(inner == 0)
    def _():
        for way in (farthest, next_one, nearest):
            for part in range(2):
                forward_copy(*way, part).start()

    def live_rows(start):
        place = dp * count + start + lax.broadcasted_iota(jnp.int32, (rows_each, 1), 0)
        return jnp.where(place < length, 1.0, 0.0)

    def norm_back(field, grad, gain):
        center = field - jnp.mean(field, axis=-1, keepdims=True)
        scale = lax.rsqrt(jnp.mean(center * center, axis=-1, keepdims=True) + EPSILON)
        unit = center * scale
        part = grad * gain
        back = scale * (
            part
            - jnp.mean(part, axis=-1, keepdims=True)
            - unit * jnp.mean(part * unit, axis=-1, keepdims=True)
        )
        return back, jnp.sum(grad * unit, axis=0, keepdims=True)

    def first_rows(n, gain_sum):
        start = pl.multiple_of(n * rows_each, rows_each)
        rows = pl.ds(start, rows_each)
        grad = jnp.dot(logit_two[rows, :], routers[...], preferred_element_type=full)
        back, gain_part = norm_back(middle[rows, :], grad, gains[1:2, :])
        total = cot[rows, :].astype(full) + returned[rows, :D] + back
        grad_middle[rows, :] = total
        branch[rows, :] = (live_rows(start) * total).astype(low)
        return gain_sum + gain_part

    gain_two_sum = lax.fori_loop(0, count // rows_each, first_rows, jnp.zeros((1, D), full))
    relays((farthest, 0))

    def square(field, live, at):
        total = jnp.sum(jnp.sum(field * field, axis=1, keepdims=True) * live, axis=0, keepdims=True)
        return jnp.where(lane == at, total, 0.0)

    def last_rows(n, sums):
        start = pl.multiple_of(n * rows_each, rows_each)
        rows = pl.ds(start, rows_each)
        live = live_rows(start)
        field = middle[rows, :]
        step = forward[z, rows, :].astype(full)
        final = field + step
        block_out[rows, :] = final.astype(low)
        source = hidden[rows, :].astype(full)
        one = jnp.ones((rows_each, 1), full)
        sums += square(source, live, 0) + square(field - source, one, 1)
        sums += square(step, one, 2) + square(final, live, 3)
        return sums + jnp.where(lane == 4, jnp.sum(live, axis=0, keepdims=True), 0.0)

    def output_rows():
        for part in range(2):
            span = pl.ds(part * (count // 2), count // 2)
            forward_copy(z, z, z, 0, part).wait_recv()
            add(forward.at[z, span], forward_in.at[z, span])

            @pl.when(inner == 1)
            def _():
                forward_copy(z, 4, z, 0, part).wait_recv()
                add(forward.at[z, span], forward_in.at[4, span])

        sums = lax.fori_loop(0, count // rows_each, last_rows, jnp.zeros((1, 128), full))
        return sums

    def weight_grad(i, turned, right):
        def some(n, carry):
            rows = pl.ds(pl.multiple_of(n * 256, 256), 256)
            value = jnp.dot(turned[rows, :], right, preferred_element_type=full).astype(low)
            own(i)[n] = value.reshape(4, 2, ROWS, pieces[i][2])
            return carry

        lax.fori_loop(0, D // 256, some, 0)
        halve_core(i)

    got["attended"].wait()
    spread_count = HEADS * VE

    def head_of(c):
        return slice((c // VE) * HEAD_DIM, (c // VE + 1) * HEAD_DIM)

    logit_one[...] = jnp.zeros(logit_one.shape, full)
    grad_att[...] = jnp.zeros(grad_att.shape, full)
    for n in range(HEADS):
        output_copy(n).wait()
        for j in range(VE):
            c = VE * n + j
            grad_mixed = dot_last(branch[...], output_part[n % 2, j * HEAD_DIM : (j + 1) * HEAD_DIM, :])
            col = spread_count + c
            grad_att[:, head_of(c)] += gates[:, col : col + 1] * grad_mixed
            dots = jnp.sum(attended[:, head_of(c)] * grad_mixed, axis=1, keepdims=True)
            logit_one[:, col : col + 1] = dots * slopes[:, col : col + 1]
        if n + 2 < HEADS:
            output_copy(n + 2).start()
    relays((farthest, 1), (backward, 0))

    pair_all = key_value.reshape(4 * count, 2 * width)
    for name in ("key_value", "probs", "queries"):
        got[name].wait()

    def leave_copy(k, h):
        rows = pl.ds(h * 2 * HEAD_DIM, 2 * HEAD_DIM)
        return pltpu.make_async_remote_copy(
            src_ref=leave.at[(dp + 4 - k) % 4, rows], dst_ref=arrive.at[k - 1, rows],
            send_sem=leave_send.at[k - 1, h], recv_sem=leave_recv.at[k - 1, h],
            device_id=((dp + 4 - k) % 4, ex), device_id_type=MESH,
        )

    def head(h, carry):
        start = pl.multiple_of(h * HEAD_DIM, HEAD_DIM)
        span = pl.ds(start, HEAD_DIM)
        grad = grad_att[:, span].astype(low)
        prob = probs[h].astype(full)
        grad_prob = dot_last(grad, pair_all[:, pl.ds(width + start, HEAD_DIM)])
        dots = jnp.sum(prob * grad_prob, axis=-1, keepdims=True)
        grad_score = (prob * (grad_prob - dots) * HEAD_DIM ** (-0.5)).astype(low)
        grad_query[:, span] = jnp.dot(grad_score, pair_all[:, span], preferred_element_type=full).astype(low)
        key_part = dot_first(queries[:, span], grad_score).astype(low)
        value_part_all = dot_first(grad, probs[h]).astype(low)
        key_rows = pl.ds(pl.multiple_of(2 * h * HEAD_DIM, 2 * HEAD_DIM), HEAD_DIM)
        value_rows = pl.ds(pl.multiple_of((2 * h + 1) * HEAD_DIM, HEAD_DIM), HEAD_DIM)
        for j in range(4):
            leave[j, key_rows, :] = key_part[:, j * count : (j + 1) * count]
            leave[j, value_rows, :] = value_part_all[:, j * count : (j + 1) * count]
        for k in (1, 2, 3):

            @pl.when(dp >= k)
            def _():
                leave_copy(k, h).start()

        return carry

    lax.fori_loop(0, HEADS, head, 0)

    relays((backward, 1), (next_one, 0), (next_one, 1))
    branch_turned[...] = branch[...].T
    for n in range(HEADS):
        for j in range(VE):
            c = VE * n + j
            gate = gates[:, spread_count + c : spread_count + c + 1]
            mixed[:, j * HEAD_DIM : (j + 1) * HEAD_DIM] = (gate * attended[:, head_of(c)]).astype(low)
        weight_grad(n, branch_turned, mixed[...])
        if n:
            halve_near(n - 1)
    for name in ("normed_one", "query_weight"):
        got[name].wait()
    one_turned[...] = normed_one[...].T
    weight_grad(4, one_turned, grad_query[...])
    halve_near(3)
    hidden_turned[...] = hidden[...].T
    returned[:, :D] = dot_last(grad_query[...], query_weight[...])
    halve_near(4)
    got["value_all"].wait()

    for h in range(HEADS):
        rows = pl.ds(h * 2 * HEAD_DIM, 2 * HEAD_DIM)
        total = leave[dp, rows, :].astype(full)
        for k in (1, 2, 3):

            @pl.when(dp + k < 4)
            def _():
                leave_copy(k, h).wait_recv()

            @pl.when(dp + k >= 4)
            def _():
                arrive[k - 1, rows, :] = jnp.zeros((2 * HEAD_DIM, count), low)

            total += arrive[k - 1, rows, :].astype(full)
        turned = total.T
        grad_key[:, h * HEAD_DIM : (h + 1) * HEAD_DIM] = turned[:, :HEAD_DIM].astype(low)
        grad = turned[:, HEAD_DIM:].astype(low).astype(full)
        for c in range(h * VE, (h + 1) * VE):
            here = slice(c * HEAD_DIM, (c + 1) * HEAD_DIM)
            grad_each[:, here] = (gates[:, c : c + 1] * grad).astype(low)
            dots = jnp.sum(value_all[:, here].astype(full) * grad, axis=1, keepdims=True)
            logit_one[:, c : c + 1] = dots * slopes[:, c : c + 1]
        weight_grad(5 + h, hidden_turned, grad_each[:, h * PIECE : (h + 1) * PIECE])
        if h:
            halve_near(4 + h)
    weight_grad(9, one_turned, grad_key[...])
    halve_near(8)
    got["key_weight"].wait()
    returned[:, :D] += dot_last(grad_key[...], key_weight[...])
    halve_near(9)
    halve_far(2)
    returned[:, :D] += jnp.dot(logit_one[...].astype(low), routers[...], preferred_element_type=full)

    def first_norm(n, gain_sum):
        rows = pl.ds(pl.multiple_of(n * rows_each, rows_each), rows_each)
        back, gain_part = norm_back(hidden[rows, :].astype(full), returned[rows, :D], gains[0:1, :])
        grad_in[rows, :] = grad_middle[rows, :] + back
        return gain_sum + gain_part

    gain_one_sum = lax.fori_loop(0, count // rows_each, first_norm, jnp.zeros((1, D), full))
    halve_far(3)
    for made in weight_copies:
        made.wait()
    got["normed_two"].wait()
    small_turned[...] = dot_first(logit_one[...].astype(low), normed_one[...]) + dot_first(
        logit_two[...], normed_two[...]
    )
    small_rows = 2 * spread_count + total_experts
    small_turned[small_rows : small_rows + 1, :] = gain_one_sum
    small_turned[small_rows + 1 : small_rows + 2, :] = gain_two_sum
    sums = output_rows()
    for i in range(5):
        small_turned[small_rows + 2 + i : small_rows + 3 + i, :] = jnp.broadcast_to(sums[:, i : i + 1], (1, D))
    grads_small[...] = small_turned[...].T.astype(low).reshape(grads_small.shape)
    halve_core(10)
    spread(2)
    halve_far(4)
    def value_side(n):
        value_copy(n).wait()
        grad_in[...] += dot_last(grad_each[:, n * PIECE : (n + 1) * PIECE], value_part[n % 2])
        if n + 2 < HEADS:
            value_copy(n + 2).start()

    for action, i in (
        (halve_near, 10), (spread, 3),
        (value_side, 0), (halve_far, 5), (halve_far, 0), (spread, 4), (finish, 2),
        (value_side, 1), (halve_far, 6), (spread, 0), (finish, 3), (spread, 5),
        (value_side, 2), (halve_far, 7), (finish, 4), (spread, 6),
        (value_side, 3), (finish, 0), (halve_far, 1), (halve_far, 8), (finish, 5), (spread, 7),
        (spread, 1), (halve_far, 9), (finish, 6), (spread, 8), (halve_far, 10), (finish, 7), (finish, 1), (spread, 9),
        (spread, 10), (finish, 8), (finish, 9), (finish, 10),
    ):
        action(i)
    for h in range(HEADS):
        for k in (1, 2, 3):

            @pl.when(dp >= k)
            def _():
                leave_copy(k, h).wait_send()

    for part in range(2):
        forward_copy(z, 0, z, 1, part).wait_send()
        forward_copy(z, 0, z, 3, part).wait_send()

        @pl.when(inner == 0)
        def _():
            forward_copy(z, 0, z, 0, part).wait_send()

        @pl.when(inner == 1)
        def _():
            forward_copy(z, 0, z, 2, part).wait_send()


def backward(total_experts, lengths, gates, slopes, routers, gains, *arrays):
    low, full = jnp.bfloat16, jnp.float32
    count = gates.shape[0]
    width, wide = HEADS * HEAD_DIM, HEADS * VE * HEAD_DIM
    vmem = pl.BlockSpec(memory_space=pltpu.VMEM)
    anywhere = pl.BlockSpec(memory_space=pl.ANY)
    dma = pltpu.SemaphoreType.DMA
    whole = [pltpu.VMEM(a.shape, a.dtype) for a in arrays[:15]]
    n = 11
    return pl.pallas_call(
        functools.partial(backward_kernel, total_experts),
        out_shape=[
            jax.ShapeDtypeStruct((count, D), low),
            jax.ShapeDtypeStruct((count, D), full),
            jax.ShapeDtypeStruct((ROWS, width), full),
            jax.ShapeDtypeStruct((ROWS, width), full),
            jax.ShapeDtypeStruct((ROWS, wide), full),
            jax.ShapeDtypeStruct((ROWS, wide), full),
            jax.ShapeDtypeStruct((ROWS, 128), full),
            jax.ShapeDtypeStruct(arrays[0].shape, low),
        ],
        in_specs=[pl.BlockSpec(memory_space=pltpu.SMEM)] + [vmem] * 4 + [anywhere] * len(arrays),
        out_specs=[vmem] * 8,
        scratch_shapes=whole
        + [
            pltpu.VMEM((2, D, PIECE), low),
            pltpu.VMEM((2, PIECE, D), low),
            pltpu.VMEM((count, D), low),
            pltpu.VMEM((D, count), low),
            pltpu.VMEM((D, count), low),
            pltpu.VMEM((D, count), low),
            pltpu.VMEM((count, width), full),
            pltpu.VMEM((count, width), low),
            pltpu.VMEM((4, 2 * width, count), low),
            pltpu.VMEM((3, 2 * width, count), low),
            pltpu.VMEM((count, width), low),
            pltpu.VMEM((count, wide), low),
            pltpu.VMEM((count, D), full),
            pltpu.VMEM((count, 128), full),
            pltpu.VMEM((count, 128), low),
            pltpu.VMEM((128, D), full),
            pltpu.VMEM((count, PIECE), low),
            pltpu.VMEM((6, 4, 4, 2, ROWS, PIECE), low),
            pltpu.VMEM((4, 4, 2, ROWS, 128), low),
            pltpu.VMEM((n, 4, 4, ROWS, PIECE), low),
            pltpu.VMEM((n, 12, ROWS, PIECE), low),
            pltpu.VMEM((n, 3, ROWS, PIECE), low),
            pltpu.VMEM((5, count, D), low),
            dma((15,)),
            dma((2, 2)),
            dma((3, HEADS)),
            dma((3, HEADS)),
            dma((n, 7)),
            dma((n, 7)),
            dma((4, 2)),
            dma((5, 2)),
            dma((2,)),
            dma((2,)),
        ],
        compiler_params=pltpu.CompilerParams(
            collective_id=3, has_side_effects=True, vmem_limit_bytes=62 * 2**20
        ),
        name="backward",
    )(lengths, gates, slopes, routers, gains, *arrays)


def expert_visit(sent, cotangent, expert_up, expert_down):
    local_experts = expert_up.shape[0]
    group = lax.axis_index("expert")
    cot_all = lax.all_gather(cotangent, "expert", axis=0, tiled=True)
    sent_all = lax.all_gather(sent, "expert", axis=0, tiled=True)
    rows_all = sent_all[:, :D]
    total_experts = sent.shape[1] - D
    gate_all = lax.dynamic_slice_in_dim(
        sent_all[:, D:], group * local_experts, local_experts, 1
    ).astype(jnp.float32).T[:, :, None]
    preact = jnp.einsum("td,xdf->xtf", rows_all, expert_up, preferred_element_type=jnp.float32)
    pre_sig = jax.nn.sigmoid(preact)
    hidden = preact * pre_sig
    back = jnp.einsum("td,xfd->xtf", cot_all, expert_down, preferred_element_type=jnp.float32)
    gate_grad = jnp.sum(hidden * back, axis=2).T
    gated = (gate_all * hidden).astype(jnp.bfloat16)
    grad_pre = (gate_all * back * (pre_sig * (1.0 + preact * (1.0 - pre_sig)))).astype(jnp.bfloat16)
    partial_out = jnp.einsum("xtf,xfd->td", gated, expert_down, preferred_element_type=jnp.float32)
    partial_grad = jnp.einsum("xtf,xdf->td", grad_pre, expert_up, preferred_element_type=jnp.float32)
    wide_grad = lax.dynamic_update_slice_in_dim(
        jnp.zeros((gate_grad.shape[0], total_experts), jnp.bfloat16),
        gate_grad.astype(jnp.bfloat16),
        group * local_experts,
        1,
    )
    returned = lax.psum_scatter(
        jnp.concatenate(
            [partial_out.astype(jnp.bfloat16), partial_grad.astype(jnp.bfloat16), wide_grad], axis=1
        ),
        "expert",
        scatter_dimension=0,
        tiled=True,
    )
    grad_down = jnp.einsum("xtf,td->xfd", gated, cot_all, preferred_element_type=jnp.float32)
    grad_up = jnp.einsum("td,xtf->xdf", rows_all, grad_pre, preferred_element_type=jnp.float32)
    return returned, grad_up, grad_down


def shards(
    hidden_in,
    lengths,
    value_pick,
    output_pick,
    expert_pick,
    query_weight,
    key_weight,
    value_weight,
    output_weight,
    value_router,
    output_router,
    expert_router,
    attention_gain,
    feedforward_gain,
    expert_up,
    expert_down,
    cotangent,
):
    row_count = hidden_in.shape[1]
    total_experts = expert_router.shape[1]
    input_low = hidden_in[0]
    input_full = input_low.astype(jnp.float32)
    length = lengths[0]
    query_pos = lax.axis_index("dp") * row_count + jnp.arange(row_count, dtype=jnp.int32)
    live_mask = (query_pos < length).astype(jnp.float32)[:, None]
    gain_one = attention_gain.astype(jnp.float32)
    gain_two = feedforward_gain.astype(jnp.float32)
    normed_one = layer_norm(input_full, gain_one)
    normed_low = normed_one.astype(jnp.bfloat16)
    queries = low_dot(normed_low, query_weight).astype(jnp.bfloat16)
    key_local = low_dot(normed_low, key_weight).astype(jnp.bfloat16)
    value_sig = jax.nn.sigmoid(low_dot(normed_low, value_router)).reshape(row_count, HEADS, VE)
    value_hot = choose(value_pick[0], VE)
    value_gate = value_sig * value_hot
    value_all = low_dot(input_low, value_weight).reshape(row_count, HEADS, VE, HEAD_DIM)
    value_local = (
        jnp.sum(value_gate[..., None] * value_all, axis=2)
        .astype(jnp.bfloat16)
        .reshape(row_count, HEADS * HEAD_DIM)
    )
    key_all, value_rows = (
        lax.all_gather(key_local, "dp", axis=0, tiled=True),
        lax.all_gather(value_local, "dp", axis=0, tiled=True),
    )
    query_heads = queries.reshape(row_count, HEADS, HEAD_DIM)
    key_heads = key_all.reshape(-1, HEADS, HEAD_DIM)
    value_heads = value_rows.reshape(-1, HEADS, HEAD_DIM)
    soft_probs = attention_probs(query_heads, key_heads, query_pos, length)
    attended = jnp.einsum(
        "hqk,khd->qhd",
        soft_probs.astype(jnp.bfloat16),
        value_heads,
        preferred_element_type=jnp.float32,
    )
    output_sig = jax.nn.sigmoid(low_dot(normed_low, output_router)).reshape(row_count, HEADS, VE)
    output_hot = choose(output_pick[0], VE)
    output_gate = output_sig * output_hot
    mixed = (
        (output_gate[..., None] * attended[:, :, None, :])
        .astype(jnp.bfloat16)
        .reshape(row_count, HEADS * VE * HEAD_DIM)
    )
    attention_out = live_mask * low_dot(mixed, output_weight)
    middle = input_full + attention_out
    normed_two = layer_norm(middle, gain_two)
    normed_two_low = normed_two.astype(jnp.bfloat16)
    router_sig = jax.nn.sigmoid(low_dot(normed_two_low, expert_router))
    hot = jnp.any(
        expert_pick[0][:, :, None] == jnp.arange(total_experts, dtype=jnp.int32), axis=1
    ).astype(jnp.float32)
    picked_hot = hot * live_mask
    expert_gate = router_sig * picked_hot
    middle_low = middle.astype(jnp.bfloat16)
    sent = jnp.concatenate([middle_low, expert_gate.astype(jnp.bfloat16)], axis=1)
    groups = lax.axis_size("expert")
    rounds = max(1, groups // 8)

    def visit(grads, item):
        returned, grad_up, grad_down = expert_visit(*item, expert_up, expert_down)
        return (grads[0] + grad_up, grads[1] + grad_down), returned

    zeros = jnp.zeros(expert_up.shape, jnp.float32), jnp.zeros(expert_down.shape, jnp.float32)
    (up_grad, down_grad), returned = lax.scan(
        visit,
        zeros,
        (
            sent.reshape(rounds, -1, sent.shape[1]),
            cotangent[0].reshape(rounds, -1, D),
        ),
    )
    returned = returned.reshape(row_count, -1).astype(jnp.float32)
    up_grad = lax.psum_scatter(
        up_grad.astype(jnp.bfloat16), "dp", scatter_dimension=1, tiled=True
    ).astype(jnp.float32)
    down_grad = lax.psum_scatter(
        down_grad.astype(jnp.bfloat16), "dp", scatter_dimension=2, tiled=True
    ).astype(jnp.float32)
    feedforward_out = returned[:, :D]
    final_rows = middle + feedforward_out
    sums = jnp.stack(
        [
            jnp.sum(live_mask * input_full * input_full),
            jnp.sum(attention_out * attention_out),
            jnp.sum(feedforward_out * feedforward_out),
            jnp.sum(live_mask * final_rows * final_rows),
            jnp.sum(live_mask),
        ]
    )
    grad_final = cotangent[0].astype(jnp.float32)
    grad_middle = grad_final + returned[:, D : 2 * D]
    grad_logit = (
        returned[:, 2 * D :] * picked_hot * router_sig * (1.0 - router_sig)
    ).astype(jnp.bfloat16)
    grad_expert_router = low_dot(normed_two_low.T, grad_logit)
    grad_normed_two = low_dot(grad_logit, expert_router.T)
    unused_two, norm_two_back = jax.vjp(layer_norm, middle, gain_two)
    grad_middle_norm, grad_gain_two = norm_two_back(grad_normed_two)
    grad_middle = grad_middle + grad_middle_norm
    grad_branch = (live_mask * grad_middle).astype(jnp.bfloat16)
    grad_mixed = jnp.einsum(
        "td,md->tm", grad_branch, output_weight, preferred_element_type=jnp.float32
    ).reshape(row_count, HEADS, VE, HEAD_DIM)
    grad_output_weight = jnp.einsum(
        "td,tm->dm", grad_branch, mixed, preferred_element_type=jnp.float32
    )
    grad_attended = jnp.sum(output_gate[..., None] * grad_mixed, axis=2)
    grad_output_logit = (
        jnp.sum(attended[:, :, None, :] * grad_mixed, axis=3)
        * output_hot
        * output_sig
        * (1.0 - output_sig)
    ).reshape(row_count, HEADS * VE)
    grad_attended_low = grad_attended.astype(jnp.bfloat16)
    grad_probs = jnp.einsum(
        "qhd,khd->hqk", grad_attended_low, value_heads, preferred_element_type=jnp.float32
    )
    row_dot = jnp.sum(soft_probs * grad_probs, axis=-1, keepdims=True)
    grad_scores = (soft_probs * (grad_probs - row_dot) * HEAD_DIM ** (-0.5)).astype(jnp.bfloat16)
    grad_query = (
        jnp.einsum("hqk,khd->qhd", grad_scores, key_heads, preferred_element_type=jnp.float32)
        .astype(jnp.bfloat16)
        .reshape(row_count, HEADS * HEAD_DIM)
    )
    grad_key_all = jnp.einsum(
        "hqk,qhd->khd", grad_scores, query_heads, preferred_element_type=jnp.float32
    ).reshape(-1, HEADS * HEAD_DIM)
    grad_value_rows = jnp.einsum(
        "hqk,qhd->khd",
        soft_probs.astype(jnp.bfloat16),
        grad_attended_low,
        preferred_element_type=jnp.float32,
    ).reshape(-1, HEADS * HEAD_DIM)
    grad_key_sum, grad_value_sum = (
        lax.psum_scatter(
            grad_key_all.astype(jnp.bfloat16), "dp", scatter_dimension=0, tiled=True
        ).astype(jnp.float32),
        lax.psum_scatter(
            grad_value_rows.astype(jnp.bfloat16), "dp", scatter_dimension=0, tiled=True
        ).astype(jnp.float32),
    )
    grad_key = grad_key_sum.astype(jnp.bfloat16)
    grad_value_low = (
        grad_value_sum.astype(jnp.bfloat16)
        .astype(jnp.float32)
        .reshape(row_count, HEADS, 1, HEAD_DIM)
    )
    grad_value_each = (
        (value_gate[..., None] * grad_value_low)
        .astype(jnp.bfloat16)
        .reshape(row_count, HEADS * VE * HEAD_DIM)
    )
    grad_value_logit = (
        jnp.sum(value_all * grad_value_low, axis=3) * value_hot * value_sig * (1.0 - value_sig)
    ).reshape(row_count, HEADS * VE)
    grad_value_weight = jnp.einsum(
        "td,tm->dm", input_low, grad_value_each, preferred_element_type=jnp.float32
    )
    grad_query_weight = jnp.einsum(
        "td,tm->dm", normed_low, grad_query, preferred_element_type=jnp.float32
    )
    grad_key_weight = jnp.einsum(
        "td,tm->dm", normed_low, grad_key, preferred_element_type=jnp.float32
    )
    grad_value_logit = grad_value_logit.astype(jnp.bfloat16)
    grad_output_logit = grad_output_logit.astype(jnp.bfloat16)
    grad_value_router = low_dot(normed_low.T, grad_value_logit)
    grad_output_router = low_dot(normed_low.T, grad_output_logit)
    grad_normed_one = (
        jnp.einsum("tm,dm->td", grad_query, query_weight, preferred_element_type=jnp.float32)
        + jnp.einsum("tm,dm->td", grad_key, key_weight, preferred_element_type=jnp.float32)
        + low_dot(grad_value_logit, value_router.T)
        + low_dot(grad_output_logit, output_router.T)
    )
    unused_one, norm_one_back = jax.vjp(layer_norm, input_full, gain_one)
    grad_input_norm, grad_gain_one = norm_one_back(grad_normed_one)
    grad_input = (
        grad_middle
        + jnp.einsum("tm,dm->td", grad_value_each, value_weight, preferred_element_type=jnp.float32)
        + grad_input_norm
    )
    small_grads = jnp.concatenate(
        [
            grad_value_router,
            grad_output_router,
            grad_expert_router,
            grad_gain_one[:, None],
            grad_gain_two[:, None],
        ],
        axis=1,
    )
    small_count = small_grads.shape[1]
    small_grads = jnp.pad(small_grads, ((0, 0), (0, -small_count % 128)))
    low_grads = [
        part.astype(jnp.bfloat16)
        for part in (
            grad_query_weight,
            grad_key_weight,
            grad_value_weight,
            grad_output_weight,
            small_grads,
        )
    ]
    summed = lax.psum_scatter(
        jnp.concatenate(low_grads, axis=1), ("dp", "expert"), scatter_dimension=0, tiled=True
    ).astype(jnp.float32)
    dense_grads = jnp.split(summed, [512, 1024, 3584, 6144], axis=1)
    total_sums = lax.psum(sums, ("dp", "expert"))
    residual_norms = jnp.sqrt(total_sums[:4] / (total_sums[4] * D))
    small = dense_grads[4]
    router_end = 2 * HEADS * VE + expert_router.shape[1]
    dense_grads = [
        dense_grads[0],
        dense_grads[1],
        dense_grads[2],
        dense_grads[3].T,
        small[:, : HEADS * VE],
        small[:, HEADS * VE : 2 * HEADS * VE],
        small[:, 2 * HEADS * VE : router_end],
        small[:, router_end],
        small[:, router_end + 1],
    ]
    return (
        final_rows.astype(jnp.bfloat16)[None],
        grad_input[None],
        dense_grads[0],
        dense_grads[1],
        dense_grads[2],
        dense_grads[3],
        dense_grads[4],
        dense_grads[5],
        dense_grads[6],
        dense_grads[7],
        dense_grads[8],
        up_grad,
        down_grad,
        residual_norms,
    )


def deliver_kernel(total, small, weights_kept, weights_in, *refs):
    count = (len(refs) - 9) // 3
    sources, targets = refs[:count], refs[count : 2 * count]
    value_out, output_out, expert_out, gains_out, norms_out, up_out, down_out = refs[2 * count : 2 * count + 7]
    held = refs[2 * count + 7 : -2]
    inward, outward = refs[-2:]
    arrived = [pltpu.make_async_copy(a, b, inward.at[i]) for i, (a, b) in enumerate(zip(sources, held))]
    left = [pltpu.make_async_copy(a, b, outward.at[i]) for i, (a, b) in enumerate(zip(held, targets))]
    for made in arrived:
        made.start()
    spread = HEADS * VE
    turned = jnp.concatenate([small[...], jnp.zeros((128 - ROWS, 128), jnp.float32)]).T
    value_out[...] = turned[:spread, :ROWS]
    output_out[...] = turned[spread : 2 * spread, :ROWS]
    expert_out[...] = small[:, 2 * spread : 2 * spread + total]
    gains_out[...] = turned[2 * spread + total : 2 * spread + total + 2, :ROWS]
    row = small[0:1, :]
    first = 2 * spread + total + 2
    norms_out[...] = jnp.sqrt(row[:, first : first + 4] / (row[:, first + 4 : first + 5] * D))
    for e in range(up_out.shape[0]):
        rows = slice(e * HEAD_DIM, (e + 1) * HEAD_DIM)
        up_sum, down_sum = [
            weights_kept[i, rows, :].astype(jnp.float32) + weights_in[i, rows, :].astype(jnp.float32)
            for i in range(2)
        ]
        up_out[e] = up_sum.T
        down_out[e] = down_sum
    for one, other in zip(arrived, left):
        one.wait()
        other.start()
    for made in left:
        made.wait()


def deliver(total, small, weights_kept, weights_in, *arrays):
    experts = weights_in.shape[1] // HEAD_DIM
    full = jnp.float32
    vmem = pl.BlockSpec(memory_space=pltpu.VMEM)
    anywhere = pl.BlockSpec(memory_space=pl.ANY)
    spread = HEADS * VE
    return pl.pallas_call(
        functools.partial(deliver_kernel, total),
        out_shape=[jax.ShapeDtypeStruct(a.shape, a.dtype) for a in arrays]
        + [
            jax.ShapeDtypeStruct((spread, ROWS), full),
            jax.ShapeDtypeStruct((spread, ROWS), full),
            jax.ShapeDtypeStruct((ROWS, total), full),
            jax.ShapeDtypeStruct((2, ROWS), full),
            jax.ShapeDtypeStruct((1, 4), full),
            jax.ShapeDtypeStruct((experts, D // 4, HEAD_DIM), full),
            jax.ShapeDtypeStruct((experts, HEAD_DIM, D // 4), full),
        ],
        in_specs=[vmem] * 3 + [anywhere] * len(arrays),
        out_specs=[anywhere] * len(arrays) + [vmem] * 7,
        scratch_shapes=[pltpu.VMEM(a.shape, a.dtype) for a in arrays]
        + [pltpu.SemaphoreType.DMA((len(arrays),))] * 2,
        compiler_params=pltpu.CompilerParams(vmem_limit_bytes=63 * 2**20),
        name="deliver",
    )(small, weights_kept, weights_in, *arrays)


def shards_fast(
    hidden_in,
    lengths,
    value_pick,
    output_pick,
    expert_pick,
    query_weight,
    key_weight,
    value_weight,
    output_weight,
    value_router,
    output_router,
    expert_router,
    attention_gain,
    feedforward_gain,
    expert_up,
    expert_down,
    cotangent,
):
    total = expert_router.shape[1]
    (
        middle,
        sent,
        normed_one,
        normed_two,
        queries,
        key_value,
        probs,
        value_all,
        attended,
        gates,
        slopes,
        cot_line,
        routers,
        gains,
    ) = attend(
        total,
        lengths,
        hidden_in[0],
        cotangent[0],
        value_pick[0].transpose(1, 2, 0),
        output_pick[0].transpose(1, 2, 0),
        expert_pick[0].T,
        value_router.T,
        output_router.T,
        expert_router.T,
        attention_gain,
        feedforward_gain,
        key_weight,
        value_weight,
        query_weight,
        output_weight,
    )
    returned, weights, weights_kept, forward = expert_kernel_visit(sent, cot_line, expert_up, expert_down)
    block_out, grad_input, grad_query, grad_key, grad_value, grad_output, small, weights_in = backward(
        total,
        lengths,
        gates,
        slopes,
        routers,
        gains,
        weights,
        forward,
        returned,
        middle,
        cotangent[0],
        hidden_in[0],
        normed_one,
        queries,
        key_value,
        probs,
        value_all,
        attended,
        normed_two,
        query_weight,
        key_weight,
        value_weight,
        output_weight,
    )
    kept = (block_out, grad_input, grad_query, grad_key, grad_value, grad_output)
    delivered = deliver(total, small, weights_kept, weights_in, *kept)
    block_out, grad_input, grad_query, grad_key, grad_value, grad_output = delivered[:6]
    value_small, output_small, expert_small, gain_grads, norms, up_grad, down_grad = delivered[6:]
    return (
        block_out[None],
        grad_input[None],
        grad_query,
        grad_key,
        grad_value,
        grad_output.T,
        value_small.T,
        output_small.T,
        expert_small,
        gain_grads[0],
        gain_grads[1],
        up_grad,
        down_grad,
        norms[0],
    )


def solution(mesh):
    placed = (
        P("expert", "dp", None),
        P("expert"),
        P("expert", "dp", None, None),
        P("expert", "dp", None, None),
        P("expert", "dp", None),
        P(),
        P(),
        P(),
        P(),
        P(),
        P(),
        P(),
        P(),
        P(),
        P("expert", None, None),
        P("expert", None, None),
        P("expert", "dp", None),
    )
    small_mesh = mesh.shape["dp"] == 4 and mesh.shape["expert"] == 8
    return jax.shard_map(
        shards_fast if small_mesh else shards,
        mesh=mesh,
        in_specs=placed,
        out_specs=(
            P("expert", "dp", None),
            P("expert", "dp", None),
            P(("dp", "expert"), None),
            P(("dp", "expert"), None),
            P(("dp", "expert"), None),
            P(None, ("dp", "expert")),
            P(("dp", "expert"), None),
            P(("dp", "expert"), None),
            P(("dp", "expert"), None),
            P(("dp", "expert")),
            P(("dp", "expert")),
            P("expert", "dp", None),
            P("expert", None, "dp"),
            P(),
        ),
        check_vma=False,
    )
```

```python
import functools

import jax
import jax.numpy as jnp
from jax import lax
from jax.experimental import pallas as pl
from jax.experimental.pallas import tpu as pltpu
from jax.sharding import PartitionSpec as P

D = 1024
HEADS = 4
HEAD_DIM = 128
VE = 5


MESH = pl.DeviceIdType.MESH
ROWS = 32
PIECE = VE * HEAD_DIM
EPSILON = 1e-05
NEGATIVE = -1000000000.0


def low_dot(left_side, right_side):
    return jnp.dot(left_side, right_side, preferred_element_type=jnp.float32)


def layer_norm(field, scale_gain):
    center = field - jnp.mean(field, axis=-1, keepdims=True)
    spread = jnp.mean(center * center, axis=-1, keepdims=True)
    return center * lax.rsqrt(spread + EPSILON) * scale_gain


def choose(select, count):
    return jnp.sum(
        (select[..., None] == jnp.arange(count, dtype=jnp.int32)).astype(jnp.float32), axis=-2
    )


def attention_probs(query_heads, key_heads, query_pos, length):
    key_pos = jnp.arange(key_heads.shape[0], dtype=jnp.int32)
    raw_scores = jnp.einsum(
        "qhd,khd->hqk", query_heads, key_heads, preferred_element_type=jnp.float32
    )
    allowed = (key_pos[None, :] <= query_pos[:, None]) & (key_pos[None, :] < length)
    scores = jnp.where(allowed[None], raw_scores * HEAD_DIM ** (-0.5), NEGATIVE)
    exp_terms = jnp.exp(scores - jnp.max(scores, axis=-1, keepdims=True))
    return exp_terms / jnp.sum(exp_terms, axis=-1, keepdims=True)


def dot_last(left_side, right_side):
    return lax.dot_general(
        left_side, right_side, (((1,), (1,)), ((), ())), preferred_element_type=jnp.float32
    )

def dot_first(left_side, right_side):
    return lax.dot_general(
        left_side, right_side, (((0,), (0,)), ((), ())), preferred_element_type=jnp.float32
    )


def visit_kernel(
    sent, cot_at, up_at, down_at, back_at, weights_out, weights_kept, forward_at,
    back_out, forward_out, cot, up, down, rows, cot_other, up_wide, chosen, cots, gated, grad_pre, forward, forward_in, gated_turned, pre_turned, partial, paired_in, chain_in, up_low, down_low, up_in, down_in,
    fetch, back_leave, forward_leave, row_send, row_recv, half_send, half_recv, cot_send, cot_recv, pair_send, pair_recv, forward_send, forward_recv, chain_send, chain_recv, grad_send, grad_recv,
):
    experts = up.shape[0]
    wide = down.shape[0]
    hidden = wide // experts
    dp, ex = lax.axis_index("dp"), lax.axis_index("expert")
    y, x, z, core = dp // 2, dp % 2, ex // 2, ex % 2
    half = z // 2
    inner = z + half * (3 - 2 * z)
    onward = 1 - 2 * half
    sibling = (dp, z * 2 + 1 - core)
    beside, behind = (y * 2 + 1 - x, ex), ((1 - y) * 2 + x, ex)

    def at_z(place):
        return (dp, place * 2 + core)

    fetched = [
        pltpu.make_async_copy(source, target, fetch.at[i])
        for i, (source, target) in enumerate(((cot_at, cot), (up_at, up), (down_at, down)))
    ]
    for made in fetched:
        made.start()
    barrier = pltpu.get_barrier_semaphore()
    for place in (sibling, beside, behind):
        pl.semaphore_signal(barrier, inc=1, device_id=place, device_id_type=MESH)

    @pl.when(z < 3)
    def _():
        pl.semaphore_signal(barrier, inc=1, device_id=at_z(z + 1), device_id_type=MESH)

    @pl.when(z > 0)
    def _():
        pl.semaphore_signal(barrier, inc=1, device_id=at_z(z - 1), device_id_type=MESH)

    pl.semaphore_wait(barrier, 4 + inner)

    def remote(source, target, send, recv, place):
        return pltpu.make_async_remote_copy(
            src_ref=source, dst_ref=target, send_sem=send, recv_sem=recv, device_id=place, device_id_type=MESH
        )

    def row_copy(at, source=None):
        block = rows.at[at] if source is None else source
        return remote(block, rows.at[4 + at], row_send.at[at], row_recv.at[at], sibling)

    def half_copy(way, at, part, source=None):
        span = pl.ds(part * (rows.shape[1] // 2), rows.shape[1] // 2)
        block = rows.at[at] if source is None else source
        return remote(
            block.at[span], rows.at[at, span], half_send.at[way, at, part], half_recv.at[at, part], at_z(z + 1 - 2 * way)
        )

    def cot_copy(at):
        return remote(cot.at[at], cot_other.at[at], cot_send.at[at], cot_recv.at[at], sibling)

    @pl.when(z < 3)
    def _():
        for part in range(2):
            half_copy(0, z, part, sent).start()

    @pl.when(z > 0)
    def _():
        for part in range(2):
            half_copy(1, z, part, sent).start()

    row_copy(z, sent).start()
    for made in fetched:
        made.wait()
    cot_copy(z).start()
    for k in (1, 2, 3):
        cot_copy((z + k) % 4).start()
    rows[z] = sent[...]
    for e in range(experts):
        up_wide[:, e * hidden : (e + 1) * hidden] = up[e]
    chosen[...] = (
        lax.broadcasted_iota(jnp.int32, (128, wide), 0)
        == 2 * HEADS * VE + ex * experts + lax.broadcasted_iota(jnp.int32, (128, wide), 1) // hidden
    ).astype(jnp.float32).astype(jnp.bfloat16)

    def order(p):
        later = (p + 2) // 3
        step = p - inner // (p + 1 - later)
        return later * (step + half * (3 - 2 * step)) + (1 - later) * z

    def pair_copy(at):
        return remote(partial.at[1, at], paired_in.at[at], pair_send.at[at], pair_recv.at[at], sibling)

    parts = 4
    size = rows.shape[1] // parts
    spans = [pl.ds(i * size, size) for i in range(parts)]

    def chain_copy(dest, slot, to, stage, part):
        span = spans[part]
        return remote(
            partial.at[0, dest, span], chain_in.at[slot, span],
            chain_send.at[stage, part], chain_recv.at[slot, part], at_z(to),
        )

    def add(target, source):
        def some(i, carry):
            part = pl.ds(pl.multiple_of(i * 32, 32), 32)
            target[part, :] = (
                target[part, :].astype(jnp.float32) + source[part, :].astype(jnp.float32)
            ).astype(target.dtype)
            return carry

        lax.fori_loop(0, target.shape[0] // 32, some, 0)

    def forward_copy(at):
        return remote(forward.at[at], forward_in.at[at], forward_send.at[at], forward_recv.at[at], sibling)

    def forward_block(block):
        at = block % 4
        def some(n, inside):
            span = pl.ds(pl.multiple_of(n * 256, 256), 256)
            value = jnp.dot(gated[block], down[:, span], preferred_element_type=jnp.float32).astype(jnp.bfloat16)

            @pl.when(block >= 4)
            def _():
                forward[at, :, span] = value

            @pl.when(block < 4)
            def _():
                forward_out[at, :, span] = value

            return inside

        lax.fori_loop(0, D // 256, some, 0)

        @pl.when(block >= 4)
        def _():
            forward_copy(at).start()

    def relay(dest, slot, to, stage, part):
        chain_copy(dest, dest, to, stage, part).wait_recv()
        add(partial.at[0, dest, spans[part]], chain_in.at[dest, spans[part]])
        chain_copy(dest, slot, to, stage, part).start()

    def visit(q, carry):
        p, other = q // 2, q % 2
        at = order(p)
        block = other * 4 + at

        @pl.when((other == 0) & (p > 0))
        def _():
            for part in range(2):
                half_copy(0, at, part).wait_recv()

                @pl.when((at < z) & (z < 3))
                def _():
                    half_copy(0, at, part).start()

                @pl.when((at > z) & (z > 0))
                def _():
                    half_copy(1, at, part).start()

            row_copy(at).start()

        @pl.when(other == 1)
        def _():
            row_copy(at).wait_recv()
            cot_copy(at).wait_recv()
            cots[...] = cot_other[at]

        @pl.when(other == 0)
        def _():
            cots[...] = cot[at]

        @pl.when((inner == 1) & (q == 7))
        def _():
            relay(*next_one, 0)
            relay(*next_one, 1)

        count = rows.shape[1]
        places = pl.ds(pl.multiple_of(block * count, count), count)

        def columns(n, gate_grad):
            span = pl.ds(pl.multiple_of(n * 256, 256), 256)
            pre = jnp.dot(rows[block, :, :D], up_wide[:, span], preferred_element_type=jnp.float32)
            back = dot_last(cots[...], down[span, :])
            mark = chosen[:, span]
            gate = jnp.dot(rows[block, :, D:], mark, preferred_element_type=jnp.float32)
            sig = jax.nn.sigmoid(pre)
            act = pre * sig
            act_low = (gate * act).astype(jnp.bfloat16)
            pre_low = (gate * back * (sig * (1.0 + pre * (1.0 - sig)))).astype(jnp.bfloat16)
            gated[block, :, span] = act_low
            grad_pre[:, span] = pre_low
            gated_turned[span, places] = act_low.T
            pre_turned[span, places] = pre_low.T
            return gate_grad + dot_last((act * back).astype(jnp.bfloat16), mark)

        partial[other, at, :, D:] = lax.fori_loop(
            0, wide // 256, columns, jnp.zeros((count, 128), jnp.float32)
        ).astype(jnp.bfloat16)

        def outward(n, carry):
            span = pl.ds(pl.multiple_of(n * 256, 256), 256)
            partial[other, at, :, span] = dot_last(grad_pre[...], up_wide[span, :]).astype(jnp.bfloat16)
            return carry

        lax.fori_loop(0, D // 256, outward, 0)

        @pl.when(other == 1)
        def _():
            pair_copy(at).start()
            pair_copy(at).wait_recv()
            add(partial.at[0, at], paired_in.at[at])

        @pl.when((inner == 0) & (q == 3))
        def _():
            for part in range(parts):
                chain_copy(*nearest, part).start()

        @pl.when((inner == 0) & (q == 5))
        def _():
            for part in range(parts):
                chain_copy(*next_one, part).start()

        @pl.when(q < 6)
        def _():
            forward_block(block)

        return carry

    nearest = (z + onward, z + onward, z + onward, 0)
    farthest = (3 * (1 - half), 3 * (1 - half), z + onward, 1)
    backward = (3 * half, 3 * half, z - onward, 2)
    next_one = (2 - half, 2 - half + inner * (2 + half), z + onward, 3)
    lax.fori_loop(0, 8, visit, 0)

    @pl.when(inner == 0)
    def _():
        for part in range(parts):
            chain_copy(*farthest, part).start()
    tokens_all = rows.reshape(rows.shape[0] * rows.shape[1], rows.shape[2])
    cots_own = cot.reshape(cot.shape[0] * cot.shape[1], D)
    cots_other = cot_other.reshape(cot.shape[0] * cot.shape[1], D)
    place = cots_own.shape[0]
    quarter = D // 4


    def up_copy(j):
        return remote(up_low.at[j], up_in.at[j], grad_send.at[0, j], grad_recv.at[0, j], behind if j == 2 else beside)

    def down_copy(j):
        return remote(down_low.at[j], down_in.at[j], grad_send.at[1, j], grad_recv.at[1, j], beside if j == 1 else behind)

    def span_of(j):
        at = (y + (1 - j % 2) * (1 - 2 * y)) * 2 + x + (1 - j // 2) * (1 - 2 * x)
        return pl.ds(pl.multiple_of(at * quarter, quarter), quarter)

    def up_quarter(j):
        up_low[j] = jnp.dot(
            pre_turned[...], tokens_all[:, span_of(j)], preferred_element_type=jnp.float32
        ).astype(jnp.bfloat16)
        if j < 2:
            up_copy(j).start()

    def down_quarter(j):
        down_low[j] = (
            jnp.dot(gated_turned[:, :place], cots_own[:, span_of(j)], preferred_element_type=jnp.float32)
            + jnp.dot(gated_turned[:, place:], cots_other[:, span_of(j)], preferred_element_type=jnp.float32)
        ).astype(jnp.bfloat16)
        if j in (0, 2):
            down_copy(j).start()

    def relays(*ways):
        @pl.when(inner == 1)
        def _():
            for way, part in ways:
                relay(*way, part)

    def forward_leaves(at):
        return pltpu.make_async_copy(forward_out.at[at], forward_at.at[at], forward_leave.at[at])

    def back_leaves(part):
        return pltpu.make_async_copy(back_out.at[spans[part]], back_at.at[spans[part]], back_leave.at[part])

    def forward_add(p):
        at = order(p)
        forward_copy(at).wait()
        add(forward_out.at[at], forward_in.at[at])
        forward_leaves(at).start()

    relays((next_one, 2), (next_one, 3))
    up_quarter(0)
    down_quarter(0)
    relays((farthest, 0))
    up_quarter(1)
    relays((farthest, 1))
    down_quarter(2)
    relays((backward, 0), (farthest, 2))
    forward_block(4 + order(3))
    relays((backward, 1), (farthest, 3))
    up_quarter(2)
    relays((backward, 2))
    forward_add(0)
    forward_add(1)
    down_quarter(1)
    relays((backward, 3))
    forward_block(order(3))
    up_quarter(3)
    down_quarter(3)
    forward_add(2)
    forward_add(3)
    for part in range(parts):
        span = spans[part]
        chain_copy(z, z, z, 0, part).wait_recv()
        back_out[span, :] = partial[0, z, span, :].astype(jnp.float32) + chain_in[z, span, :].astype(jnp.float32)

        @pl.when(inner == 1)
        def _():
            chain_copy(z, 4, z, 0, part).wait_recv()
            back_out[span, :] = back_out[span, :] + chain_in[4, span, :].astype(jnp.float32)

        back_leaves(part).start()

    ends = (
        (up_copy(0), up_low, 2, up_in, 0, weights_out.at[0]),
        (up_copy(1), up_low, 3, up_in, 1, weights_kept.at[0]),
        (down_copy(0), down_low, 1, down_in, 0, weights_out.at[1]),
        (down_copy(2), down_low, 3, down_in, 2, weights_kept.at[1]),
    )
    for made, mine, j, other, slot, target in ends:
        made.wait()
        target[...] = mine[j]
        add(target, other.at[slot])

    for at in range(4):
        row_copy(at).wait_send()
        cot_copy(at).wait_send()
        pair_copy(at).wait_send()
        for part in range(2):

            @pl.when((at <= z) & (z < 3))
            def _():
                half_copy(0, at, part).wait_send()

            @pl.when((at >= z) & (z > 0))
            def _():
                half_copy(1, at, part).wait_send()

    for part in range(parts):

        @pl.when(inner == 0)
        def _():
            chain_copy(z, 0, z, 0, part).wait_send()

        @pl.when(inner == 1)
        def _():
            chain_copy(z, 0, z, 2, part).wait_send()

        chain_copy(z, 0, z, 1, part).wait_send()
        chain_copy(z, 0, z, 3, part).wait_send()

    for at in range(4):
        forward_leaves(at).wait()
        back_leaves(at).wait()


def expert_kernel_visit(sent, cot_line, up, down):
    tokens = sent.shape[0]
    experts, _, hidden = up.shape
    wide = experts * hidden
    low = jnp.bfloat16
    vmem = pl.BlockSpec(memory_space=pltpu.VMEM)
    dma = pltpu.SemaphoreType.DMA
    f32 = jnp.float32
    return pl.pallas_call(
        visit_kernel,
        out_shape=[
            jax.ShapeDtypeStruct((tokens, D + 128), f32),
            jax.ShapeDtypeStruct((2, wide, D // 4), low),
            jax.ShapeDtypeStruct((2, wide, D // 4), low),
            jax.ShapeDtypeStruct((4, tokens, D), low),
        ],
        in_specs=[vmem] + [pl.BlockSpec(memory_space=pl.ANY)] * 3,
        out_specs=[pl.BlockSpec(memory_space=pl.ANY), vmem, vmem, pl.BlockSpec(memory_space=pl.ANY)],
        scratch_shapes=[
            pltpu.VMEM((tokens, D + 128), f32),
            pltpu.VMEM((4, tokens, D), low),
            pltpu.VMEM((4, tokens, D), low),
            pltpu.VMEM((experts, D, hidden), low),
            pltpu.VMEM((wide, D), low),
            pltpu.VMEM((8, tokens, D + 128), low),
            pltpu.VMEM((4, tokens, D), low),
            pltpu.VMEM((D, wide), low),
            pltpu.VMEM((128, wide), low),
            pltpu.VMEM((tokens, D), low),
            pltpu.VMEM((8, tokens, wide), low),
            pltpu.VMEM((tokens, wide), low),
            pltpu.VMEM((4, tokens, D), low),
            pltpu.VMEM((4, tokens, D), low),
            pltpu.VMEM((wide, 8 * tokens), low),
            pltpu.VMEM((wide, 8 * tokens), low),
            pltpu.VMEM((2, 4, tokens, D + 128), low),
            pltpu.VMEM((4, tokens, D + 128), low),
            pltpu.VMEM((5, tokens, D + 128), low),
            pltpu.VMEM((4, wide, D // 4), low),
            pltpu.VMEM((4, wide, D // 4), low),
            pltpu.VMEM((3, wide, D // 4), low),
            pltpu.VMEM((3, wide, D // 4), low),
            dma((3,)), dma((4,)), dma((4,)), dma((4,)), dma((4,)), dma((2, 4, 2)), dma((4, 2)), dma((4,)), dma((4,)), dma((4,)), dma((4,)), dma((4,)), dma((4,)), dma((4, 4)), dma((5, 4)), dma((2, 3)), dma((2, 3)),
        ],
        compiler_params=pltpu.CompilerParams(collective_id=2, has_side_effects=True, vmem_limit_bytes=58 * 2**20),
        name="expert_visit",
    )(sent, cot_line, up, down.reshape(wide, D))


def attend_kernel(
    expert_total, lengths, hidden, cot, value_pick, output_pick, expert_pick, value_router, output_router, expert_router,
    gain_one, gain_two,
    key_weight_at, value_weight_at, query_weight_at, output_weight_at,
    middle_at, sent_at, normed_one_at, normed_two_at, queries_at, key_value_at, probs_at, value_all_at, attended_at,
    gates_at, slopes_at, cot_line_at, routers_at, gains_at,
    middle, sent, normed_one, normed_two, queries, key_value, probs, value_all, attended,
    gates, slopes, cot_line, routers, gains, routers_full,
    key_weight, value_weight, query_weight, output_weight, mixed, hot_turned, hot,
    fetch, leave, pair_send, pair_recv, cot_send, cot_recv, own_sem,
):
    dp, ex = lax.axis_index("dp"), lax.axis_index("expert")
    z, core = ex // 2, ex % 2
    half = z // 2
    inner = z + half * (3 - 2 * z)
    count = hidden.shape[0]
    width = HEADS * HEAD_DIM
    low = jnp.bfloat16
    length = lengths[0]
    spread = HEADS * VE
    total = expert_total
    weights = [
        pltpu.make_async_copy(source, target, fetch.at[i])
        for i, (source, target) in enumerate(
            (
                (key_weight_at, key_weight),
                (value_weight_at, value_weight),
                (query_weight_at, query_weight),
                (output_weight_at, output_weight),
            )
        )
    ]
    for made in weights:
        made.start()
    results = (
        (middle, middle_at), (sent, sent_at), (normed_one, normed_one_at), (normed_two, normed_two_at),
        (queries, queries_at), (key_value, key_value_at), (probs, probs_at), (value_all, value_all_at),
        (attended, attended_at), (gates, gates_at), (slopes, slopes_at), (cot_line, cot_line_at),
        (routers, routers_at), (gains, gains_at),
    )
    leaving = [pltpu.make_async_copy(source, target, leave.at[i]) for i, (source, target) in enumerate(results)]

    def at_z(place):
        return (dp, place * 2 + core)

    barrier = pltpu.get_barrier_semaphore()
    for k in (1, 2, 3):
        pl.semaphore_signal(barrier, inc=1, device_id=((dp + k) % 4, ex), device_id_type=MESH)

    @pl.when(z < 3)
    def _():
        pl.semaphore_signal(barrier, inc=1, device_id=at_z(z + 1), device_id_type=MESH)

    @pl.when(z > 0)
    def _():
        pl.semaphore_signal(barrier, inc=1, device_id=at_z(z - 1), device_id_type=MESH)

    pl.semaphore_wait(barrier, 4 + inner)

    def cot_copy(way, at, source=None):
        block = cot_line.at[at]
        return pltpu.make_async_remote_copy(
            src_ref=block if source is None else source, dst_ref=block,
            send_sem=cot_send.at[way, at], recv_sem=cot_recv.at[at],
            device_id=at_z(z + 1 - 2 * way), device_id_type=MESH,
        )

    def pass_on(distance):
        @pl.when(z >= distance)
        def _():
            cot_copy(0, z - distance).wait_recv()

        @pl.when((z >= distance) & (z < 3))
        def _():
            cot_copy(0, z - distance).start()

        @pl.when(z + distance <= 3)
        def _():
            cot_copy(1, z + distance).wait_recv()

        @pl.when((z + distance <= 3) & (z > 0))
        def _():
            cot_copy(1, z + distance).start()

    @pl.when(z < 3)
    def _():
        cot_copy(0, z, cot).start()

    @pl.when(z > 0)
    def _():
        cot_copy(1, z, cot).start()

    keep = pltpu.make_async_copy(cot, cot_line.at[z], own_sem)
    keep.start()

    def norm(field, gain):
        center = field - jnp.mean(field, axis=-1, keepdims=True)
        spread = jnp.mean(center * center, axis=-1, keepdims=True)
        return (center * lax.rsqrt(spread + EPSILON) * gain).astype(low)

    parts = (pl.ds(0, width), pl.ds(width, width))

    def pair_copy(step, part, block):
        return pltpu.make_async_remote_copy(
            src_ref=key_value.at[block, :, parts[part]], dst_ref=key_value.at[block, :, parts[part]],
            send_sem=pair_send.at[step, part], recv_sem=pair_recv.at[block, part],
            device_id=((dp + step) % 4, ex), device_id_type=MESH,
        )

    def send_part(part):
        for step in (1, 2, 3):

            @pl.when(dp + step < 4)
            def _():
                pair_copy(step, part, dp).start()

    gains[0:1, :] = gain_one[...].astype(jnp.float32).reshape(1, D)
    gains[1:2, :] = gain_two[...].astype(jnp.float32).reshape(1, D)
    normed_one[...] = norm(hidden[...].astype(jnp.float32), gains[0:1, :])
    leaving[2].start()
    weights[0].wait()
    key_value[dp, :, parts[0]] = jnp.dot(
        normed_one[...], key_weight[...], preferred_element_type=jnp.float32
    ).astype(low)
    send_part(0)

    routers_full[...] = jnp.zeros(routers_full.shape, jnp.float32)
    routers_full[0:spread, :] = value_router[...].astype(jnp.float32)
    routers_full[spread : 2 * spread, :] = output_router[...].astype(jnp.float32)
    routers_full[2 * spread : 2 * spread + total, :] = expert_router[...].astype(jnp.float32)
    routers[...] = routers_full[...].astype(low)
    leaving[12].start()
    leaving[13].start()
    hot_turned[...] = jnp.zeros(hot_turned.shape, jnp.float32)

    def mark(picks, base, size):
        place = lax.broadcasted_iota(jnp.int32, (size, count), 0)
        found = jnp.zeros((size, count), jnp.float32)
        for pick in picks:
            found = jnp.where(place == pick, 1.0, found)
        hot_turned[base : base + size, :] = found

    mark([value_pick[h, i : i + 1, :] + h * VE for h in range(HEADS) for i in range(value_pick.shape[1])], 0, spread)
    mark(
        [output_pick[h, i : i + 1, :] + h * VE for h in range(HEADS) for i in range(output_pick.shape[1])],
        spread,
        spread,
    )
    mark([expert_pick[i : i + 1, :] for i in range(expert_pick.shape[0])], 2 * spread, total)
    hot[...] = hot_turned[...].T
    sig = jax.nn.sigmoid(dot_last(normed_one[...], routers[...]))
    gates[...] = sig * hot[...]
    slopes[...] = gates[...] * (1.0 - sig)
    weights[1].wait()

    def values(n, carry):
        span = pl.ds(pl.multiple_of(n * 256, 256), 256)
        value_all[:, span] = jnp.dot(
            hidden[...], value_weight[:, span], preferred_element_type=jnp.float32
        ).astype(low)
        return carry

    lax.fori_loop(0, HEADS * VE * HEAD_DIM // 256, values, 0)
    leaving[7].start()
    for h in range(HEADS):
        row = jnp.zeros((count, HEAD_DIM), jnp.float32)
        for e in range(h * VE, (h + 1) * VE):
            row += gates[:, e : e + 1] * value_all[:, e * HEAD_DIM : (e + 1) * HEAD_DIM].astype(jnp.float32)
        key_value[dp, :, width + h * HEAD_DIM : width + (h + 1) * HEAD_DIM] = row.astype(low)
    send_part(1)

    weights[2].wait()
    queries[...] = jnp.dot(normed_one[...], query_weight[...], preferred_element_type=jnp.float32).astype(low)
    leaving[4].start()
    for block in range(4):

        @pl.when(block > dp)
        def _():
            key_value[block] = jnp.zeros((count, 2 * width), low)

    pass_on(1)

    def wait_part(part):
        for block in range(3):

            @pl.when(block < dp)
            def _():
                pair_copy(1, part, block).wait_recv()

    wait_part(0)
    pair_all = key_value.reshape(4 * count, 2 * width)
    query_pos = dp * count + lax.broadcasted_iota(jnp.int32, (count, 4 * count), 0)
    key_pos = lax.broadcasted_iota(jnp.int32, (count, 4 * count), 1)
    allowed = (key_pos <= query_pos) & (key_pos < length)

    def score(h, carry):
        span = pl.ds(pl.multiple_of(h * HEAD_DIM, HEAD_DIM), HEAD_DIM)
        raw = dot_last(queries[:, span], pair_all[:, span])
        scores = jnp.where(allowed, raw * HEAD_DIM ** (-0.5), NEGATIVE)
        terms = jnp.exp(scores - jnp.max(scores, axis=-1, keepdims=True))
        probs[h] = (terms * (1.0 / jnp.sum(terms, axis=-1, keepdims=True))).astype(low)
        return carry

    lax.fori_loop(0, HEADS, score, 0)
    leaving[6].start()
    leaving[9].start()
    pass_on(2)
    wait_part(1)
    leaving[5].start()

    def collect(h, carry):
        span = pl.ds(pl.multiple_of(h * HEAD_DIM, HEAD_DIM), HEAD_DIM)
        value_span = pl.ds(pl.multiple_of(width + h * HEAD_DIM, HEAD_DIM), HEAD_DIM)
        attended[:, span] = jnp.dot(probs[h], pair_all[:, value_span], preferred_element_type=jnp.float32)
        return carry

    lax.fori_loop(0, HEADS, collect, 0)
    leaving[8].start()
    for h in range(HEADS):
        row = attended[:, h * HEAD_DIM : (h + 1) * HEAD_DIM]
        for e in range(h * VE, (h + 1) * VE):
            mixed[:, e * HEAD_DIM : (e + 1) * HEAD_DIM] = (gates[:, spread + e : spread + e + 1] * row).astype(low)

    place = dp * count + lax.broadcasted_iota(jnp.int32, (count, 1), 0)
    live = jnp.where(place < length, 1.0, 0.0)
    weights[3].wait()

    def outward(n, carry):
        span = pl.ds(pl.multiple_of(n * 256, 256), 256)
        branch = jnp.dot(mixed[...], output_weight[:, span], preferred_element_type=jnp.float32)
        middle[:, span] = hidden[:, span].astype(jnp.float32) + live * branch
        return carry

    lax.fori_loop(0, D // 256, outward, 0)
    leaving[0].start()
    sent[:, :D] = middle[...].astype(low)
    normed_two[...] = norm(middle[...], gains[1:2, :])
    sig = jax.nn.sigmoid(dot_last(normed_two[...], routers[...]))
    gate = sig * hot[...] * live
    sent[:, D:] = gate.astype(low)
    lane = lax.broadcasted_iota(jnp.int32, (count, 128), 1)
    slopes[...] = jnp.where(lane < 2 * spread, slopes[...], gate * (1.0 - sig))

    for i in (1, 3, 10):
        leaving[i].start()
    pass_on(3)
    keep.wait()
    leaving[11].start()
    for part in range(2):
        for step in (1, 2, 3):

            @pl.when(dp + step < 4)
            def _():
                pair_copy(step, part, dp).wait_send()

    for at in range(4):

        @pl.when((at <= z) & (z < 3))
        def _():
            cot_copy(0, at).wait_send()

        @pl.when((at >= z) & (z > 0))
        def _():
            cot_copy(1, at).wait_send()

    for made in leaving:
        made.wait()


def attend(total, lengths, *operands):
    count = operands[0].shape[0]
    low, full = jnp.bfloat16, jnp.float32
    vmem = pl.BlockSpec(memory_space=pltpu.VMEM)
    anywhere = pl.BlockSpec(memory_space=pl.ANY)
    dma = pltpu.SemaphoreType.DMA
    width, wide = HEADS * HEAD_DIM, HEADS * VE * HEAD_DIM
    shapes = [
        ((count, D), full),
        ((count, D + 128), low),
        ((count, D), low),
        ((count, D), low),
        ((count, width), low),
        ((4, count, 2 * width), low),
        ((HEADS, count, 4 * count), low),
        ((count, wide), low),
        ((count, width), full),
        ((count, 128), full),
        ((count, 128), full),
        ((4, count, D), low),
        ((128, D), low),
        ((2, D), full),
    ]
    return pl.pallas_call(
        functools.partial(attend_kernel, total),
        out_shape=[jax.ShapeDtypeStruct(*shape) for shape in shapes],
        in_specs=[pl.BlockSpec(memory_space=pltpu.SMEM)] + [vmem] * (len(operands) - 4) + [anywhere] * 4,
        out_specs=[anywhere] * len(shapes),
        scratch_shapes=[pltpu.VMEM(*shape) for shape in shapes]
        + [pltpu.VMEM((128, D), full)]
        + [pltpu.VMEM(a.shape, a.dtype) for a in operands[-4:]]
        + [
            pltpu.VMEM((count, wide), low),
            pltpu.VMEM((128, count), full),
            pltpu.VMEM((count, 128), full),
            dma((4,)),
            dma((len(shapes),)),
            dma((4, 2)),
            dma((4, 2)),
            dma((2, 4)),
            dma((4,)),
            dma,
        ],
        compiler_params=pltpu.CompilerParams(
            collective_id=1, has_side_effects=True, vmem_limit_bytes=58 * 2**20
        ),
        name="attend",
    )(lengths, *operands)


def backward_kernel(
    total_experts, lengths, gates, slopes, routers, gains,
    weights_at, forward_at, returned_at, middle_at, cot_at, hidden_at, normed_one_at, queries_at, key_value_at, probs_at, value_all_at,
    attended_at, normed_two_at, query_weight_at, key_weight_at, value_weight_at, output_weight_at,
    block_at, grad_at, out_query, out_key, out_value, out_output, out_small, weights_in,
    block_out, grad_in, weights, forward, returned, middle, cot, hidden, normed_one, queries, key_value, probs, value_all,
    attended, normed_two, query_weight, key_weight, value_part, output_part,
    branch, branch_turned, one_turned, hidden_turned, grad_att, grad_query, leave, arrive, grad_key,
    grad_each, grad_middle, logit_one, logit_two, small_turned, mixed,
    grads, grads_small, core_in, plane_in, last_in, forward_in,
    fetch, out_leave, part_fetch, leave_send, leave_recv, send, recv, forward_send, forward_recv, weights_send, weights_recv,
):
    dp, ex = lax.axis_index("dp"), lax.axis_index("expert")
    y, x, z, core = dp // 2, dp % 2, ex // 2, ex % 2
    count = hidden.shape[0]
    width = HEADS * HEAD_DIM
    low, full = jnp.bfloat16, jnp.float32
    length = lengths[0]
    sibling = (dp, z * 2 + 1 - core)
    beside = (y * 2 + 1 - x, ex)
    behind = ((1 - y) * 2 + x, ex)
    across = ((1 - y) * 2 + 1 - x, ex)
    line = [(dp, ((z + k) % 4) * 2 + core) for k in (1, 2, 3)]
    barrier = pltpu.get_barrier_semaphore()
    for place in (sibling, beside, behind, across, *line):
        pl.semaphore_signal(barrier, inc=1, device_id=place, device_id_type=MESH)

    held = dict(
        weights=(weights_at, weights),
        forward=(forward_at, forward),
        returned=(returned_at, returned),
        middle=(middle_at, middle),
        cot=(cot_at, cot),
        hidden=(hidden_at, hidden),
        attended=(attended_at, attended),
        key_value=(key_value_at, key_value),
        probs=(probs_at, probs),
        queries=(queries_at, queries),
        normed_one=(normed_one_at, normed_one),
        query_weight=(query_weight_at, query_weight),
        value_all=(value_all_at, value_all),
        key_weight=(key_weight_at, key_weight),
        normed_two=(normed_two_at, normed_two),
    )
    got = {
        name: pltpu.make_async_copy(source, target, fetch.at[i])
        for i, (name, (source, target)) in enumerate(held.items())
    }

    def output_copy(n):
        return pltpu.make_async_copy(
            output_weight_at.at[pl.ds(n * PIECE, PIECE)], output_part.at[n % 2], part_fetch.at[0, n % 2]
        )

    def value_copy(n):
        return pltpu.make_async_copy(
            value_weight_at.at[:, pl.ds(n * PIECE, PIECE)], value_part.at[n % 2], part_fetch.at[1, n % 2]
        )

    first_held = ("weights", "forward", "returned", "middle", "cot", "hidden")
    for name in first_held:
        got[name].start()
    for n in range(2):
        output_copy(n).start()
    for name in held:
        if name not in first_held:
            got[name].start()
    for n in range(2):
        value_copy(n).start()

    pieces = (
        [(out_output, PIECE * n, PIECE, n) for n in range(HEADS)]
        + [(out_query, 0, width, 4)]
        + [(out_value, PIECE * n, PIECE, n) for n in range(HEADS)]
        + [(out_key, 0, width, 5), (out_small, 0, 128, None)]
    )
    along_line = (0, 1)
    in_plane = [i for i in range(len(pieces)) if i not in along_line]
    x_first = {i: n % 2 == 0 for n, i in enumerate(in_plane)}

    def remote(source, target, slot, place):
        return pltpu.make_async_remote_copy(
            src_ref=source, dst_ref=target, send_sem=send.at[slot], recv_sem=recv.at[slot],
            device_id=place, device_id_type=MESH,
        )

    def add(target, source):
        target[...] = (target[...].astype(full) + source[...].astype(full)).astype(target.dtype)

    def own(i):
        slot = pieces[i][3]
        return grads_small if slot is None else grads.at[slot, :, :, :, :, columns(i)]

    def columns(i):
        return pl.ds(0, pieces[i][2])

    started = {}

    def begin(key, source, target, slot, place):
        started[key] = remote(source, target, slot, place)
        started[key].start()

    def halve_core(i):
        begin((i, 0), own(i).at[:, :, 1 - core], core_in.at[i, :, :, :, columns(i)], (i, 0), sibling)

    def halve_near(i):
        span = columns(i)
        started[i, 0].wait()
        add(core_in.at[i, :, :, :, span], own(i).at[:, :, core])
        if i in along_line:
            for k in (1, 2, 3):
                begin(
                    (i, k), core_in.at[i, :, (z + k) % 4, :, span],
                    plane_in.at[i, pl.ds(4 * k - 4, 4), :, span], (i, k), line[k - 1],
                )
            return
        for part in range(2):
            if x_first[i]:
                source = core_in.at[i, part * 2 + 1 - x, :, :, span]
            else:
                source = core_in.at[i, (1 - y) * 2 + part, :, :, span]
            target = plane_in.at[i, pl.ds(part * 4, 4), :, span]
            begin((i, 1 + part), source, target, (i, 1 + part), beside if x_first[i] else behind)

    def halve_far(i):
        span = columns(i)
        if i in along_line:
            held = core_in.at[i, :, z, :, span]
            for k in (1, 2, 3):
                started[i, k].wait()
                add(held, plane_in.at[i, pl.ds(4 * k - 4, 4), :, span])
            for part in range(2):
                begin(
                    (i, 4 + part), core_in.at[i, part * 2 + 1 - x, z, :, span],
                    last_in.at[i, part, :, span], (i, 4 + part), beside,
                )
            return
        for part in range(2):
            started[i, 1 + part].wait()
            kept = part * 2 + x if x_first[i] else y * 2 + part
            add(plane_in.at[i, pl.ds(part * 4, 4), :, span], core_in.at[i, kept, :, :, span])
        other = 1 - y if x_first[i] else 1 - x
        begin(
            (i, 3), plane_in.at[i, pl.ds(other * 4, 4), :, span], plane_in.at[i, pl.ds(8, 4), :, span],
            (i, 3), behind if x_first[i] else beside,
        )

    def spread(i):
        span = columns(i)
        if i in along_line:
            for part in range(2):
                started[i, 4 + part].wait()
                add(last_in.at[i, part, :, span], core_in.at[i, part * 2 + x, z, :, span])
            begin((i, 6), last_in.at[i, 1 - y, :, span], last_in.at[i, 2, :, span], (i, 6), behind)
            return
        started[i, 3].wait()
        add(plane_in.at[i, pl.ds(8, 4), :, span], plane_in.at[i, pl.ds((y if x_first[i] else x) * 4, 4), :, span])
        for k in (1, 2, 3):
            begin(
                (i, 3 + k), plane_in.at[i, 8 + (z + k) % 4, :, span],
                last_in.at[i, k - 1, :, span], (i, 3 + k), line[k - 1],
            )

    def finish(i):
        out, start, size, _ = pieces[i]
        span = columns(i)
        if i in along_line:
            started[i, 6].wait()
            total = last_in[i, y, :, span].astype(full) + last_in[i, 2, :, span].astype(full)
        else:
            total = plane_in[i, 8 + z, :, span].astype(full)
            for k in (1, 2, 3):
                started[i, 3 + k].wait()
                total = total + last_in[i, k - 1, :, span].astype(full)
        out[:, pl.ds(start, size)] = total

    rows_each = 64
    lane = lax.broadcasted_iota(jnp.int32, (1, 128), 1)
    for name in first_held:
        got[name].wait()
    logit_two[...] = (returned[:, D:] * slopes[...]).astype(low)

    half = z // 2
    inner = z + half * (3 - 2 * z)
    onward = 1 - 2 * half
    nearest = (z + onward, z + onward, z + onward, 0)
    farthest = (3 * (1 - half), 3 * (1 - half), z + onward, 1)
    backward = (3 * half, 3 * half, z - onward, 2)
    next_one = (2 - half, 2 - half + inner * (2 + half), z + onward, 3)

    def forward_copy(dest, slot, to, stage, part):
        span = pl.ds(part * (count // 2), count // 2)
        return pltpu.make_async_remote_copy(
            src_ref=forward.at[dest, span], dst_ref=forward_in.at[slot, span],
            send_sem=forward_send.at[stage, part], recv_sem=forward_recv.at[slot, part],
            device_id=(dp, to * 2 + core), device_id_type=MESH,
        )

    def relays(*ways):
        @pl.when(inner == 1)
        def _():
            for (dest, slot, to, stage), part in ways:
                span = pl.ds(part * (count // 2), count // 2)
                forward_copy(dest, dest, to, stage, part).wait_recv()
                add(forward.at[dest, span], forward_in.at[dest, span])
                forward_copy(dest, slot, to, stage, part).start()

    pl.semaphore_wait(barrier, 7)
    weight_copies = [
        pltpu.make_async_remote_copy(
            src_ref=weights.at[i], dst_ref=weights_in.at[i], send_sem=weights_send.at[i],
            recv_sem=weights_recv.at[i], device_id=place, device_id_type=MESH,
        )
        for i, place in enumerate((behind, beside))
    ]
    for made in weight_copies:
        made.start()

    @pl.when(inner == 0)
    def _():
        for way in (farthest, next_one, nearest):
            for part in range(2):
                forward_copy(*way, part).start()

    def live_rows(start):
        place = dp * count + start + lax.broadcasted_iota(jnp.int32, (rows_each, 1), 0)
        return jnp.where(place < length, 1.0, 0.0)

    def norm_back(field, grad, gain):
        center = field - jnp.mean(field, axis=-1, keepdims=True)
        scale = lax.rsqrt(jnp.mean(center * center, axis=-1, keepdims=True) + EPSILON)
        unit = center * scale
        part = grad * gain
        back = scale * (
            part
            - jnp.mean(part, axis=-1, keepdims=True)
            - unit * jnp.mean(part * unit, axis=-1, keepdims=True)
        )
        return back, jnp.sum(grad * unit, axis=0, keepdims=True)

    def first_rows(n, gain_sum):
        start = pl.multiple_of(n * rows_each, rows_each)
        rows = pl.ds(start, rows_each)
        grad = jnp.dot(logit_two[rows, :], routers[...], preferred_element_type=full)
        back, gain_part = norm_back(middle[rows, :], grad, gains[1:2, :])
        total = cot[rows, :].astype(full) + returned[rows, :D] + back
        grad_middle[rows, :] = total
        branch[rows, :] = (live_rows(start) * total).astype(low)
        return gain_sum + gain_part

    gain_two_sum = lax.fori_loop(0, count // rows_each, first_rows, jnp.zeros((1, D), full))
    relays((farthest, 0))

    def square(field, live, at):
        total = jnp.sum(jnp.sum(field * field, axis=1, keepdims=True) * live, axis=0, keepdims=True)
        return jnp.where(lane == at, total, 0.0)

    def last_rows(n, sums):
        start = pl.multiple_of(n * rows_each, rows_each)
        rows = pl.ds(start, rows_each)
        live = live_rows(start)
        field = middle[rows, :]
        step = forward[z, rows, :].astype(full)
        final = field + step
        block_out[rows, :] = final.astype(low)
        source = hidden[rows, :].astype(full)
        one = jnp.ones((rows_each, 1), full)
        sums += square(source, live, 0) + square(field - source, one, 1)
        sums += square(step, one, 2) + square(final, live, 3)
        return sums + jnp.where(lane == 4, jnp.sum(live, axis=0, keepdims=True), 0.0)

    def output_rows():
        for part in range(2):
            span = pl.ds(part * (count // 2), count // 2)
            forward_copy(z, z, z, 0, part).wait_recv()
            add(forward.at[z, span], forward_in.at[z, span])

            @pl.when(inner == 1)
            def _():
                forward_copy(z, 4, z, 0, part).wait_recv()
                add(forward.at[z, span], forward_in.at[4, span])

        sums = lax.fori_loop(0, count // rows_each, last_rows, jnp.zeros((1, 128), full))
        return sums

    def weight_grad(i, turned, right):
        def some(n, carry):
            rows = pl.ds(pl.multiple_of(n * 256, 256), 256)
            value = jnp.dot(turned[rows, :], right, preferred_element_type=full).astype(low)
            own(i)[n] = value.reshape(4, 2, ROWS, pieces[i][2])
            return carry

        lax.fori_loop(0, D // 256, some, 0)
        halve_core(i)

    got["attended"].wait()
    spread_count = HEADS * VE

    def head_of(c):
        return slice((c // VE) * HEAD_DIM, (c // VE + 1) * HEAD_DIM)

    logit_one[...] = jnp.zeros(logit_one.shape, full)
    grad_att[...] = jnp.zeros(grad_att.shape, full)
    for n in range(HEADS):
        output_copy(n).wait()
        for j in range(VE):
            c = VE * n + j
            grad_mixed = dot_last(branch[...], output_part[n % 2, j * HEAD_DIM : (j + 1) * HEAD_DIM, :])
            col = spread_count + c
            grad_att[:, head_of(c)] += gates[:, col : col + 1] * grad_mixed
            dots = jnp.sum(attended[:, head_of(c)] * grad_mixed, axis=1, keepdims=True)
            logit_one[:, col : col + 1] = dots * slopes[:, col : col + 1]
        if n + 2 < HEADS:
            output_copy(n + 2).start()
    relays((farthest, 1), (backward, 0))

    pair_all = key_value.reshape(4 * count, 2 * width)
    for name in ("key_value", "probs", "queries"):
        got[name].wait()

    def leave_copy(k, h):
        rows = pl.ds(h * 2 * HEAD_DIM, 2 * HEAD_DIM)
        return pltpu.make_async_remote_copy(
            src_ref=leave.at[(dp + 4 - k) % 4, rows], dst_ref=arrive.at[k - 1, rows],
            send_sem=leave_send.at[k - 1, h], recv_sem=leave_recv.at[k - 1, h],
            device_id=((dp + 4 - k) % 4, ex), device_id_type=MESH,
        )

    def head(h, carry):
        start = pl.multiple_of(h * HEAD_DIM, HEAD_DIM)
        span = pl.ds(start, HEAD_DIM)
        grad = grad_att[:, span].astype(low)
        prob = probs[h].astype(full)
        grad_prob = dot_last(grad, pair_all[:, pl.ds(width + start, HEAD_DIM)])
        dots = jnp.sum(prob * grad_prob, axis=-1, keepdims=True)
        grad_score = (prob * (grad_prob - dots) * HEAD_DIM ** (-0.5)).astype(low)
        grad_query[:, span] = jnp.dot(grad_score, pair_all[:, span], preferred_element_type=full).astype(low)
        key_part = dot_first(queries[:, span], grad_score).astype(low)
        value_part_all = dot_first(grad, probs[h]).astype(low)
        key_rows = pl.ds(pl.multiple_of(2 * h * HEAD_DIM, 2 * HEAD_DIM), HEAD_DIM)
        value_rows = pl.ds(pl.multiple_of((2 * h + 1) * HEAD_DIM, HEAD_DIM), HEAD_DIM)
        for j in range(4):
            leave[j, key_rows, :] = key_part[:, j * count : (j + 1) * count]
            leave[j, value_rows, :] = value_part_all[:, j * count : (j + 1) * count]
        for k in (1, 2, 3):

            @pl.when(dp >= k)
            def _():
                leave_copy(k, h).start()

        return carry

    lax.fori_loop(0, HEADS, head, 0)

    relays((backward, 1), (next_one, 0), (next_one, 1))
    branch_turned[...] = branch[...].T
    for n in range(HEADS):
        for j in range(VE):
            c = VE * n + j
            gate = gates[:, spread_count + c : spread_count + c + 1]
            mixed[:, j * HEAD_DIM : (j + 1) * HEAD_DIM] = (gate * attended[:, head_of(c)]).astype(low)
        weight_grad(n, branch_turned, mixed[...])
        if n:
            halve_near(n - 1)
    for name in ("normed_one", "query_weight"):
        got[name].wait()
    one_turned[...] = normed_one[...].T
    weight_grad(4, one_turned, grad_query[...])
    halve_near(3)
    hidden_turned[...] = hidden[...].T
    returned[:, :D] = dot_last(grad_query[...], query_weight[...])
    halve_near(4)
    got["value_all"].wait()

    for h in range(HEADS):
        rows = pl.ds(h * 2 * HEAD_DIM, 2 * HEAD_DIM)
        total = leave[dp, rows, :].astype(full)
        for k in (1, 2, 3):

            @pl.when(dp + k < 4)
            def _():
                leave_copy(k, h).wait_recv()

            @pl.when(dp + k >= 4)
            def _():
                arrive[k - 1, rows, :] = jnp.zeros((2 * HEAD_DIM, count), low)

            total += arrive[k - 1, rows, :].astype(full)
        turned = total.T
        grad_key[:, h * HEAD_DIM : (h + 1) * HEAD_DIM] = turned[:, :HEAD_DIM].astype(low)
        grad = turned[:, HEAD_DIM:].astype(low).astype(full)
        for c in range(h * VE, (h + 1) * VE):
            here = slice(c * HEAD_DIM, (c + 1) * HEAD_DIM)
            grad_each[:, here] = (gates[:, c : c + 1] * grad).astype(low)
            dots = jnp.sum(value_all[:, here].astype(full) * grad, axis=1, keepdims=True)
            logit_one[:, c : c + 1] = dots * slopes[:, c : c + 1]
        weight_grad(5 + h, hidden_turned, grad_each[:, h * PIECE : (h + 1) * PIECE])
        if h:
            halve_near(4 + h)
    weight_grad(9, one_turned, grad_key[...])
    halve_near(8)
    got["key_weight"].wait()
    returned[:, :D] += dot_last(grad_key[...], key_weight[...])
    halve_near(9)
    halve_far(2)
    returned[:, :D] += jnp.dot(logit_one[...].astype(low), routers[...], preferred_element_type=full)

    def first_norm(n, gain_sum):
        rows = pl.ds(pl.multiple_of(n * rows_each, rows_each), rows_each)
        back, gain_part = norm_back(hidden[rows, :].astype(full), returned[rows, :D], gains[0:1, :])
        grad_in[rows, :] = grad_middle[rows, :] + back
        return gain_sum + gain_part

    gain_one_sum = lax.fori_loop(0, count // rows_each, first_norm, jnp.zeros((1, D), full))
    halve_far(3)
    for made in weight_copies:
        made.wait()
    got["normed_two"].wait()
    small_turned[...] = dot_first(logit_one[...].astype(low), normed_one[...]) + dot_first(
        logit_two[...], normed_two[...]
    )
    small_rows = 2 * spread_count + total_experts
    small_turned[small_rows : small_rows + 1, :] = gain_one_sum
    small_turned[small_rows + 1 : small_rows + 2, :] = gain_two_sum
    sums = output_rows()
    block_leaves = pltpu.make_async_copy(block_out, block_at, out_leave.at[0])
    block_leaves.start()
    grad_leaves = pltpu.make_async_copy(grad_in, grad_at, out_leave.at[1])
    for i in range(5):
        small_turned[small_rows + 2 + i : small_rows + 3 + i, :] = jnp.broadcast_to(sums[:, i : i + 1], (1, D))
    grads_small[...] = small_turned[...].T.astype(low).reshape(grads_small.shape)
    halve_core(10)
    spread(2)
    halve_far(4)
    def value_side(n):
        value_copy(n).wait()
        grad_in[...] += dot_last(grad_each[:, n * PIECE : (n + 1) * PIECE], value_part[n % 2])
        if n + 2 < HEADS:
            value_copy(n + 2).start()
        if n == HEADS - 1:
            grad_leaves.start()

    for action, i in (
        (halve_near, 10), (spread, 3),
        (value_side, 0), (halve_far, 5), (halve_far, 0), (spread, 4), (finish, 2),
        (value_side, 1), (halve_far, 6), (spread, 0), (finish, 3), (spread, 5),
        (value_side, 2), (halve_far, 7), (finish, 4), (spread, 6),
        (value_side, 3), (finish, 0), (halve_far, 1), (halve_far, 8), (finish, 5), (spread, 7),
        (spread, 1), (halve_far, 9), (finish, 6), (spread, 8), (halve_far, 10), (finish, 7), (finish, 1), (spread, 9),
        (spread, 10), (finish, 8), (finish, 9), (finish, 10),
    ):
        action(i)
    for h in range(HEADS):
        for k in (1, 2, 3):

            @pl.when(dp >= k)
            def _():
                leave_copy(k, h).wait_send()

    for part in range(2):
        forward_copy(z, 0, z, 1, part).wait_send()
        forward_copy(z, 0, z, 3, part).wait_send()

        @pl.when(inner == 0)
        def _():
            forward_copy(z, 0, z, 0, part).wait_send()

        @pl.when(inner == 1)
        def _():
            forward_copy(z, 0, z, 2, part).wait_send()

    block_leaves.wait()
    grad_leaves.wait()


def backward(total_experts, lengths, gates, slopes, routers, gains, *arrays):
    low, full = jnp.bfloat16, jnp.float32
    count = gates.shape[0]
    width, wide = HEADS * HEAD_DIM, HEADS * VE * HEAD_DIM
    vmem = pl.BlockSpec(memory_space=pltpu.VMEM)
    anywhere = pl.BlockSpec(memory_space=pl.ANY)
    dma = pltpu.SemaphoreType.DMA
    whole = [pltpu.VMEM(a.shape, a.dtype) for a in arrays[:15]]
    n = 11
    return pl.pallas_call(
        functools.partial(backward_kernel, total_experts),
        out_shape=[
            jax.ShapeDtypeStruct((count, D), low),
            jax.ShapeDtypeStruct((count, D), full),
            jax.ShapeDtypeStruct((ROWS, width), full),
            jax.ShapeDtypeStruct((ROWS, width), full),
            jax.ShapeDtypeStruct((ROWS, wide), full),
            jax.ShapeDtypeStruct((ROWS, wide), full),
            jax.ShapeDtypeStruct((ROWS, 128), full),
            jax.ShapeDtypeStruct(arrays[0].shape, low),
        ],
        in_specs=[pl.BlockSpec(memory_space=pltpu.SMEM)] + [vmem] * 4 + [anywhere] * len(arrays),
        out_specs=[anywhere] * 2 + [vmem] * 6,
        scratch_shapes=[pltpu.VMEM((count, D), low), pltpu.VMEM((count, D), full)]
        + whole
        + [
            pltpu.VMEM((2, D, PIECE), low),
            pltpu.VMEM((2, PIECE, D), low),
            pltpu.VMEM((count, D), low),
            pltpu.VMEM((D, count), low),
            pltpu.VMEM((D, count), low),
            pltpu.VMEM((D, count), low),
            pltpu.VMEM((count, width), full),
            pltpu.VMEM((count, width), low),
            pltpu.VMEM((4, 2 * width, count), low),
            pltpu.VMEM((3, 2 * width, count), low),
            pltpu.VMEM((count, width), low),
            pltpu.VMEM((count, wide), low),
            pltpu.VMEM((count, D), full),
            pltpu.VMEM((count, 128), full),
            pltpu.VMEM((count, 128), low),
            pltpu.VMEM((128, D), full),
            pltpu.VMEM((count, PIECE), low),
            pltpu.VMEM((6, 4, 4, 2, ROWS, PIECE), low),
            pltpu.VMEM((4, 4, 2, ROWS, 128), low),
            pltpu.VMEM((n, 4, 4, ROWS, PIECE), low),
            pltpu.VMEM((n, 12, ROWS, PIECE), low),
            pltpu.VMEM((n, 3, ROWS, PIECE), low),
            pltpu.VMEM((5, count, D), low),
            dma((15,)),
            dma((2,)),
            dma((2, 2)),
            dma((3, HEADS)),
            dma((3, HEADS)),
            dma((n, 7)),
            dma((n, 7)),
            dma((4, 2)),
            dma((5, 2)),
            dma((2,)),
            dma((2,)),
        ],
        compiler_params=pltpu.CompilerParams(
            collective_id=3, has_side_effects=True, vmem_limit_bytes=62 * 2**20
        ),
        name="backward",
    )(lengths, gates, slopes, routers, gains, *arrays)


def expert_visit(sent, cotangent, expert_up, expert_down):
    local_experts = expert_up.shape[0]
    group = lax.axis_index("expert")
    cot_all = lax.all_gather(cotangent, "expert", axis=0, tiled=True)
    sent_all = lax.all_gather(sent, "expert", axis=0, tiled=True)
    rows_all = sent_all[:, :D]
    total_experts = sent.shape[1] - D
    gate_all = lax.dynamic_slice_in_dim(
        sent_all[:, D:], group * local_experts, local_experts, 1
    ).astype(jnp.float32).T[:, :, None]
    preact = jnp.einsum("td,xdf->xtf", rows_all, expert_up, preferred_element_type=jnp.float32)
    pre_sig = jax.nn.sigmoid(preact)
    hidden = preact * pre_sig
    back = jnp.einsum("td,xfd->xtf", cot_all, expert_down, preferred_element_type=jnp.float32)
    gate_grad = jnp.sum(hidden * back, axis=2).T
    gated = (gate_all * hidden).astype(jnp.bfloat16)
    grad_pre = (gate_all * back * (pre_sig * (1.0 + preact * (1.0 - pre_sig)))).astype(jnp.bfloat16)
    partial_out = jnp.einsum("xtf,xfd->td", gated, expert_down, preferred_element_type=jnp.float32)
    partial_grad = jnp.einsum("xtf,xdf->td", grad_pre, expert_up, preferred_element_type=jnp.float32)
    wide_grad = lax.dynamic_update_slice_in_dim(
        jnp.zeros((gate_grad.shape[0], total_experts), jnp.bfloat16),
        gate_grad.astype(jnp.bfloat16),
        group * local_experts,
        1,
    )
    returned = lax.psum_scatter(
        jnp.concatenate(
            [partial_out.astype(jnp.bfloat16), partial_grad.astype(jnp.bfloat16), wide_grad], axis=1
        ),
        "expert",
        scatter_dimension=0,
        tiled=True,
    )
    grad_down = jnp.einsum("xtf,td->xfd", gated, cot_all, preferred_element_type=jnp.float32)
    grad_up = jnp.einsum("td,xtf->xdf", rows_all, grad_pre, preferred_element_type=jnp.float32)
    return returned, grad_up, grad_down


def shards(
    hidden_in,
    lengths,
    value_pick,
    output_pick,
    expert_pick,
    query_weight,
    key_weight,
    value_weight,
    output_weight,
    value_router,
    output_router,
    expert_router,
    attention_gain,
    feedforward_gain,
    expert_up,
    expert_down,
    cotangent,
):
    row_count = hidden_in.shape[1]
    total_experts = expert_router.shape[1]
    input_low = hidden_in[0]
    input_full = input_low.astype(jnp.float32)
    length = lengths[0]
    query_pos = lax.axis_index("dp") * row_count + jnp.arange(row_count, dtype=jnp.int32)
    live_mask = (query_pos < length).astype(jnp.float32)[:, None]
    gain_one = attention_gain.astype(jnp.float32)
    gain_two = feedforward_gain.astype(jnp.float32)
    normed_one = layer_norm(input_full, gain_one)
    normed_low = normed_one.astype(jnp.bfloat16)
    queries = low_dot(normed_low, query_weight).astype(jnp.bfloat16)
    key_local = low_dot(normed_low, key_weight).astype(jnp.bfloat16)
    value_sig = jax.nn.sigmoid(low_dot(normed_low, value_router)).reshape(row_count, HEADS, VE)
    value_hot = choose(value_pick[0], VE)
    value_gate = value_sig * value_hot
    value_all = low_dot(input_low, value_weight).reshape(row_count, HEADS, VE, HEAD_DIM)
    value_local = (
        jnp.sum(value_gate[..., None] * value_all, axis=2)
        .astype(jnp.bfloat16)
        .reshape(row_count, HEADS * HEAD_DIM)
    )
    key_all, value_rows = (
        lax.all_gather(key_local, "dp", axis=0, tiled=True),
        lax.all_gather(value_local, "dp", axis=0, tiled=True),
    )
    query_heads = queries.reshape(row_count, HEADS, HEAD_DIM)
    key_heads = key_all.reshape(-1, HEADS, HEAD_DIM)
    value_heads = value_rows.reshape(-1, HEADS, HEAD_DIM)
    soft_probs = attention_probs(query_heads, key_heads, query_pos, length)
    attended = jnp.einsum(
        "hqk,khd->qhd",
        soft_probs.astype(jnp.bfloat16),
        value_heads,
        preferred_element_type=jnp.float32,
    )
    output_sig = jax.nn.sigmoid(low_dot(normed_low, output_router)).reshape(row_count, HEADS, VE)
    output_hot = choose(output_pick[0], VE)
    output_gate = output_sig * output_hot
    mixed = (
        (output_gate[..., None] * attended[:, :, None, :])
        .astype(jnp.bfloat16)
        .reshape(row_count, HEADS * VE * HEAD_DIM)
    )
    attention_out = live_mask * low_dot(mixed, output_weight)
    middle = input_full + attention_out
    normed_two = layer_norm(middle, gain_two)
    normed_two_low = normed_two.astype(jnp.bfloat16)
    router_sig = jax.nn.sigmoid(low_dot(normed_two_low, expert_router))
    hot = jnp.any(
        expert_pick[0][:, :, None] == jnp.arange(total_experts, dtype=jnp.int32), axis=1
    ).astype(jnp.float32)
    picked_hot = hot * live_mask
    expert_gate = router_sig * picked_hot
    middle_low = middle.astype(jnp.bfloat16)
    sent = jnp.concatenate([middle_low, expert_gate.astype(jnp.bfloat16)], axis=1)
    groups = lax.axis_size("expert")
    rounds = max(1, groups // 8)

    def visit(grads, item):
        returned, grad_up, grad_down = expert_visit(*item, expert_up, expert_down)
        return (grads[0] + grad_up, grads[1] + grad_down), returned

    zeros = jnp.zeros(expert_up.shape, jnp.float32), jnp.zeros(expert_down.shape, jnp.float32)
    (up_grad, down_grad), returned = lax.scan(
        visit,
        zeros,
        (
            sent.reshape(rounds, -1, sent.shape[1]),
            cotangent[0].reshape(rounds, -1, D),
        ),
    )
    returned = returned.reshape(row_count, -1).astype(jnp.float32)
    up_grad = lax.psum_scatter(
        up_grad.astype(jnp.bfloat16), "dp", scatter_dimension=1, tiled=True
    ).astype(jnp.float32)
    down_grad = lax.psum_scatter(
        down_grad.astype(jnp.bfloat16), "dp", scatter_dimension=2, tiled=True
    ).astype(jnp.float32)
    feedforward_out = returned[:, :D]
    final_rows = middle + feedforward_out
    sums = jnp.stack(
        [
            jnp.sum(live_mask * input_full * input_full),
            jnp.sum(attention_out * attention_out),
            jnp.sum(feedforward_out * feedforward_out),
            jnp.sum(live_mask * final_rows * final_rows),
            jnp.sum(live_mask),
        ]
    )
    grad_final = cotangent[0].astype(jnp.float32)
    grad_middle = grad_final + returned[:, D : 2 * D]
    grad_logit = (
        returned[:, 2 * D :] * picked_hot * router_sig * (1.0 - router_sig)
    ).astype(jnp.bfloat16)
    grad_expert_router = low_dot(normed_two_low.T, grad_logit)
    grad_normed_two = low_dot(grad_logit, expert_router.T)
    unused_two, norm_two_back = jax.vjp(layer_norm, middle, gain_two)
    grad_middle_norm, grad_gain_two = norm_two_back(grad_normed_two)
    grad_middle = grad_middle + grad_middle_norm
    grad_branch = (live_mask * grad_middle).astype(jnp.bfloat16)
    grad_mixed = jnp.einsum(
        "td,md->tm", grad_branch, output_weight, preferred_element_type=jnp.float32
    ).reshape(row_count, HEADS, VE, HEAD_DIM)
    grad_output_weight = jnp.einsum(
        "td,tm->dm", grad_branch, mixed, preferred_element_type=jnp.float32
    )
    grad_attended = jnp.sum(output_gate[..., None] * grad_mixed, axis=2)
    grad_output_logit = (
        jnp.sum(attended[:, :, None, :] * grad_mixed, axis=3)
        * output_hot
        * output_sig
        * (1.0 - output_sig)
    ).reshape(row_count, HEADS * VE)
    grad_attended_low = grad_attended.astype(jnp.bfloat16)
    grad_probs = jnp.einsum(
        "qhd,khd->hqk", grad_attended_low, value_heads, preferred_element_type=jnp.float32
    )
    row_dot = jnp.sum(soft_probs * grad_probs, axis=-1, keepdims=True)
    grad_scores = (soft_probs * (grad_probs - row_dot) * HEAD_DIM ** (-0.5)).astype(jnp.bfloat16)
    grad_query = (
        jnp.einsum("hqk,khd->qhd", grad_scores, key_heads, preferred_element_type=jnp.float32)
        .astype(jnp.bfloat16)
        .reshape(row_count, HEADS * HEAD_DIM)
    )
    grad_key_all = jnp.einsum(
        "hqk,qhd->khd", grad_scores, query_heads, preferred_element_type=jnp.float32
    ).reshape(-1, HEADS * HEAD_DIM)
    grad_value_rows = jnp.einsum(
        "hqk,qhd->khd",
        soft_probs.astype(jnp.bfloat16),
        grad_attended_low,
        preferred_element_type=jnp.float32,
    ).reshape(-1, HEADS * HEAD_DIM)
    grad_key_sum, grad_value_sum = (
        lax.psum_scatter(
            grad_key_all.astype(jnp.bfloat16), "dp", scatter_dimension=0, tiled=True
        ).astype(jnp.float32),
        lax.psum_scatter(
            grad_value_rows.astype(jnp.bfloat16), "dp", scatter_dimension=0, tiled=True
        ).astype(jnp.float32),
    )
    grad_key = grad_key_sum.astype(jnp.bfloat16)
    grad_value_low = (
        grad_value_sum.astype(jnp.bfloat16)
        .astype(jnp.float32)
        .reshape(row_count, HEADS, 1, HEAD_DIM)
    )
    grad_value_each = (
        (value_gate[..., None] * grad_value_low)
        .astype(jnp.bfloat16)
        .reshape(row_count, HEADS * VE * HEAD_DIM)
    )
    grad_value_logit = (
        jnp.sum(value_all * grad_value_low, axis=3) * value_hot * value_sig * (1.0 - value_sig)
    ).reshape(row_count, HEADS * VE)
    grad_value_weight = jnp.einsum(
        "td,tm->dm", input_low, grad_value_each, preferred_element_type=jnp.float32
    )
    grad_query_weight = jnp.einsum(
        "td,tm->dm", normed_low, grad_query, preferred_element_type=jnp.float32
    )
    grad_key_weight = jnp.einsum(
        "td,tm->dm", normed_low, grad_key, preferred_element_type=jnp.float32
    )
    grad_value_logit = grad_value_logit.astype(jnp.bfloat16)
    grad_output_logit = grad_output_logit.astype(jnp.bfloat16)
    grad_value_router = low_dot(normed_low.T, grad_value_logit)
    grad_output_router = low_dot(normed_low.T, grad_output_logit)
    grad_normed_one = (
        jnp.einsum("tm,dm->td", grad_query, query_weight, preferred_element_type=jnp.float32)
        + jnp.einsum("tm,dm->td", grad_key, key_weight, preferred_element_type=jnp.float32)
        + low_dot(grad_value_logit, value_router.T)
        + low_dot(grad_output_logit, output_router.T)
    )
    unused_one, norm_one_back = jax.vjp(layer_norm, input_full, gain_one)
    grad_input_norm, grad_gain_one = norm_one_back(grad_normed_one)
    grad_input = (
        grad_middle
        + jnp.einsum("tm,dm->td", grad_value_each, value_weight, preferred_element_type=jnp.float32)
        + grad_input_norm
    )
    small_grads = jnp.concatenate(
        [
            grad_value_router,
            grad_output_router,
            grad_expert_router,
            grad_gain_one[:, None],
            grad_gain_two[:, None],
        ],
        axis=1,
    )
    small_count = small_grads.shape[1]
    small_grads = jnp.pad(small_grads, ((0, 0), (0, -small_count % 128)))
    low_grads = [
        part.astype(jnp.bfloat16)
        for part in (
            grad_query_weight,
            grad_key_weight,
            grad_value_weight,
            grad_output_weight,
            small_grads,
        )
    ]
    summed = lax.psum_scatter(
        jnp.concatenate(low_grads, axis=1), ("dp", "expert"), scatter_dimension=0, tiled=True
    ).astype(jnp.float32)
    dense_grads = jnp.split(summed, [512, 1024, 3584, 6144], axis=1)
    total_sums = lax.psum(sums, ("dp", "expert"))
    residual_norms = jnp.sqrt(total_sums[:4] / (total_sums[4] * D))
    small = dense_grads[4]
    router_end = 2 * HEADS * VE + expert_router.shape[1]
    dense_grads = [
        dense_grads[0],
        dense_grads[1],
        dense_grads[2],
        dense_grads[3].T,
        small[:, : HEADS * VE],
        small[:, HEADS * VE : 2 * HEADS * VE],
        small[:, 2 * HEADS * VE : router_end],
        small[:, router_end],
        small[:, router_end + 1],
    ]
    return (
        final_rows.astype(jnp.bfloat16)[None],
        grad_input[None],
        dense_grads[0],
        dense_grads[1],
        dense_grads[2],
        dense_grads[3],
        dense_grads[4],
        dense_grads[5],
        dense_grads[6],
        dense_grads[7],
        dense_grads[8],
        up_grad,
        down_grad,
        residual_norms,
    )


def deliver_kernel(total, small, weights_kept_at, weights_in_at, *refs):
    weights_kept, weights_in, up_out, down_out, weights_sem = refs[-5:]
    refs = refs[:-5]
    count = (len(refs) - 9) // 3
    sources, targets = refs[:count], refs[count : 2 * count]
    value_out, output_out, expert_out, gains_out, norms_out, up_at, down_at = refs[2 * count : 2 * count + 7]
    held = refs[2 * count + 7 : -2]
    inward, outward = refs[-2:]
    arrived = [pltpu.make_async_copy(a, b, inward.at[i]) for i, (a, b) in enumerate(zip(sources, held))]
    left = [pltpu.make_async_copy(a, b, outward.at[i]) for i, (a, b) in enumerate(zip(held, targets))]
    weights = [
        pltpu.make_async_copy(weights_kept_at, weights_kept, weights_sem.at[0]),
        pltpu.make_async_copy(weights_in_at, weights_in, weights_sem.at[1]),
    ]
    summed = [
        pltpu.make_async_copy(up_out, up_at, weights_sem.at[2]),
        pltpu.make_async_copy(down_out, down_at, weights_sem.at[3]),
    ]
    for made in arrived + weights:
        made.start()
    spread = HEADS * VE
    turned = jnp.concatenate([small[...], jnp.zeros((128 - ROWS, 128), jnp.float32)]).T
    value_out[...] = turned[:spread, :ROWS]
    output_out[...] = turned[spread : 2 * spread, :ROWS]
    expert_out[...] = small[:, 2 * spread : 2 * spread + total]
    gains_out[...] = turned[2 * spread + total : 2 * spread + total + 2, :ROWS]
    row = small[0:1, :]
    first = 2 * spread + total + 2
    norms_out[...] = jnp.sqrt(row[:, first : first + 4] / (row[:, first + 4 : first + 5] * D))
    for one, other in zip(arrived, left):
        one.wait()
        other.start()
    for made in weights:
        made.wait()
    for e in range(up_out.shape[0]):
        rows = slice(e * HEAD_DIM, (e + 1) * HEAD_DIM)
        up_sum, down_sum = [
            weights_kept[i, rows, :].astype(jnp.float32) + weights_in[i, rows, :].astype(jnp.float32)
            for i in range(2)
        ]
        up_out[e] = up_sum.T
        down_out[e] = down_sum
    for made in summed:
        made.start()
    for made in left + summed:
        made.wait()


def deliver(total, small, weights_kept, weights_in, *arrays):
    experts = weights_in.shape[1] // HEAD_DIM
    full = jnp.float32
    vmem = pl.BlockSpec(memory_space=pltpu.VMEM)
    anywhere = pl.BlockSpec(memory_space=pl.ANY)
    spread = HEADS * VE
    return pl.pallas_call(
        functools.partial(deliver_kernel, total),
        out_shape=[jax.ShapeDtypeStruct(a.shape, a.dtype) for a in arrays]
        + [
            jax.ShapeDtypeStruct((spread, ROWS), full),
            jax.ShapeDtypeStruct((spread, ROWS), full),
            jax.ShapeDtypeStruct((ROWS, total), full),
            jax.ShapeDtypeStruct((2, ROWS), full),
            jax.ShapeDtypeStruct((1, 4), full),
            jax.ShapeDtypeStruct((experts, D // 4, HEAD_DIM), full),
            jax.ShapeDtypeStruct((experts, HEAD_DIM, D // 4), full),
        ],
        in_specs=[vmem] + [anywhere] * (2 + len(arrays)),
        out_specs=[anywhere] * len(arrays) + [vmem] * 5 + [anywhere] * 2,
        scratch_shapes=[pltpu.VMEM(a.shape, a.dtype) for a in arrays]
        + [pltpu.SemaphoreType.DMA((len(arrays),))] * 2
        + [
            pltpu.VMEM(weights_kept.shape, weights_kept.dtype),
            pltpu.VMEM(weights_in.shape, weights_in.dtype),
            pltpu.VMEM((experts, D // 4, HEAD_DIM), full),
            pltpu.VMEM((experts, HEAD_DIM, D // 4), full),
            pltpu.SemaphoreType.DMA((4,)),
        ],
        compiler_params=pltpu.CompilerParams(vmem_limit_bytes=63 * 2**20),
        name="deliver",
    )(small, weights_kept, weights_in, *arrays)


def shards_fast(
    hidden_in,
    lengths,
    value_pick,
    output_pick,
    expert_pick,
    query_weight,
    key_weight,
    value_weight,
    output_weight,
    value_router,
    output_router,
    expert_router,
    attention_gain,
    feedforward_gain,
    expert_up,
    expert_down,
    cotangent,
):
    total = expert_router.shape[1]
    (
        middle,
        sent,
        normed_one,
        normed_two,
        queries,
        key_value,
        probs,
        value_all,
        attended,
        gates,
        slopes,
        cot_line,
        routers,
        gains,
    ) = attend(
        total,
        lengths,
        hidden_in[0],
        cotangent[0],
        value_pick[0].transpose(1, 2, 0),
        output_pick[0].transpose(1, 2, 0),
        expert_pick[0].T,
        value_router.T,
        output_router.T,
        expert_router.T,
        attention_gain,
        feedforward_gain,
        key_weight,
        value_weight,
        query_weight,
        output_weight,
    )
    returned, weights, weights_kept, forward = expert_kernel_visit(sent, cot_line, expert_up, expert_down)
    block_out, grad_input, grad_query, grad_key, grad_value, grad_output, small, weights_in = backward(
        total,
        lengths,
        gates,
        slopes,
        routers,
        gains,
        weights,
        forward,
        returned,
        middle,
        cotangent[0],
        hidden_in[0],
        normed_one,
        queries,
        key_value,
        probs,
        value_all,
        attended,
        normed_two,
        query_weight,
        key_weight,
        value_weight,
        output_weight,
    )
    kept = (block_out, grad_input, grad_query, grad_key, grad_value, grad_output)
    delivered = deliver(total, small, weights_kept, weights_in, *kept)
    block_out, grad_input, grad_query, grad_key, grad_value, grad_output = delivered[:6]
    value_small, output_small, expert_small, gain_grads, norms, up_grad, down_grad = delivered[6:]
    return (
        block_out[None],
        grad_input[None],
        grad_query,
        grad_key,
        grad_value,
        grad_output.T,
        value_small.T,
        output_small.T,
        expert_small,
        gain_grads[0],
        gain_grads[1],
        up_grad,
        down_grad,
        norms[0],
    )


def solution(mesh):
    placed = (
        P("expert", "dp", None),
        P("expert"),
        P("expert", "dp", None, None),
        P("expert", "dp", None, None),
        P("expert", "dp", None),
        P(),
        P(),
        P(),
        P(),
        P(),
        P(),
        P(),
        P(),
        P(),
        P("expert", None, None),
        P("expert", None, None),
        P("expert", "dp", None),
    )
    small_mesh = mesh.shape["dp"] == 4 and mesh.shape["expert"] == 8
    return jax.shard_map(
        shards_fast if small_mesh else shards,
        mesh=mesh,
        in_specs=placed,
        out_specs=(
            P("expert", "dp", None),
            P("expert", "dp", None),
            P(("dp", "expert"), None),
            P(("dp", "expert"), None),
            P(("dp", "expert"), None),
            P(None, ("dp", "expert")),
            P(("dp", "expert"), None),
            P(("dp", "expert"), None),
            P(("dp", "expert"), None),
            P(("dp", "expert")),
            P(("dp", "expert")),
            P("expert", "dp", None),
            P("expert", None, "dp"),
            P(),
        ),
        check_vma=False,
    )
```

```python
import functools

import jax
import jax.numpy as jnp
from jax import lax
from jax.experimental import pallas as pl
from jax.experimental.pallas import tpu as pltpu
from jax.sharding import PartitionSpec as P

D = 1024
HEADS = 4
HEAD_DIM = 128
VE = 5


MESH = pl.DeviceIdType.MESH
ROWS = 32
PIECE = VE * HEAD_DIM
EPSILON = 1e-05
NEGATIVE = -1000000000.0


def low_dot(left_side, right_side):
    return jnp.dot(left_side, right_side, preferred_element_type=jnp.float32)


def layer_norm(field, scale_gain):
    center = field - jnp.mean(field, axis=-1, keepdims=True)
    spread = jnp.mean(center * center, axis=-1, keepdims=True)
    return center * lax.rsqrt(spread + EPSILON) * scale_gain


def choose(select, count):
    return jnp.sum(
        (select[..., None] == jnp.arange(count, dtype=jnp.int32)).astype(jnp.float32), axis=-2
    )


def attention_probs(query_heads, key_heads, query_pos, length):
    key_pos = jnp.arange(key_heads.shape[0], dtype=jnp.int32)
    raw_scores = jnp.einsum(
        "qhd,khd->hqk", query_heads, key_heads, preferred_element_type=jnp.float32
    )
    allowed = (key_pos[None, :] <= query_pos[:, None]) & (key_pos[None, :] < length)
    scores = jnp.where(allowed[None], raw_scores * HEAD_DIM ** (-0.5), NEGATIVE)
    exp_terms = jnp.exp(scores - jnp.max(scores, axis=-1, keepdims=True))
    return exp_terms / jnp.sum(exp_terms, axis=-1, keepdims=True)


def dot_last(left_side, right_side):
    return lax.dot_general(
        left_side, right_side, (((1,), (1,)), ((), ())), preferred_element_type=jnp.float32
    )

def dot_first(left_side, right_side):
    return lax.dot_general(
        left_side, right_side, (((0,), (0,)), ((), ())), preferred_element_type=jnp.float32
    )


def visit_kernel(
    sent, cot_at, up_at, down_at, back_at, weights_out, weights_kept, forward_at,
    back_out, forward_out, cot, up, down, rows, cot_other, up_wide, chosen, cots, gated, grad_pre, forward, forward_in, gated_turned, pre_turned, partial, paired_in, chain_in, up_low, down_low, up_in, down_in,
    fetch, back_leave, forward_leave, row_send, row_recv, half_send, half_recv, cot_send, cot_recv, pair_send, pair_recv, forward_send, forward_recv, chain_send, chain_recv, grad_send, grad_recv,
):
    experts = up.shape[0]
    wide = down.shape[0]
    hidden = wide // experts
    dp, ex = lax.axis_index("dp"), lax.axis_index("expert")
    y, x, z, core = dp // 2, dp % 2, ex // 2, ex % 2
    half = z // 2
    inner = z + half * (3 - 2 * z)
    onward = 1 - 2 * half
    sibling = (dp, z * 2 + 1 - core)
    beside, behind = (y * 2 + 1 - x, ex), ((1 - y) * 2 + x, ex)

    def at_z(place):
        return (dp, place * 2 + core)

    fetched = [
        pltpu.make_async_copy(source, target, fetch.at[i])
        for i, (source, target) in enumerate(((cot_at, cot), (up_at, up), (down_at, down)))
    ]
    for made in fetched:
        made.start()
    barrier = pltpu.get_barrier_semaphore()
    for place in (sibling, beside, behind):
        pl.semaphore_signal(barrier, inc=1, device_id=place, device_id_type=MESH)

    @pl.when(z < 3)
    def _():
        pl.semaphore_signal(barrier, inc=1, device_id=at_z(z + 1), device_id_type=MESH)

    @pl.when(z > 0)
    def _():
        pl.semaphore_signal(barrier, inc=1, device_id=at_z(z - 1), device_id_type=MESH)

    pl.semaphore_wait(barrier, 4 + inner)

    def remote(source, target, send, recv, place):
        return pltpu.make_async_remote_copy(
            src_ref=source, dst_ref=target, send_sem=send, recv_sem=recv, device_id=place, device_id_type=MESH
        )

    def row_copy(at, source=None):
        block = rows.at[at] if source is None else source
        return remote(block, rows.at[4 + at], row_send.at[at], row_recv.at[at], sibling)

    def half_copy(way, at, part, source=None):
        span = pl.ds(part * (rows.shape[1] // 2), rows.shape[1] // 2)
        block = rows.at[at] if source is None else source
        return remote(
            block.at[span], rows.at[at, span], half_send.at[way, at, part], half_recv.at[at, part], at_z(z + 1 - 2 * way)
        )

    def cot_copy(at):
        return remote(cot.at[at], cot_other.at[at], cot_send.at[at], cot_recv.at[at], sibling)

    @pl.when(z < 3)
    def _():
        for part in range(2):
            half_copy(0, z, part, sent).start()

    @pl.when(z > 0)
    def _():
        for part in range(2):
            half_copy(1, z, part, sent).start()

    row_copy(z, sent).start()
    for made in fetched:
        made.wait()
    cot_copy(z).start()
    for k in (1, 2, 3):
        cot_copy((z + k) % 4).start()
    rows[z] = sent[...]
    for e in range(experts):
        up_wide[:, e * hidden : (e + 1) * hidden] = up[e]
    chosen[...] = (
        lax.broadcasted_iota(jnp.int32, (128, wide), 0)
        == 2 * HEADS * VE + ex * experts + lax.broadcasted_iota(jnp.int32, (128, wide), 1) // hidden
    ).astype(jnp.float32).astype(jnp.bfloat16)

    def order(p):
        later = (p + 2) // 3
        step = p - inner // (p + 1 - later)
        return later * (step + half * (3 - 2 * step)) + (1 - later) * z

    def pair_copy(at):
        return remote(partial.at[1, at], paired_in.at[at], pair_send.at[at], pair_recv.at[at], sibling)

    parts = 4
    size = rows.shape[1] // parts
    spans = [pl.ds(i * size, size) for i in range(parts)]

    def chain_copy(dest, slot, to, stage, part):
        span = spans[part]
        return remote(
            partial.at[0, dest, span], chain_in.at[slot, span],
            chain_send.at[stage, part], chain_recv.at[slot, part], at_z(to),
        )

    def add(target, source):
        def some(i, carry):
            part = pl.ds(pl.multiple_of(i * 32, 32), 32)
            target[part, :] = (
                target[part, :].astype(jnp.float32) + source[part, :].astype(jnp.float32)
            ).astype(target.dtype)
            return carry

        lax.fori_loop(0, target.shape[0] // 32, some, 0)

    def forward_copy(at):
        return remote(forward.at[at], forward_in.at[at], forward_send.at[at], forward_recv.at[at], sibling)

    def forward_block(block):
        at = block % 4
        def some(n, inside):
            span = pl.ds(pl.multiple_of(n * 256, 256), 256)
            value = jnp.dot(gated[block], down[:, span], preferred_element_type=jnp.float32).astype(jnp.bfloat16)

            @pl.when(block >= 4)
            def _():
                forward[at, :, span] = value

            @pl.when(block < 4)
            def _():
                forward_out[at, :, span] = value

            return inside

        lax.fori_loop(0, D // 256, some, 0)

        @pl.when(block >= 4)
        def _():
            forward_copy(at).start()

    def relay(dest, slot, to, stage, part):
        chain_copy(dest, dest, to, stage, part).wait_recv()
        add(partial.at[0, dest, spans[part]], chain_in.at[dest, spans[part]])
        chain_copy(dest, slot, to, stage, part).start()

    def visit(q, carry):
        p, other = q // 2, q % 2
        at = order(p)
        block = other * 4 + at

        @pl.when((other == 0) & (p > 0))
        def _():
            for part in range(2):
                half_copy(0, at, part).wait_recv()

                @pl.when((at < z) & (z < 3))
                def _():
                    half_copy(0, at, part).start()

                @pl.when((at > z) & (z > 0))
                def _():
                    half_copy(1, at, part).start()

            row_copy(at).start()

        @pl.when(other == 1)
        def _():
            row_copy(at).wait_recv()
            cot_copy(at).wait_recv()
            cots[...] = cot_other[at]

        @pl.when(other == 0)
        def _():
            cots[...] = cot[at]

        @pl.when((inner == 1) & (q == 7))
        def _():
            relay(*next_one, 0)
            relay(*next_one, 1)

        count = rows.shape[1]
        places = pl.ds(pl.multiple_of(block * count, count), count)

        def columns(n, gate_grad):
            span = pl.ds(pl.multiple_of(n * 256, 256), 256)
            pre = jnp.dot(rows[block, :, :D], up_wide[:, span], preferred_element_type=jnp.float32)
            back = dot_last(cots[...], down[span, :])
            mark = chosen[:, span]
            gate = jnp.dot(rows[block, :, D:], mark, preferred_element_type=jnp.float32)
            sig = jax.nn.sigmoid(pre)
            act = pre * sig
            act_low = (gate * act).astype(jnp.bfloat16)
            pre_low = (gate * back * (sig * (1.0 + pre * (1.0 - sig)))).astype(jnp.bfloat16)
            gated[block, :, span] = act_low
            grad_pre[:, span] = pre_low
            gated_turned[span, places] = act_low.T
            pre_turned[span, places] = pre_low.T
            return gate_grad + dot_last((act * back).astype(jnp.bfloat16), mark)

        partial[other, at, :, D:] = lax.fori_loop(
            0, wide // 256, columns, jnp.zeros((count, 128), jnp.float32)
        ).astype(jnp.bfloat16)

        def outward(n, carry):
            span = pl.ds(pl.multiple_of(n * 256, 256), 256)
            partial[other, at, :, span] = dot_last(grad_pre[...], up_wide[span, :]).astype(jnp.bfloat16)
            return carry

        lax.fori_loop(0, D // 256, outward, 0)

        @pl.when(other == 1)
        def _():
            pair_copy(at).start()
            pair_copy(at).wait_recv()
            add(partial.at[0, at], paired_in.at[at])

        @pl.when((inner == 0) & (q == 3))
        def _():
            for part in range(parts):
                chain_copy(*nearest, part).start()

        @pl.when((inner == 0) & (q == 5))
        def _():
            for part in range(parts):
                chain_copy(*next_one, part).start()

        @pl.when(q < 6)
        def _():
            forward_block(block)

        return carry

    nearest = (z + onward, z + onward, z + onward, 0)
    farthest = (3 * (1 - half), 3 * (1 - half), z + onward, 1)
    backward = (3 * half, 3 * half, z - onward, 2)
    next_one = (2 - half, 2 - half + inner * (2 + half), z + onward, 3)
    lax.fori_loop(0, 8, visit, 0)

    @pl.when(inner == 0)
    def _():
        for part in range(parts):
            chain_copy(*farthest, part).start()
    tokens_all = rows.reshape(rows.shape[0] * rows.shape[1], rows.shape[2])
    cots_own = cot.reshape(cot.shape[0] * cot.shape[1], D)
    cots_other = cot_other.reshape(cot.shape[0] * cot.shape[1], D)
    place = cots_own.shape[0]
    quarter = D // 4


    def up_copy(j):
        return remote(up_low.at[j], up_in.at[j], grad_send.at[0, j], grad_recv.at[0, j], behind if j == 2 else beside)

    def down_copy(j):
        return remote(down_low.at[j], down_in.at[j], grad_send.at[1, j], grad_recv.at[1, j], beside if j == 1 else behind)

    def span_of(j):
        at = (y + (1 - j % 2) * (1 - 2 * y)) * 2 + x + (1 - j // 2) * (1 - 2 * x)
        return pl.ds(pl.multiple_of(at * quarter, quarter), quarter)

    def up_quarter(j):
        up_low[j] = jnp.dot(
            pre_turned[...], tokens_all[:, span_of(j)], preferred_element_type=jnp.float32
        ).astype(jnp.bfloat16)
        if j < 2:
            up_copy(j).start()

    def down_quarter(j):
        down_low[j] = (
            jnp.dot(gated_turned[:, :place], cots_own[:, span_of(j)], preferred_element_type=jnp.float32)
            + jnp.dot(gated_turned[:, place:], cots_other[:, span_of(j)], preferred_element_type=jnp.float32)
        ).astype(jnp.bfloat16)
        if j in (0, 2):
            down_copy(j).start()

    def relays(*ways):
        @pl.when(inner == 1)
        def _():
            for way, part in ways:
                relay(*way, part)

    def forward_leaves(at):
        return pltpu.make_async_copy(forward_out.at[at], forward_at.at[at], forward_leave.at[at])

    def back_leaves(part):
        return pltpu.make_async_copy(back_out.at[spans[part]], back_at.at[spans[part]], back_leave.at[part])

    def forward_add(p):
        at = order(p)
        forward_copy(at).wait()
        add(forward_out.at[at], forward_in.at[at])
        forward_leaves(at).start()

    relays((next_one, 2), (next_one, 3))
    up_quarter(0)
    down_quarter(0)
    relays((farthest, 0))
    up_quarter(1)
    relays((farthest, 1))
    down_quarter(2)
    relays((backward, 0), (farthest, 2))
    forward_block(4 + order(3))
    relays((backward, 1), (farthest, 3))
    up_quarter(2)
    relays((backward, 2))
    forward_add(0)
    forward_add(1)
    down_quarter(1)
    relays((backward, 3))
    forward_block(order(3))
    up_quarter(3)
    down_quarter(3)
    forward_add(2)
    forward_add(3)
    for part in range(parts):
        span = spans[part]
        chain_copy(z, z, z, 0, part).wait_recv()
        back_out[span, :] = partial[0, z, span, :].astype(jnp.float32) + chain_in[z, span, :].astype(jnp.float32)

        @pl.when(inner == 1)
        def _():
            chain_copy(z, 4, z, 0, part).wait_recv()
            back_out[span, :] = back_out[span, :] + chain_in[4, span, :].astype(jnp.float32)

        back_leaves(part).start()

    ends = (
        (up_copy(0), up_low, 2, up_in, 0, weights_out.at[0]),
        (up_copy(1), up_low, 3, up_in, 1, weights_kept.at[0]),
        (down_copy(0), down_low, 1, down_in, 0, weights_out.at[1]),
        (down_copy(2), down_low, 3, down_in, 2, weights_kept.at[1]),
    )
    for made, mine, j, other, slot, target in ends:
        made.wait()
        target[...] = mine[j]
        add(target, other.at[slot])

    for at in range(4):
        row_copy(at).wait_send()
        cot_copy(at).wait_send()
        pair_copy(at).wait_send()
        for part in range(2):

            @pl.when((at <= z) & (z < 3))
            def _():
                half_copy(0, at, part).wait_send()

            @pl.when((at >= z) & (z > 0))
            def _():
                half_copy(1, at, part).wait_send()

    for part in range(parts):

        @pl.when(inner == 0)
        def _():
            chain_copy(z, 0, z, 0, part).wait_send()

        @pl.when(inner == 1)
        def _():
            chain_copy(z, 0, z, 2, part).wait_send()

        chain_copy(z, 0, z, 1, part).wait_send()
        chain_copy(z, 0, z, 3, part).wait_send()

    for at in range(4):
        forward_leaves(at).wait()
        back_leaves(at).wait()


def expert_kernel_visit(sent, cot_line, up, down):
    tokens = sent.shape[0]
    experts, _, hidden = up.shape
    wide = experts * hidden
    low = jnp.bfloat16
    vmem = pl.BlockSpec(memory_space=pltpu.VMEM)
    dma = pltpu.SemaphoreType.DMA
    f32 = jnp.float32
    return pl.pallas_call(
        visit_kernel,
        out_shape=[
            jax.ShapeDtypeStruct((tokens, D + 128), f32),
            jax.ShapeDtypeStruct((2, wide, D // 4), low),
            jax.ShapeDtypeStruct((2, wide, D // 4), low),
            jax.ShapeDtypeStruct((4, tokens, D), low),
        ],
        in_specs=[vmem] + [pl.BlockSpec(memory_space=pl.ANY)] * 3,
        out_specs=[pl.BlockSpec(memory_space=pl.ANY), vmem, vmem, pl.BlockSpec(memory_space=pl.ANY)],
        scratch_shapes=[
            pltpu.VMEM((tokens, D + 128), f32),
            pltpu.VMEM((4, tokens, D), low),
            pltpu.VMEM((4, tokens, D), low),
            pltpu.VMEM((experts, D, hidden), low),
            pltpu.VMEM((wide, D), low),
            pltpu.VMEM((8, tokens, D + 128), low),
            pltpu.VMEM((4, tokens, D), low),
            pltpu.VMEM((D, wide), low),
            pltpu.VMEM((128, wide), low),
            pltpu.VMEM((tokens, D), low),
            pltpu.VMEM((8, tokens, wide), low),
            pltpu.VMEM((tokens, wide), low),
            pltpu.VMEM((4, tokens, D), low),
            pltpu.VMEM((4, tokens, D), low),
            pltpu.VMEM((wide, 8 * tokens), low),
            pltpu.VMEM((wide, 8 * tokens), low),
            pltpu.VMEM((2, 4, tokens, D + 128), low),
            pltpu.VMEM((4, tokens, D + 128), low),
            pltpu.VMEM((5, tokens, D + 128), low),
            pltpu.VMEM((4, wide, D // 4), low),
            pltpu.VMEM((4, wide, D // 4), low),
            pltpu.VMEM((3, wide, D // 4), low),
            pltpu.VMEM((3, wide, D // 4), low),
            dma((3,)), dma((4,)), dma((4,)), dma((4,)), dma((4,)), dma((2, 4, 2)), dma((4, 2)), dma((4,)), dma((4,)), dma((4,)), dma((4,)), dma((4,)), dma((4,)), dma((4, 4)), dma((5, 4)), dma((2, 3)), dma((2, 3)),
        ],
        compiler_params=pltpu.CompilerParams(collective_id=2, has_side_effects=True, vmem_limit_bytes=58 * 2**20),
        name="expert_visit",
    )(sent, cot_line, up, down.reshape(wide, D))


def attend_kernel(
    expert_total, lengths, hidden, cot, value_pick, output_pick, expert_pick, value_router, output_router, expert_router,
    gain_one, gain_two,
    key_weight_at, value_weight_at, query_weight_at, output_weight_at,
    middle_at, sent_at, normed_one_at, normed_two_at, queries_at, key_value_at, probs_at, value_all_at, attended_at,
    gates_at, slopes_at, cot_line_at, routers_at, gains_at,
    middle, sent, normed_one, normed_two, queries, key_value, probs, value_all, attended,
    gates, slopes, cot_line, routers, gains, routers_full,
    key_weight, value_weight, query_weight, output_weight, mixed, hot_turned, hot,
    fetch, leave, pair_send, pair_recv, cot_send, cot_recv, own_sem,
):
    dp, ex = lax.axis_index("dp"), lax.axis_index("expert")
    z, core = ex // 2, ex % 2
    half = z // 2
    inner = z + half * (3 - 2 * z)
    count = hidden.shape[0]
    width = HEADS * HEAD_DIM
    low = jnp.bfloat16
    length = lengths[0]
    spread = HEADS * VE
    total = expert_total
    weights = [
        pltpu.make_async_copy(source, target, fetch.at[i])
        for i, (source, target) in enumerate(
            (
                (key_weight_at, key_weight),
                (value_weight_at, value_weight),
                (query_weight_at, query_weight),
                (output_weight_at, output_weight),
            )
        )
    ]
    for made in weights:
        made.start()
    results = (
        (middle, middle_at), (sent, sent_at), (normed_one, normed_one_at), (normed_two, normed_two_at),
        (queries, queries_at), (key_value, key_value_at), (probs, probs_at), (value_all, value_all_at),
        (attended, attended_at), (gates, gates_at), (slopes, slopes_at), (cot_line, cot_line_at),
        (routers, routers_at), (gains, gains_at),
    )
    leaving = [pltpu.make_async_copy(source, target, leave.at[i]) for i, (source, target) in enumerate(results)]

    def at_z(place):
        return (dp, place * 2 + core)

    barrier = pltpu.get_barrier_semaphore()
    for k in (1, 2, 3):
        pl.semaphore_signal(barrier, inc=1, device_id=((dp + k) % 4, ex), device_id_type=MESH)

    @pl.when(z < 3)
    def _():
        pl.semaphore_signal(barrier, inc=1, device_id=at_z(z + 1), device_id_type=MESH)

    @pl.when(z > 0)
    def _():
        pl.semaphore_signal(barrier, inc=1, device_id=at_z(z - 1), device_id_type=MESH)

    pl.semaphore_wait(barrier, 4 + inner)

    def cot_copy(way, at, part, source=None):
        span = pl.ds(part * (count // 2), count // 2)
        block = cot_line.at[at, span]
        return pltpu.make_async_remote_copy(
            src_ref=block if source is None else source.at[span], dst_ref=block,
            send_sem=cot_send.at[way, at, part], recv_sem=cot_recv.at[at, part],
            device_id=at_z(z + 1 - 2 * way), device_id_type=MESH,
        )

    def pass_on(distance, part):
        @pl.when(z >= distance)
        def _():
            cot_copy(0, z - distance, part).wait_recv()

        @pl.when((z >= distance) & (z < 3))
        def _():
            cot_copy(0, z - distance, part).start()

        @pl.when(z + distance <= 3)
        def _():
            cot_copy(1, z + distance, part).wait_recv()

        @pl.when((z + distance <= 3) & (z > 0))
        def _():
            cot_copy(1, z + distance, part).start()

    for part in range(2):

        @pl.when(z < 3)
        def _():
            cot_copy(0, z, part, cot).start()

        @pl.when(z > 0)
        def _():
            cot_copy(1, z, part, cot).start()

    keep = pltpu.make_async_copy(cot, cot_line.at[z], own_sem)
    keep.start()

    def norm(field, gain):
        center = field - jnp.mean(field, axis=-1, keepdims=True)
        spread = jnp.mean(center * center, axis=-1, keepdims=True)
        return (center * lax.rsqrt(spread + EPSILON) * gain).astype(low)

    parts = (pl.ds(0, width), pl.ds(width, width))

    def pair_copy(step, part, block):
        return pltpu.make_async_remote_copy(
            src_ref=key_value.at[block, :, parts[part]], dst_ref=key_value.at[block, :, parts[part]],
            send_sem=pair_send.at[step, part], recv_sem=pair_recv.at[block, part],
            device_id=((dp + step) % 4, ex), device_id_type=MESH,
        )

    def send_part(part):
        for step in (1, 2, 3):

            @pl.when(dp + step < 4)
            def _():
                pair_copy(step, part, dp).start()

    gains[0:1, :] = gain_one[...].astype(jnp.float32).reshape(1, D)
    gains[1:2, :] = gain_two[...].astype(jnp.float32).reshape(1, D)
    normed_one[...] = norm(hidden[...].astype(jnp.float32), gains[0:1, :])
    leaving[2].start()
    weights[0].wait()
    key_value[dp, :, parts[0]] = jnp.dot(
        normed_one[...], key_weight[...], preferred_element_type=jnp.float32
    ).astype(low)
    send_part(0)

    routers_full[...] = jnp.zeros(routers_full.shape, jnp.float32)
    routers_full[0:spread, :] = value_router[...].astype(jnp.float32)
    routers_full[spread : 2 * spread, :] = output_router[...].astype(jnp.float32)
    routers_full[2 * spread : 2 * spread + total, :] = expert_router[...].astype(jnp.float32)
    routers[...] = routers_full[...].astype(low)
    leaving[12].start()
    leaving[13].start()
    hot_turned[...] = jnp.zeros(hot_turned.shape, jnp.float32)

    def mark(picks, base, size):
        place = lax.broadcasted_iota(jnp.int32, (size, count), 0)
        found = jnp.zeros((size, count), jnp.float32)
        for pick in picks:
            found = jnp.where(place == pick, 1.0, found)
        hot_turned[base : base + size, :] = found

    mark([value_pick[h, i : i + 1, :] + h * VE for h in range(HEADS) for i in range(value_pick.shape[1])], 0, spread)
    mark(
        [output_pick[h, i : i + 1, :] + h * VE for h in range(HEADS) for i in range(output_pick.shape[1])],
        spread,
        spread,
    )
    mark([expert_pick[i : i + 1, :] for i in range(expert_pick.shape[0])], 2 * spread, total)
    hot[...] = hot_turned[...].T
    sig = jax.nn.sigmoid(dot_last(normed_one[...], routers[...]))
    gates[...] = sig * hot[...]
    slopes[...] = gates[...] * (1.0 - sig)
    weights[1].wait()

    def values(n, carry):
        span = pl.ds(pl.multiple_of(n * 256, 256), 256)
        value_all[:, span] = jnp.dot(
            hidden[...], value_weight[:, span], preferred_element_type=jnp.float32
        ).astype(low)
        return carry

    lax.fori_loop(0, HEADS * VE * HEAD_DIM // 256, values, 0)
    leaving[7].start()
    for h in range(HEADS):
        row = jnp.zeros((count, HEAD_DIM), jnp.float32)
        for e in range(h * VE, (h + 1) * VE):
            row += gates[:, e : e + 1] * value_all[:, e * HEAD_DIM : (e + 1) * HEAD_DIM].astype(jnp.float32)
        key_value[dp, :, width + h * HEAD_DIM : width + (h + 1) * HEAD_DIM] = row.astype(low)
    send_part(1)
    pass_on(1, 0)

    weights[2].wait()
    queries[...] = jnp.dot(normed_one[...], query_weight[...], preferred_element_type=jnp.float32).astype(low)
    leaving[4].start()
    for block in range(4):

        @pl.when(block > dp)
        def _():
            key_value[block] = jnp.zeros((count, 2 * width), low)

    pass_on(1, 1)

    def wait_part(part):
        for block in range(3):

            @pl.when(block < dp)
            def _():
                pair_copy(1, part, block).wait_recv()

    wait_part(0)
    pair_all = key_value.reshape(4 * count, 2 * width)
    query_pos = dp * count + lax.broadcasted_iota(jnp.int32, (count, 4 * count), 0)
    key_pos = lax.broadcasted_iota(jnp.int32, (count, 4 * count), 1)
    allowed = (key_pos <= query_pos) & (key_pos < length)

    def score(h, carry):
        span = pl.ds(pl.multiple_of(h * HEAD_DIM, HEAD_DIM), HEAD_DIM)
        raw = dot_last(queries[:, span], pair_all[:, span])
        scores = jnp.where(allowed, raw * HEAD_DIM ** (-0.5), NEGATIVE)
        terms = jnp.exp(scores - jnp.max(scores, axis=-1, keepdims=True))
        probs[h] = (terms * (1.0 / jnp.sum(terms, axis=-1, keepdims=True))).astype(low)
        return carry

    lax.fori_loop(0, HEADS, score, 0)
    leaving[6].start()
    leaving[9].start()
    pass_on(2, 0)
    pass_on(2, 1)
    wait_part(1)
    leaving[5].start()

    def collect(h, carry):
        span = pl.ds(pl.multiple_of(h * HEAD_DIM, HEAD_DIM), HEAD_DIM)
        value_span = pl.ds(pl.multiple_of(width + h * HEAD_DIM, HEAD_DIM), HEAD_DIM)
        attended[:, span] = jnp.dot(probs[h], pair_all[:, value_span], preferred_element_type=jnp.float32)
        return carry

    lax.fori_loop(0, HEADS, collect, 0)
    leaving[8].start()
    for h in range(HEADS):
        row = attended[:, h * HEAD_DIM : (h + 1) * HEAD_DIM]
        for e in range(h * VE, (h + 1) * VE):
            mixed[:, e * HEAD_DIM : (e + 1) * HEAD_DIM] = (gates[:, spread + e : spread + e + 1] * row).astype(low)

    place = dp * count + lax.broadcasted_iota(jnp.int32, (count, 1), 0)
    live = jnp.where(place < length, 1.0, 0.0)
    weights[3].wait()

    def outward(n, carry):
        span = pl.ds(pl.multiple_of(n * 256, 256), 256)
        branch = jnp.dot(mixed[...], output_weight[:, span], preferred_element_type=jnp.float32)
        middle[:, span] = hidden[:, span].astype(jnp.float32) + live * branch
        return carry

    lax.fori_loop(0, D // 256, outward, 0)
    leaving[0].start()
    sent[:, :D] = middle[...].astype(low)
    normed_two[...] = norm(middle[...], gains[1:2, :])
    sig = jax.nn.sigmoid(dot_last(normed_two[...], routers[...]))
    gate = sig * hot[...] * live
    sent[:, D:] = gate.astype(low)
    lane = lax.broadcasted_iota(jnp.int32, (count, 128), 1)
    slopes[...] = jnp.where(lane < 2 * spread, slopes[...], gate * (1.0 - sig))

    for i in (1, 3, 10):
        leaving[i].start()
    pass_on(3, 0)
    pass_on(3, 1)
    keep.wait()
    leaving[11].start()
    for part in range(2):
        for step in (1, 2, 3):

            @pl.when(dp + step < 4)
            def _():
                pair_copy(step, part, dp).wait_send()

    for at in range(4):
        for part in range(2):

            @pl.when((at <= z) & (z < 3))
            def _():
                cot_copy(0, at, part).wait_send()

            @pl.when((at >= z) & (z > 0))
            def _():
                cot_copy(1, at, part).wait_send()

    for made in leaving:
        made.wait()


def attend(total, lengths, *operands):
    count = operands[0].shape[0]
    low, full = jnp.bfloat16, jnp.float32
    vmem = pl.BlockSpec(memory_space=pltpu.VMEM)
    anywhere = pl.BlockSpec(memory_space=pl.ANY)
    dma = pltpu.SemaphoreType.DMA
    width, wide = HEADS * HEAD_DIM, HEADS * VE * HEAD_DIM
    shapes = [
        ((count, D), full),
        ((count, D + 128), low),
        ((count, D), low),
        ((count, D), low),
        ((count, width), low),
        ((4, count, 2 * width), low),
        ((HEADS, count, 4 * count), low),
        ((count, wide), low),
        ((count, width), full),
        ((count, 128), full),
        ((count, 128), full),
        ((4, count, D), low),
        ((128, D), low),
        ((2, D), full),
    ]
    return pl.pallas_call(
        functools.partial(attend_kernel, total),
        out_shape=[jax.ShapeDtypeStruct(*shape) for shape in shapes],
        in_specs=[pl.BlockSpec(memory_space=pltpu.SMEM)] + [vmem] * (len(operands) - 4) + [anywhere] * 4,
        out_specs=[anywhere] * len(shapes),
        scratch_shapes=[pltpu.VMEM(*shape) for shape in shapes]
        + [pltpu.VMEM((128, D), full)]
        + [pltpu.VMEM(a.shape, a.dtype) for a in operands[-4:]]
        + [
            pltpu.VMEM((count, wide), low),
            pltpu.VMEM((128, count), full),
            pltpu.VMEM((count, 128), full),
            dma((4,)),
            dma((len(shapes),)),
            dma((4, 2)),
            dma((4, 2)),
            dma((2, 4, 2)),
            dma((4, 2)),
            dma,
        ],
        compiler_params=pltpu.CompilerParams(
            collective_id=1, has_side_effects=True, vmem_limit_bytes=58 * 2**20
        ),
        name="attend",
    )(lengths, *operands)


def backward_kernel(
    total_experts, lengths, gates, slopes, routers, gains,
    weights_at, forward_at, returned_at, middle_at, cot_at, hidden_at, normed_one_at, queries_at, key_value_at, probs_at, value_all_at,
    attended_at, normed_two_at, query_weight_at, key_weight_at, value_weight_at, output_weight_at,
    block_at, grad_at, out_query, out_key, out_value, out_output, out_small, weights_in,
    block_out, grad_in, weights, forward, returned, middle, cot, hidden, normed_one, queries, key_value, probs, value_all,
    attended, normed_two, query_weight, key_weight, value_part, output_part,
    branch, branch_turned, one_turned, hidden_turned, grad_att, grad_query, leave, arrive, grad_key,
    grad_each, grad_middle, logit_one, logit_two, small_turned, mixed,
    grads, grads_small, core_in, plane_in, last_in, forward_in,
    fetch, out_leave, part_fetch, leave_send, leave_recv, send, recv, forward_send, forward_recv, weights_send, weights_recv,
):
    dp, ex = lax.axis_index("dp"), lax.axis_index("expert")
    y, x, z, core = dp // 2, dp % 2, ex // 2, ex % 2
    count = hidden.shape[0]
    width = HEADS * HEAD_DIM
    low, full = jnp.bfloat16, jnp.float32
    length = lengths[0]
    sibling = (dp, z * 2 + 1 - core)
    beside = (y * 2 + 1 - x, ex)
    behind = ((1 - y) * 2 + x, ex)
    across = ((1 - y) * 2 + 1 - x, ex)
    line = [(dp, ((z + k) % 4) * 2 + core) for k in (1, 2, 3)]
    barrier = pltpu.get_barrier_semaphore()
    for place in (sibling, beside, behind, across, *line):
        pl.semaphore_signal(barrier, inc=1, device_id=place, device_id_type=MESH)

    held = dict(
        weights=(weights_at, weights),
        forward=(forward_at, forward),
        returned=(returned_at, returned),
        middle=(middle_at, middle),
        cot=(cot_at, cot),
        hidden=(hidden_at, hidden),
        attended=(attended_at, attended),
        key_value=(key_value_at, key_value),
        probs=(probs_at, probs),
        queries=(queries_at, queries),
        normed_one=(normed_one_at, normed_one),
        query_weight=(query_weight_at, query_weight),
        value_all=(value_all_at, value_all),
        key_weight=(key_weight_at, key_weight),
        normed_two=(normed_two_at, normed_two),
    )
    got = {
        name: pltpu.make_async_copy(source, target, fetch.at[i])
        for i, (name, (source, target)) in enumerate(held.items())
    }

    def output_copy(n):
        return pltpu.make_async_copy(
            output_weight_at.at[pl.ds(n * PIECE, PIECE)], output_part.at[n % 2], part_fetch.at[0, n % 2]
        )

    def value_copy(n):
        return pltpu.make_async_copy(
            value_weight_at.at[:, pl.ds(n * PIECE, PIECE)], value_part.at[n % 2], part_fetch.at[1, n % 2]
        )

    first_held = ("weights", "forward", "returned", "middle", "cot", "hidden")
    for name in first_held:
        got[name].start()
    for n in range(2):
        output_copy(n).start()
    for name in held:
        if name not in first_held:
            got[name].start()
    for n in range(2):
        value_copy(n).start()

    pieces = (
        [(out_output, PIECE * n, PIECE, n) for n in range(HEADS)]
        + [(out_query, 0, width, 4)]
        + [(out_value, PIECE * n, PIECE, n) for n in range(HEADS)]
        + [(out_key, 0, width, 5), (out_small, 0, 128, None)]
    )
    along_line = (0, 1)
    in_plane = [i for i in range(len(pieces)) if i not in along_line]
    x_first = {i: n % 2 == 0 for n, i in enumerate(in_plane)}

    def remote(source, target, slot, place):
        return pltpu.make_async_remote_copy(
            src_ref=source, dst_ref=target, send_sem=send.at[slot], recv_sem=recv.at[slot],
            device_id=place, device_id_type=MESH,
        )

    def add(target, source):
        target[...] = (target[...].astype(full) + source[...].astype(full)).astype(target.dtype)

    def own(i):
        slot = pieces[i][3]
        return grads_small if slot is None else grads.at[slot, :, :, :, :, columns(i)]

    def columns(i):
        return pl.ds(0, pieces[i][2])

    started = {}

    def begin(key, source, target, slot, place):
        started[key] = remote(source, target, slot, place)
        started[key].start()

    def halve_core(i):
        begin((i, 0), own(i).at[:, :, 1 - core], core_in.at[i, :, :, :, columns(i)], (i, 0), sibling)

    def halve_near(i):
        span = columns(i)
        started[i, 0].wait()
        add(core_in.at[i, :, :, :, span], own(i).at[:, :, core])
        if i in along_line:
            for k in (1, 2, 3):
                begin(
                    (i, k), core_in.at[i, :, (z + k) % 4, :, span],
                    plane_in.at[i, pl.ds(4 * k - 4, 4), :, span], (i, k), line[k - 1],
                )
            return
        for part in range(2):
            if x_first[i]:
                source = core_in.at[i, part * 2 + 1 - x, :, :, span]
            else:
                source = core_in.at[i, (1 - y) * 2 + part, :, :, span]
            target = plane_in.at[i, pl.ds(part * 4, 4), :, span]
            begin((i, 1 + part), source, target, (i, 1 + part), beside if x_first[i] else behind)

    def halve_far(i):
        span = columns(i)
        if i in along_line:
            held = core_in.at[i, :, z, :, span]
            for k in (1, 2, 3):
                started[i, k].wait()
                add(held, plane_in.at[i, pl.ds(4 * k - 4, 4), :, span])
            for part in range(2):
                begin(
                    (i, 4 + part), core_in.at[i, part * 2 + 1 - x, z, :, span],
                    last_in.at[i, part, :, span], (i, 4 + part), beside,
                )
            return
        for part in range(2):
            started[i, 1 + part].wait()
            kept = part * 2 + x if x_first[i] else y * 2 + part
            add(plane_in.at[i, pl.ds(part * 4, 4), :, span], core_in.at[i, kept, :, :, span])
        other = 1 - y if x_first[i] else 1 - x
        begin(
            (i, 3), plane_in.at[i, pl.ds(other * 4, 4), :, span], plane_in.at[i, pl.ds(8, 4), :, span],
            (i, 3), behind if x_first[i] else beside,
        )

    def spread(i):
        span = columns(i)
        if i in along_line:
            for part in range(2):
                started[i, 4 + part].wait()
                add(last_in.at[i, part, :, span], core_in.at[i, part * 2 + x, z, :, span])
            begin((i, 6), last_in.at[i, 1 - y, :, span], last_in.at[i, 2, :, span], (i, 6), behind)
            return
        started[i, 3].wait()
        add(plane_in.at[i, pl.ds(8, 4), :, span], plane_in.at[i, pl.ds((y if x_first[i] else x) * 4, 4), :, span])
        for k in (1, 2, 3):
            begin(
                (i, 3 + k), plane_in.at[i, 8 + (z + k) % 4, :, span],
                last_in.at[i, k - 1, :, span], (i, 3 + k), line[k - 1],
            )

    def finish(i):
        out, start, size, _ = pieces[i]
        span = columns(i)
        if i in along_line:
            started[i, 6].wait()
            total = last_in[i, y, :, span].astype(full) + last_in[i, 2, :, span].astype(full)
        else:
            total = plane_in[i, 8 + z, :, span].astype(full)
            for k in (1, 2, 3):
                started[i, 3 + k].wait()
                total = total + last_in[i, k - 1, :, span].astype(full)
        out[:, pl.ds(start, size)] = total

    rows_each = 64
    lane = lax.broadcasted_iota(jnp.int32, (1, 128), 1)
    for name in first_held:
        got[name].wait()
    logit_two[...] = (returned[:, D:] * slopes[...]).astype(low)

    half = z // 2
    inner = z + half * (3 - 2 * z)
    onward = 1 - 2 * half
    nearest = (z + onward, z + onward, z + onward, 0)
    farthest = (3 * (1 - half), 3 * (1 - half), z + onward, 1)
    backward = (3 * half, 3 * half, z - onward, 2)
    next_one = (2 - half, 2 - half + inner * (2 + half), z + onward, 3)

    def forward_copy(dest, slot, to, stage, part):
        span = pl.ds(part * (count // 2), count // 2)
        return pltpu.make_async_remote_copy(
            src_ref=forward.at[dest, span], dst_ref=forward_in.at[slot, span],
            send_sem=forward_send.at[stage, part], recv_sem=forward_recv.at[slot, part],
            device_id=(dp, to * 2 + core), device_id_type=MESH,
        )

    def relays(*ways):
        @pl.when(inner == 1)
        def _():
            for (dest, slot, to, stage), part in ways:
                span = pl.ds(part * (count // 2), count // 2)
                forward_copy(dest, dest, to, stage, part).wait_recv()
                add(forward.at[dest, span], forward_in.at[dest, span])
                forward_copy(dest, slot, to, stage, part).start()

    pl.semaphore_wait(barrier, 7)
    weight_copies = [
        pltpu.make_async_remote_copy(
            src_ref=weights.at[i], dst_ref=weights_in.at[i], send_sem=weights_send.at[i],
            recv_sem=weights_recv.at[i], device_id=place, device_id_type=MESH,
        )
        for i, place in enumerate((behind, beside))
    ]
    for made in weight_copies:
        made.start()

    @pl.when(inner == 0)
    def _():
        for way in (farthest, next_one, nearest):
            for part in range(2):
                forward_copy(*way, part).start()

    def live_rows(start):
        place = dp * count + start + lax.broadcasted_iota(jnp.int32, (rows_each, 1), 0)
        return jnp.where(place < length, 1.0, 0.0)

    def norm_back(field, grad, gain):
        center = field - jnp.mean(field, axis=-1, keepdims=True)
        scale = lax.rsqrt(jnp.mean(center * center, axis=-1, keepdims=True) + EPSILON)
        unit = center * scale
        part = grad * gain
        back = scale * (
            part
            - jnp.mean(part, axis=-1, keepdims=True)
            - unit * jnp.mean(part * unit, axis=-1, keepdims=True)
        )
        return back, jnp.sum(grad * unit, axis=0, keepdims=True)

    def first_rows(n, gain_sum):
        start = pl.multiple_of(n * rows_each, rows_each)
        rows = pl.ds(start, rows_each)
        grad = jnp.dot(logit_two[rows, :], routers[...], preferred_element_type=full)
        back, gain_part = norm_back(middle[rows, :], grad, gains[1:2, :])
        total = cot[rows, :].astype(full) + returned[rows, :D] + back
        grad_middle[rows, :] = total
        branch[rows, :] = (live_rows(start) * total).astype(low)
        return gain_sum + gain_part

    gain_two_sum = lax.fori_loop(0, count // rows_each, first_rows, jnp.zeros((1, D), full))
    relays((farthest, 0))

    def square(field, live, at):
        total = jnp.sum(jnp.sum(field * field, axis=1, keepdims=True) * live, axis=0, keepdims=True)
        return jnp.where(lane == at, total, 0.0)

    def last_rows(n, sums):
        start = pl.multiple_of(n * rows_each, rows_each)
        rows = pl.ds(start, rows_each)
        live = live_rows(start)
        field = middle[rows, :]
        step = forward[z, rows, :].astype(full)
        final = field + step
        block_out[rows, :] = final.astype(low)
        source = hidden[rows, :].astype(full)
        one = jnp.ones((rows_each, 1), full)
        sums += square(source, live, 0) + square(field - source, one, 1)
        sums += square(step, one, 2) + square(final, live, 3)
        return sums + jnp.where(lane == 4, jnp.sum(live, axis=0, keepdims=True), 0.0)

    def output_rows():
        for part in range(2):
            span = pl.ds(part * (count // 2), count // 2)
            forward_copy(z, z, z, 0, part).wait_recv()
            add(forward.at[z, span], forward_in.at[z, span])

            @pl.when(inner == 1)
            def _():
                forward_copy(z, 4, z, 0, part).wait_recv()
                add(forward.at[z, span], forward_in.at[4, span])

        sums = lax.fori_loop(0, count // rows_each, last_rows, jnp.zeros((1, 128), full))
        return sums

    def weight_grad(i, turned, right):
        def some(n, carry):
            rows = pl.ds(pl.multiple_of(n * 256, 256), 256)
            value = jnp.dot(turned[rows, :], right, preferred_element_type=full).astype(low)
            own(i)[n] = value.reshape(4, 2, ROWS, pieces[i][2])
            return carry

        lax.fori_loop(0, D // 256, some, 0)
        halve_core(i)

    got["attended"].wait()
    spread_count = HEADS * VE

    def head_of(c):
        return slice((c // VE) * HEAD_DIM, (c // VE + 1) * HEAD_DIM)

    logit_one[...] = jnp.zeros(logit_one.shape, full)
    grad_att[...] = jnp.zeros(grad_att.shape, full)
    for n in range(HEADS):
        output_copy(n).wait()
        for j in range(VE):
            c = VE * n + j
            grad_mixed = dot_last(branch[...], output_part[n % 2, j * HEAD_DIM : (j + 1) * HEAD_DIM, :])
            col = spread_count + c
            grad_att[:, head_of(c)] += gates[:, col : col + 1] * grad_mixed
            dots = jnp.sum(attended[:, head_of(c)] * grad_mixed, axis=1, keepdims=True)
            logit_one[:, col : col + 1] = dots * slopes[:, col : col + 1]
        if n + 2 < HEADS:
            output_copy(n + 2).start()
    relays((farthest, 1), (backward, 0))

    pair_all = key_value.reshape(4 * count, 2 * width)
    for name in ("key_value", "probs", "queries"):
        got[name].wait()

    def leave_copy(k, h):
        rows = pl.ds(h * 2 * HEAD_DIM, 2 * HEAD_DIM)
        return pltpu.make_async_remote_copy(
            src_ref=leave.at[(dp + 4 - k) % 4, rows], dst_ref=arrive.at[k - 1, rows],
            send_sem=leave_send.at[k - 1, h], recv_sem=leave_recv.at[k - 1, h],
            device_id=((dp + 4 - k) % 4, ex), device_id_type=MESH,
        )

    def head(h, carry):
        start = pl.multiple_of(h * HEAD_DIM, HEAD_DIM)
        span = pl.ds(start, HEAD_DIM)
        grad = grad_att[:, span].astype(low)
        prob = probs[h].astype(full)
        grad_prob = dot_last(grad, pair_all[:, pl.ds(width + start, HEAD_DIM)])
        dots = jnp.sum(prob * grad_prob, axis=-1, keepdims=True)
        grad_score = (prob * (grad_prob - dots) * HEAD_DIM ** (-0.5)).astype(low)
        grad_query[:, span] = jnp.dot(grad_score, pair_all[:, span], preferred_element_type=full).astype(low)
        key_part = dot_first(queries[:, span], grad_score).astype(low)
        value_part_all = dot_first(grad, probs[h]).astype(low)
        key_rows = pl.ds(pl.multiple_of(2 * h * HEAD_DIM, 2 * HEAD_DIM), HEAD_DIM)
        value_rows = pl.ds(pl.multiple_of((2 * h + 1) * HEAD_DIM, HEAD_DIM), HEAD_DIM)
        for j in range(4):
            leave[j, key_rows, :] = key_part[:, j * count : (j + 1) * count]
            leave[j, value_rows, :] = value_part_all[:, j * count : (j + 1) * count]
        for k in (1, 2, 3):

            @pl.when(dp >= k)
            def _():
                leave_copy(k, h).start()

        return carry

    lax.fori_loop(0, HEADS, head, 0)

    relays((backward, 1), (next_one, 0), (next_one, 1))
    branch_turned[...] = branch[...].T
    for n in range(HEADS):
        for j in range(VE):
            c = VE * n + j
            gate = gates[:, spread_count + c : spread_count + c + 1]
            mixed[:, j * HEAD_DIM : (j + 1) * HEAD_DIM] = (gate * attended[:, head_of(c)]).astype(low)
        weight_grad(n, branch_turned, mixed[...])
        if n:
            halve_near(n - 1)
    for name in ("normed_one", "query_weight"):
        got[name].wait()
    one_turned[...] = normed_one[...].T
    weight_grad(4, one_turned, grad_query[...])
    halve_near(3)
    hidden_turned[...] = hidden[...].T
    returned[:, :D] = dot_last(grad_query[...], query_weight[...])
    halve_near(4)
    got["value_all"].wait()

    for h in range(HEADS):
        rows = pl.ds(h * 2 * HEAD_DIM, 2 * HEAD_DIM)
        total = leave[dp, rows, :].astype(full)
        for k in (1, 2, 3):

            @pl.when(dp + k < 4)
            def _():
                leave_copy(k, h).wait_recv()

            @pl.when(dp + k >= 4)
            def _():
                arrive[k - 1, rows, :] = jnp.zeros((2 * HEAD_DIM, count), low)

            total += arrive[k - 1, rows, :].astype(full)
        turned = total.T
        grad_key[:, h * HEAD_DIM : (h + 1) * HEAD_DIM] = turned[:, :HEAD_DIM].astype(low)
        grad = turned[:, HEAD_DIM:].astype(low).astype(full)
        for c in range(h * VE, (h + 1) * VE):
            here = slice(c * HEAD_DIM, (c + 1) * HEAD_DIM)
            grad_each[:, here] = (gates[:, c : c + 1] * grad).astype(low)
            dots = jnp.sum(value_all[:, here].astype(full) * grad, axis=1, keepdims=True)
            logit_one[:, c : c + 1] = dots * slopes[:, c : c + 1]
        weight_grad(5 + h, hidden_turned, grad_each[:, h * PIECE : (h + 1) * PIECE])
        if h:
            halve_near(4 + h)
    weight_grad(9, one_turned, grad_key[...])
    halve_near(8)
    got["key_weight"].wait()
    returned[:, :D] += dot_last(grad_key[...], key_weight[...])
    halve_near(9)
    halve_far(2)
    returned[:, :D] += jnp.dot(logit_one[...].astype(low), routers[...], preferred_element_type=full)

    def first_norm(n, gain_sum):
        rows = pl.ds(pl.multiple_of(n * rows_each, rows_each), rows_each)
        back, gain_part = norm_back(hidden[rows, :].astype(full), returned[rows, :D], gains[0:1, :])
        grad_in[rows, :] = grad_middle[rows, :] + back
        return gain_sum + gain_part

    gain_one_sum = lax.fori_loop(0, count // rows_each, first_norm, jnp.zeros((1, D), full))
    halve_far(3)
    for made in weight_copies:
        made.wait()
    got["normed_two"].wait()
    small_turned[...] = dot_first(logit_one[...].astype(low), normed_one[...]) + dot_first(
        logit_two[...], normed_two[...]
    )
    small_rows = 2 * spread_count + total_experts
    small_turned[small_rows : small_rows + 1, :] = gain_one_sum
    small_turned[small_rows + 1 : small_rows + 2, :] = gain_two_sum
    sums = output_rows()
    block_leaves = pltpu.make_async_copy(block_out, block_at, out_leave.at[0])
    block_leaves.start()
    grad_leaves = pltpu.make_async_copy(grad_in, grad_at, out_leave.at[1])
    for i in range(5):
        small_turned[small_rows + 2 + i : small_rows + 3 + i, :] = jnp.broadcast_to(sums[:, i : i + 1], (1, D))
    grads_small[...] = small_turned[...].T.astype(low).reshape(grads_small.shape)
    halve_core(10)
    spread(2)
    halve_far(4)
    def value_side(n):
        value_copy(n).wait()
        grad_in[...] += dot_last(grad_each[:, n * PIECE : (n + 1) * PIECE], value_part[n % 2])
        if n + 2 < HEADS:
            value_copy(n + 2).start()
        if n == HEADS - 1:
            grad_leaves.start()

    for action, i in (
        (halve_near, 10), (spread, 3),
        (value_side, 0), (halve_far, 5), (halve_far, 0), (spread, 4), (finish, 2),
        (value_side, 1), (halve_far, 6), (spread, 0), (finish, 3), (spread, 5),
        (value_side, 2), (halve_far, 7), (finish, 4), (spread, 6),
        (value_side, 3), (finish, 0), (halve_far, 1), (halve_far, 8), (finish, 5), (spread, 7),
        (spread, 1), (halve_far, 9), (finish, 6), (spread, 8), (halve_far, 10), (finish, 7), (finish, 1), (spread, 9),
        (spread, 10), (finish, 8), (finish, 9), (finish, 10),
    ):
        action(i)
    for h in range(HEADS):
        for k in (1, 2, 3):

            @pl.when(dp >= k)
            def _():
                leave_copy(k, h).wait_send()

    for part in range(2):
        forward_copy(z, 0, z, 1, part).wait_send()
        forward_copy(z, 0, z, 3, part).wait_send()

        @pl.when(inner == 0)
        def _():
            forward_copy(z, 0, z, 0, part).wait_send()

        @pl.when(inner == 1)
        def _():
            forward_copy(z, 0, z, 2, part).wait_send()

    block_leaves.wait()
    grad_leaves.wait()


def backward(total_experts, lengths, gates, slopes, routers, gains, *arrays):
    low, full = jnp.bfloat16, jnp.float32
    count = gates.shape[0]
    width, wide = HEADS * HEAD_DIM, HEADS * VE * HEAD_DIM
    vmem = pl.BlockSpec(memory_space=pltpu.VMEM)
    anywhere = pl.BlockSpec(memory_space=pl.ANY)
    dma = pltpu.SemaphoreType.DMA
    whole = [pltpu.VMEM(a.shape, a.dtype) for a in arrays[:15]]
    n = 11
    return pl.pallas_call(
        functools.partial(backward_kernel, total_experts),
        out_shape=[
            jax.ShapeDtypeStruct((count, D), low),
            jax.ShapeDtypeStruct((count, D), full),
            jax.ShapeDtypeStruct((ROWS, width), full),
            jax.ShapeDtypeStruct((ROWS, width), full),
            jax.ShapeDtypeStruct((ROWS, wide), full),
            jax.ShapeDtypeStruct((ROWS, wide), full),
            jax.ShapeDtypeStruct((ROWS, 128), full),
            jax.ShapeDtypeStruct(arrays[0].shape, low),
        ],
        in_specs=[pl.BlockSpec(memory_space=pltpu.SMEM)] + [vmem] * 4 + [anywhere] * len(arrays),
        out_specs=[anywhere] * 2 + [vmem] * 6,
        scratch_shapes=[pltpu.VMEM((count, D), low), pltpu.VMEM((count, D), full)]
        + whole
        + [
            pltpu.VMEM((2, D, PIECE), low),
            pltpu.VMEM((2, PIECE, D), low),
            pltpu.VMEM((count, D), low),
            pltpu.VMEM((D, count), low),
            pltpu.VMEM((D, count), low),
            pltpu.VMEM((D, count), low),
            pltpu.VMEM((count, width), full),
            pltpu.VMEM((count, width), low),
            pltpu.VMEM((4, 2 * width, count), low),
            pltpu.VMEM((3, 2 * width, count), low),
            pltpu.VMEM((count, width), low),
            pltpu.VMEM((count, wide), low),
            pltpu.VMEM((count, D), full),
            pltpu.VMEM((count, 128), full),
            pltpu.VMEM((count, 128), low),
            pltpu.VMEM((128, D), full),
            pltpu.VMEM((count, PIECE), low),
            pltpu.VMEM((6, 4, 4, 2, ROWS, PIECE), low),
            pltpu.VMEM((4, 4, 2, ROWS, 128), low),
            pltpu.VMEM((n, 4, 4, ROWS, PIECE), low),
            pltpu.VMEM((n, 12, ROWS, PIECE), low),
            pltpu.VMEM((n, 3, ROWS, PIECE), low),
            pltpu.VMEM((5, count, D), low),
            dma((15,)),
            dma((2,)),
            dma((2, 2)),
            dma((3, HEADS)),
            dma((3, HEADS)),
            dma((n, 7)),
            dma((n, 7)),
            dma((4, 2)),
            dma((5, 2)),
            dma((2,)),
            dma((2,)),
        ],
        compiler_params=pltpu.CompilerParams(
            collective_id=3, has_side_effects=True, vmem_limit_bytes=62 * 2**20
        ),
        name="backward",
    )(lengths, gates, slopes, routers, gains, *arrays)


def expert_visit(sent, cotangent, expert_up, expert_down):
    local_experts = expert_up.shape[0]
    group = lax.axis_index("expert")
    cot_all = lax.all_gather(cotangent, "expert", axis=0, tiled=True)
    sent_all = lax.all_gather(sent, "expert", axis=0, tiled=True)
    rows_all = sent_all[:, :D]
    total_experts = sent.shape[1] - D
    gate_all = lax.dynamic_slice_in_dim(
        sent_all[:, D:], group * local_experts, local_experts, 1
    ).astype(jnp.float32).T[:, :, None]
    preact = jnp.einsum("td,xdf->xtf", rows_all, expert_up, preferred_element_type=jnp.float32)
    pre_sig = jax.nn.sigmoid(preact)
    hidden = preact * pre_sig
    back = jnp.einsum("td,xfd->xtf", cot_all, expert_down, preferred_element_type=jnp.float32)
    gate_grad = jnp.sum(hidden * back, axis=2).T
    gated = (gate_all * hidden).astype(jnp.bfloat16)
    grad_pre = (gate_all * back * (pre_sig * (1.0 + preact * (1.0 - pre_sig)))).astype(jnp.bfloat16)
    partial_out = jnp.einsum("xtf,xfd->td", gated, expert_down, preferred_element_type=jnp.float32)
    partial_grad = jnp.einsum("xtf,xdf->td", grad_pre, expert_up, preferred_element_type=jnp.float32)
    wide_grad = lax.dynamic_update_slice_in_dim(
        jnp.zeros((gate_grad.shape[0], total_experts), jnp.bfloat16),
        gate_grad.astype(jnp.bfloat16),
        group * local_experts,
        1,
    )
    returned = lax.psum_scatter(
        jnp.concatenate(
            [partial_out.astype(jnp.bfloat16), partial_grad.astype(jnp.bfloat16), wide_grad], axis=1
        ),
        "expert",
        scatter_dimension=0,
        tiled=True,
    )
    grad_down = jnp.einsum("xtf,td->xfd", gated, cot_all, preferred_element_type=jnp.float32)
    grad_up = jnp.einsum("td,xtf->xdf", rows_all, grad_pre, preferred_element_type=jnp.float32)
    return returned, grad_up, grad_down


def shards(
    hidden_in,
    lengths,
    value_pick,
    output_pick,
    expert_pick,
    query_weight,
    key_weight,
    value_weight,
    output_weight,
    value_router,
    output_router,
    expert_router,
    attention_gain,
    feedforward_gain,
    expert_up,
    expert_down,
    cotangent,
):
    row_count = hidden_in.shape[1]
    total_experts = expert_router.shape[1]
    input_low = hidden_in[0]
    input_full = input_low.astype(jnp.float32)
    length = lengths[0]
    query_pos = lax.axis_index("dp") * row_count + jnp.arange(row_count, dtype=jnp.int32)
    live_mask = (query_pos < length).astype(jnp.float32)[:, None]
    gain_one = attention_gain.astype(jnp.float32)
    gain_two = feedforward_gain.astype(jnp.float32)
    normed_one = layer_norm(input_full, gain_one)
    normed_low = normed_one.astype(jnp.bfloat16)
    queries = low_dot(normed_low, query_weight).astype(jnp.bfloat16)
    key_local = low_dot(normed_low, key_weight).astype(jnp.bfloat16)
    value_sig = jax.nn.sigmoid(low_dot(normed_low, value_router)).reshape(row_count, HEADS, VE)
    value_hot = choose(value_pick[0], VE)
    value_gate = value_sig * value_hot
    value_all = low_dot(input_low, value_weight).reshape(row_count, HEADS, VE, HEAD_DIM)
    value_local = (
        jnp.sum(value_gate[..., None] * value_all, axis=2)
        .astype(jnp.bfloat16)
        .reshape(row_count, HEADS * HEAD_DIM)
    )
    key_all, value_rows = (
        lax.all_gather(key_local, "dp", axis=0, tiled=True),
        lax.all_gather(value_local, "dp", axis=0, tiled=True),
    )
    query_heads = queries.reshape(row_count, HEADS, HEAD_DIM)
    key_heads = key_all.reshape(-1, HEADS, HEAD_DIM)
    value_heads = value_rows.reshape(-1, HEADS, HEAD_DIM)
    soft_probs = attention_probs(query_heads, key_heads, query_pos, length)
    attended = jnp.einsum(
        "hqk,khd->qhd",
        soft_probs.astype(jnp.bfloat16),
        value_heads,
        preferred_element_type=jnp.float32,
    )
    output_sig = jax.nn.sigmoid(low_dot(normed_low, output_router)).reshape(row_count, HEADS, VE)
    output_hot = choose(output_pick[0], VE)
    output_gate = output_sig * output_hot
    mixed = (
        (output_gate[..., None] * attended[:, :, None, :])
        .astype(jnp.bfloat16)
        .reshape(row_count, HEADS * VE * HEAD_DIM)
    )
    attention_out = live_mask * low_dot(mixed, output_weight)
    middle = input_full + attention_out
    normed_two = layer_norm(middle, gain_two)
    normed_two_low = normed_two.astype(jnp.bfloat16)
    router_sig = jax.nn.sigmoid(low_dot(normed_two_low, expert_router))
    hot = jnp.any(
        expert_pick[0][:, :, None] == jnp.arange(total_experts, dtype=jnp.int32), axis=1
    ).astype(jnp.float32)
    picked_hot = hot * live_mask
    expert_gate = router_sig * picked_hot
    middle_low = middle.astype(jnp.bfloat16)
    sent = jnp.concatenate([middle_low, expert_gate.astype(jnp.bfloat16)], axis=1)
    groups = lax.axis_size("expert")
    rounds = max(1, groups // 8)

    def visit(grads, item):
        returned, grad_up, grad_down = expert_visit(*item, expert_up, expert_down)
        return (grads[0] + grad_up, grads[1] + grad_down), returned

    zeros = jnp.zeros(expert_up.shape, jnp.float32), jnp.zeros(expert_down.shape, jnp.float32)
    (up_grad, down_grad), returned = lax.scan(
        visit,
        zeros,
        (
            sent.reshape(rounds, -1, sent.shape[1]),
            cotangent[0].reshape(rounds, -1, D),
        ),
    )
    returned = returned.reshape(row_count, -1).astype(jnp.float32)
    up_grad = lax.psum_scatter(
        up_grad.astype(jnp.bfloat16), "dp", scatter_dimension=1, tiled=True
    ).astype(jnp.float32)
    down_grad = lax.psum_scatter(
        down_grad.astype(jnp.bfloat16), "dp", scatter_dimension=2, tiled=True
    ).astype(jnp.float32)
    feedforward_out = returned[:, :D]
    final_rows = middle + feedforward_out
    sums = jnp.stack(
        [
            jnp.sum(live_mask * input_full * input_full),
            jnp.sum(attention_out * attention_out),
            jnp.sum(feedforward_out * feedforward_out),
            jnp.sum(live_mask * final_rows * final_rows),
            jnp.sum(live_mask),
        ]
    )
    grad_final = cotangent[0].astype(jnp.float32)
    grad_middle = grad_final + returned[:, D : 2 * D]
    grad_logit = (
        returned[:, 2 * D :] * picked_hot * router_sig * (1.0 - router_sig)
    ).astype(jnp.bfloat16)
    grad_expert_router = low_dot(normed_two_low.T, grad_logit)
    grad_normed_two = low_dot(grad_logit, expert_router.T)
    unused_two, norm_two_back = jax.vjp(layer_norm, middle, gain_two)
    grad_middle_norm, grad_gain_two = norm_two_back(grad_normed_two)
    grad_middle = grad_middle + grad_middle_norm
    grad_branch = (live_mask * grad_middle).astype(jnp.bfloat16)
    grad_mixed = jnp.einsum(
        "td,md->tm", grad_branch, output_weight, preferred_element_type=jnp.float32
    ).reshape(row_count, HEADS, VE, HEAD_DIM)
    grad_output_weight = jnp.einsum(
        "td,tm->dm", grad_branch, mixed, preferred_element_type=jnp.float32
    )
    grad_attended = jnp.sum(output_gate[..., None] * grad_mixed, axis=2)
    grad_output_logit = (
        jnp.sum(attended[:, :, None, :] * grad_mixed, axis=3)
        * output_hot
        * output_sig
        * (1.0 - output_sig)
    ).reshape(row_count, HEADS * VE)
    grad_attended_low = grad_attended.astype(jnp.bfloat16)
    grad_probs = jnp.einsum(
        "qhd,khd->hqk", grad_attended_low, value_heads, preferred_element_type=jnp.float32
    )
    row_dot = jnp.sum(soft_probs * grad_probs, axis=-1, keepdims=True)
    grad_scores = (soft_probs * (grad_probs - row_dot) * HEAD_DIM ** (-0.5)).astype(jnp.bfloat16)
    grad_query = (
        jnp.einsum("hqk,khd->qhd", grad_scores, key_heads, preferred_element_type=jnp.float32)
        .astype(jnp.bfloat16)
        .reshape(row_count, HEADS * HEAD_DIM)
    )
    grad_key_all = jnp.einsum(
        "hqk,qhd->khd", grad_scores, query_heads, preferred_element_type=jnp.float32
    ).reshape(-1, HEADS * HEAD_DIM)
    grad_value_rows = jnp.einsum(
        "hqk,qhd->khd",
        soft_probs.astype(jnp.bfloat16),
        grad_attended_low,
        preferred_element_type=jnp.float32,
    ).reshape(-1, HEADS * HEAD_DIM)
    grad_key_sum, grad_value_sum = (
        lax.psum_scatter(
            grad_key_all.astype(jnp.bfloat16), "dp", scatter_dimension=0, tiled=True
        ).astype(jnp.float32),
        lax.psum_scatter(
            grad_value_rows.astype(jnp.bfloat16), "dp", scatter_dimension=0, tiled=True
        ).astype(jnp.float32),
    )
    grad_key = grad_key_sum.astype(jnp.bfloat16)
    grad_value_low = (
        grad_value_sum.astype(jnp.bfloat16)
        .astype(jnp.float32)
        .reshape(row_count, HEADS, 1, HEAD_DIM)
    )
    grad_value_each = (
        (value_gate[..., None] * grad_value_low)
        .astype(jnp.bfloat16)
        .reshape(row_count, HEADS * VE * HEAD_DIM)
    )
    grad_value_logit = (
        jnp.sum(value_all * grad_value_low, axis=3) * value_hot * value_sig * (1.0 - value_sig)
    ).reshape(row_count, HEADS * VE)
    grad_value_weight = jnp.einsum(
        "td,tm->dm", input_low, grad_value_each, preferred_element_type=jnp.float32
    )
    grad_query_weight = jnp.einsum(
        "td,tm->dm", normed_low, grad_query, preferred_element_type=jnp.float32
    )
    grad_key_weight = jnp.einsum(
        "td,tm->dm", normed_low, grad_key, preferred_element_type=jnp.float32
    )
    grad_value_logit = grad_value_logit.astype(jnp.bfloat16)
    grad_output_logit = grad_output_logit.astype(jnp.bfloat16)
    grad_value_router = low_dot(normed_low.T, grad_value_logit)
    grad_output_router = low_dot(normed_low.T, grad_output_logit)
    grad_normed_one = (
        jnp.einsum("tm,dm->td", grad_query, query_weight, preferred_element_type=jnp.float32)
        + jnp.einsum("tm,dm->td", grad_key, key_weight, preferred_element_type=jnp.float32)
        + low_dot(grad_value_logit, value_router.T)
        + low_dot(grad_output_logit, output_router.T)
    )
    unused_one, norm_one_back = jax.vjp(layer_norm, input_full, gain_one)
    grad_input_norm, grad_gain_one = norm_one_back(grad_normed_one)
    grad_input = (
        grad_middle
        + jnp.einsum("tm,dm->td", grad_value_each, value_weight, preferred_element_type=jnp.float32)
        + grad_input_norm
    )
    small_grads = jnp.concatenate(
        [
            grad_value_router,
            grad_output_router,
            grad_expert_router,
            grad_gain_one[:, None],
            grad_gain_two[:, None],
        ],
        axis=1,
    )
    small_count = small_grads.shape[1]
    small_grads = jnp.pad(small_grads, ((0, 0), (0, -small_count % 128)))
    low_grads = [
        part.astype(jnp.bfloat16)
        for part in (
            grad_query_weight,
            grad_key_weight,
            grad_value_weight,
            grad_output_weight,
            small_grads,
        )
    ]
    summed = lax.psum_scatter(
        jnp.concatenate(low_grads, axis=1), ("dp", "expert"), scatter_dimension=0, tiled=True
    ).astype(jnp.float32)
    dense_grads = jnp.split(summed, [512, 1024, 3584, 6144], axis=1)
    total_sums = lax.psum(sums, ("dp", "expert"))
    residual_norms = jnp.sqrt(total_sums[:4] / (total_sums[4] * D))
    small = dense_grads[4]
    router_end = 2 * HEADS * VE + expert_router.shape[1]
    dense_grads = [
        dense_grads[0],
        dense_grads[1],
        dense_grads[2],
        dense_grads[3].T,
        small[:, : HEADS * VE],
        small[:, HEADS * VE : 2 * HEADS * VE],
        small[:, 2 * HEADS * VE : router_end],
        small[:, router_end],
        small[:, router_end + 1],
    ]
    return (
        final_rows.astype(jnp.bfloat16)[None],
        grad_input[None],
        dense_grads[0],
        dense_grads[1],
        dense_grads[2],
        dense_grads[3],
        dense_grads[4],
        dense_grads[5],
        dense_grads[6],
        dense_grads[7],
        dense_grads[8],
        up_grad,
        down_grad,
        residual_norms,
    )


def deliver_kernel(total, small, weights_kept_at, weights_in_at, *refs):
    weights_kept, weights_in, up_out, down_out, weights_sem = refs[-5:]
    refs = refs[:-5]
    count = (len(refs) - 9) // 3
    sources, targets = refs[:count], refs[count : 2 * count]
    value_out, output_out, expert_out, gains_out, norms_out, up_at, down_at = refs[2 * count : 2 * count + 7]
    held = refs[2 * count + 7 : -2]
    inward, outward = refs[-2:]
    arrived = [pltpu.make_async_copy(a, b, inward.at[i]) for i, (a, b) in enumerate(zip(sources, held))]
    left = [pltpu.make_async_copy(a, b, outward.at[i]) for i, (a, b) in enumerate(zip(held, targets))]
    weights = [
        pltpu.make_async_copy(weights_kept_at, weights_kept, weights_sem.at[0]),
        pltpu.make_async_copy(weights_in_at, weights_in, weights_sem.at[1]),
    ]
    summed = [
        pltpu.make_async_copy(up_out, up_at, weights_sem.at[2]),
        pltpu.make_async_copy(down_out, down_at, weights_sem.at[3]),
    ]
    for made in arrived + weights:
        made.start()
    spread = HEADS * VE
    turned = jnp.concatenate([small[...], jnp.zeros((128 - ROWS, 128), jnp.float32)]).T
    value_out[...] = turned[:spread, :ROWS]
    output_out[...] = turned[spread : 2 * spread, :ROWS]
    expert_out[...] = small[:, 2 * spread : 2 * spread + total]
    gains_out[...] = turned[2 * spread + total : 2 * spread + total + 2, :ROWS]
    row = small[0:1, :]
    first = 2 * spread + total + 2
    norms_out[...] = jnp.sqrt(row[:, first : first + 4] / (row[:, first + 4 : first + 5] * D))
    for one, other in zip(arrived, left):
        one.wait()
        other.start()
    for made in weights:
        made.wait()
    for e in range(up_out.shape[0]):
        rows = slice(e * HEAD_DIM, (e + 1) * HEAD_DIM)
        up_sum, down_sum = [
            weights_kept[i, rows, :].astype(jnp.float32) + weights_in[i, rows, :].astype(jnp.float32)
            for i in range(2)
        ]
        up_out[e] = up_sum.T
        down_out[e] = down_sum
    for made in summed:
        made.start()
    for made in left + summed:
        made.wait()


def deliver(total, small, weights_kept, weights_in, *arrays):
    experts = weights_in.shape[1] // HEAD_DIM
    full = jnp.float32
    vmem = pl.BlockSpec(memory_space=pltpu.VMEM)
    anywhere = pl.BlockSpec(memory_space=pl.ANY)
    spread = HEADS * VE
    return pl.pallas_call(
        functools.partial(deliver_kernel, total),
        out_shape=[jax.ShapeDtypeStruct(a.shape, a.dtype) for a in arrays]
        + [
            jax.ShapeDtypeStruct((spread, ROWS), full),
            jax.ShapeDtypeStruct((spread, ROWS), full),
            jax.ShapeDtypeStruct((ROWS, total), full),
            jax.ShapeDtypeStruct((2, ROWS), full),
            jax.ShapeDtypeStruct((1, 4), full),
            jax.ShapeDtypeStruct((experts, D // 4, HEAD_DIM), full),
            jax.ShapeDtypeStruct((experts, HEAD_DIM, D // 4), full),
        ],
        in_specs=[vmem] + [anywhere] * (2 + len(arrays)),
        out_specs=[anywhere] * len(arrays) + [vmem] * 5 + [anywhere] * 2,
        scratch_shapes=[pltpu.VMEM(a.shape, a.dtype) for a in arrays]
        + [pltpu.SemaphoreType.DMA((len(arrays),))] * 2
        + [
            pltpu.VMEM(weights_kept.shape, weights_kept.dtype),
            pltpu.VMEM(weights_in.shape, weights_in.dtype),
            pltpu.VMEM((experts, D // 4, HEAD_DIM), full),
            pltpu.VMEM((experts, HEAD_DIM, D // 4), full),
            pltpu.SemaphoreType.DMA((4,)),
        ],
        compiler_params=pltpu.CompilerParams(vmem_limit_bytes=63 * 2**20),
        name="deliver",
    )(small, weights_kept, weights_in, *arrays)


def shards_fast(
    hidden_in,
    lengths,
    value_pick,
    output_pick,
    expert_pick,
    query_weight,
    key_weight,
    value_weight,
    output_weight,
    value_router,
    output_router,
    expert_router,
    attention_gain,
    feedforward_gain,
    expert_up,
    expert_down,
    cotangent,
):
    total = expert_router.shape[1]
    (
        middle,
        sent,
        normed_one,
        normed_two,
        queries,
        key_value,
        probs,
        value_all,
        attended,
        gates,
        slopes,
        cot_line,
        routers,
        gains,
    ) = attend(
        total,
        lengths,
        hidden_in[0],
        cotangent[0],
        value_pick[0].transpose(1, 2, 0),
        output_pick[0].transpose(1, 2, 0),
        expert_pick[0].T,
        value_router.T,
        output_router.T,
        expert_router.T,
        attention_gain,
        feedforward_gain,
        key_weight,
        value_weight,
        query_weight,
        output_weight,
    )
    returned, weights, weights_kept, forward = expert_kernel_visit(sent, cot_line, expert_up, expert_down)
    block_out, grad_input, grad_query, grad_key, grad_value, grad_output, small, weights_in = backward(
        total,
        lengths,
        gates,
        slopes,
        routers,
        gains,
        weights,
        forward,
        returned,
        middle,
        cotangent[0],
        hidden_in[0],
        normed_one,
        queries,
        key_value,
        probs,
        value_all,
        attended,
        normed_two,
        query_weight,
        key_weight,
        value_weight,
        output_weight,
    )
    kept = (block_out, grad_input, grad_query, grad_key, grad_value, grad_output)
    delivered = deliver(total, small, weights_kept, weights_in, *kept)
    block_out, grad_input, grad_query, grad_key, grad_value, grad_output = delivered[:6]
    value_small, output_small, expert_small, gain_grads, norms, up_grad, down_grad = delivered[6:]
    return (
        block_out[None],
        grad_input[None],
        grad_query,
        grad_key,
        grad_value,
        grad_output.T,
        value_small.T,
        output_small.T,
        expert_small,
        gain_grads[0],
        gain_grads[1],
        up_grad,
        down_grad,
        norms[0],
    )


def solution(mesh):
    placed = (
        P("expert", "dp", None),
        P("expert"),
        P("expert", "dp", None, None),
        P("expert", "dp", None, None),
        P("expert", "dp", None),
        P(),
        P(),
        P(),
        P(),
        P(),
        P(),
        P(),
        P(),
        P(),
        P("expert", None, None),
        P("expert", None, None),
        P("expert", "dp", None),
    )
    small_mesh = mesh.shape["dp"] == 4 and mesh.shape["expert"] == 8
    return jax.shard_map(
        shards_fast if small_mesh else shards,
        mesh=mesh,
        in_specs=placed,
        out_specs=(
            P("expert", "dp", None),
            P("expert", "dp", None),
            P(("dp", "expert"), None),
            P(("dp", "expert"), None),
            P(("dp", "expert"), None),
            P(None, ("dp", "expert")),
            P(("dp", "expert"), None),
            P(("dp", "expert"), None),
            P(("dp", "expert"), None),
            P(("dp", "expert")),
            P(("dp", "expert")),
            P("expert", "dp", None),
            P("expert", None, "dp"),
            P(),
        ),
        check_vma=False,
    )
```
